32 devices in a mesh: ctx: 8 (over y, x, core), fsdp: 4 (over z).
Axes of the slice: x: 2, y: 2, z: 4, core: 2. Of those that a mesh axis runs over, the one named last changes fastest.
Arguments:
- query_mr: bfloat16 [1024, 4096], P('ctx', 'fsdp'), may hold values from -6 to 6
- key_mr: bfloat16 [1024, 4096], P('ctx', 'fsdp'), may hold values from -6 to 6
- value_mr: bfloat16 [1024, 4096], P('ctx', 'fsdp'), may hold values from -6 to 6
- query_li: bfloat16 [1024, 4096], P('ctx', 'fsdp'), may hold values from -6 to 6
- key_li: bfloat16 [1024, 4096], P('ctx', 'fsdp'), may hold values from -6 to 6
- mr_taps: float32 [128, 4096], P(None, 'fsdp'), may hold values from -0.5 to 0.5
- li_time: float32 [16, 4096], P(None, 'fsdp'), may hold values from 30 to 20480
- li_residue: float32 [16, 4096], P(None, 'fsdp'), may hold values from -5 to 5
- li_skip: float32 [4096], P('fsdp'), may hold values from -6 to 6
- out_weight: bfloat16 [4096, 4096], P('ctx', 'fsdp'), may hold values from -0.09375 to 0.09375
- cotangent: bfloat16 [1024, 4096], P('ctx', 'fsdp'), may hold values from -6 to 6
Outputs:
- output: float32 [1024, 4096], P('ctx', 'fsdp')
- grad_query_mr: float32 [1024, 4096], P('ctx', 'fsdp')
- grad_key_mr: float32 [1024, 4096], P('ctx', 'fsdp')
- grad_value_mr: float32 [1024, 4096], P('ctx', 'fsdp')
- grad_query_li: float32 [1024, 4096], P('ctx', 'fsdp')
- grad_key_li: float32 [1024, 4096], P('ctx', 'fsdp')
- grad_taps: float32 [128, 4096], P(None, 'fsdp')
- grad_weight: float32 [4096, 4096], P('ctx', 'fsdp')
The draws below stay inside these ranges and needn't reach their ends.
All inputs are finite; a program needn't handle non-finite values.
Results may differ from the reference program's by a relative error of at most 0.014.
Values may be sent and summed in bfloat16 or wider, within the bound.
No kernel may reach another device: no remote copies, remote signals or barrier semaphores. Data moves between devices by JAX's collectives and lax.ppermute only.
A program may use at most 128 MiB of HBM per device.

```python
import math
import jax
import jax.numpy as jnp
from jax import lax

WIDTH = 4096
CHANNELS = 4096
TAPS = 128
MODES = 16
SEQ = 1024
N_FSDP = 4


def draw_li_time(key, part):
    choose_key, fast_key, middle_key, slow_key = jax.random.split(key, 4)
    array_shape = (MODES, CHANNELS)
    quick_share = 0.2
    middle_share = 0.3
    quick_times = 30.0 + 20.0 * jax.random.uniform(fast_key, array_shape, jnp.float32)
    middle_top = 0.5 * SEQ
    middle_span = jnp.log(jnp.float32(middle_top / 50.0))
    middle_times = jnp.clip(50.0 * jnp.exp(middle_span * jax.random.uniform(middle_key, array_shape, jnp.float32)), 50.0, middle_top)
    slow_times = jnp.clip(0.5 * SEQ * jnp.exp(3.6888794541139363 * jax.random.uniform(slow_key, array_shape, jnp.float32)), 0.5 * SEQ, 20.0 * SEQ)
    chooser = jax.random.uniform(choose_key, array_shape, jnp.float32)
    picked = jnp.where(chooser < quick_share, quick_times, jnp.where(chooser < quick_share + middle_share, middle_times, slow_times))
    return jnp.clip(picked, 30.0, 20.0 * SEQ).astype(jnp.float32)


def steps_of(stream_key, shape, cuts, low, high):
    level = 1.0
    for axis_at, shards_of in cuts:
        heights = jax.random.uniform(jax.random.fold_in(jax.random.fold_in(stream_key, 6), axis_at), (shards_of,), jnp.float32, low / len(cuts), high / len(cuts))
        level = level * jnp.repeat(jnp.exp(heights), shape[axis_at] // shards_of).reshape((-1,) + (1,) * (len(shape) - 1 - axis_at))
    return level


def scatter_about(key, shape, deviation, reach, cuts=(), kind=jnp.bfloat16):
    loudness = steps_of(key, shape, cuts, -0.22, 0.18) if cuts else 1.0
    values = jax.random.normal(key, shape, jnp.float32) * deviation * loudness
    return jnp.minimum(jnp.maximum(values, -reach), reach).astype(kind)


def setup_inputs(seed: int = 0) -> dict:
    splits = jax.random.split(jax.random.key(seed), 12)
    return {
        "query_mr": scatter_about(splits[0], (SEQ, CHANNELS), 1.0, 6.0, ((0, 8), (1, 4))),
        "key_mr": scatter_about(splits[1], (SEQ, CHANNELS), 1.0, 6.0, ((0, 8), (1, 4))),
        "value_mr": scatter_about(splits[2], (SEQ, CHANNELS), 1.0, 6.0, ((0, 8), (1, 4))),
        "query_li": scatter_about(splits[3], (SEQ, CHANNELS), 1.0, 6.0, ((0, 8), (1, 4))),
        "key_li": scatter_about(splits[4], (SEQ, CHANNELS), 1.0, 6.0, ((0, 8), (1, 4))),
        "mr_taps": scatter_about(splits[5], (TAPS, CHANNELS), TAPS ** -0.5, 0.5, ((1, 4),), jnp.float32),
        "li_time": draw_li_time(jax.random.fold_in(splits[11], 71), 0),
        "li_residue": scatter_about(splits[7], (MODES, CHANNELS), 0.35, 5.0, ((1, 4),), jnp.float32),
        "li_skip": scatter_about(splits[8], (CHANNELS,), 0.5, 6.0, ((0, 4),), jnp.float32),
        "out_weight": scatter_about(splits[9], (WIDTH, CHANNELS), CHANNELS ** -0.5, 0.09375, ((0, 8), (1, 4))),
        "cotangent": scatter_about(splits[10], (SEQ, WIDTH), 1.0, 6.0, ((0, 8), (1, 4))),
    }


def shifted_taps(padded, tap_weights, row_count, backward):
    rim_size = tap_weights.shape[0] - 1

    def one_tap(tap_index, running):
        tap_index = jnp.asarray(tap_index).astype(jnp.int32)
        if backward:
            first_row = tap_index
        else:
            first_row = (rim_size - tap_index).astype(jnp.int32)
        window = lax.dynamic_slice_in_dim(padded, first_row, row_count, 0).astype(jnp.float32)
        weight_row = lax.dynamic_index_in_dim(tap_weights, tap_index, 0, keepdims=False)
        return running + weight_row[None, :] * window
    return lax.fori_loop(0, tap_weights.shape[0], one_tap, jnp.zeros((row_count, padded.shape[1]), jnp.float32))

def tap_gradient(grad_conv, padded, tap_count):
    row_count = grad_conv.shape[0]
    rim_size = tap_count - 1

    def one_tap(tap_index):
        first_row = (rim_size - tap_index).astype(jnp.int32)
        window = lax.dynamic_slice_in_dim(padded, first_row, row_count, 0).astype(jnp.float32)
        return lax.optimization_barrier(jnp.sum(grad_conv * window, axis=0))
    return lax.map(one_tap, jnp.arange(tap_count).astype(jnp.int32))

def causal_conv(signal, kernel):
    length = signal.shape[0]
    doubled = 2 * length
    spectrum = jnp.fft.rfft(signal, n=doubled, axis=0) * jnp.fft.rfft(kernel, n=doubled, axis=0)
    return jnp.fft.irfft(spectrum, n=doubled, axis=0)[:length]

def long_filter(li_time, li_residue, length):
    rate = 1.0 / li_time
    mode_coef = li_residue * jnp.sqrt(-jnp.expm1(-2.0 * rate))
    places = jnp.arange(length).astype(jnp.float32)
    kernel = jnp.zeros((length, li_time.shape[1]), jnp.float32)
    for mode_index in range(li_time.shape[0]):
        kernel = kernel + mode_coef[mode_index][None, :] * jnp.exp(-rate[mode_index][None, :] * places[:, None])
    return kernel

def reference(query_mr, key_mr, value_mr, query_li, key_li, mr_taps, li_time, li_residue, li_skip, out_weight, cotangent):
    groups = N_FSDP
    chan_dev = CHANNELS // groups
    length = query_mr.shape[0]
    rim_size = mr_taps.shape[0] - 1
    grad_scale = 1.0 / math.sqrt(length)

    def split_cols(array):
        return array.reshape(array.shape[0], groups, chan_dev).transpose(1, 0, 2)

    def merge_cols(array):
        return array.transpose(1, 0, 2).reshape(array.shape[1], groups * chan_dev)
    stacked = (split_cols(query_mr), split_cols(key_mr), split_cols(value_mr), split_cols(query_li), split_cols(key_li), split_cols(mr_taps), split_cols(li_time), split_cols(li_residue), split_cols(out_weight), li_skip.reshape(groups, chan_dev))

    def one_group(running, pieces):
        query_mr, key_mr, value_mr, query_li, key_li, mr_taps, li_time, li_residue, out_weight, li_skip = pieces
        mr_product = (key_mr.astype(jnp.float32) * value_mr.astype(jnp.float32)).astype(jnp.bfloat16)
        padded = jnp.concatenate([jnp.zeros((rim_size, chan_dev), jnp.bfloat16), mr_product], axis=0)
        mr_conv = shifted_taps(padded, mr_taps, length, False)
        mixed_mr = (query_mr.astype(jnp.float32) * mr_conv).astype(jnp.bfloat16)
        li_input = (key_li.astype(jnp.float32) * mixed_mr.astype(jnp.float32)).astype(jnp.bfloat16)
        kernel = long_filter(li_time, li_residue, length)
        li_signal = li_input.astype(jnp.float32)
        li_out = li_skip[None, :] * li_signal + causal_conv(li_signal, kernel)
        mixed_li = (query_li.astype(jnp.float32) * li_out).astype(jnp.bfloat16)
        group_part = lax.dot_general(mixed_li, out_weight, (((1,), (1,)), ((), ())), preferred_element_type=jnp.float32)
        running = running + group_part
        grad_mixed = jnp.dot(cotangent, out_weight, preferred_element_type=jnp.float32)
        grad_query_li = grad_mixed * li_out
        grad_li_out = grad_mixed * query_li.astype(jnp.float32)
        grad_li_input = li_skip[None, :] * grad_li_out + causal_conv(grad_li_out[::-1], kernel)[::-1]
        grad_key_li = grad_li_input * mixed_mr.astype(jnp.float32)
        grad_mixed_mr = grad_li_input * key_li.astype(jnp.float32)
        grad_query_mr = grad_mixed_mr * mr_conv
        grad_conv = grad_mixed_mr * query_mr.astype(jnp.float32)
        grad_padded = jnp.concatenate([grad_conv, jnp.zeros((rim_size, chan_dev), jnp.float32)], axis=0)
        grad_product = shifted_taps(grad_padded, mr_taps, length, True)
        grad_key_mr = grad_product * value_mr.astype(jnp.float32)
        grad_value_mr = grad_product * key_mr.astype(jnp.float32)
        grad_taps = tap_gradient(grad_conv, padded, mr_taps.shape[0]) * grad_scale
        grad_weight = lax.dot_general(cotangent, mixed_li, (((0,), (0,)), ((), ())), preferred_element_type=jnp.float32) * grad_scale
        return (running, (grad_query_mr, grad_key_mr, grad_value_mr, grad_query_li, grad_key_li, grad_taps, grad_weight))
    starting = jnp.zeros((length, cotangent.shape[1]), jnp.float32)
    running, results = lax.scan(one_group, starting, stacked)
    return (running, merge_cols(results[0]), merge_cols(results[1]), merge_cols(results[2]), merge_cols(results[3]), merge_cols(results[4]), merge_cols(results[5]), merge_cols(results[6]))
```

```python
import functools
import math

import jax
import jax.numpy as jnp
import ml_dtypes
import numpy as np
from jax import lax
from jax.experimental import pallas as pl
from jax.experimental.pallas import tpu as pltpu
from jax.sharding import PartitionSpec as P

F32 = jnp.float32
BF16 = jnp.bfloat16
TILE = 256
GROUP = 8


def split_parts(matrix):
    high = matrix.astype(ml_dtypes.bfloat16)
    low = (matrix - high.astype(np.float64)).astype(ml_dtypes.bfloat16)
    return high, low


def two_fold(matrix):
    high, low = split_parts(matrix)
    return np.concatenate([high, low], axis=1)


def three_fold(matrix):
    high, low = split_parts(matrix)
    return np.concatenate([high, low, high], axis=1)


@functools.lru_cache(maxsize=None)
def dft_tables(rows):
    size = 2 * rows
    angle = 2.0 * np.pi * (np.arange(rows)[:, None] + 0.5) * np.arange(size)[None, :] / size
    ahead = np.concatenate([np.cos(angle), -np.sin(angle)], axis=0)
    back = ahead.T * (2.0 / size)
    signed = np.concatenate([back[:rows], -back[rows:]], axis=0)
    lags = back[rows - np.arange(rows)]
    return {
        "full2": two_fold(ahead),
        "half2": two_fold(ahead[:, :rows]),
        "half3": three_fold(ahead[:, :rows]),
        "first3": three_fold(back[:rows]),
        "last3": three_fold(back[rows:]),
        "both3": three_fold(signed),
        "lags3": three_fold(lags),
    }


def apply2(table, x):
    return jnp.dot(table, jnp.concatenate([x, x], axis=0), preferred_element_type=F32)


def apply3(table, x):
    high = x.astype(BF16)
    low = (x - high.astype(F32)).astype(BF16)
    return jnp.dot(table, jnp.concatenate([high, high, low], axis=0), preferred_element_type=F32)


def times(x, y):
    half = x.shape[0] // 2
    xr, xi, yr, yi = x[:half], x[half:], y[:half], y[half:]
    return jnp.concatenate([xr * yr - xi * yi, xr * yi + xi * yr], axis=0)


def times_conj(x, y):
    half = x.shape[0] // 2
    xr, xi, yr, yi = x[:half], x[half:], y[:half], y[half:]
    return jnp.concatenate([xr * yr + xi * yi, xi * yr - xr * yi], axis=0)


def group_places(columns):
    return lax.broadcasted_iota(jnp.int32, (GROUP, columns), 0).astype(F32)


def spread_modes(rate, weight, rows, shift, backward):
    columns = rate.shape[1]
    places = group_places(columns)
    if backward:
        places = (GROUP - 1.0) - places
    count = rows // GROUP
    order = range(count - 1, -1, -1) if backward else range(count)
    sums = [None] * count
    for m in range(rate.shape[0]):
        rate_m = rate[m : m + 1]
        current = weight[m : m + 1] * jnp.exp(-rate_m * (places + shift))
        stride = jnp.broadcast_to(jnp.exp(-rate_m * GROUP), current.shape)
        for step, g in enumerate(order):
            sums[g] = current if sums[g] is None else sums[g] + current
            if step < count - 1:
                current = current * stride
    return jnp.concatenate(sums, axis=0)


def fold_modes(signal, rate, backward):
    columns = rate.shape[1]
    places = group_places(columns)
    if not backward:
        places = (GROUP - 1.0) - places
    count = signal.shape[0] // GROUP
    order = range(count - 1, -1, -1) if backward else range(count)
    found = []
    for m in range(rate.shape[0]):
        rate_m = rate[m : m + 1]
        stride = jnp.broadcast_to(jnp.exp(-rate_m * GROUP), (GROUP, columns))
        running = None
        for g in order:
            piece = signal[g * GROUP : (g + 1) * GROUP]
            running = piece if running is None else running * stride + piece
        found.append(jnp.sum(running * jnp.exp(-rate_m * places), axis=0, keepdims=True))
    return jnp.concatenate(found, axis=0)


def gather_states(rate, gaps, states, sibling, inner, rows):
    total = jnp.zeros_like(rate)
    for gap, state in zip(gaps, states):
        weight = jnp.exp(-rate * (jnp.maximum(gap, 0.0) * (2.0 * rows)))
        total = total + jnp.where(gap >= 0.0, weight * state, 0.0)
    return jnp.where(inner > 0.0, jnp.exp(-rate * float(rows)) * total + sibling, total)


def spectra_body(taps, rate, coef, skip, half3, mr_spec, li_spec):
    rows = taps.shape[0]
    mr_spec[...] = apply3(half3[...], taps[...])
    kernel = spread_modes(rate[...], coef[...], rows, 0.0, False)
    first = lax.broadcasted_iota(jnp.int32, kernel.shape, 0) == 0
    kernel = kernel + jnp.where(first, skip[...], 0.0)
    li_spec[...] = apply3(half3[...], kernel)


def short_body(before, product, query, key, mr_spec, rate, full2, last3, spec, conv, mixed, signal, ends):
    x = jnp.concatenate([before[...], product[...]], axis=0)
    found = apply2(full2[...], x)
    spec[...] = found
    filtered = apply3(last3[...], times(found, mr_spec[...]))
    conv[...] = filtered
    mixed_rows = (query[...].astype(F32) * filtered).astype(BF16)
    mixed[...] = mixed_rows
    rounded = (key[...].astype(F32) * mixed_rows.astype(F32)).astype(BF16)
    signal[...] = rounded
    ends[...] = fold_modes(rounded.astype(F32), rate[...], False)


def inner_body(signal, li_spec, half2, first3, inner):
    inner[...] = apply3(first3[...], times(apply2(half2[...], signal[...]), li_spec[...]))


def long_body(count, scalars, inner, query, rate, coef, sibling, *rest):
    states, (li_out, mixed) = rest[:count], rest[count:]
    rows = inner.shape[0]
    rates = rate[...]
    entering = gather_states(
        rates,
        [scalars[1 + k] for k in range(count)],
        [state[...] for state in states],
        sibling[...],
        scalars[0],
        rows,
    )
    total = inner[...] + spread_modes(rates, coef[...] * entering, rows, 1.0, False)
    li_out[...] = total
    mixed[...] = (query[...].astype(F32) * total).astype(BF16)


def grad_gate_body(count, own, query, rate, *rest):
    parts, (grad_mixed, grad_out, ends) = rest[:count], rest[count:]
    total = own[...]
    for part in parts:
        total = total + part[...].astype(F32)
    grad_mixed[...] = total
    gated = total * query[...].astype(F32)
    grad_out[...] = gated
    ends[...] = fold_modes(gated, rate[...], True)


def grad_inner_body(grad_out, li_spec, half3, first3, inner):
    inner[...] = apply3(first3[...], times_conj(apply3(half3[...], grad_out[...]), li_spec[...]))


def grad_long_body(
    count, scalars, inner, rate, coef, sibling, mixed_mr, key_li, query_mr, conv, spec, mr_spec, half3, both3, lags3, *rest
):
    states = rest[:count]
    grad_key_li, grad_query_mr, own_product, prev_product, taps = rest[count:]
    rows = inner.shape[0]
    rates = rate[...]
    entering = gather_states(
        rates,
        [scalars[1 + k] for k in range(count)],
        [state[...] for state in states],
        sibling[...],
        scalars[0],
        rows,
    )
    grad_input = inner[...] + spread_modes(rates, coef[...] * entering, rows, 1.0, True)
    grad_key_li[...] = grad_input * mixed_mr[...].astype(F32)
    grad_mixed_mr = grad_input * key_li[...].astype(F32)
    grad_query_mr[...] = grad_mixed_mr * conv[...]
    grad_conv = grad_mixed_mr * query_mr[...].astype(F32)
    found = apply3(half3[...], grad_conv)
    products = apply3(both3[...], times_conj(found, mr_spec[...]))
    own_product[...] = products[:rows]
    prev_product[...] = products[rows:].astype(BF16)
    taps[...] = apply3(lags3[...], times_conj(spec[...], found))


def grad_product_body(own, arrived, key, value, grad_key, grad_value):
    total = own[...] + arrived[...].astype(F32)
    grad_key[...] = total * value[...].astype(F32)
    grad_value[...] = total * key[...].astype(F32)


def run(body, columns, inputs, outputs, flops):
    tile = min(TILE, columns)
    in_specs = []
    moved = 0
    for kind, array in inputs:
        if kind == "tile":
            in_specs.append(pl.BlockSpec((array.shape[0], tile), lambda c: (0, c)))
        elif kind == "whole":
            in_specs.append(pl.BlockSpec(array.shape, lambda c: (0, 0)))
        else:
            in_specs.append(pl.BlockSpec(memory_space=pltpu.SMEM))
        moved += math.prod(array.shape) * array.dtype.itemsize
    for rows, dtype in outputs:
        moved += rows * columns * jnp.dtype(dtype).itemsize
    return pl.pallas_call(
        body,
        grid=(columns // tile,),
        in_specs=in_specs,
        out_specs=[pl.BlockSpec((rows, tile), lambda c: (0, c)) for rows, _ in outputs],
        out_shape=[jax.ShapeDtypeStruct((rows, columns), dtype) for rows, dtype in outputs],
        compiler_params=pltpu.CompilerParams(vmem_limit_bytes=32 * 1024 * 1024),
        cost_estimate=pl.CostEstimate(flops=flops, bytes_accessed=moved, transcendentals=0),
    )(*[array for _, array in inputs])


def chip_swap(x, by):
    size = lax.axis_size("ctx")
    return lax.ppermute(x, "ctx", [(i, i ^ (2 * by)) for i in range(size)])


def core_swap(x):
    size = lax.axis_size("ctx")
    return lax.ppermute(x, "ctx", [(i, i ^ 1) for i in range(size)])


def line_swap(x, by):
    size = lax.axis_size("fsdp")
    return lax.ppermute(x, "fsdp", [(i, i ^ by) for i in range(size)])


def shifted(x, by):
    size = lax.axis_size("ctx")
    return lax.ppermute(x, "ctx", [(i, i + by) for i in range(size) if 0 <= i + by < size])


def columns_at(x, index, width):
    return lax.dynamic_slice_in_dim(x, index * width, width, 1)


def placed(pieces):
    width = pieces[0][1].shape[1]
    whole = jnp.zeros((pieces[0][1].shape[0], width * len(pieces)), pieces[0][1].dtype)
    for index, piece in pieces:
        whole = lax.dynamic_update_slice_in_dim(whole, piece, index * width, 1)
    return whole


def pair_sum(values):
    while len(values) > 1:
        values = [values[k] + values[k + 1] for k in range(0, len(values), 2)]
    return values[0]


def shards(
    query_mr,
    key_mr,
    value_mr,
    query_li,
    key_li,
    mr_taps,
    li_time,
    li_residue,
    li_skip,
    out_weight,
    cotangent,
):
    rows, columns = query_mr.shape
    ctx_count = lax.axis_size("ctx")
    line_count = lax.axis_size("fsdp")
    chips = ctx_count // 2
    here = lax.axis_index("ctx")
    chip, core = here // 2, here % 2
    line = lax.axis_index("fsdp")
    grad_scale = 1.0 / math.sqrt(rows * ctx_count)
    tables = {name: jnp.asarray(table) for name, table in dft_tables(rows).items()}
    width = out_weight.shape[0]
    chip_width = 2 * width
    pass_flops = 2 * (2 * rows) * (2 * rows) * columns

    def tile(x):
        return ("tile", x)

    def table(name):
        return ("whole", tables[name])

    mr_product = (key_mr.astype(F32) * value_mr.astype(F32)).astype(BF16)
    before = shifted(mr_product, 1)

    cot_line = [cotangent] + [line_swap(cotangent, r) for r in range(1, line_count)]
    other_weight = core_swap(out_weight)
    weight_pair = jnp.where(
        core == 0,
        jnp.concatenate([out_weight, other_weight], axis=0),
        jnp.concatenate([other_weight, out_weight], axis=0),
    )
    cot_full = placed([(line ^ r, piece) for r, piece in enumerate(cot_line)])
    cot_parts = [columns_at(cot_full, chip, chip_width)]
    for s in range(1, chips):
        cot_parts.append(chip_swap(columns_at(cot_full, chip ^ s, chip_width), s))

    rate = 1.0 / li_time
    coef = li_residue * jnp.sqrt(-jnp.expm1(-2.0 * rate))
    block_decay = jnp.exp(-rate * float(rows))
    inner_ahead = (core == 1).astype(F32)[None]
    peers = jnp.stack([chip ^ s for s in range(1, chips)]).astype(F32)
    chip_f = chip.astype(F32)
    ahead_scalars = jnp.concatenate([inner_ahead, chip_f - 1.0 - peers])
    back_scalars = jnp.concatenate([1.0 - inner_ahead, peers - chip_f - 1.0])

    mr_spec, li_spec = run(
        spectra_body,
        columns,
        [tile(mr_taps), tile(rate), tile(coef), tile(li_skip[None, :]), table("half3")],
        [(2 * rows, F32), (2 * rows, F32)],
        3 * pass_flops,
    )
    spec, mr_conv, mixed_mr, li_input, ends = run(
        short_body,
        columns,
        [
            tile(before),
            tile(mr_product),
            tile(query_mr),
            tile(key_li),
            tile(mr_spec),
            tile(rate),
            table("full2"),
            table("last3"),
        ],
        [(2 * rows, F32), (rows, F32), (rows, BF16), (rows, BF16), (rate.shape[0], F32)],
        4 * pass_flops,
    )

    def exchange(ends, backward):
        sibling = core_swap(ends)
        near, far = (sibling, ends) if backward else (ends, sibling)
        chip_state = jnp.where(core == 0, block_decay * near + far, block_decay * far + near)
        return sibling, [chip_swap(chip_state, s) for s in range(1, chips)]

    sibling, states = exchange(ends, False)
    (li_inner,) = run(
        inner_body,
        columns,
        [tile(li_input), tile(li_spec), table("half2"), table("first3")],
        [(rows, F32)],
        3 * pass_flops,
    )
    li_out, mixed_li = run(
        functools.partial(long_body, chips - 1),
        columns,
        [("scalar", ahead_scalars), tile(li_inner), tile(query_li), tile(rate), tile(coef), tile(sibling)]
        + [tile(state) for state in states],
        [(rows, F32), (rows, BF16)],
        pass_flops,
    )

    mixed_parts = [mixed_li] + [chip_swap(mixed_li, s) for s in range(1, chips)]
    out_parts = []
    for s, part in enumerate(mixed_parts):
        found = lax.dot_general(
            part, weight_pair, (((1,), (1,)), ((), ())), preferred_element_type=F32
        ).astype(BF16)
        out_parts.append((chip ^ s, found if s == 0 else chip_swap(found, s)))
    out_full = placed(out_parts)
    line_width = out_full.shape[1] // line_count
    out_sum = columns_at(out_full, line, line_width).astype(F32)
    for r in range(1, line_count):
        out_sum = out_sum + line_swap(columns_at(out_full, line ^ r, line_width), r).astype(F32)
    output = out_sum

    grad_parts = []
    for s, part in enumerate(cot_parts):
        found = jnp.dot(part, weight_pair, preferred_element_type=F32)
        grad_parts.append(found if s == 0 else chip_swap(found.astype(BF16), s))
    grad_mixed, grad_li_out, back_ends = run(
        functools.partial(grad_gate_body, chips - 1),
        columns,
        [tile(grad_parts[0]), tile(query_li), tile(rate)] + [tile(part) for part in grad_parts[1:]],
        [(rows, F32), (rows, F32), (rate.shape[0], F32)],
        pass_flops,
    )
    back_sibling, back_states = exchange(back_ends, True)
    (grad_inner,) = run(
        grad_inner_body,
        columns,
        [tile(grad_li_out), tile(li_spec), table("half3"), table("first3")],
        [(rows, F32)],
        3 * pass_flops,
    )
    grad_query_li = grad_mixed * li_out
    grad_key_li, grad_query_mr, own_product, prev_product, tap_partial = run(
        functools.partial(grad_long_body, chips - 1),
        columns,
        [
            ("scalar", back_scalars),
            tile(grad_inner),
            tile(rate),
            tile(coef),
            tile(back_sibling),
            tile(mixed_mr),
            tile(key_li),
            tile(query_mr),
            tile(mr_conv),
            tile(spec),
            tile(mr_spec),
            table("half3"),
            table("both3"),
            table("lags3"),
        ]
        + [tile(state) for state in back_states],
        [(rows, F32), (rows, F32), (rows, F32), (rows, BF16), (rows, F32)],
        7 * pass_flops,
    )
    arrived = shifted(prev_product, -1)
    grad_key_mr, grad_value_mr = run(
        grad_product_body,
        columns,
        [tile(own_product), tile(arrived), tile(key_mr), tile(value_mr)],
        [(rows, F32), (rows, F32)],
        rows * columns,
    )

    tap_half = tap_partial.shape[0] // 2
    halves = tap_partial.reshape(2, tap_half, columns)
    own_half = lax.dynamic_index_in_dim(halves, core, 0, keepdims=False)
    far_half = lax.dynamic_index_in_dim(halves, 1 - core, 0, keepdims=False)
    chip_half = (own_half + core_swap(far_half)).astype(BF16)
    everywhere = [chip_half] + [chip_swap(chip_half, s) for s in range(1, chips)]
    plane_half = pair_sum([part.astype(F32) for part in everywhere]) * grad_scale
    other_half = core_swap(plane_half)
    grad_taps = jnp.where(
        core == 0,
        jnp.concatenate([plane_half, other_half], axis=0),
        jnp.concatenate([other_half, plane_half], axis=0),
    )

    cot_rows = jnp.concatenate(cot_parts, axis=0)
    mixed_rows = jnp.concatenate(mixed_parts, axis=0)

    def weight_share(which):
        return lax.dot_general(
            columns_at(cot_rows, which, width),
            mixed_rows,
            (((0,), (0,)), ((), ())),
            preferred_element_type=F32,
        )

    far_share = core_swap(weight_share(1 - core).astype(BF16))
    grad_weight = (weight_share(core) + far_share.astype(F32)) * grad_scale
    return (
        output,
        grad_query_mr,
        grad_key_mr,
        grad_value_mr,
        grad_query_li,
        grad_key_li,
        grad_taps,
        grad_weight,
    )


def solution(mesh):
    rows = P("ctx", "fsdp")
    channels = P(None, "fsdp")
    return jax.shard_map(
        shards,
        mesh=mesh,
        in_specs=(rows,) * 5 + (channels,) * 3 + (P("fsdp"),) + (rows,) * 2,
        out_specs=(rows,) * 6 + (channels, rows),
        check_vma=False,
    )
```

```python
import functools
import math

import jax
import jax.numpy as jnp
import ml_dtypes
import numpy as np
from jax import lax
from jax.experimental import pallas as pl
from jax.experimental.pallas import tpu as pltpu
from jax.sharding import PartitionSpec as P

F32 = jnp.float32
BF16 = jnp.bfloat16
TILE = 256
GROUP = 8


def split_parts(matrix):
    high = matrix.astype(ml_dtypes.bfloat16)
    low = (matrix - high.astype(np.float64)).astype(ml_dtypes.bfloat16)
    return high, low


def two_fold(matrix):
    high, low = split_parts(matrix)
    return np.concatenate([high, low], axis=1)


def three_fold(matrix):
    high, low = split_parts(matrix)
    return np.concatenate([high, low, high], axis=1)


@functools.lru_cache(maxsize=None)
def dft_tables(rows):
    size = 2 * rows
    angle = 2.0 * np.pi * (np.arange(rows)[:, None] + 0.5) * np.arange(size)[None, :] / size
    ahead = np.concatenate([np.cos(angle), -np.sin(angle)], axis=0)
    back = ahead.T * (2.0 / size)
    signed = np.concatenate([back[:rows], -back[rows:]], axis=0)
    lags = back[rows - np.arange(rows)]
    return {
        "full2": two_fold(ahead),
        "half2": two_fold(ahead[:, :rows]),
        "half3": three_fold(ahead[:, :rows]),
        "first3": three_fold(back[:rows]),
        "last3": three_fold(back[rows:]),
        "both3": three_fold(signed),
        "lags3": three_fold(lags),
    }


def apply2(table, x):
    return jnp.dot(table, jnp.concatenate([x, x], axis=0), preferred_element_type=F32)


def apply3(table, x):
    high = x.astype(BF16)
    low = (x - high.astype(F32)).astype(BF16)
    return jnp.dot(table, jnp.concatenate([high, high, low], axis=0), preferred_element_type=F32)


def times(x, y):
    half = x.shape[0] // 2
    xr, xi, yr, yi = x[:half], x[half:], y[:half], y[half:]
    return jnp.concatenate([xr * yr - xi * yi, xr * yi + xi * yr], axis=0)


def times_conj(x, y):
    half = x.shape[0] // 2
    xr, xi, yr, yi = x[:half], x[half:], y[:half], y[half:]
    return jnp.concatenate([xr * yr + xi * yi, xi * yr - xr * yi], axis=0)


def group_places(columns):
    return lax.broadcasted_iota(jnp.int32, (GROUP, columns), 0).astype(F32)


def spread_modes(rate, weight, rows, shift, backward):
    columns = rate.shape[1]
    places = group_places(columns)
    if backward:
        places = (GROUP - 1.0) - places
    count = rows // GROUP
    order = range(count - 1, -1, -1) if backward else range(count)
    sums = [None] * count
    for m in range(rate.shape[0]):
        rate_m = rate[m : m + 1]
        current = weight[m : m + 1] * jnp.exp(-rate_m * (places + shift))
        stride = jnp.broadcast_to(jnp.exp(-rate_m * GROUP), current.shape)
        for step, g in enumerate(order):
            sums[g] = current if sums[g] is None else sums[g] + current
            if step < count - 1:
                current = current * stride
    return jnp.concatenate(sums, axis=0)


def fold_modes(signal, rate, backward):
    columns = rate.shape[1]
    places = group_places(columns)
    if not backward:
        places = (GROUP - 1.0) - places
    count = signal.shape[0] // GROUP
    order = range(count - 1, -1, -1) if backward else range(count)
    found = []
    for m in range(rate.shape[0]):
        rate_m = rate[m : m + 1]
        stride = jnp.broadcast_to(jnp.exp(-rate_m * GROUP), (GROUP, columns))
        running = None
        for g in order:
            piece = signal[g * GROUP : (g + 1) * GROUP]
            running = piece if running is None else running * stride + piece
        found.append(jnp.sum(running * jnp.exp(-rate_m * places), axis=0, keepdims=True))
    return jnp.concatenate(found, axis=0)


def spectra_body(taps, rate, coef, skip, half3, mr_spec, li_spec):
    rows = taps.shape[0]
    mr_spec[...] = apply3(half3[...], taps[...])
    kernel = spread_modes(rate[...], coef[...], rows, 0.0, False)
    first = lax.broadcasted_iota(jnp.int32, kernel.shape, 0) == 0
    kernel = kernel + jnp.where(first, skip[...], 0.0)
    li_spec[...] = apply3(half3[...], kernel)


def short_body(before, product, query, key, mr_spec, rate, full2, last3, spec, conv, mixed, signal, ends):
    x = jnp.concatenate([before[...], product[...]], axis=0)
    found = apply2(full2[...], x)
    spec[...] = found
    filtered = apply3(last3[...], times(found, mr_spec[...]))
    conv[...] = filtered
    mixed_rows = (query[...].astype(F32) * filtered).astype(BF16)
    mixed[...] = mixed_rows
    rounded = (key[...].astype(F32) * mixed_rows.astype(F32)).astype(BF16)
    signal[...] = rounded
    ends[...] = fold_modes(rounded.astype(F32), rate[...], False)


def inner_body(signal, li_spec, half2, first3, inner):
    inner[...] = apply3(first3[...], times(apply2(half2[...], signal[...]), li_spec[...]))


def long_body(inner, query, rate, coef, entering, li_out, mixed):
    rows = inner.shape[0]
    total = inner[...] + spread_modes(rate[...], coef[...] * entering[...], rows, 1.0, False)
    li_out[...] = total
    mixed[...] = (query[...].astype(F32) * total).astype(BF16)


def grad_gate_body(parts, query, rate, grad_mixed, grad_out, ends):
    rows = query.shape[0]
    total = parts[:rows].astype(F32)
    for k in range(1, parts.shape[0] // rows):
        total = total + parts[k * rows : (k + 1) * rows].astype(F32)
    grad_mixed[...] = total
    gated = total * query[...].astype(F32)
    grad_out[...] = gated
    ends[...] = fold_modes(gated, rate[...], True)


def grad_inner_body(grad_out, li_spec, half3, first3, inner):
    inner[...] = apply3(first3[...], times_conj(apply3(half3[...], grad_out[...]), li_spec[...]))


def grad_long_body(
    inner, rate, coef, entering, mixed_mr, key_li, query_mr, conv, spec, mr_spec, half3, both3, lags3,
    grad_key_li, grad_query_mr, own_product, prev_product, taps,
):
    rows = inner.shape[0]
    grad_input = inner[...] + spread_modes(rate[...], coef[...] * entering[...], rows, 1.0, True)
    grad_key_li[...] = grad_input * mixed_mr[...].astype(F32)
    grad_mixed_mr = grad_input * key_li[...].astype(F32)
    grad_query_mr[...] = grad_mixed_mr * conv[...]
    grad_conv = grad_mixed_mr * query_mr[...].astype(F32)
    found = apply3(half3[...], grad_conv)
    products = apply3(both3[...], times_conj(found, mr_spec[...]))
    own_product[...] = products[:rows]
    prev_product[...] = products[rows:].astype(BF16)
    taps[...] = apply3(lags3[...], times_conj(spec[...], found))


def grad_product_body(own, arrived, key, value, grad_key, grad_value):
    total = own[...] + arrived[...].astype(F32)
    grad_key[...] = total * value[...].astype(F32)
    grad_value[...] = total * key[...].astype(F32)


def run(body, columns, inputs, outputs, flops):
    tile = min(TILE, columns)
    in_specs = []
    moved = 0
    for kind, array in inputs:
        if kind == "tile":
            in_specs.append(pl.BlockSpec((array.shape[0], tile), lambda c: (0, c)))
        else:
            in_specs.append(pl.BlockSpec(array.shape, lambda c: (0, 0)))
        moved += math.prod(array.shape) * array.dtype.itemsize
    for rows, dtype in outputs:
        moved += rows * columns * jnp.dtype(dtype).itemsize
    return pl.pallas_call(
        body,
        grid=(columns // tile,),
        in_specs=in_specs,
        out_specs=[pl.BlockSpec((rows, tile), lambda c: (0, c)) for rows, _ in outputs],
        out_shape=[jax.ShapeDtypeStruct((rows, columns), dtype) for rows, dtype in outputs],
        compiler_params=pltpu.CompilerParams(vmem_limit_bytes=32 * 1024 * 1024),
        cost_estimate=pl.CostEstimate(flops=flops, bytes_accessed=moved, transcendentals=0),
    )(*[array for _, array in inputs])


def core_swap(x):
    size = lax.axis_size("ctx")
    return lax.ppermute(x, "ctx", [(i, i ^ 1) for i in range(size)])


def shifted(x, by):
    size = lax.axis_size("ctx")
    return lax.ppermute(x, "ctx", [(i, i + by) for i in range(size) if 0 <= i + by < size])


def plane_trade(x):
    size = lax.axis_size("ctx")
    groups = [list(range(core, size, 2)) for core in range(2)]
    return lax.all_to_all(x, "ctx", 0, 0, axis_index_groups=groups, tiled=True)


def line_trade(x):
    return lax.all_to_all(x, "fsdp", 0, 0, tiled=True)


def copies(x, count):
    return jnp.concatenate([x] * count, axis=0)


def rows_to_columns(x, count):
    return jnp.concatenate(jnp.split(x, count, axis=0), axis=1)


def columns_to_rows(x, count):
    return jnp.concatenate(jnp.split(x, count, axis=1), axis=0)


def after(x, *others):
    return lax.optimization_barrier((x,) + others)[0]


def entering_state(ends, rate, rows, here, backward):
    size = lax.axis_size("ctx")
    total, entering = ends, jnp.zeros_like(ends)
    by = 1
    while by < size:
        arrived = lax.ppermute(total, "ctx", [(i, i ^ by) for i in range(size)])
        later = (here & by) != 0
        offset = here & (by - 1)
        if backward:
            later = jnp.logical_not(later)
            offset = by - 1 - offset
        to_here = jnp.exp(-rate * (rows * offset).astype(F32))
        entering = entering + jnp.where(later, to_here * arrived, 0.0)
        across = jnp.exp(-rate * float(rows * by))
        total = jnp.where(later, across * arrived + total, across * total + arrived)
        by *= 2
    return entering


def shards(
    query_mr,
    key_mr,
    value_mr,
    query_li,
    key_li,
    mr_taps,
    li_time,
    li_residue,
    li_skip,
    out_weight,
    cotangent,
):
    rows, columns = query_mr.shape
    ctx_count = lax.axis_size("ctx")
    line_count = lax.axis_size("fsdp")
    chips = ctx_count // 2
    here = lax.axis_index("ctx")
    core = here % 2
    grad_scale = 1.0 / math.sqrt(rows * ctx_count)
    tables = {name: jnp.asarray(table) for name, table in dft_tables(rows).items()}
    width = out_weight.shape[0]
    pass_flops = 2 * (2 * rows) * (2 * rows) * columns

    def tile(x):
        return ("tile", x)

    def table(name):
        return ("whole", tables[name])

    mr_product = (key_mr.astype(F32) * value_mr.astype(F32)).astype(BF16)
    before = shifted(mr_product, 1)

    cot_line = line_trade(copies(cotangent, line_count))

    rate = 1.0 / li_time
    coef = li_residue * jnp.sqrt(-jnp.expm1(-2.0 * rate))
    mr_spec, li_spec = run(
        spectra_body,
        columns,
        [tile(mr_taps), tile(rate), tile(coef), tile(li_skip[None, :]), table("half3")],
        [(2 * rows, F32), (2 * rows, F32)],
        3 * pass_flops,
    )
    other_weight = core_swap(after(out_weight, mr_spec))
    spec, mr_conv, mixed_mr, li_input, ends = run(
        short_body,
        columns,
        [
            tile(before),
            tile(mr_product),
            tile(query_mr),
            tile(key_li),
            tile(mr_spec),
            tile(rate),
            table("full2"),
            table("last3"),
        ],
        [(2 * rows, F32), (rows, F32), (rows, BF16), (rows, BF16), (rate.shape[0], F32)],
        4 * pass_flops,
    )
    entering = entering_state(ends, rate, rows, here, False)
    (li_inner,) = run(
        inner_body,
        columns,
        [tile(li_input), tile(li_spec), table("half2"), table("first3")],
        [(rows, F32)],
        3 * pass_flops,
    )
    li_out, mixed_li = run(
        long_body,
        columns,
        [tile(li_inner), tile(query_li), tile(rate), tile(coef), tile(entering)],
        [(rows, F32), (rows, BF16)],
        pass_flops,
    )

    mixed_rows = plane_trade(copies(mixed_li, chips))
    cot_full = rows_to_columns(after(cot_line, mixed_li), line_count)
    cot_rows = plane_trade(columns_to_rows(cot_full, chips))
    weight_pair = jnp.where(
        core == 0,
        jnp.concatenate([out_weight, other_weight], axis=0),
        jnp.concatenate([other_weight, out_weight], axis=0),
    )

    grad_share = jnp.dot(cot_rows, weight_pair, preferred_element_type=F32).astype(BF16)
    grad_parts = plane_trade(grad_share)

    out_share = lax.dot_general(
        mixed_rows, after(weight_pair, grad_share), (((1,), (1,)), ((), ())), preferred_element_type=F32
    ).astype(BF16)
    out_full = rows_to_columns(plane_trade(out_share), chips)
    out_parts = line_trade(columns_to_rows(out_full, line_count)).reshape(line_count, rows, -1)
    output = jnp.sum(out_parts.astype(F32), axis=0)

    mixed_after = after(mixed_rows, out_share)

    def weight_share(which):
        return lax.dot_general(
            lax.dynamic_slice_in_dim(cot_rows, which * width, width, 1),
            mixed_after,
            (((0,), (0,)), ((), ())),
            preferred_element_type=F32,
        )

    sent_share = weight_share(1 - core).astype(BF16)
    far_share = core_swap(sent_share)
    grad_weight = (weight_share(core) + far_share.astype(F32)) * grad_scale

    grad_mixed, grad_li_out, back_ends = run(
        grad_gate_body,
        columns,
        [tile(after(grad_parts, sent_share)), tile(query_li), tile(rate)],
        [(rows, F32), (rows, F32), (rate.shape[0], F32)],
        pass_flops,
    )
    back_entering = entering_state(back_ends, rate, rows, here, True)
    (grad_inner,) = run(
        grad_inner_body,
        columns,
        [tile(grad_li_out), tile(li_spec), table("half3"), table("first3")],
        [(rows, F32)],
        3 * pass_flops,
    )
    grad_query_li = grad_mixed * li_out
    grad_key_li, grad_query_mr, own_product, prev_product, tap_partial = run(
        grad_long_body,
        columns,
        [
            tile(grad_inner),
            tile(rate),
            tile(coef),
            tile(back_entering),
            tile(mixed_mr),
            tile(key_li),
            tile(query_mr),
            tile(mr_conv),
            tile(spec),
            tile(mr_spec),
            table("half3"),
            table("both3"),
            table("lags3"),
        ],
        [(rows, F32), (rows, F32), (rows, F32), (rows, BF16), (rows, F32)],
        7 * pass_flops,
    )
    arrived = shifted(prev_product, -1)
    grad_key_mr, grad_value_mr = run(
        grad_product_body,
        columns,
        [tile(own_product), tile(arrived), tile(key_mr), tile(value_mr)],
        [(rows, F32), (rows, F32)],
        rows * columns,
    )

    tap_half = tap_partial.shape[0] // 2
    halves = tap_partial.reshape(2, tap_half, columns)
    own_half = lax.dynamic_index_in_dim(halves, core, 0, keepdims=False)
    far_half = lax.dynamic_index_in_dim(halves, 1 - core, 0, keepdims=False)
    chip_half = (own_half + core_swap(far_half)).astype(BF16)
    everywhere = plane_trade(copies(chip_half, chips)).reshape(chips, tap_half, columns)
    plane_half = jnp.sum(everywhere.astype(F32), axis=0) * grad_scale
    other_half = core_swap(plane_half)
    grad_taps = jnp.where(
        core == 0,
        jnp.concatenate([plane_half, other_half], axis=0),
        jnp.concatenate([other_half, plane_half], axis=0),
    )
    return (
        output,
        grad_query_mr,
        grad_key_mr,
        grad_value_mr,
        grad_query_li,
        grad_key_li,
        grad_taps,
        grad_weight,
    )


def solution(mesh):
    rows = P("ctx", "fsdp")
    channels = P(None, "fsdp")
    return jax.shard_map(
        shards,
        mesh=mesh,
        in_specs=(rows,) * 5 + (channels,) * 3 + (P("fsdp"),) + (rows,) * 2,
        out_specs=(rows,) * 6 + (channels, rows),
        check_vma=False,
    )
```

```python
import functools
import math

import jax
import jax.numpy as jnp
import ml_dtypes
import numpy as np
from jax import lax
from jax.experimental import pallas as pl
from jax.experimental.pallas import tpu as pltpu
from jax.sharding import PartitionSpec as P

F32 = jnp.float32
BF16 = jnp.bfloat16
TILE = 256
GROUP = 8


def split_parts(matrix):
    high = matrix.astype(ml_dtypes.bfloat16)
    low = (matrix - high.astype(np.float64)).astype(ml_dtypes.bfloat16)
    return high, low


def two_fold(matrix):
    high, low = split_parts(matrix)
    return np.concatenate([high, low], axis=1)


def three_fold(matrix):
    high, low = split_parts(matrix)
    return np.concatenate([high, low, high], axis=1)


@functools.lru_cache(maxsize=None)
def dft_tables(rows):
    size = 2 * rows
    angle = 2.0 * np.pi * (np.arange(rows)[:, None] + 0.5) * np.arange(size)[None, :] / size
    ahead = np.concatenate([np.cos(angle), -np.sin(angle)], axis=0)
    back = ahead.T * (2.0 / size)
    signed = np.concatenate([back[:rows], -back[rows:]], axis=0)
    lags = back[rows - np.arange(rows)]
    return {
        "full2": two_fold(ahead),
        "half2": two_fold(ahead[:, :rows]),
        "half3": three_fold(ahead[:, :rows]),
        "first3": three_fold(back[:rows]),
        "last3": three_fold(back[rows:]),
        "both3": three_fold(signed),
        "lags3": three_fold(lags),
    }


def apply2(table, x):
    return jnp.dot(table, jnp.concatenate([x, x], axis=0), preferred_element_type=F32)


def apply3(table, x):
    high = x.astype(BF16)
    low = (x - high.astype(F32)).astype(BF16)
    return jnp.dot(table, jnp.concatenate([high, high, low], axis=0), preferred_element_type=F32)


def times(x, y):
    half = x.shape[0] // 2
    xr, xi, yr, yi = x[:half], x[half:], y[:half], y[half:]
    return jnp.concatenate([xr * yr - xi * yi, xr * yi + xi * yr], axis=0)


def times_conj(x, y):
    half = x.shape[0] // 2
    xr, xi, yr, yi = x[:half], x[half:], y[:half], y[half:]
    return jnp.concatenate([xr * yr + xi * yi, xi * yr - xr * yi], axis=0)


def group_places(columns):
    return lax.broadcasted_iota(jnp.int32, (GROUP, columns), 0).astype(F32)


def spread_modes(rate, weight, rows, shift, backward):
    columns = rate.shape[1]
    places = group_places(columns)
    if backward:
        places = (GROUP - 1.0) - places
    count = rows // GROUP
    order = range(count - 1, -1, -1) if backward else range(count)
    sums = [None] * count
    for m in range(rate.shape[0]):
        rate_m = rate[m : m + 1]
        current = weight[m : m + 1] * jnp.exp(-rate_m * (places + shift))
        stride = jnp.broadcast_to(jnp.exp(-rate_m * GROUP), current.shape)
        for step, g in enumerate(order):
            sums[g] = current if sums[g] is None else sums[g] + current
            if step < count - 1:
                current = current * stride
    return jnp.concatenate(sums, axis=0)


def fold_modes(signal, rate, backward):
    columns = rate.shape[1]
    places = group_places(columns)
    if not backward:
        places = (GROUP - 1.0) - places
    count = signal.shape[0] // GROUP
    order = range(count - 1, -1, -1) if backward else range(count)
    found = []
    for m in range(rate.shape[0]):
        rate_m = rate[m : m + 1]
        stride = jnp.broadcast_to(jnp.exp(-rate_m * GROUP), (GROUP, columns))
        running = None
        for g in order:
            piece = signal[g * GROUP : (g + 1) * GROUP]
            running = piece if running is None else running * stride + piece
        found.append(jnp.sum(running * jnp.exp(-rate_m * places), axis=0, keepdims=True))
    return jnp.concatenate(found, axis=0)


def spectra_body(taps, rate, coef, skip, half3, mr_spec, li_spec):
    rows = taps.shape[0]
    mr_spec[...] = apply3(half3[...], taps[...])
    kernel = spread_modes(rate[...], coef[...], rows, 0.0, False)
    first = lax.broadcasted_iota(jnp.int32, kernel.shape, 0) == 0
    kernel = kernel + jnp.where(first, skip[...], 0.0)
    li_spec[...] = apply3(half3[...], kernel)


def short_body(before, product, query, key, mr_spec, rate, full2, last3, spec, conv, mixed, signal, ends):
    x = jnp.concatenate([before[...], product[...]], axis=0)
    found = apply2(full2[...], x)
    spec[...] = found
    filtered = apply3(last3[...], times(found, mr_spec[...]))
    conv[...] = filtered
    mixed_rows = (query[...].astype(F32) * filtered).astype(BF16)
    mixed[...] = mixed_rows
    rounded = (key[...].astype(F32) * mixed_rows.astype(F32)).astype(BF16)
    signal[...] = rounded
    ends[...] = fold_modes(rounded.astype(F32), rate[...], False)


def inner_body(signal, li_spec, half2, first3, inner):
    inner[...] = apply3(first3[...], times(apply2(half2[...], signal[...]), li_spec[...]))


def long_body(inner, query, rate, coef, entering, li_out, mixed):
    rows = inner.shape[0]
    total = inner[...] + spread_modes(rate[...], coef[...] * entering[...], rows, 1.0, False)
    li_out[...] = total
    mixed[...] = (query[...].astype(F32) * total).astype(BF16)


def weighted(total, starts, cotangent, pieces):
    for k, piece in enumerate(pieces):
        count = piece.shape[0]
        block = cotangent[:, pl.ds(pl.multiple_of(starts[k], 128), count)]
        found = jnp.dot(block, piece[...], preferred_element_type=F32)
        total = found if total is None else total + found
    return total


def grad_early_body(starts, cotangent, *rest):
    pieces, (total,) = rest[:-1], rest[-1:]
    total[...] = weighted(None, starts, cotangent, pieces)


def grad_gate_body(count, starts, early, cotangent, query, rate, *rest):
    pieces, (grad_mixed, grad_out, ends) = rest[:count], rest[count:]
    total = weighted(early[...], starts, cotangent, pieces)
    grad_mixed[...] = total
    gated = total * query[...].astype(F32)
    grad_out[...] = gated
    ends[...] = fold_modes(gated, rate[...], True)


def out_block(starts, mixed, pieces, result):
    for k, piece in enumerate(pieces):
        count = piece.shape[0]
        found = lax.dot_general(mixed[...], piece[...], (((1,), (1,)), ((), ())), preferred_element_type=F32)
        result[:, pl.ds(pl.multiple_of(starts[k], 128), count)] = found.astype(BF16)


def out_early_body(starts, mixed, *rest):
    out_block(starts, mixed, rest[:-1], rest[-1])


def out_late_body(count, starts, early, mixed, *rest):
    pieces, parts, whole = rest[:count], rest[count:-1], rest[-1]
    whole[...] = early[...]
    out_block(starts, mixed, pieces, whole)
    width = parts[0].shape[1]
    for r, part in enumerate(parts):
        part[...] = whole[:, pl.ds(pl.multiple_of(starts[count + r], 128), width)]


def grad_inner_body(grad_out, li_spec, half3, first3, inner):
    inner[...] = apply3(first3[...], times_conj(apply3(half3[...], grad_out[...]), li_spec[...]))


def grad_long_body(
    inner, rate, coef, entering, mixed_mr, key_li, query_mr, conv, spec, half3, lags3,
    grad_key_li, grad_query_mr, grad_spec, taps,
):
    rows = inner.shape[0]
    grad_input = inner[...] + spread_modes(rate[...], coef[...] * entering[...], rows, 1.0, True)
    grad_key_li[...] = grad_input * mixed_mr[...].astype(F32)
    grad_mixed_mr = grad_input * key_li[...].astype(F32)
    grad_query_mr[...] = grad_mixed_mr * conv[...]
    grad_conv = grad_mixed_mr * query_mr[...].astype(F32)
    found = apply3(half3[...], grad_conv)
    grad_spec[...] = found
    taps[...] = apply3(lags3[...], times_conj(spec[...], found))


def grad_taps_body(grad_spec, mr_spec, both3, own_product, prev_product):
    rows = own_product.shape[0]
    products = apply3(both3[...], times_conj(grad_spec[...], mr_spec[...]))
    own_product[...] = products[:rows]
    prev_product[...] = products[rows:].astype(BF16)


def grad_product_body(own, arrived, key, value, grad_key, grad_value):
    total = own[...] + arrived[...].astype(F32)
    grad_key[...] = total * value[...].astype(F32)
    grad_value[...] = total * key[...].astype(F32)


def run(body, columns, inputs, outputs, flops):
    tile = min(TILE, columns)
    in_specs = []
    moved = 0
    for kind, array in inputs:
        if kind == "tile":
            in_specs.append(pl.BlockSpec((array.shape[0], tile), lambda c: (0, c)))
        elif kind == "whole":
            in_specs.append(pl.BlockSpec(array.shape, lambda c: (0, 0)))
        else:
            in_specs.append(pl.BlockSpec(memory_space=pltpu.SMEM))
        moved += math.prod(array.shape) * array.dtype.itemsize
    for rows, dtype in outputs:
        moved += rows * columns * jnp.dtype(dtype).itemsize
    return pl.pallas_call(
        body,
        grid=(columns // tile,),
        in_specs=in_specs,
        out_specs=[pl.BlockSpec((rows, tile), lambda c: (0, c)) for rows, _ in outputs],
        out_shape=[jax.ShapeDtypeStruct((rows, columns), dtype) for rows, dtype in outputs],
        compiler_params=pltpu.CompilerParams(vmem_limit_bytes=32 * 1024 * 1024),
        cost_estimate=pl.CostEstimate(flops=flops, bytes_accessed=moved, transcendentals=0),
    )(*[array for _, array in inputs])


def run_once(body, inputs, outputs, scratch, flops):
    moved = sum(math.prod(array.shape) * array.dtype.itemsize for array in inputs)
    return pl.pallas_call(
        body,
        in_specs=[pl.BlockSpec(memory_space=pltpu.SMEM)]
        + [pl.BlockSpec(memory_space=pltpu.VMEM)] * (len(inputs) - 1),
        out_specs=[pl.BlockSpec(memory_space=pltpu.VMEM)] * len(outputs),
        out_shape=[jax.ShapeDtypeStruct(shape, dtype) for shape, dtype in outputs],
        scratch_shapes=scratch,
        compiler_params=pltpu.CompilerParams(vmem_limit_bytes=32 * 1024 * 1024),
        cost_estimate=pl.CostEstimate(flops=flops, bytes_accessed=moved, transcendentals=0),
    )(*inputs)


def core_swap(x):
    size = lax.axis_size("ctx")
    return lax.ppermute(x, "ctx", [(i, i ^ 1) for i in range(size)])


def shifted(x, by):
    size = lax.axis_size("ctx")
    return lax.ppermute(x, "ctx", [(i, i + by) for i in range(size) if 0 <= i + by < size])


def chip_swap(x, by):
    size = lax.axis_size("ctx")
    return lax.ppermute(x, "ctx", [(i, i ^ (2 * by)) for i in range(size)])


def line_swap(x, by):
    size = lax.axis_size("fsdp")
    return lax.ppermute(x, "fsdp", [(i, i ^ by) for i in range(size)])


def plane_trade(x):
    size = lax.axis_size("ctx")
    groups = [list(range(core, size, 2)) for core in range(2)]
    return lax.all_to_all(x, "ctx", 0, 0, axis_index_groups=groups, tiled=True)


def columns_to_rows(x, count):
    return jnp.concatenate(jnp.split(x, count, axis=1), axis=0)


def placed(pieces):
    width = pieces[0][1].shape[1]
    whole = jnp.zeros((pieces[0][1].shape[0], width * len(pieces)), pieces[0][1].dtype)
    for index, piece in pieces:
        whole = lax.dynamic_update_slice_in_dim(whole, piece, index * width, 1)
    return whole


def columns_at(x, index, width):
    return lax.dynamic_slice_in_dim(x, index * width, width, 1)


def weight_arrivals(weight, chips):
    direct = (1, 2) if chips == 4 else range(1, chips)
    return [(s, chip_swap(weight, s)) for s in direct]


def weight_pieces(weight, arrivals, chips):
    early = [(0, 0, weight)] + [(2 * s, 0, piece) for s, piece in arrivals]
    if chips == 4:
        (_, beside), (_, across) = arrivals
        half = weight.shape[0] // 2
        late = [(6, 0, chip_swap(across[:half], 1)), (6, half, chip_swap(beside[half:], 2))]
    else:
        late = [early.pop()]
    return [
        pieces + [(mask ^ 1, first, core_swap(piece)) for mask, first, piece in pieces]
        for pieces in (early, late)
    ]


def after(x, *others):
    return lax.optimization_barrier((x,) + others)[0]


def entering_state(ends, rate, rows, here, backward):
    size = lax.axis_size("ctx")
    total, entering = ends, jnp.zeros_like(ends)
    by = 1
    while by < size:
        arrived = lax.ppermute(total, "ctx", [(i, i ^ by) for i in range(size)])
        later = (here & by) != 0
        offset = here & (by - 1)
        if backward:
            later = jnp.logical_not(later)
            offset = by - 1 - offset
        to_here = jnp.exp(-rate * (rows * offset).astype(F32))
        entering = entering + jnp.where(later, to_here * arrived, 0.0)
        across = jnp.exp(-rate * float(rows * by))
        total = jnp.where(later, across * arrived + total, across * total + arrived)
        by *= 2
    return entering


def entering_direct(ends, rate, rows, here, backward):
    chips = lax.axis_size("ctx") // 2
    chip, later_core = here // 2, (here & 1) != 0
    if backward:
        later_core = jnp.logical_not(later_core)
    sibling = core_swap(ends)
    block = jnp.exp(-rate * float(rows))
    total = jnp.where(later_core, block * sibling + ends, block * ends + sibling)
    entering = jnp.zeros_like(ends)
    for s in range(1, chips):
        gap = (chip ^ s) - chip - 1 if backward else chip - (chip ^ s) - 1
        weight = jnp.exp(-rate * (2 * rows * jnp.maximum(gap, 0)).astype(F32))
        entering = entering + jnp.where(gap >= 0, weight * chip_swap(total, s), 0.0)
    return jnp.where(later_core, block * entering + sibling, entering)


def shards(
    query_mr,
    key_mr,
    value_mr,
    query_li,
    key_li,
    mr_taps,
    li_time,
    li_residue,
    li_skip,
    out_weight,
    cotangent,
):
    rows, columns = query_mr.shape
    ctx_count = lax.axis_size("ctx")
    line_count = lax.axis_size("fsdp")
    chips = ctx_count // 2
    here = lax.axis_index("ctx")
    core = here % 2
    line = lax.axis_index("fsdp")
    grad_scale = 1.0 / math.sqrt(rows * ctx_count)
    tables = {name: jnp.asarray(table) for name, table in dft_tables(rows).items()}
    width = out_weight.shape[0]
    pass_flops = 2 * (2 * rows) * (2 * rows) * columns

    def tile(x):
        return ("tile", x)

    def table(name):
        return ("whole", tables[name])

    mr_product = (key_mr.astype(F32) * value_mr.astype(F32)).astype(BF16)
    before = shifted(mr_product, 1)
    arrivals = weight_arrivals(out_weight, chips)
    cot_line = [(line, cotangent)]
    for r in range(1, line_count):
        cot_line.append((line ^ r, line_swap(cotangent, r)))

    def starts_of(pieces):
        return [(here ^ mask) * width + first for mask, first, piece in pieces]

    def arrays_of(pieces):
        return [piece for mask, first, piece in pieces]

    rate = 1.0 / li_time
    coef = li_residue * jnp.sqrt(-jnp.expm1(-2.0 * rate))
    mr_spec, li_spec = run(
        spectra_body,
        columns,
        [tile(mr_taps), tile(rate), tile(coef), tile(li_skip[None, :]), table("half3")],
        [(2 * rows, F32), (2 * rows, F32)],
        3 * pass_flops,
    )
    spec, mr_conv, mixed_mr, li_input, ends = run(
        short_body,
        columns,
        [
            tile(after(before, cot_line[1][1])),
            tile(mr_product),
            tile(query_mr),
            tile(key_li),
            tile(mr_spec),
            tile(rate),
            table("full2"),
            table("last3"),
        ],
        [(2 * rows, F32), (rows, F32), (rows, BF16), (rows, BF16), (rate.shape[0], F32)],
        4 * pass_flops,
    )
    entering = entering_state(ends, rate, rows, here, False)
    arrivals = [(s, after(piece, entering)) for s, piece in arrivals]
    early, late = weight_pieces(out_weight, arrivals, chips)
    (li_inner,) = run(
        inner_body,
        columns,
        [tile(after(li_input, *[piece for _, piece in cot_line])), tile(li_spec), table("half2"), table("first3")],
        [(rows, F32)],
        3 * pass_flops,
    )
    li_out, mixed_li = run(
        long_body,
        columns,
        [tile(li_inner), tile(query_li), tile(rate), tile(coef), tile(entering)],
        [(rows, F32), (rows, BF16)],
        pass_flops,
    )

    mixed_all = lax.all_gather(mixed_li, "ctx", axis=0, tiled=True)
    cot_full = placed([(index, after(piece, mixed_li)) for index, piece in cot_line])

    full_width = cot_full.shape[1]
    line_width = full_width // line_count
    whole_flops = 2 * rows * columns * full_width
    (out_early,) = run_once(
        out_early_body,
        [jnp.stack(starts_of(early)), mixed_li] + arrays_of(early),
        [((rows, full_width), BF16)],
        [],
        whole_flops,
    )
    cot_full = after(cot_full, out_early)
    (grad_early,) = run(
        grad_early_body,
        columns,
        [("scalar", jnp.stack(starts_of(early))), ("whole", cot_full)] + [tile(piece) for piece in arrays_of(early)],
        [(rows, F32)],
        whole_flops,
    )
    cot_rows = plane_trade(columns_to_rows(after(cot_full, grad_early), chips))
    grad_mixed, grad_li_out, back_ends = run(
        functools.partial(grad_gate_body, len(late)),
        columns,
        [
            ("scalar", jnp.stack(starts_of(late))),
            tile(grad_early),
            ("whole", cot_full),
            tile(query_li),
            tile(rate),
        ]
        + [tile(piece) for piece in arrays_of(late)],
        [(rows, F32), (rows, F32), (rate.shape[0], F32)],
        whole_flops,
    )
    out_starts = starts_of(late) + [(line ^ r) * line_width for r in range(line_count)]
    out_parts = run_once(
        functools.partial(out_late_body, len(late)),
        [jnp.stack(out_starts), after(out_early, back_ends), mixed_li] + arrays_of(late),
        [((rows, line_width), BF16)] * line_count,
        [pltpu.VMEM((rows, full_width), BF16)],
        whole_flops,
    )
    output = out_parts[0].astype(F32)
    for r in range(1, line_count):
        output = output + line_swap(out_parts[r], r).astype(F32)

    back_entering = entering_direct(back_ends, rate, rows, here, True)
    (grad_inner,) = run(
        grad_inner_body,
        columns,
        [tile(after(grad_li_out, out_parts[0])), tile(li_spec), table("half3"), table("first3")],
        [(rows, F32)],
        3 * pass_flops,
    )
    grad_query_li = grad_mixed * li_out
    grad_key_li, grad_query_mr, grad_spec, tap_partial = run(
        grad_long_body,
        columns,
        [
            tile(grad_inner),
            tile(rate),
            tile(coef),
            tile(back_entering),
            tile(mixed_mr),
            tile(key_li),
            tile(query_mr),
            tile(mr_conv),
            tile(spec),
            table("half3"),
            table("lags3"),
        ],
        [(rows, F32), (rows, F32), (2 * rows, F32), (rows, F32)],
        4 * pass_flops,
    )
    own_product, prev_product = run(
        grad_taps_body,
        columns,
        [tile(grad_spec), tile(mr_spec), table("both3")],
        [(rows, F32), (rows, BF16)],
        3 * pass_flops,
    )
    arrived = shifted(prev_product, -1)
    grad_key_mr, grad_value_mr = run(
        grad_product_body,
        columns,
        [tile(own_product), tile(arrived), tile(key_mr), tile(value_mr)],
        [(rows, F32), (rows, F32)],
        rows * columns,
    )

    tap_half = tap_partial.shape[0] // 2
    halves = tap_partial.reshape(2, tap_half, columns)
    own_half = lax.dynamic_index_in_dim(halves, core, 0, keepdims=False)
    far_half = lax.dynamic_index_in_dim(halves, 1 - core, 0, keepdims=False)
    plane_half = own_half + core_swap(far_half)
    by = 1
    while by < chips:
        sent = plane_half.astype(BF16)
        plane_half = sent.astype(F32) + chip_swap(sent, by).astype(F32)
        by *= 2
    plane_half = plane_half * grad_scale
    other_half = core_swap(plane_half)
    grad_taps = jnp.where(
        core == 0,
        jnp.concatenate([plane_half, other_half], axis=0),
        jnp.concatenate([other_half, plane_half], axis=0),
    )

    near_rows = columns_at(cot_rows, core, width).reshape(chips, 1, rows, width)
    far_rows = core_swap(columns_at(cot_rows, 1 - core, width)).reshape(chips, 1, rows, width)
    both = jnp.zeros((chips, 2, rows, width), BF16)
    both = lax.dynamic_update_slice_in_dim(both, near_rows, core, 1)
    both = lax.dynamic_update_slice_in_dim(both, far_rows, 1 - core, 1)
    grad_weight = (
        lax.dot_general(
            both.reshape(rows * ctx_count, width),
            mixed_all,
            (((0,), (0,)), ((), ())),
            preferred_element_type=F32,
        )
        * grad_scale
    )
    return (
        output,
        grad_query_mr,
        grad_key_mr,
        grad_value_mr,
        grad_query_li,
        grad_key_li,
        grad_taps,
        grad_weight,
    )


def solution(mesh):
    rows = P("ctx", "fsdp")
    channels = P(None, "fsdp")
    return jax.shard_map(
        shards,
        mesh=mesh,
        in_specs=(rows,) * 5 + (channels,) * 3 + (P("fsdp"),) + (rows,) * 2,
        out_specs=(rows,) * 6 + (channels, rows),
        check_vma=False,
    )
```

```python
import functools
import math

import jax
import jax.numpy as jnp
import ml_dtypes
import numpy as np
from jax import lax
from jax.experimental import pallas as pl
from jax.experimental.pallas import tpu as pltpu
from jax.sharding import PartitionSpec as P

F32 = jnp.float32
BF16 = jnp.bfloat16
TILE = 256
GROUP = 8
SWAPS = 3


def split_parts(matrix):
    high = matrix.astype(ml_dtypes.bfloat16)
    low = (matrix - high.astype(np.float64)).astype(ml_dtypes.bfloat16)
    return high, low


def two_fold(matrix):
    high, low = split_parts(matrix)
    return np.concatenate([high, low], axis=1)


def three_fold(matrix):
    high, low = split_parts(matrix)
    return np.concatenate([high, low, high], axis=1)


@functools.lru_cache(maxsize=None)
def dft_tables(rows):
    size = 2 * rows
    angle = 2.0 * np.pi * (np.arange(rows)[:, None] + 0.5) * np.arange(size)[None, :] / size
    ahead = np.concatenate([np.cos(angle), -np.sin(angle)], axis=0)
    back = ahead.T * (2.0 / size)
    signed = np.concatenate([back[:rows], -back[rows:]], axis=0)
    lags = back[rows - np.arange(rows)]
    return {"ahead": two_fold(ahead), "back": three_fold(signed), "lags": three_fold(lags)}


def half_table(ahead):
    rows = ahead.shape[0] // 2
    high, low = ahead[:, :rows], ahead[:, 2 * rows : 3 * rows]
    return high, low


def apply2(table, x):
    return jnp.dot(table, jnp.concatenate([x, x], axis=0), preferred_element_type=F32)


def apply3(table, x):
    high = x.astype(BF16)
    low = (x - high.astype(F32)).astype(BF16)
    return jnp.dot(table, jnp.concatenate([high, high, low], axis=0), preferred_element_type=F32)


def to_spectrum(ahead, x):
    high, low = half_table(ahead)
    return apply3(jnp.concatenate([high, low, high], axis=1), x)


def to_spectrum_exact(ahead, x):
    return apply2(jnp.concatenate(half_table(ahead), axis=1), x)


def times(x, y):
    half = x.shape[0] // 2
    xr, xi, yr, yi = x[:half], x[half:], y[:half], y[half:]
    return jnp.concatenate([xr * yr - xi * yi, xr * yi + xi * yr], axis=0)


def times_conj(x, y):
    half = x.shape[0] // 2
    xr, xi, yr, yi = x[:half], x[half:], y[:half], y[half:]
    return jnp.concatenate([xr * yr + xi * yi, xi * yr - xr * yi], axis=0)


def group_places(columns):
    return lax.broadcasted_iota(jnp.int32, (GROUP, columns), 0).astype(F32)


def spread_modes(rate, weight, rows, shift, backward):
    columns = rate.shape[1]
    places = group_places(columns)
    if backward:
        places = (GROUP - 1.0) - places
    count = rows // GROUP
    order = range(count - 1, -1, -1) if backward else range(count)
    sums = [None] * count
    for m in range(rate.shape[0]):
        rate_m = rate[m : m + 1]
        current = weight[m : m + 1] * jnp.exp(-rate_m * (places + shift))
        stride = jnp.broadcast_to(jnp.exp(-rate_m * GROUP), current.shape)
        for step, g in enumerate(order):
            sums[g] = current if sums[g] is None else sums[g] + current
            if step < count - 1:
                current = current * stride
    return jnp.concatenate(sums, axis=0)


def fold_modes(signal, rate, backward):
    columns = rate.shape[1]
    places = group_places(columns)
    if not backward:
        places = (GROUP - 1.0) - places
    count = signal.shape[0] // GROUP
    order = range(count - 1, -1, -1) if backward else range(count)
    found = []
    for m in range(rate.shape[0]):
        rate_m = rate[m : m + 1]
        stride = jnp.broadcast_to(jnp.exp(-rate_m * GROUP), (GROUP, columns))
        running = None
        for g in order:
            piece = signal[g * GROUP : (g + 1) * GROUP]
            running = piece if running is None else running * stride + piece
        found.append(jnp.sum(running * jnp.exp(-rate_m * places), axis=0, keepdims=True))
    return jnp.concatenate(found, axis=0)


def spectra_body(taps, rate, coef, skip, ahead, mr_spec, li_spec):
    rows = taps.shape[0]
    table = ahead[...]
    mr_spec[...] = to_spectrum(table, taps[...])
    kernel = spread_modes(rate[...], coef[...], rows, 0.0, False)
    first = lax.broadcasted_iota(jnp.int32, kernel.shape, 0) == 0
    kernel = kernel + jnp.where(first, skip[...], 0.0)
    li_spec[...] = to_spectrum(table, kernel)


def short_body(before, product, query, key, mr_spec, rate, ahead, back, spec, conv, mixed, signal, ends):
    rows = product.shape[0]
    x = jnp.concatenate([before[...], product[...]], axis=0)
    found = apply2(ahead[...], x)
    spec[...] = found
    filtered = -apply3(back[rows:], times(found, mr_spec[...]))
    conv[...] = filtered
    mixed_rows = (query[...].astype(F32) * filtered).astype(BF16)
    mixed[...] = mixed_rows
    rounded = (key[...].astype(F32) * mixed_rows.astype(F32)).astype(BF16)
    signal[...] = rounded
    ends[...] = fold_modes(rounded.astype(F32), rate[...], False)


def inner_body(signal, li_spec, ahead, back, inner):
    rows = signal.shape[0]
    inner[...] = apply3(back[:rows], times(to_spectrum_exact(ahead[...], signal[...]), li_spec[...]))


def long_body(inner, query, rate, coef, entering, li_out, mixed):
    rows = inner.shape[0]
    total = inner[...] + spread_modes(rate[...], coef[...] * entering[...], rows, 1.0, False)
    li_out[...] = total
    mixed[...] = (query[...].astype(F32) * total).astype(BF16)


def split_body(width, count, starts, *rest):
    pieces, near, shares = rest[:count], rest[count], rest[count + 1 : -1]
    far = rest[-1]
    for r, piece in enumerate(pieces):
        for k in range(piece.shape[1] // (2 * width)):
            place = pl.multiple_of(starts[r], 128) + k * width
            near[:, pl.ds(place, width)] = piece[:, pl.ds(pl.multiple_of(starts[count], 128) + 2 * k * width, width)]
            far[:, pl.ds(place, width)] = piece[:, pl.ds(pl.multiple_of(starts[count + 1], 128) + 2 * k * width, width)]
    part = far.shape[1] // len(shares)
    for k, share in enumerate(shares):
        share[...] = far[:, k * part : (k + 1) * part]


def grad_share_body(near, far, weight, own, sent):
    own[...] = jnp.dot(near[...], weight[...], preferred_element_type=F32)
    sent[...] = jnp.dot(far[...], weight[...], preferred_element_type=F32).astype(BF16)


def grad_gate_body(own, arrived, query, rate, grad_mixed, grad_out, ends):
    total = own[...] + arrived[...].astype(F32)
    grad_mixed[...] = total
    gated = total * query[...].astype(F32)
    grad_out[...] = gated
    ends[...] = fold_modes(gated, rate[...], True)


def out_share_body(starts, near, far, weight, *rest):
    parts, whole = rest[:-1], rest[-1]
    rows = near.shape[0]
    contract = (((1,), (1,)), ((), ()))
    whole[:rows] = lax.dot_general(near[...], weight[...], contract, preferred_element_type=F32).astype(BF16)
    whole[rows:] = lax.dot_general(far[...], weight[...], contract, preferred_element_type=F32).astype(BF16)
    width = parts[0].shape[1]
    for r, part in enumerate(parts):
        part[...] = whole[:, pl.ds(pl.multiple_of(starts[r], 128), width)]


def grad_inner_body(grad_out, li_spec, ahead, back, inner):
    rows = grad_out.shape[0]
    inner[...] = apply3(back[:rows], times_conj(to_spectrum(ahead[...], grad_out[...]), li_spec[...]))


def grad_long_body(
    inner, rate, coef, entering, mixed_mr, key_li, query_mr, conv, spec, ahead, lags,
    grad_key_li, grad_query_mr, grad_spec, taps,
):
    rows = inner.shape[0]
    grad_input = inner[...] + spread_modes(rate[...], coef[...] * entering[...], rows, 1.0, True)
    grad_key_li[...] = grad_input * mixed_mr[...].astype(F32)
    grad_mixed_mr = grad_input * key_li[...].astype(F32)
    grad_query_mr[...] = grad_mixed_mr * conv[...]
    grad_conv = grad_mixed_mr * query_mr[...].astype(F32)
    found = to_spectrum(ahead[...], grad_conv)
    grad_spec[...] = found
    taps[...] = apply3(lags[...], times_conj(spec[...], found))


def grad_taps_body(grad_spec, mr_spec, back, own_product, prev_product):
    rows = own_product.shape[0]
    products = apply3(back[...], times_conj(grad_spec[...], mr_spec[...]))
    own_product[...] = products[:rows]
    prev_product[...] = products[rows:].astype(BF16)


def grad_product_body(own, arrived, key, value, grad_key, grad_value):
    total = own[...] + arrived[...].astype(F32)
    grad_key[...] = total * value[...].astype(F32)
    grad_value[...] = total * key[...].astype(F32)


def run(body, columns, inputs, outputs, flops):
    tile = min(TILE, columns)
    in_specs = []
    moved = 0
    for kind, array in inputs:
        if kind == "tile":
            in_specs.append(pl.BlockSpec((array.shape[0], tile), lambda c: (0, c)))
        elif kind == "whole":
            in_specs.append(pl.BlockSpec(array.shape, lambda c: (0, 0)))
        else:
            in_specs.append(pl.BlockSpec(memory_space=pltpu.SMEM))
        moved += math.prod(array.shape) * array.dtype.itemsize
    for rows, dtype in outputs:
        moved += rows * columns * jnp.dtype(dtype).itemsize
    return pl.pallas_call(
        body,
        grid=(columns // tile,),
        in_specs=in_specs,
        out_specs=[pl.BlockSpec((rows, tile), lambda c: (0, c)) for rows, _ in outputs],
        out_shape=[jax.ShapeDtypeStruct((rows, columns), dtype) for rows, dtype in outputs],
        compiler_params=pltpu.CompilerParams(vmem_limit_bytes=32 * 1024 * 1024),
        cost_estimate=pl.CostEstimate(flops=flops, bytes_accessed=moved, transcendentals=0),
    )(*[array for _, array in inputs])


def run_once(body, inputs, outputs, scratch, flops):
    moved = sum(math.prod(array.shape) * array.dtype.itemsize for array in inputs)
    return pl.pallas_call(
        body,
        in_specs=[pl.BlockSpec(memory_space=pltpu.SMEM)]
        + [pl.BlockSpec(memory_space=pltpu.VMEM)] * (len(inputs) - 1),
        out_specs=[pl.BlockSpec(memory_space=pltpu.VMEM)] * len(outputs),
        out_shape=[jax.ShapeDtypeStruct(shape, dtype) for shape, dtype in outputs],
        scratch_shapes=scratch,
        compiler_params=pltpu.CompilerParams(vmem_limit_bytes=32 * 1024 * 1024),
        cost_estimate=pl.CostEstimate(flops=flops, bytes_accessed=moved, transcendentals=0),
    )(*inputs)


def core_swap(x):
    size = lax.axis_size("ctx")
    return lax.ppermute(x, "ctx", [(i, i ^ 1) for i in range(size)])


def shifted(x, by):
    size = lax.axis_size("ctx")
    return lax.ppermute(x, "ctx", [(i, i + by) for i in range(size) if 0 <= i + by < size])


def chip_swap(x, by):
    size = lax.axis_size("ctx")
    return lax.ppermute(x, "ctx", [(i, i ^ (2 * by)) for i in range(size)])


def line_swap(x, by):
    size = lax.axis_size("fsdp")
    return lax.ppermute(x, "fsdp", [(i, i ^ by) for i in range(size)])


def plane_trade(x):
    return lax.all_to_all(x, "ctx", 0, 0, axis_index_groups=plane_groups(), tiled=True)


def columns_to_rows(x, count):
    return jnp.concatenate(jnp.split(x, count, axis=1), axis=0)


def plane_groups():
    size = lax.axis_size("ctx")
    return [list(range(core, size, 2)) for core in range(2)]


def after(x, *others):
    return lax.optimization_barrier((x,) + others)[0]


def doubling_factors(rate, rows, here, backward):
    factors = []
    by = 1
    while by < lax.axis_size("ctx"):
        offset = here & (by - 1)
        if backward:
            offset = by - 1 - offset
        factors.append((jnp.exp(-rate * (rows * offset).astype(F32)), jnp.exp(-rate * float(rows * by))))
        by *= 2
    return factors


def entering_state(ends, factors, here, backward):
    size = lax.axis_size("ctx")
    total, entering = ends, jnp.zeros_like(ends)
    by = 1
    for to_here, across in factors:
        arrived = lax.ppermute(total, "ctx", [(i, i ^ by) for i in range(size)])
        later = ((here & by) != 0) != backward
        entering = entering + jnp.where(later, to_here * arrived, 0.0)
        total = jnp.where(later, across * arrived + total, across * total + arrived)
        by *= 2
    return entering


def direct_factors(rate, rows, chip, backward):
    factors = [jnp.exp(-rate * float(rows))]
    for s in range(1, lax.axis_size("ctx") // 2):
        gap = (chip ^ s) - chip - 1 if backward else chip - (chip ^ s) - 1
        weight = jnp.exp(-rate * (2 * rows * jnp.maximum(gap, 0)).astype(F32))
        factors.append(jnp.where(gap >= 0, weight, 0.0))
    return factors


def entering_direct(ends, factors, here, backward):
    block = factors[0]
    later_core = ((here & 1) != 0) != backward
    sibling = core_swap(ends)
    total = jnp.where(later_core, block * sibling + ends, block * ends + sibling)
    entering = jnp.zeros_like(ends)
    for s, weight in enumerate(factors[1:], 1):
        entering = entering + weight * chip_swap(total, s)
    return jnp.where(later_core, block * entering + sibling, entering)


def shards(
    query_mr,
    key_mr,
    value_mr,
    query_li,
    key_li,
    mr_taps,
    li_time,
    li_residue,
    li_skip,
    out_weight,
    cotangent,
):
    rows, columns = query_mr.shape
    ctx_count = lax.axis_size("ctx")
    line_count = lax.axis_size("fsdp")
    chips = ctx_count // 2
    here = lax.axis_index("ctx")
    core = here % 2
    line = lax.axis_index("fsdp")
    grad_scale = 1.0 / math.sqrt(rows * ctx_count)
    tables = {name: jnp.asarray(table) for name, table in dft_tables(rows).items()}
    width = out_weight.shape[0]
    pass_flops = 2 * (2 * rows) * (2 * rows) * columns

    def tile(x):
        return ("tile", x)

    def table(name):
        return ("whole", tables[name])

    mr_product = (key_mr.astype(F32) * value_mr.astype(F32)).astype(BF16)
    before = shifted(mr_product, 1)
    weight_rows = lax.all_gather(out_weight, "ctx", axis=0, tiled=True, axis_index_groups=plane_groups())
    cot_line = [(line, cotangent)]
    for r in range(1, line_count):
        cot_line.append((line ^ r, line_swap(cotangent, r)))

    rate = 1.0 / li_time
    coef = li_residue * jnp.sqrt(-jnp.expm1(-2.0 * rate))
    ahead_factors, back_factors = lax.optimization_barrier(
        (doubling_factors(rate, rows, here, False), direct_factors(rate, rows, here // 2, True))
    )
    mr_spec, li_spec = run(
        spectra_body,
        columns,
        [tile(mr_taps), tile(rate), tile(coef), tile(li_skip[None, :]), table("ahead")],
        [(2 * rows, F32), (2 * rows, F32)],
        3 * pass_flops,
    )
    spec, mr_conv, mixed_mr, li_input, ends = run(
        short_body,
        columns,
        [
            tile(before),
            tile(mr_product),
            tile(query_mr),
            tile(key_li),
            tile(mr_spec),
            tile(rate),
            table("ahead"),
            table("back"),
        ],
        [(2 * rows, F32), (rows, F32), (rows, BF16), (rows, BF16), (rate.shape[0], F32)],
        4 * pass_flops,
    )
    entering = entering_state(ends, ahead_factors, here, False)
    (li_inner,) = run(
        inner_body,
        columns,
        [tile(li_input), tile(li_spec), table("ahead"), table("back")],
        [(rows, F32)],
        3 * pass_flops,
    )
    li_out, mixed_li = run(
        long_body,
        columns,
        [tile(li_inner), tile(query_li), tile(rate), tile(coef), tile(entering)],
        [(rows, F32), (rows, BF16)],
        pass_flops,
    )

    other_mixed = core_swap(mixed_li)
    mixed_all = lax.all_gather(mixed_li, "ctx", axis=0, tiled=True)

    part_width = chips * width // line_count
    near, *to_far = run_once(
        functools.partial(split_body, width, line_count),
        [jnp.stack([index * part_width for index, _ in cot_line] + [core * width, (1 - core) * width])]
        + [piece for _, piece in cot_line],
        [((rows, chips * width), BF16)] + [((rows, chips * width // 4), BF16)] * 4,
        [pltpu.VMEM((rows, chips * width), BF16)],
        0,
    )
    far_parts = [core_swap(to_far[0]), core_swap(to_far[1])]
    for part in to_far[2:]:
        far_parts.append(core_swap(after(part, far_parts[-1])))
    far = jnp.concatenate(far_parts, axis=1)
    near = after(near, mixed_li)
    cot_rows = plane_trade(
        columns_to_rows(
            jnp.where(core == 0, jnp.concatenate([near, far], axis=0), jnp.concatenate([far, near], axis=0)), chips
        )
    )

    share_flops = 4 * rows * columns * chips * width
    own_share, sent_share = run(
        grad_share_body,
        columns,
        [("whole", near), ("whole", far), tile(weight_rows)],
        [(rows, F32), (rows, BF16)],
        share_flops,
    )
    arrived_share = core_swap(sent_share)
    out_parts = run_once(
        out_share_body,
        [
            jnp.stack([(line ^ r) * part_width for r in range(line_count)]),
            after(mixed_li, sent_share),
            other_mixed,
            weight_rows,
        ],
        [((2 * rows, part_width), BF16)] * line_count,
        [pltpu.VMEM((2 * rows, chips * width), BF16)],
        share_flops,
    )
    out_sum = out_parts[0].astype(F32)
    for r in range(1, line_count):
        out_sum = out_sum + line_swap(out_parts[r], r).astype(F32)
    near_out, far_out = out_sum[:rows], core_swap(out_sum[rows:])
    output = jnp.where(
        core == 0, jnp.concatenate([near_out, far_out], axis=1), jnp.concatenate([far_out, near_out], axis=1)
    )

    grad_mixed, grad_li_out, back_ends = run(
        grad_gate_body,
        columns,
        [tile(after(own_share, out_parts[0])), tile(arrived_share), tile(query_li), tile(rate)],
        [(rows, F32), (rows, F32), (rate.shape[0], F32)],
        rows * columns,
    )
    back_entering = entering_direct(back_ends, back_factors, here, True)
    (grad_inner,) = run(
        grad_inner_body,
        columns,
        [tile(grad_li_out), tile(li_spec), table("ahead"), table("back")],
        [(rows, F32)],
        3 * pass_flops,
    )
    grad_query_li = grad_mixed * li_out
    grad_key_li, grad_query_mr, grad_spec, tap_partial = run(
        grad_long_body,
        columns,
        [
            tile(grad_inner),
            tile(rate),
            tile(coef),
            tile(back_entering),
            tile(mixed_mr),
            tile(key_li),
            tile(query_mr),
            tile(mr_conv),
            tile(spec),
            table("ahead"),
            table("lags"),
        ],
        [(rows, F32), (rows, F32), (2 * rows, F32), (rows, F32)],
        4 * pass_flops,
    )
    own_product, prev_product = run(
        grad_taps_body,
        columns,
        [tile(grad_spec), tile(mr_spec), table("back")],
        [(rows, F32), (rows, BF16)],
        3 * pass_flops,
    )
    arrived = shifted(prev_product, -1)
    grad_key_mr, grad_value_mr = run(
        grad_product_body,
        columns,
        [tile(own_product), tile(arrived), tile(key_mr), tile(value_mr)],
        [(rows, F32), (rows, F32)],
        rows * columns,
    )

    tap_half = tap_partial.shape[0] // 2
    halves = tap_partial.reshape(2, tap_half, columns)
    own_half = lax.dynamic_index_in_dim(halves, core, 0, keepdims=False)
    far_half = lax.dynamic_index_in_dim(halves, 1 - core, 0, keepdims=False)
    plane_half = own_half + core_swap(far_half)
    by = 1
    while by < chips:
        sent = plane_half.astype(BF16)
        plane_half = sent.astype(F32) + chip_swap(sent, by).astype(F32)
        by *= 2
    plane_half = plane_half * grad_scale
    other_half = core_swap(plane_half)
    grad_taps = jnp.where(
        core == 0,
        jnp.concatenate([plane_half, other_half], axis=0),
        jnp.concatenate([other_half, plane_half], axis=0),
    )

    grad_weight = (
        lax.dot_general(cot_rows, mixed_all, (((0,), (0,)), ((), ())), preferred_element_type=F32) * grad_scale
    )
    return (
        output,
        grad_query_mr,
        grad_key_mr,
        grad_value_mr,
        grad_query_li,
        grad_key_li,
        grad_taps,
        grad_weight,
    )


def solution(mesh):
    rows = P("ctx", "fsdp")
    channels = P(None, "fsdp")
    return jax.shard_map(
        shards,
        mesh=mesh,
        in_specs=(rows,) * 5 + (channels,) * 3 + (P("fsdp"),) + (rows,) * 2,
        out_specs=(rows,) * 6 + (channels, rows),
        check_vma=False,
    )
```

```python
import functools
import math

import jax
import jax.numpy as jnp
import ml_dtypes
import numpy as np
from jax import lax
from jax.experimental import pallas as pl
from jax.experimental.pallas import tpu as pltpu
from jax.sharding import PartitionSpec as P

F32 = jnp.float32
BF16 = jnp.bfloat16
TILE = 256
GROUP = 8


def split_parts(matrix):
    high = matrix.astype(ml_dtypes.bfloat16)
    low = (matrix - high.astype(np.float64)).astype(ml_dtypes.bfloat16)
    return high, low


def two_fold(matrix):
    high, low = split_parts(matrix)
    return np.concatenate([high, low], axis=1)


def three_fold(matrix):
    high, low = split_parts(matrix)
    return np.concatenate([high, low, high], axis=1)


@functools.lru_cache(maxsize=None)
def dft_tables(rows):
    size = 2 * rows
    angle = 2.0 * np.pi * (np.arange(rows)[:, None] + 0.5) * np.arange(size)[None, :] / size
    ahead = np.concatenate([np.cos(angle), -np.sin(angle)], axis=0)
    back = ahead.T * (2.0 / size)
    signed = np.concatenate([back[:rows], -back[rows:]], axis=0)
    lags = back[rows - np.arange(rows)]
    return {"ahead": two_fold(ahead), "back": three_fold(signed), "lags": three_fold(lags)}


def half_table(ahead):
    rows = ahead.shape[0] // 2
    high, low = ahead[:, :rows], ahead[:, 2 * rows : 3 * rows]
    return high, low


def apply2(table, x):
    return jnp.dot(table, jnp.concatenate([x, x], axis=0), preferred_element_type=F32)


def apply3(table, x):
    high = x.astype(BF16)
    low = (x - high.astype(F32)).astype(BF16)
    return jnp.dot(table, jnp.concatenate([high, high, low], axis=0), preferred_element_type=F32)


def to_spectrum(ahead, x):
    high, low = half_table(ahead)
    return apply3(jnp.concatenate([high, low, high], axis=1), x)


def to_spectrum_exact(ahead, x):
    return apply2(jnp.concatenate(half_table(ahead), axis=1), x)


def times(x, y):
    half = x.shape[0] // 2
    xr, xi, yr, yi = x[:half], x[half:], y[:half], y[half:]
    return jnp.concatenate([xr * yr - xi * yi, xr * yi + xi * yr], axis=0)


def times_conj(x, y):
    half = x.shape[0] // 2
    xr, xi, yr, yi = x[:half], x[half:], y[:half], y[half:]
    return jnp.concatenate([xr * yr + xi * yi, xi * yr - xr * yi], axis=0)


def group_places(columns):
    return lax.broadcasted_iota(jnp.int32, (GROUP, columns), 0).astype(F32)


def spread_modes(rate, weight, rows, shift, backward):
    columns = rate.shape[1]
    places = group_places(columns)
    if backward:
        places = (GROUP - 1.0) - places
    count = rows // GROUP
    order = range(count - 1, -1, -1) if backward else range(count)
    sums = [None] * count
    for m in range(rate.shape[0]):
        rate_m = rate[m : m + 1]
        current = weight[m : m + 1] * jnp.exp(-rate_m * (places + shift))
        stride = jnp.broadcast_to(jnp.exp(-rate_m * GROUP), current.shape)
        for step, g in enumerate(order):
            sums[g] = current if sums[g] is None else sums[g] + current
            if step < count - 1:
                current = current * stride
    return jnp.concatenate(sums, axis=0)


def fold_modes(signal, rate, backward):
    columns = rate.shape[1]
    places = group_places(columns)
    if not backward:
        places = (GROUP - 1.0) - places
    count = signal.shape[0] // GROUP
    order = range(count - 1, -1, -1) if backward else range(count)
    found = []
    for m in range(rate.shape[0]):
        rate_m = rate[m : m + 1]
        stride = jnp.broadcast_to(jnp.exp(-rate_m * GROUP), (GROUP, columns))
        running = None
        for g in order:
            piece = signal[g * GROUP : (g + 1) * GROUP]
            running = piece if running is None else running * stride + piece
        found.append(jnp.sum(running * jnp.exp(-rate_m * places), axis=0, keepdims=True))
    return jnp.concatenate(found, axis=0)


def spectra_body(taps, rate, coef, skip, ahead, mr_spec, li_spec):
    rows = taps.shape[0]
    table = ahead[...]
    mr_spec[...] = to_spectrum(table, taps[...])
    kernel = spread_modes(rate[...], coef[...], rows, 0.0, False)
    first = lax.broadcasted_iota(jnp.int32, kernel.shape, 0) == 0
    kernel = kernel + jnp.where(first, skip[...], 0.0)
    li_spec[...] = to_spectrum(table, kernel)


def short_body(before, product, query, key, mr_spec, rate, ahead, back, spec, conv, mixed, signal, ends):
    rows = product.shape[0]
    x = jnp.concatenate([before[...], product[...]], axis=0)
    found = apply2(ahead[...], x)
    spec[...] = found
    filtered = -apply3(back[rows:], times(found, mr_spec[...]))
    conv[...] = filtered
    mixed_rows = (query[...].astype(F32) * filtered).astype(BF16)
    mixed[...] = mixed_rows
    rounded = (key[...].astype(F32) * mixed_rows.astype(F32)).astype(BF16)
    signal[...] = rounded
    ends[...] = fold_modes(rounded.astype(F32), rate[...], False)


def inner_body(signal, li_spec, ahead, back, inner):
    rows = signal.shape[0]
    inner[...] = apply3(back[:rows], times(to_spectrum_exact(ahead[...], signal[...]), li_spec[...]))


def long_body(inner, query, rate, coef, entering, li_out, mixed):
    rows = inner.shape[0]
    total = inner[...] + spread_modes(rate[...], coef[...] * entering[...], rows, 1.0, False)
    li_out[...] = total
    mixed[...] = (query[...].astype(F32) * total).astype(BF16)


def split_body(width, starts, *rest):
    pieces, (first, second, stack) = rest[:-3], rest[-3:]
    rows = first.shape[0]
    half = width // 2
    for r, piece in enumerate(pieces):
        for k in range(piece.shape[1] // width):
            block = starts[r] + k
            place = pl.ds(pl.multiple_of(block * half, 128), half)
            first[:, place] = piece[:, k * width : k * width + half]
            second[:, place] = piece[:, k * width + half : (k + 1) * width]
            stack[pl.ds(pl.multiple_of(block * rows, 128), rows), :] = piece[:, k * width : (k + 1) * width]


def grad_early_body(cotangent, weight, total):
    total[...] = jnp.dot(cotangent[...], weight[...], preferred_element_type=F32)


def grad_gate_body(early, cotangent, weight, query, rate, grad_mixed, grad_out, ends):
    total = early[...] + jnp.dot(cotangent[...], weight[...], preferred_element_type=F32)
    grad_mixed[...] = total
    gated = total * query[...].astype(F32)
    grad_out[...] = gated
    ends[...] = fold_modes(gated, rate[...], True)


def out_body(starts, mixed, weight, *rest):
    parts, whole = rest[:-1], rest[-1]
    contract = (((1,), (1,)), ((), ()))
    whole[...] = lax.dot_general(mixed[...], weight[...], contract, preferred_element_type=F32).astype(BF16)
    width = parts[0].shape[1]
    for r, part in enumerate(parts):
        part[...] = whole[:, pl.ds(pl.multiple_of(starts[r], 128), width)]


def out_sum_body(width, count, *rest):
    parts, result = rest[:-1], rest[-1]
    half = width // 2
    for h in range(2):
        total = parts[h * count][...].astype(F32)
        for part in parts[h * count + 1 : (h + 1) * count]:
            total = total + part[...].astype(F32)
        for k in range(total.shape[1] // half):
            result[:, k * width + h * half : k * width + (h + 1) * half] = total[:, k * half : (k + 1) * half]


def grad_inner_body(grad_out, li_spec, ahead, back, inner):
    rows = grad_out.shape[0]
    inner[...] = apply3(back[:rows], times_conj(to_spectrum(ahead[...], grad_out[...]), li_spec[...]))


def grad_long_body(
    inner, rate, coef, entering, mixed_mr, key_li, query_mr, conv, spec, ahead, lags,
    grad_key_li, grad_query_mr, grad_spec, taps,
):
    rows = inner.shape[0]
    grad_input = inner[...] + spread_modes(rate[...], coef[...] * entering[...], rows, 1.0, True)
    grad_key_li[...] = grad_input * mixed_mr[...].astype(F32)
    grad_mixed_mr = grad_input * key_li[...].astype(F32)
    grad_query_mr[...] = grad_mixed_mr * conv[...]
    grad_conv = grad_mixed_mr * query_mr[...].astype(F32)
    found = to_spectrum(ahead[...], grad_conv)
    grad_spec[...] = found
    taps[...] = apply3(lags[...], times_conj(spec[...], found))


def grad_taps_body(grad_spec, mr_spec, back, own_product, prev_product):
    rows = own_product.shape[0]
    products = apply3(back[...], times_conj(grad_spec[...], mr_spec[...]))
    own_product[...] = products[:rows]
    prev_product[...] = products[rows:].astype(BF16)


def grad_product_body(own, arrived, key, value, grad_key, grad_value):
    total = own[...] + arrived[...].astype(F32)
    grad_key[...] = total * value[...].astype(F32)
    grad_value[...] = total * key[...].astype(F32)


def run(body, columns, inputs, outputs, flops):
    tile = min(TILE, columns)
    in_specs = []
    moved = 0
    for kind, array in inputs:
        if kind == "tile":
            in_specs.append(pl.BlockSpec((array.shape[0], tile), lambda c: (0, c)))
        elif kind == "whole":
            in_specs.append(pl.BlockSpec(array.shape, lambda c: (0, 0)))
        else:
            in_specs.append(pl.BlockSpec(memory_space=pltpu.SMEM))
        moved += math.prod(array.shape) * array.dtype.itemsize
    for rows, dtype in outputs:
        moved += rows * columns * jnp.dtype(dtype).itemsize
    return pl.pallas_call(
        body,
        grid=(columns // tile,),
        in_specs=in_specs,
        out_specs=[pl.BlockSpec((rows, tile), lambda c: (0, c)) for rows, _ in outputs],
        out_shape=[jax.ShapeDtypeStruct((rows, columns), dtype) for rows, dtype in outputs],
        compiler_params=pltpu.CompilerParams(vmem_limit_bytes=32 * 1024 * 1024),
        cost_estimate=pl.CostEstimate(flops=flops, bytes_accessed=moved, transcendentals=0),
    )(*[array for _, array in inputs])


def run_once(body, inputs, outputs, scratch, flops):
    in_specs = [pl.BlockSpec(memory_space=pltpu.VMEM)] * (len(inputs) - 1)
    if inputs[0] is None:
        inputs = inputs[1:]
    else:
        in_specs = [pl.BlockSpec(memory_space=pltpu.SMEM)] + in_specs
    moved = sum(math.prod(array.shape) * array.dtype.itemsize for array in inputs)
    return pl.pallas_call(
        body,
        in_specs=in_specs,
        out_specs=[pl.BlockSpec(memory_space=pltpu.VMEM)] * len(outputs),
        out_shape=[jax.ShapeDtypeStruct(shape, dtype) for shape, dtype in outputs],
        scratch_shapes=scratch,
        compiler_params=pltpu.CompilerParams(vmem_limit_bytes=32 * 1024 * 1024),
        cost_estimate=pl.CostEstimate(flops=flops, bytes_accessed=moved, transcendentals=0),
    )(*inputs)


def core_swap(x):
    size = lax.axis_size("ctx")
    return lax.ppermute(x, "ctx", [(i, i ^ 1) for i in range(size)])


def shifted(x, by):
    size = lax.axis_size("ctx")
    return lax.ppermute(x, "ctx", [(i, i + by) for i in range(size) if 0 <= i + by < size])


def chip_swap(x, by):
    size = lax.axis_size("ctx")
    return lax.ppermute(x, "ctx", [(i, i ^ (2 * by)) for i in range(size)])


def line_swap(x, by):
    size = lax.axis_size("fsdp")
    return lax.ppermute(x, "fsdp", [(i, i ^ by) for i in range(size)])


def columns_to_rows(x, count):
    return jnp.concatenate(jnp.split(x, count, axis=1), axis=0)


def after(x, *others):
    return lax.optimization_barrier((x,) + others)[0]


def doubling_factors(rate, rows, here, backward):
    factors = []
    by = 1
    while by < lax.axis_size("ctx"):
        offset = here & (by - 1)
        if backward:
            offset = by - 1 - offset
        factors.append((jnp.exp(-rate * (rows * offset).astype(F32)), jnp.exp(-rate * float(rows * by))))
        by *= 2
    return factors


def entering_state(ends, factors, here, backward):
    size = lax.axis_size("ctx")
    total, entering = ends, jnp.zeros_like(ends)
    by = 1
    for to_here, across in factors:
        arrived = lax.ppermute(total, "ctx", [(i, i ^ by) for i in range(size)])
        later = ((here & by) != 0) != backward
        entering = entering + jnp.where(later, to_here * arrived, 0.0)
        total = jnp.where(later, across * arrived + total, across * total + arrived)
        by *= 2
    return entering


def direct_factors(rate, rows, chip, backward):
    factors = [jnp.exp(-rate * float(rows))]
    for s in range(1, lax.axis_size("ctx") // 2):
        gap = (chip ^ s) - chip - 1 if backward else chip - (chip ^ s) - 1
        weight = jnp.exp(-rate * (2 * rows * jnp.maximum(gap, 0)).astype(F32))
        factors.append(jnp.where(gap >= 0, weight, 0.0))
    return factors


def entering_direct(ends, factors, here, backward):
    block = factors[0]
    later_core = ((here & 1) != 0) != backward
    sibling = core_swap(ends)
    total = jnp.where(later_core, block * sibling + ends, block * ends + sibling)
    entering = jnp.zeros_like(ends)
    for s, weight in enumerate(factors[1:], 1):
        entering = entering + weight * chip_swap(total, s)
    return jnp.where(later_core, block * entering + sibling, entering)


def shards(
    query_mr,
    key_mr,
    value_mr,
    query_li,
    key_li,
    mr_taps,
    li_time,
    li_residue,
    li_skip,
    out_weight,
    cotangent,
):
    rows, columns = query_mr.shape
    ctx_count = lax.axis_size("ctx")
    line_count = lax.axis_size("fsdp")
    chips = ctx_count // 2
    here = lax.axis_index("ctx")
    core = here % 2
    line = lax.axis_index("fsdp")
    grad_scale = 1.0 / math.sqrt(rows * ctx_count)
    tables = {name: jnp.asarray(table) for name, table in dft_tables(rows).items()}
    width = out_weight.shape[0]
    pass_flops = 2 * (2 * rows) * (2 * rows) * columns

    def tile(x):
        return ("tile", x)

    def table(name):
        return ("whole", tables[name])

    mr_product = (key_mr.astype(F32) * value_mr.astype(F32)).astype(BF16)
    before = shifted(mr_product, 1)
    half = width // 2
    weight_halves = [
        lax.all_gather(out_weight[h * half : (h + 1) * half], "ctx", axis=0, tiled=True) for h in range(2)
    ]
    cot_line = [(line, cotangent)]
    for r in range(1, line_count):
        cot_line.append((line ^ r, line_swap(cotangent, r)))

    rate = 1.0 / li_time
    coef = li_residue * jnp.sqrt(-jnp.expm1(-2.0 * rate))
    ahead_factors, back_factors = lax.optimization_barrier(
        (doubling_factors(rate, rows, here, False), direct_factors(rate, rows, here // 2, True))
    )
    mr_spec, li_spec = run(
        spectra_body,
        columns,
        [tile(mr_taps), tile(rate), tile(coef), tile(li_skip[None, :]), table("ahead")],
        [(2 * rows, F32), (2 * rows, F32)],
        3 * pass_flops,
    )
    spec, mr_conv, mixed_mr, li_input, ends = run(
        short_body,
        columns,
        [
            tile(before),
            tile(mr_product),
            tile(query_mr),
            tile(key_li),
            tile(mr_spec),
            tile(rate),
            table("ahead"),
            table("back"),
        ],
        [(2 * rows, F32), (rows, F32), (rows, BF16), (rows, BF16), (rate.shape[0], F32)],
        4 * pass_flops,
    )
    entering = entering_state(ends, ahead_factors, here, False)
    (li_inner,) = run(
        inner_body,
        columns,
        [tile(li_input), tile(li_spec), table("ahead"), table("back")],
        [(rows, F32)],
        3 * pass_flops,
    )
    li_out, mixed_li = run(
        long_body,
        columns,
        [tile(li_inner), tile(query_li), tile(rate), tile(coef), tile(entering)],
        [(rows, F32), (rows, BF16)],
        pass_flops,
    )

    mixed_all = lax.all_gather(mixed_li, "ctx", axis=0, tiled=True)

    blocks = ctx_count // line_count
    first, second, stack = run_once(
        functools.partial(split_body, width),
        [jnp.stack([index * blocks for index, _ in cot_line])] + [piece for _, piece in cot_line],
        [((rows, ctx_count * half), BF16)] * 2 + [((ctx_count * rows, width), BF16)],
        [],
        0,
    )
    cot_rows = lax.all_to_all(stack, "ctx", 0, 0, tiled=True)

    share_flops = rows * columns * ctx_count * width
    part_width = blocks * half
    out_starts = jnp.stack([(line ^ r) * part_width for r in range(line_count)])

    (grad_early,) = run(
        grad_early_body,
        columns,
        [("whole", first), tile(weight_halves[0])],
        [(rows, F32)],
        share_flops,
    )
    out_early = run_once(
        out_body,
        [out_starts, mixed_li, weight_halves[0]],
        [((rows, part_width), BF16)] * line_count,
        [pltpu.VMEM((rows, ctx_count * half), BF16)],
        share_flops,
    )
    out_arrived = [out_early[0]] + [line_swap(out_early[r], r) for r in range(1, line_count)]
    grad_mixed, grad_li_out, back_ends = run(
        grad_gate_body,
        columns,
        [
            tile(after(grad_early, cot_rows, *out_arrived)),
            ("whole", second),
            tile(weight_halves[1]),
            tile(query_li),
            tile(rate),
        ],
        [(rows, F32), (rows, F32), (rate.shape[0], F32)],
        share_flops,
    )
    out_late = run_once(
        out_body,
        [out_starts, after(mixed_li, back_ends), weight_halves[1]],
        [((rows, part_width), BF16)] * line_count,
        [pltpu.VMEM((rows, ctx_count * half), BF16)],
        share_flops,
    )
    late_arrived = [out_late[0]] + [line_swap(out_late[r], r) for r in range(1, line_count)]
    (output,) = run_once(
        functools.partial(out_sum_body, width, line_count),
        [None] + out_arrived + late_arrived,
        [((rows, 2 * part_width), F32)],
        [],
        0,
    )
    back_entering = entering_direct(back_ends, back_factors, here, True)
    (grad_inner,) = run(
        grad_inner_body,
        columns,
        [tile(after(grad_li_out, out_late[0])), tile(li_spec), table("ahead"), table("back")],
        [(rows, F32)],
        3 * pass_flops,
    )
    grad_query_li = grad_mixed * li_out
    grad_key_li, grad_query_mr, grad_spec, tap_partial = run(
        grad_long_body,
        columns,
        [
            tile(grad_inner),
            tile(rate),
            tile(coef),
            tile(back_entering),
            tile(mixed_mr),
            tile(key_li),
            tile(query_mr),
            tile(mr_conv),
            tile(spec),
            table("ahead"),
            table("lags"),
        ],
        [(rows, F32), (rows, F32), (2 * rows, F32), (rows, F32)],
        4 * pass_flops,
    )
    own_product, prev_product = run(
        grad_taps_body,
        columns,
        [tile(grad_spec), tile(mr_spec), table("back")],
        [(rows, F32), (rows, BF16)],
        3 * pass_flops,
    )
    arrived = shifted(prev_product, -1)
    grad_key_mr, grad_value_mr = run(
        grad_product_body,
        columns,
        [tile(own_product), tile(arrived), tile(key_mr), tile(value_mr)],
        [(rows, F32), (rows, F32)],
        rows * columns,
    )

    tap_half = tap_partial.shape[0] // 2
    halves = tap_partial.reshape(2, tap_half, columns)
    own_half = lax.dynamic_index_in_dim(halves, core, 0, keepdims=False)
    far_half = lax.dynamic_index_in_dim(halves, 1 - core, 0, keepdims=False)
    plane_half = own_half + core_swap(far_half)
    by = 1
    while by < chips:
        sent = plane_half.astype(BF16)
        plane_half = sent.astype(F32) + chip_swap(sent, by).astype(F32)
        by *= 2
    plane_half = after(plane_half * grad_scale, *late_arrived)
    other_half = core_swap(plane_half)
    grad_taps = jnp.where(
        core == 0,
        jnp.concatenate([plane_half, other_half], axis=0),
        jnp.concatenate([other_half, plane_half], axis=0),
    )

    grad_weight = (
        lax.dot_general(cot_rows, mixed_all, (((0,), (0,)), ((), ())), preferred_element_type=F32) * grad_scale
    )
    return (
        output,
        grad_query_mr,
        grad_key_mr,
        grad_value_mr,
        grad_query_li,
        grad_key_li,
        grad_taps,
        grad_weight,
    )


def solution(mesh):
    rows = P("ctx", "fsdp")
    channels = P(None, "fsdp")
    return jax.shard_map(
        shards,
        mesh=mesh,
        in_specs=(rows,) * 5 + (channels,) * 3 + (P("fsdp"),) + (rows,) * 2,
        out_specs=(rows,) * 6 + (channels, rows),
        check_vma=False,
    )
```

```python
import functools
import math

import jax
import jax.numpy as jnp
import ml_dtypes
import numpy as np
from jax import lax
from jax.experimental import pallas as pl
from jax.experimental.pallas import tpu as pltpu
from jax.sharding import PartitionSpec as P

F32 = jnp.float32
BF16 = jnp.bfloat16
TILE = 256
GROUP = 8


def split_parts(matrix):
    high = matrix.astype(ml_dtypes.bfloat16)
    low = (matrix - high.astype(np.float64)).astype(ml_dtypes.bfloat16)
    return high, low


def two_fold(matrix):
    high, low = split_parts(matrix)
    return np.concatenate([high, low], axis=1)


def three_fold(matrix):
    high, low = split_parts(matrix)
    return np.concatenate([high, low, high], axis=1)


@functools.lru_cache(maxsize=None)
def dft_tables(rows):
    size = 2 * rows
    angle = 2.0 * np.pi * (np.arange(rows)[:, None] + 0.5) * np.arange(size)[None, :] / size
    ahead = np.concatenate([np.cos(angle), -np.sin(angle)], axis=0)
    back = ahead.T * (2.0 / size)
    signed = np.concatenate([back[:rows], -back[rows:]], axis=0)
    lags = back[rows - np.arange(rows)]
    return {"ahead": two_fold(ahead), "back": three_fold(signed), "lags": three_fold(lags)}


def half_table(ahead):
    rows = ahead.shape[0] // 2
    high, low = ahead[:, :rows], ahead[:, 2 * rows : 3 * rows]
    return high, low


def apply2(table, x):
    return jnp.dot(table, jnp.concatenate([x, x], axis=0), preferred_element_type=F32)


def apply3(table, x):
    high = x.astype(BF16)
    low = (x - high.astype(F32)).astype(BF16)
    return jnp.dot(table, jnp.concatenate([high, high, low], axis=0), preferred_element_type=F32)


def to_spectrum(ahead, x):
    high, low = half_table(ahead)
    return apply3(jnp.concatenate([high, low, high], axis=1), x)


def to_spectrum_exact(ahead, x):
    return apply2(jnp.concatenate(half_table(ahead), axis=1), x)


def times(x, y):
    half = x.shape[0] // 2
    xr, xi, yr, yi = x[:half], x[half:], y[:half], y[half:]
    return jnp.concatenate([xr * yr - xi * yi, xr * yi + xi * yr], axis=0)


def times_conj(x, y):
    half = x.shape[0] // 2
    xr, xi, yr, yi = x[:half], x[half:], y[:half], y[half:]
    return jnp.concatenate([xr * yr + xi * yi, xi * yr - xr * yi], axis=0)


def group_places(columns):
    return lax.broadcasted_iota(jnp.int32, (GROUP, columns), 0).astype(F32)


def spread_modes(rate, weight, rows, shift, backward):
    columns = rate.shape[1]
    places = group_places(columns)
    if backward:
        places = (GROUP - 1.0) - places
    count = rows // GROUP
    order = range(count - 1, -1, -1) if backward else range(count)
    sums = [None] * count
    for m in range(rate.shape[0]):
        rate_m = rate[m : m + 1]
        current = weight[m : m + 1] * jnp.exp(-rate_m * (places + shift))
        stride = jnp.broadcast_to(jnp.exp(-rate_m * GROUP), current.shape)
        for step, g in enumerate(order):
            sums[g] = current if sums[g] is None else sums[g] + current
            if step < count - 1:
                current = current * stride
    return jnp.concatenate(sums, axis=0)


def fold_modes(signal, rate, backward):
    columns = rate.shape[1]
    places = group_places(columns)
    if not backward:
        places = (GROUP - 1.0) - places
    count = signal.shape[0] // GROUP
    order = range(count - 1, -1, -1) if backward else range(count)
    found = []
    for m in range(rate.shape[0]):
        rate_m = rate[m : m + 1]
        stride = jnp.broadcast_to(jnp.exp(-rate_m * GROUP), (GROUP, columns))
        running = None
        for g in order:
            piece = signal[g * GROUP : (g + 1) * GROUP]
            running = piece if running is None else running * stride + piece
        found.append(jnp.sum(running * jnp.exp(-rate_m * places), axis=0, keepdims=True))
    return jnp.concatenate(found, axis=0)


def spectra_body(taps, rate, coef, skip, ahead, mr_spec, li_spec):
    rows = taps.shape[0]
    table = ahead[...]
    mr_spec[...] = to_spectrum(table, taps[...])
    kernel = spread_modes(rate[...], coef[...], rows, 0.0, False)
    first = lax.broadcasted_iota(jnp.int32, kernel.shape, 0) == 0
    kernel = kernel + jnp.where(first, skip[...], 0.0)
    li_spec[...] = to_spectrum(table, kernel)


def short_body(before, product, query, key, mr_spec, rate, ahead, back, spec, conv, mixed, signal, ends):
    rows = product.shape[0]
    x = jnp.concatenate([before[...], product[...]], axis=0)
    found = apply2(ahead[...], x)
    spec[...] = found
    filtered = -apply3(back[rows:], times(found, mr_spec[...]))
    conv[...] = filtered
    mixed_rows = (query[...].astype(F32) * filtered).astype(BF16)
    mixed[...] = mixed_rows
    rounded = (key[...].astype(F32) * mixed_rows.astype(F32)).astype(BF16)
    signal[...] = rounded
    ends[...] = fold_modes(rounded.astype(F32), rate[...], False)


def inner_body(signal, li_spec, ahead, back, inner):
    rows = signal.shape[0]
    inner[...] = apply3(back[:rows], times(to_spectrum_exact(ahead[...], signal[...]), li_spec[...]))


def gather_states(rate, gaps, states, rows):
    modes = rate.shape[0]
    total = jnp.zeros_like(rate)
    for k in range(states.shape[0] // modes):
        weight = jnp.exp(-rate * (jnp.maximum(gaps[k], 0.0) * float(rows)))
        total = total + jnp.where(gaps[k] >= 0.0, weight * states[k * modes : (k + 1) * modes], 0.0)
    return total


def long_body(gaps, inner, query, rate, coef, states, li_out, mixed):
    rows = inner.shape[0]
    entering = gather_states(rate[...], gaps, states, rows)
    total = inner[...] + spread_modes(rate[...], coef[...] * entering, rows, 1.0, False)
    li_out[...] = total
    mixed[...] = (query[...].astype(F32) * total).astype(BF16)


def split_body(width, starts, *rest):
    pieces, (whole, stack) = rest[:-2], rest[-2:]
    rows = whole.shape[0]
    for r, piece in enumerate(pieces):
        span = piece.shape[1]
        whole[:, pl.ds(pl.multiple_of(starts[r] * width, 128), span)] = piece[...]
        for k in range(span // width):
            stack[pl.ds(pl.multiple_of((starts[r] + k) * rows, 128), rows), :] = piece[:, k * width : (k + 1) * width]


def grad_gate_body(cotangent, weight, query, rate, grad_mixed, grad_out, ends):
    total = jnp.dot(cotangent[...], weight[...], preferred_element_type=F32)
    grad_mixed[...] = total
    gated = total * query[...].astype(F32)
    grad_out[...] = gated
    ends[...] = fold_modes(gated, rate[...], True)


def out_body(mixed, weight, stack):
    stack[...] = lax.dot_general(
        mixed[...], weight[...], (((1,), (1,)), ((), ())), preferred_element_type=F32
    ).astype(BF16)


def grad_inner_body(grad_out, li_spec, ahead, back, inner):
    rows = grad_out.shape[0]
    inner[...] = apply3(back[:rows], times_conj(to_spectrum(ahead[...], grad_out[...]), li_spec[...]))


def grad_long_body(
    inner, rate, coef, entering, mixed_mr, key_li, query_mr, conv, spec, ahead, lags,
    grad_key_li, grad_query_mr, grad_spec, taps,
):
    rows = inner.shape[0]
    grad_input = inner[...] + spread_modes(rate[...], coef[...] * entering[...], rows, 1.0, True)
    grad_key_li[...] = grad_input * mixed_mr[...].astype(F32)
    grad_mixed_mr = grad_input * key_li[...].astype(F32)
    grad_query_mr[...] = grad_mixed_mr * conv[...]
    grad_conv = grad_mixed_mr * query_mr[...].astype(F32)
    found = to_spectrum(ahead[...], grad_conv)
    grad_spec[...] = found
    taps[...] = apply3(lags[...], times_conj(spec[...], found))


def grad_taps_body(grad_spec, mr_spec, back, own_product, prev_product):
    rows = own_product.shape[0]
    products = apply3(back[...], times_conj(grad_spec[...], mr_spec[...]))
    own_product[...] = products[:rows]
    prev_product[...] = products[rows:].astype(BF16)


def grad_product_body(own, arrived, key, value, grad_key, grad_value):
    total = own[...] + arrived[...].astype(F32)
    grad_key[...] = total * value[...].astype(F32)
    grad_value[...] = total * key[...].astype(F32)


def run(body, columns, inputs, outputs, flops):
    tile = min(TILE, columns)
    in_specs = []
    moved = 0
    for kind, array in inputs:
        if kind == "tile":
            in_specs.append(pl.BlockSpec((array.shape[0], tile), lambda c: (0, c)))
        elif kind == "whole":
            in_specs.append(pl.BlockSpec(array.shape, lambda c: (0, 0)))
        else:
            in_specs.append(pl.BlockSpec(memory_space=pltpu.SMEM))
        moved += math.prod(array.shape) * array.dtype.itemsize
    for rows, dtype in outputs:
        moved += rows * columns * jnp.dtype(dtype).itemsize
    return pl.pallas_call(
        body,
        grid=(columns // tile,),
        in_specs=in_specs,
        out_specs=[pl.BlockSpec((rows, tile), lambda c: (0, c)) for rows, _ in outputs],
        out_shape=[jax.ShapeDtypeStruct((rows, columns), dtype) for rows, dtype in outputs],
        compiler_params=pltpu.CompilerParams(vmem_limit_bytes=12 * 1024 * 1024),
        cost_estimate=pl.CostEstimate(flops=flops, bytes_accessed=moved, transcendentals=0),
    )(*[array for _, array in inputs])


def run_lines(body, lines, x, weight, flops):
    rows, depth = x.shape
    span = weight.shape[0] // lines
    return pl.pallas_call(
        body,
        grid=(lines,),
        in_specs=[pl.BlockSpec((rows, depth), lambda k: (0, 0)), pl.BlockSpec((span, depth), lambda k: (k, 0))],
        out_specs=pl.BlockSpec((rows, span), lambda k: (k, 0)),
        out_shape=jax.ShapeDtypeStruct((lines * rows, span), BF16),
        compiler_params=pltpu.CompilerParams(vmem_limit_bytes=16 * 1024 * 1024),
        cost_estimate=pl.CostEstimate(flops=flops, bytes_accessed=2 * weight.size, transcendentals=0),
    )(x, weight)


def run_once(body, inputs, outputs, flops):
    in_specs = [pl.BlockSpec(memory_space=pltpu.VMEM)] * (len(inputs) - 1)
    if inputs[0] is None:
        inputs = inputs[1:]
    else:
        in_specs = [pl.BlockSpec(memory_space=pltpu.SMEM)] + in_specs
    moved = sum(math.prod(array.shape) * array.dtype.itemsize for array in inputs)
    return pl.pallas_call(
        body,
        in_specs=in_specs,
        out_specs=[pl.BlockSpec(memory_space=pltpu.VMEM)] * len(outputs),
        out_shape=[jax.ShapeDtypeStruct(shape, dtype) for shape, dtype in outputs],
        compiler_params=pltpu.CompilerParams(vmem_limit_bytes=24 * 1024 * 1024),
        cost_estimate=pl.CostEstimate(flops=flops, bytes_accessed=moved, transcendentals=0),
    )(*inputs)


def core_swap(x):
    size = lax.axis_size("ctx")
    return lax.ppermute(x, "ctx", [(i, i ^ 1) for i in range(size)])


def shifted(x, by):
    size = lax.axis_size("ctx")
    return lax.ppermute(x, "ctx", [(i, i + by) for i in range(size) if 0 <= i + by < size])


def chip_swap(x, by):
    size = lax.axis_size("ctx")
    return lax.ppermute(x, "ctx", [(i, i ^ (2 * by)) for i in range(size)])


def line_swap(x, by):
    size = lax.axis_size("fsdp")
    return lax.ppermute(x, "fsdp", [(i, i ^ by) for i in range(size)])


def columns_to_rows(x, count):
    return jnp.concatenate(jnp.split(x, count, axis=1), axis=0)


def after(x, *others):
    return lax.optimization_barrier((x,) + others)[0]


def direct_factors(rate, rows, chip, backward):
    factors = [jnp.exp(-rate * float(rows))]
    for s in range(1, lax.axis_size("ctx") // 2):
        gap = (chip ^ s) - chip - 1 if backward else chip - (chip ^ s) - 1
        weight = jnp.exp(-rate * (2 * rows * jnp.maximum(gap, 0)).astype(F32))
        factors.append(jnp.where(gap >= 0, weight, 0.0))
    return factors


def entering_direct(ends, factors, here, backward):
    block = factors[0]
    later_core = ((here & 1) != 0) != backward
    sibling = core_swap(ends)
    total = jnp.where(later_core, block * sibling + ends, block * ends + sibling)
    entering = jnp.zeros_like(ends)
    for s, weight in enumerate(factors[1:], 1):
        entering = entering + weight * chip_swap(total, s)
    return jnp.where(later_core, block * entering + sibling, entering)


def shards(
    query_mr,
    key_mr,
    value_mr,
    query_li,
    key_li,
    mr_taps,
    li_time,
    li_residue,
    li_skip,
    out_weight,
    cotangent,
):
    rows, columns = query_mr.shape
    ctx_count = lax.axis_size("ctx")
    line_count = lax.axis_size("fsdp")
    chips = ctx_count // 2
    here = lax.axis_index("ctx")
    core = here % 2
    line = lax.axis_index("fsdp")
    grad_scale = 1.0 / math.sqrt(rows * ctx_count)
    tables = {name: jnp.asarray(table) for name, table in dft_tables(rows).items()}
    width = out_weight.shape[0]
    pass_flops = 2 * (2 * rows) * (2 * rows) * columns

    def tile(x):
        return ("tile", x)

    def table(name):
        return ("whole", tables[name])

    mr_product = (key_mr.astype(F32) * value_mr.astype(F32)).astype(BF16)
    before = shifted(mr_product, 1)
    weight_rows = lax.all_gather(out_weight, "ctx", axis=0, tiled=True)
    cot_line = [(line, cotangent)]
    for r in range(1, line_count):
        cot_line.append((line ^ r, line_swap(cotangent, r)))

    rate = 1.0 / li_time
    coef = li_residue * jnp.sqrt(-jnp.expm1(-2.0 * rate))
    back_factors = lax.optimization_barrier(direct_factors(rate, rows, here // 2, True))
    mr_spec, li_spec = run(
        spectra_body,
        columns,
        [tile(mr_taps), tile(rate), tile(coef), tile(li_skip[None, :]), table("ahead")],
        [(2 * rows, F32), (2 * rows, F32)],
        3 * pass_flops,
    )
    spec, mr_conv, mixed_mr, li_input, ends = run(
        short_body,
        columns,
        [
            tile(before),
            tile(mr_product),
            tile(query_mr),
            tile(key_li),
            tile(mr_spec),
            tile(rate),
            table("ahead"),
            table("back"),
        ],
        [(2 * rows, F32), (rows, F32), (rows, BF16), (rows, BF16), (rate.shape[0], F32)],
        4 * pass_flops,
    )
    states = lax.all_gather(ends, "ctx").reshape(-1, columns)
    gaps = (here - 1 - jnp.arange(ctx_count, dtype=jnp.int32)).astype(F32)
    (li_inner,) = run(
        inner_body,
        columns,
        [tile(li_input), tile(li_spec), table("ahead"), table("back")],
        [(rows, F32)],
        3 * pass_flops,
    )
    li_out, mixed_li = run(
        long_body,
        columns,
        [("scalar", gaps), tile(li_inner), tile(query_li), tile(rate), tile(coef), tile(states)],
        [(rows, F32), (rows, BF16)],
        pass_flops,
    )

    mixed_all = lax.all_gather(mixed_li, "ctx", axis=0, tiled=True)

    blocks = ctx_count // line_count
    cot_full, stack = run_once(
        functools.partial(split_body, width),
        [jnp.stack([index * blocks for index, _ in cot_line])] + [piece for _, piece in cot_line],
        [((rows, ctx_count * width), BF16), ((ctx_count * rows, width), BF16)],
        0,
    )
    cot_rows = lax.all_to_all(stack, "ctx", 0, 0, tiled=True)

    share_flops = 2 * rows * columns * ctx_count * width
    grad_mixed, grad_li_out, back_ends = run(
        grad_gate_body,
        columns,
        [("whole", after(cot_full, mixed_li, cot_rows)), tile(weight_rows), tile(query_li), tile(rate)],
        [(rows, F32), (rows, F32), (rate.shape[0], F32)],
        share_flops,
    )
    out_stack = run_lines(out_body, line_count, after(mixed_li, back_ends), weight_rows, share_flops)
    out_parts = lax.all_to_all(out_stack, "fsdp", 0, 0, tiled=True).reshape(line_count, rows, -1)
    output = jnp.sum(out_parts.astype(F32), axis=0)
    back_entering = entering_direct(back_ends, back_factors, here, True)
    (grad_inner,) = run(
        grad_inner_body,
        columns,
        [tile(after(grad_li_out, out_stack)), tile(li_spec), table("ahead"), table("back")],
        [(rows, F32)],
        3 * pass_flops,
    )
    grad_query_li = grad_mixed * li_out
    grad_key_li, grad_query_mr, grad_spec, tap_partial = run(
        grad_long_body,
        columns,
        [
            tile(grad_inner),
            tile(rate),
            tile(coef),
            tile(back_entering),
            tile(mixed_mr),
            tile(key_li),
            tile(query_mr),
            tile(mr_conv),
            tile(spec),
            table("ahead"),
            table("lags"),
        ],
        [(rows, F32), (rows, F32), (2 * rows, F32), (rows, F32)],
        4 * pass_flops,
    )
    own_product, prev_product = run(
        grad_taps_body,
        columns,
        [tile(grad_spec), tile(mr_spec), table("back")],
        [(rows, F32), (rows, BF16)],
        3 * pass_flops,
    )
    arrived = shifted(prev_product, -1)
    grad_key_mr, grad_value_mr = run(
        grad_product_body,
        columns,
        [tile(own_product), tile(arrived), tile(key_mr), tile(value_mr)],
        [(rows, F32), (rows, F32)],
        rows * columns,
    )

    tap_half = tap_partial.shape[0] // 2
    halves = tap_partial.reshape(2, tap_half, columns)
    own_half = lax.dynamic_index_in_dim(halves, core, 0, keepdims=False)
    far_half = lax.dynamic_index_in_dim(halves, 1 - core, 0, keepdims=False)
    plane_half = own_half + core_swap(far_half)
    by = 1
    while by < chips:
        sent = plane_half.astype(BF16)
        plane_half = sent.astype(F32) + chip_swap(sent, by).astype(F32)
        by *= 2
    plane_half = plane_half * grad_scale
    other_half = core_swap(plane_half)
    grad_taps = jnp.where(
        core == 0,
        jnp.concatenate([plane_half, other_half], axis=0),
        jnp.concatenate([other_half, plane_half], axis=0),
    )

    grad_weight = (
        lax.dot_general(cot_rows, mixed_all, (((0,), (0,)), ((), ())), preferred_element_type=F32) * grad_scale
    )
    return (
        output,
        grad_query_mr,
        grad_key_mr,
        grad_value_mr,
        grad_query_li,
        grad_key_li,
        grad_taps,
        grad_weight,
    )


def solution(mesh):
    rows = P("ctx", "fsdp")
    channels = P(None, "fsdp")
    return jax.shard_map(
        shards,
        mesh=mesh,
        in_specs=(rows,) * 5 + (channels,) * 3 + (P("fsdp"),) + (rows,) * 2,
        out_specs=(rows,) * 6 + (channels, rows),
        check_vma=False,
    )
```

```python
import functools
import math

import jax
import jax.numpy as jnp
import ml_dtypes
import numpy as np
from jax import lax
from jax.experimental import pallas as pl
from jax.experimental.pallas import tpu as pltpu
from jax.sharding import PartitionSpec as P

F32 = jnp.float32
BF16 = jnp.bfloat16
TILE = 256
GROUP = 8


def split_parts(matrix):
    high = matrix.astype(ml_dtypes.bfloat16)
    low = (matrix - high.astype(np.float64)).astype(ml_dtypes.bfloat16)
    return high, low


def two_fold(matrix):
    high, low = split_parts(matrix)
    return np.concatenate([high, low], axis=1)


def three_fold(matrix):
    high, low = split_parts(matrix)
    return np.concatenate([high, low, high], axis=1)


@functools.lru_cache(maxsize=None)
def dft_tables(rows):
    size = 2 * rows
    angle = 2.0 * np.pi * (np.arange(rows)[:, None] + 0.5) * np.arange(size)[None, :] / size
    ahead = np.concatenate([np.cos(angle), -np.sin(angle)], axis=0)
    back = ahead.T * (2.0 / size)
    signed = np.concatenate([back[:rows], -back[rows:]], axis=0)
    lags = back[rows - np.arange(rows)]
    return {"ahead": two_fold(ahead), "back": three_fold(signed), "lags": three_fold(lags)}


def half_table(ahead):
    rows = ahead.shape[0] // 2
    high, low = ahead[:, :rows], ahead[:, 2 * rows : 3 * rows]
    return high, low


def apply2(table, x):
    return jnp.dot(table, jnp.concatenate([x, x], axis=0), preferred_element_type=F32)


def apply3(table, x):
    high = x.astype(BF16)
    low = (x - high.astype(F32)).astype(BF16)
    return jnp.dot(table, jnp.concatenate([high, high, low], axis=0), preferred_element_type=F32)


def to_spectrum(ahead, x):
    high, low = half_table(ahead)
    return apply3(jnp.concatenate([high, low, high], axis=1), x)


def to_spectrum_exact(ahead, x):
    return apply2(jnp.concatenate(half_table(ahead), axis=1), x)


def times(x, y):
    half = x.shape[0] // 2
    xr, xi, yr, yi = x[:half], x[half:], y[:half], y[half:]
    return jnp.concatenate([xr * yr - xi * yi, xr * yi + xi * yr], axis=0)


def times_conj(x, y):
    half = x.shape[0] // 2
    xr, xi, yr, yi = x[:half], x[half:], y[:half], y[half:]
    return jnp.concatenate([xr * yr + xi * yi, xi * yr - xr * yi], axis=0)


def group_places(columns):
    return lax.broadcasted_iota(jnp.int32, (GROUP, columns), 0).astype(F32)


def spread_modes(rate, weight, rows, shift, backward):
    columns = rate.shape[1]
    places = group_places(columns)
    if backward:
        places = (GROUP - 1.0) - places
    count = rows // GROUP
    order = range(count - 1, -1, -1) if backward else range(count)
    sums = [None] * count
    for m in range(rate.shape[0]):
        rate_m = rate[m : m + 1]
        current = weight[m : m + 1] * jnp.exp(-rate_m * (places + shift))
        stride = jnp.broadcast_to(jnp.exp(-rate_m * GROUP), current.shape)
        for step, g in enumerate(order):
            sums[g] = current if sums[g] is None else sums[g] + current
            if step < count - 1:
                current = current * stride
    return jnp.concatenate(sums, axis=0)


def fold_modes(signal, rate, backward):
    columns = rate.shape[1]
    places = group_places(columns)
    if not backward:
        places = (GROUP - 1.0) - places
    count = signal.shape[0] // GROUP
    order = range(count - 1, -1, -1) if backward else range(count)
    found = []
    for m in range(rate.shape[0]):
        rate_m = rate[m : m + 1]
        stride = jnp.broadcast_to(jnp.exp(-rate_m * GROUP), (GROUP, columns))
        running = None
        for g in order:
            piece = signal[g * GROUP : (g + 1) * GROUP]
            running = piece if running is None else running * stride + piece
        found.append(jnp.sum(running * jnp.exp(-rate_m * places), axis=0, keepdims=True))
    return jnp.concatenate(found, axis=0)


def spectra_body(taps, rate, coef, skip, ahead, mr_spec, li_spec):
    rows = taps.shape[0]
    table = ahead[...]
    mr_spec[...] = to_spectrum(table, taps[...])
    kernel = spread_modes(rate[...], coef[...], rows, 0.0, False)
    first = lax.broadcasted_iota(jnp.int32, kernel.shape, 0) == 0
    kernel = kernel + jnp.where(first, skip[...], 0.0)
    li_spec[...] = to_spectrum(table, kernel)


def short_body(before, product, query, key, mr_spec, rate, ahead, back, spec, conv, mixed, signal, ends):
    rows = product.shape[0]
    x = jnp.concatenate([before[...], product[...]], axis=0)
    found = apply2(ahead[...], x)
    spec[...] = found
    filtered = -apply3(back[rows:], times(found, mr_spec[...]))
    conv[...] = filtered
    mixed_rows = (query[...].astype(F32) * filtered).astype(BF16)
    mixed[...] = mixed_rows
    rounded = (key[...].astype(F32) * mixed_rows.astype(F32)).astype(BF16)
    signal[...] = rounded
    ends[...] = fold_modes(rounded.astype(F32), rate[...], False)


def inner_body(signal, li_spec, ahead, back, inner):
    rows = signal.shape[0]
    inner[...] = apply3(back[:rows], times(to_spectrum_exact(ahead[...], signal[...]), li_spec[...]))


def gather_states(rate, gaps, states, rows):
    modes = rate.shape[0]
    total = jnp.zeros_like(rate)
    for k in range(states.shape[0] // modes):
        weight = jnp.exp(-rate * (jnp.maximum(gaps[k], 0.0) * float(rows)))
        total = total + jnp.where(gaps[k] >= 0.0, weight * states[k * modes : (k + 1) * modes], 0.0)
    return total


def long_body(gaps, inner, query, rate, coef, states, li_out, mixed):
    rows = inner.shape[0]
    entering = gather_states(rate[...], gaps, states, rows)
    total = inner[...] + spread_modes(rate[...], coef[...] * entering, rows, 1.0, False)
    li_out[...] = total
    mixed[...] = (query[...].astype(F32) * total).astype(BF16)


def split_body(width, starts, *rest):
    pieces, whole = rest[:-1], rest[-1]
    for r, piece in enumerate(pieces):
        whole[:, pl.ds(pl.multiple_of(starts[r] * width, 128), piece.shape[1])] = piece[...]


def grad_gate_body(cotangent, weight, query, rate, grad_mixed, grad_out, ends):
    total = jnp.dot(cotangent[...], weight[...], preferred_element_type=F32)
    grad_mixed[...] = total
    gated = total * query[...].astype(F32)
    grad_out[...] = gated
    ends[...] = fold_modes(gated, rate[...], True)


def out_body(mixed, weight, stack):
    stack[...] = lax.dot_general(
        mixed[...], weight[...], (((1,), (1,)), ((), ())), preferred_element_type=F32
    ).astype(BF16)


def grad_inner_body(grad_out, li_spec, ahead, back, inner):
    rows = grad_out.shape[0]
    inner[...] = apply3(back[:rows], times_conj(to_spectrum(ahead[...], grad_out[...]), li_spec[...]))


def grad_long_body(
    inner, rate, coef, entering, mixed_mr, key_li, query_mr, conv, spec, ahead, lags,
    grad_key_li, grad_query_mr, grad_spec, taps,
):
    rows = inner.shape[0]
    grad_input = inner[...] + spread_modes(rate[...], coef[...] * entering[...], rows, 1.0, True)
    grad_key_li[...] = grad_input * mixed_mr[...].astype(F32)
    grad_mixed_mr = grad_input * key_li[...].astype(F32)
    grad_query_mr[...] = grad_mixed_mr * conv[...]
    grad_conv = grad_mixed_mr * query_mr[...].astype(F32)
    found = to_spectrum(ahead[...], grad_conv)
    grad_spec[...] = found
    taps[...] = apply3(lags[...], times_conj(spec[...], found))


def grad_taps_body(grad_spec, mr_spec, back, own_product, prev_product):
    rows = own_product.shape[0]
    products = apply3(back[...], times_conj(grad_spec[...], mr_spec[...]))
    own_product[...] = products[:rows]
    prev_product[...] = products[rows:].astype(BF16)


def grad_product_body(own, arrived, key, value, grad_key, grad_value):
    total = own[...] + arrived[...].astype(F32)
    grad_key[...] = total * value[...].astype(F32)
    grad_value[...] = total * key[...].astype(F32)


def run(body, columns, inputs, outputs, flops, limit=12):
    tile = min(TILE, columns)
    in_specs = []
    moved = 0
    for kind, array in inputs:
        if kind == "tile":
            in_specs.append(pl.BlockSpec((array.shape[0], tile), lambda c: (0, c)))
        elif kind == "whole":
            in_specs.append(pl.BlockSpec(array.shape, lambda c: (0, 0)))
        else:
            in_specs.append(pl.BlockSpec(memory_space=pltpu.SMEM))
        moved += math.prod(array.shape) * array.dtype.itemsize
    for rows, dtype in outputs:
        moved += rows * columns * jnp.dtype(dtype).itemsize
    return pl.pallas_call(
        body,
        grid=(columns // tile,),
        in_specs=in_specs,
        out_specs=[pl.BlockSpec((rows, tile), lambda c: (0, c)) for rows, _ in outputs],
        out_shape=[jax.ShapeDtypeStruct((rows, columns), dtype) for rows, dtype in outputs],
        compiler_params=pltpu.CompilerParams(vmem_limit_bytes=limit * 1024 * 1024),
        cost_estimate=pl.CostEstimate(flops=flops, bytes_accessed=moved, transcendentals=0),
    )(*[array for _, array in inputs])


def run_lines(body, lines, x, weight, flops):
    rows, depth = x.shape
    span = weight.shape[0] // lines
    return pl.pallas_call(
        body,
        grid=(lines,),
        in_specs=[pl.BlockSpec((rows, depth), lambda k: (0, 0)), pl.BlockSpec((span, depth), lambda k: (k, 0))],
        out_specs=pl.BlockSpec((rows, span), lambda k: (k, 0)),
        out_shape=jax.ShapeDtypeStruct((lines * rows, span), BF16),
        compiler_params=pltpu.CompilerParams(vmem_limit_bytes=48 * 1024 * 1024),
        cost_estimate=pl.CostEstimate(flops=flops, bytes_accessed=2 * weight.size, transcendentals=0),
    )(x, weight)


def run_once(body, inputs, outputs, flops):
    in_specs = [pl.BlockSpec(memory_space=pltpu.VMEM)] * (len(inputs) - 1)
    if inputs[0] is None:
        inputs = inputs[1:]
    else:
        in_specs = [pl.BlockSpec(memory_space=pltpu.SMEM)] + in_specs
    moved = sum(math.prod(array.shape) * array.dtype.itemsize for array in inputs)
    return pl.pallas_call(
        body,
        in_specs=in_specs,
        out_specs=[pl.BlockSpec(memory_space=pltpu.VMEM)] * len(outputs),
        out_shape=[jax.ShapeDtypeStruct(shape, dtype) for shape, dtype in outputs],
        compiler_params=pltpu.CompilerParams(vmem_limit_bytes=24 * 1024 * 1024),
        cost_estimate=pl.CostEstimate(flops=flops, bytes_accessed=moved, transcendentals=0),
    )(*inputs)


def core_swap(x):
    size = lax.axis_size("ctx")
    return lax.ppermute(x, "ctx", [(i, i ^ 1) for i in range(size)])


def shifted(x, by):
    size = lax.axis_size("ctx")
    return lax.ppermute(x, "ctx", [(i, i + by) for i in range(size) if 0 <= i + by < size])


def chip_swap(x, by):
    size = lax.axis_size("ctx")
    return lax.ppermute(x, "ctx", [(i, i ^ (2 * by)) for i in range(size)])


def line_swap(x, by):
    size = lax.axis_size("fsdp")
    return lax.ppermute(x, "fsdp", [(i, i ^ by) for i in range(size)])


def columns_to_rows(x, count):
    return jnp.concatenate(jnp.split(x, count, axis=1), axis=0)


def after(x, *others):
    return lax.optimization_barrier((x,) + others)[0]


def direct_factors(rate, rows, chip, backward):
    factors = [jnp.exp(-rate * float(rows))]
    for s in range(1, lax.axis_size("ctx") // 2):
        gap = (chip ^ s) - chip - 1 if backward else chip - (chip ^ s) - 1
        weight = jnp.exp(-rate * (2 * rows * jnp.maximum(gap, 0)).astype(F32))
        factors.append(jnp.where(gap >= 0, weight, 0.0))
    return factors


def entering_direct(ends, factors, here, backward):
    block = factors[0]
    later_core = ((here & 1) != 0) != backward
    sibling = core_swap(ends)
    total = jnp.where(later_core, block * sibling + ends, block * ends + sibling)
    entering = jnp.zeros_like(ends)
    for s, weight in enumerate(factors[1:], 1):
        entering = entering + weight * chip_swap(total, s)
    return jnp.where(later_core, block * entering + sibling, entering)


def shards(
    query_mr,
    key_mr,
    value_mr,
    query_li,
    key_li,
    mr_taps,
    li_time,
    li_residue,
    li_skip,
    out_weight,
    cotangent,
):
    rows, columns = query_mr.shape
    ctx_count = lax.axis_size("ctx")
    line_count = lax.axis_size("fsdp")
    chips = ctx_count // 2
    here = lax.axis_index("ctx")
    core = here % 2
    line = lax.axis_index("fsdp")
    grad_scale = 1.0 / math.sqrt(rows * ctx_count)
    tables = {name: jnp.asarray(table) for name, table in dft_tables(rows).items()}
    width = out_weight.shape[0]
    pass_flops = 2 * (2 * rows) * (2 * rows) * columns

    def tile(x):
        return ("tile", x)

    def table(name):
        return ("whole", tables[name])

    mr_product = (key_mr.astype(F32) * value_mr.astype(F32)).astype(BF16)
    before = shifted(mr_product, 1)
    weight_rows = lax.all_gather(out_weight, "ctx", axis=0, tiled=True)
    cot_line = [(line, cotangent)]
    for r in range(1, line_count):
        cot_line.append((line ^ r, line_swap(cotangent, r)))

    blocks = ctx_count // line_count
    (cot_full,) = run_once(
        functools.partial(split_body, width),
        [jnp.stack([index * blocks for index, _ in cot_line])] + [piece for _, piece in cot_line],
        [((rows, ctx_count * width), BF16)],
        0,
    )

    rate = 1.0 / li_time
    coef = li_residue * jnp.sqrt(-jnp.expm1(-2.0 * rate))
    back_factors = lax.optimization_barrier(direct_factors(rate, rows, here // 2, True))
    mr_spec, li_spec = run(
        spectra_body,
        columns,
        [tile(mr_taps), tile(rate), tile(coef), tile(li_skip[None, :]), table("ahead")],
        [(2 * rows, F32), (2 * rows, F32)],
        3 * pass_flops,
    )
    spec, mr_conv, mixed_mr, li_input, ends = run(
        short_body,
        columns,
        [
            tile(before),
            tile(mr_product),
            tile(query_mr),
            tile(key_li),
            tile(mr_spec),
            tile(rate),
            table("ahead"),
            table("back"),
        ],
        [(2 * rows, F32), (rows, F32), (rows, BF16), (rows, BF16), (rate.shape[0], F32)],
        4 * pass_flops,
    )
    states = lax.all_gather(after(ends, cot_full), "ctx").reshape(-1, columns)
    gaps = (here - 1 - jnp.arange(ctx_count, dtype=jnp.int32)).astype(F32)
    (li_inner,) = run(
        inner_body,
        columns,
        [tile(li_input), tile(li_spec), table("ahead"), table("back")],
        [(rows, F32)],
        3 * pass_flops,
    )
    li_out, mixed_li = run(
        long_body,
        columns,
        [("scalar", gaps), tile(li_inner), tile(query_li), tile(rate), tile(coef), tile(states)],
        [(rows, F32), (rows, BF16)],
        pass_flops,
    )

    mixed_all = lax.all_gather(mixed_li, "ctx", axis=0, tiled=True)

    def columns_at(x, index, count):
        return lax.dynamic_slice_in_dim(x, index * count, count, 1)

    chip = here // 2
    parts = [columns_at(cot_full, chip ^ s, 2 * width) for s in range(chips)]
    parts = [parts[0]] + [chip_swap(after(parts[s], ends), s) for s in range(1, chips)]
    near = [columns_at(part, core, width) for part in parts]
    far = core_swap(jnp.concatenate([columns_at(part, 1 - core, width) for part in parts], axis=0))
    cot_rows = jnp.zeros((rows * ctx_count, width), BF16)
    for s in range(chips):
        cot_rows = lax.dynamic_update_slice_in_dim(cot_rows, near[s], (here ^ (2 * s)) * rows, 0)
        cot_rows = lax.dynamic_update_slice_in_dim(
            cot_rows, far[s * rows : (s + 1) * rows], (here ^ (2 * s) ^ 1) * rows, 0
        )

    share_flops = 2 * rows * columns * ctx_count * width
    grad_mixed, grad_li_out, back_ends = run(
        grad_gate_body,
        columns,
        [("whole", after(cot_full, mixed_li, cot_rows)), tile(weight_rows), tile(query_li), tile(rate)],
        [(rows, F32), (rows, F32), (rate.shape[0], F32)],
        share_flops,
        48,
    )
    out_stack = run_lines(out_body, line_count, after(mixed_li, back_ends), weight_rows, share_flops)
    out_parts = lax.all_to_all(out_stack, "fsdp", 0, 0, tiled=True).reshape(line_count, rows, -1)
    output = jnp.sum(out_parts.astype(F32), axis=0)
    back_entering = entering_direct(back_ends, back_factors, here, True)
    (grad_inner,) = run(
        grad_inner_body,
        columns,
        [tile(after(grad_li_out, out_stack)), tile(li_spec), table("ahead"), table("back")],
        [(rows, F32)],
        3 * pass_flops,
    )
    grad_query_li = grad_mixed * li_out
    grad_key_li, grad_query_mr, grad_spec, tap_partial = run(
        grad_long_body,
        columns,
        [
            tile(grad_inner),
            tile(rate),
            tile(coef),
            tile(back_entering),
            tile(mixed_mr),
            tile(key_li),
            tile(query_mr),
            tile(mr_conv),
            tile(spec),
            table("ahead"),
            table("lags"),
        ],
        [(rows, F32), (rows, F32), (2 * rows, F32), (rows, F32)],
        4 * pass_flops,
    )
    own_product, prev_product = run(
        grad_taps_body,
        columns,
        [tile(grad_spec), tile(mr_spec), table("back")],
        [(rows, F32), (rows, BF16)],
        3 * pass_flops,
    )
    arrived = shifted(prev_product, -1)
    grad_key_mr, grad_value_mr = run(
        grad_product_body,
        columns,
        [tile(own_product), tile(arrived), tile(key_mr), tile(value_mr)],
        [(rows, F32), (rows, F32)],
        rows * columns,
    )

    tap_half = tap_partial.shape[0] // 2
    halves = tap_partial.reshape(2, tap_half, columns)
    own_half = lax.dynamic_index_in_dim(halves, core, 0, keepdims=False)
    far_half = lax.dynamic_index_in_dim(halves, 1 - core, 0, keepdims=False)
    plane_half = own_half + core_swap(far_half)
    by = 1
    while by < chips:
        sent = plane_half.astype(BF16)
        plane_half = sent.astype(F32) + chip_swap(sent, by).astype(F32)
        by *= 2
    plane_half = plane_half * grad_scale
    other_half = core_swap(plane_half)
    grad_taps = jnp.where(
        core == 0,
        jnp.concatenate([plane_half, other_half], axis=0),
        jnp.concatenate([other_half, plane_half], axis=0),
    )

    grad_weight = (
        lax.dot_general(cot_rows, mixed_all, (((0,), (0,)), ((), ())), preferred_element_type=F32) * grad_scale
    )
    return (
        output,
        grad_query_mr,
        grad_key_mr,
        grad_value_mr,
        grad_query_li,
        grad_key_li,
        grad_taps,
        grad_weight,
    )


def solution(mesh):
    rows = P("ctx", "fsdp")
    channels = P(None, "fsdp")
    return jax.shard_map(
        shards,
        mesh=mesh,
        in_specs=(rows,) * 5 + (channels,) * 3 + (P("fsdp"),) + (rows,) * 2,
        out_specs=(rows,) * 6 + (channels, rows),
        check_vma=False,
    )
```

```python
import functools
import math

import jax
import jax.numpy as jnp
import ml_dtypes
import numpy as np
from jax import lax
from jax.experimental import pallas as pl
from jax.experimental.pallas import tpu as pltpu
from jax.sharding import PartitionSpec as P

F32 = jnp.float32
BF16 = jnp.bfloat16
TILE = 256
GROUP = 8


def split_parts(matrix):
    high = matrix.astype(ml_dtypes.bfloat16)
    low = (matrix - high.astype(np.float64)).astype(ml_dtypes.bfloat16)
    return high, low


def two_fold(matrix):
    high, low = split_parts(matrix)
    return np.concatenate([high, low], axis=1)


def three_fold(matrix):
    high, low = split_parts(matrix)
    return np.concatenate([high, low, high], axis=1)


@functools.lru_cache(maxsize=None)
def dft_tables(rows):
    size = 2 * rows
    angle = 2.0 * np.pi * (np.arange(rows)[:, None] + 0.5) * np.arange(size)[None, :] / size
    ahead = np.concatenate([np.cos(angle), -np.sin(angle)], axis=0)
    back = ahead.T * (2.0 / size)
    signed = np.concatenate([back[:rows], -back[rows:]], axis=0)
    lags = back[rows - np.arange(rows)]
    return {"ahead": two_fold(ahead), "back": three_fold(signed), "lags": three_fold(lags)}


def half_table(ahead):
    rows = ahead.shape[0] // 2
    high, low = ahead[:, :rows], ahead[:, 2 * rows : 3 * rows]
    return high, low


def apply2(table, x):
    return jnp.dot(table, jnp.concatenate([x, x], axis=0), preferred_element_type=F32)


def apply3(table, x):
    high = x.astype(BF16)
    low = (x - high.astype(F32)).astype(BF16)
    return jnp.dot(table, jnp.concatenate([high, high, low], axis=0), preferred_element_type=F32)


def to_spectrum(ahead, x):
    high, low = half_table(ahead)
    return apply3(jnp.concatenate([high, low, high], axis=1), x)


def to_spectrum_exact(ahead, x):
    return apply2(jnp.concatenate(half_table(ahead), axis=1), x)


def times(x, y):
    half = x.shape[0] // 2
    xr, xi, yr, yi = x[:half], x[half:], y[:half], y[half:]
    return jnp.concatenate([xr * yr - xi * yi, xr * yi + xi * yr], axis=0)


def times_conj(x, y):
    half = x.shape[0] // 2
    xr, xi, yr, yi = x[:half], x[half:], y[:half], y[half:]
    return jnp.concatenate([xr * yr + xi * yi, xi * yr - xr * yi], axis=0)


def group_places(columns):
    return lax.broadcasted_iota(jnp.int32, (GROUP, columns), 0).astype(F32)


def spread_modes(rate, weight, rows, shift, backward):
    columns = rate.shape[1]
    places = group_places(columns)
    if backward:
        places = (GROUP - 1.0) - places
    count = rows // GROUP
    order = range(count - 1, -1, -1) if backward else range(count)
    sums = [None] * count
    for m in range(rate.shape[0]):
        rate_m = rate[m : m + 1]
        current = weight[m : m + 1] * jnp.exp(-rate_m * (places + shift))
        stride = jnp.broadcast_to(jnp.exp(-rate_m * GROUP), current.shape)
        for step, g in enumerate(order):
            sums[g] = current if sums[g] is None else sums[g] + current
            if step < count - 1:
                current = current * stride
    return jnp.concatenate(sums, axis=0)


def fold_modes(signal, rate, backward):
    columns = rate.shape[1]
    places = group_places(columns)
    if not backward:
        places = (GROUP - 1.0) - places
    count = signal.shape[0] // GROUP
    order = range(count - 1, -1, -1) if backward else range(count)
    found = []
    for m in range(rate.shape[0]):
        rate_m = rate[m : m + 1]
        stride = jnp.broadcast_to(jnp.exp(-rate_m * GROUP), (GROUP, columns))
        running = None
        for g in order:
            piece = signal[g * GROUP : (g + 1) * GROUP]
            running = piece if running is None else running * stride + piece
        found.append(jnp.sum(running * jnp.exp(-rate_m * places), axis=0, keepdims=True))
    return jnp.concatenate(found, axis=0)


def spectra_body(taps, rate, coef, skip, ahead, mr_spec, li_spec):
    rows = taps.shape[0]
    table = ahead[...]
    mr_spec[...] = to_spectrum(table, taps[...])
    kernel = spread_modes(rate[...], coef[...], rows, 0.0, False)
    first = lax.broadcasted_iota(jnp.int32, kernel.shape, 0) == 0
    kernel = kernel + jnp.where(first, skip[...], 0.0)
    li_spec[...] = to_spectrum(table, kernel)


def short_body(before, product, query, key, mr_spec, rate, ahead, back, spec, conv, mixed, signal, ends):
    rows = product.shape[0]
    x = jnp.concatenate([before[...], product[...]], axis=0)
    found = apply2(ahead[...], x)
    spec[...] = found
    filtered = -apply3(back[rows:], times(found, mr_spec[...]))
    conv[...] = filtered
    mixed_rows = (query[...].astype(F32) * filtered).astype(BF16)
    mixed[...] = mixed_rows
    rounded = (key[...].astype(F32) * mixed_rows.astype(F32)).astype(BF16)
    signal[...] = rounded
    ends[...] = fold_modes(rounded.astype(F32), rate[...], False)


def inner_body(signal, li_spec, ahead, back, inner):
    rows = signal.shape[0]
    inner[...] = apply3(back[:rows], times(to_spectrum_exact(ahead[...], signal[...]), li_spec[...]))


def gather_states(rate, gaps, states, rows):
    modes = rate.shape[0]
    total = jnp.zeros_like(rate)
    for k in range(states.shape[0] // modes):
        weight = jnp.exp(-rate * (jnp.maximum(gaps[k], 0.0) * float(rows)))
        total = total + jnp.where(gaps[k] >= 0.0, weight * states[k * modes : (k + 1) * modes], 0.0)
    return total


def long_body(gaps, inner, query, rate, coef, states, li_out, mixed):
    rows = inner.shape[0]
    entering = gather_states(rate[...], gaps, states, rows)
    total = inner[...] + spread_modes(rate[...], coef[...] * entering, rows, 1.0, False)
    li_out[...] = total
    mixed[...] = (query[...].astype(F32) * total).astype(BF16)


def grad_gate_body(count, own, query, rate, *rest):
    parts, (grad_mixed, grad_out, ends) = rest[:count], rest[count:]
    total = own[...]
    for part in parts:
        total = total + part[...].astype(F32)
    grad_mixed[...] = total
    gated = total * query[...].astype(F32)
    grad_out[...] = gated
    ends[...] = fold_modes(gated, rate[...], True)


def grad_inner_body(grad_out, li_spec, ahead, back, inner):
    rows = grad_out.shape[0]
    inner[...] = apply3(back[:rows], times_conj(to_spectrum(ahead[...], grad_out[...]), li_spec[...]))


def grad_long_body(
    inner, rate, coef, entering, mixed_mr, key_li, query_mr, conv, spec, ahead, lags,
    grad_key_li, grad_query_mr, grad_spec, taps,
):
    rows = inner.shape[0]
    grad_input = inner[...] + spread_modes(rate[...], coef[...] * entering[...], rows, 1.0, True)
    grad_key_li[...] = grad_input * mixed_mr[...].astype(F32)
    grad_mixed_mr = grad_input * key_li[...].astype(F32)
    grad_query_mr[...] = grad_mixed_mr * conv[...]
    grad_conv = grad_mixed_mr * query_mr[...].astype(F32)
    found = to_spectrum(ahead[...], grad_conv)
    grad_spec[...] = found
    taps[...] = apply3(lags[...], times_conj(spec[...], found))


def grad_taps_body(grad_spec, mr_spec, back, own_product, prev_product):
    rows = own_product.shape[0]
    products = apply3(back[...], times_conj(grad_spec[...], mr_spec[...]))
    own_product[...] = products[:rows]
    prev_product[...] = products[rows:].astype(BF16)


def grad_product_body(own, arrived, key, value, grad_key, grad_value):
    total = own[...] + arrived[...].astype(F32)
    grad_key[...] = total * value[...].astype(F32)
    grad_value[...] = total * key[...].astype(F32)


def run(body, columns, inputs, outputs, flops):
    tile = min(TILE, columns)
    in_specs = []
    moved = 0
    for kind, array in inputs:
        if kind == "tile":
            in_specs.append(pl.BlockSpec((array.shape[0], tile), lambda c: (0, c)))
        elif kind == "whole":
            in_specs.append(pl.BlockSpec(array.shape, lambda c: (0, 0)))
        else:
            in_specs.append(pl.BlockSpec(memory_space=pltpu.SMEM))
        moved += math.prod(array.shape) * array.dtype.itemsize
    for rows, dtype in outputs:
        moved += rows * columns * jnp.dtype(dtype).itemsize
    return pl.pallas_call(
        body,
        grid=(columns // tile,),
        in_specs=in_specs,
        out_specs=[pl.BlockSpec((rows, tile), lambda c: (0, c)) for rows, _ in outputs],
        out_shape=[jax.ShapeDtypeStruct((rows, columns), dtype) for rows, dtype in outputs],
        compiler_params=pltpu.CompilerParams(vmem_limit_bytes=12 * 1024 * 1024),
        cost_estimate=pl.CostEstimate(flops=flops, bytes_accessed=moved, transcendentals=0),
    )(*[array for _, array in inputs])


def chip_swap(x, by):
    size = lax.axis_size("ctx")
    return lax.ppermute(x, "ctx", [(i, i ^ (2 * by)) for i in range(size)])


def core_swap(x):
    size = lax.axis_size("ctx")
    return lax.ppermute(x, "ctx", [(i, i ^ 1) for i in range(size)])


def shifted(x, by):
    size = lax.axis_size("ctx")
    return lax.ppermute(x, "ctx", [(i, i + by) for i in range(size) if 0 <= i + by < size])


def columns_at(x, index, width):
    return lax.dynamic_slice_in_dim(x, index * width, width, 1)


def placed(pieces):
    width = pieces[0][1].shape[1]
    whole = jnp.zeros((pieces[0][1].shape[0], width * len(pieces)), pieces[0][1].dtype)
    for index, piece in pieces:
        whole = lax.dynamic_update_slice_in_dim(whole, piece, index * width, 1)
    return whole


def pair_sum(values):
    while len(values) > 1:
        values = [values[k] + values[k + 1] for k in range(0, len(values), 2)]
    return values[0]


def after(x, *others):
    return lax.optimization_barrier((x,) + others)[0]


def direct_factors(rate, rows, chip, backward):
    factors = [jnp.exp(-rate * float(rows))]
    for s in range(1, lax.axis_size("ctx") // 2):
        gap = (chip ^ s) - chip - 1 if backward else chip - (chip ^ s) - 1
        weight = jnp.exp(-rate * (2 * rows * jnp.maximum(gap, 0)).astype(F32))
        factors.append(jnp.where(gap >= 0, weight, 0.0))
    return factors


def entering_direct(ends, factors, here, backward):
    block = factors[0]
    later_core = ((here & 1) != 0) != backward
    sibling = core_swap(ends)
    total = jnp.where(later_core, block * sibling + ends, block * ends + sibling)
    entering = jnp.zeros_like(ends)
    for s, weight in enumerate(factors[1:], 1):
        entering = entering + weight * chip_swap(total, s)
    return jnp.where(later_core, block * entering + sibling, entering)


def shards(
    query_mr,
    key_mr,
    value_mr,
    query_li,
    key_li,
    mr_taps,
    li_time,
    li_residue,
    li_skip,
    out_weight,
    cotangent,
):
    rows, columns = query_mr.shape
    ctx_count = lax.axis_size("ctx")
    line_count = lax.axis_size("fsdp")
    chips = ctx_count // 2
    here = lax.axis_index("ctx")
    chip, core = here // 2, here % 2
    line = lax.axis_index("fsdp")
    grad_scale = 1.0 / math.sqrt(rows * ctx_count)
    tables = {name: jnp.asarray(table) for name, table in dft_tables(rows).items()}
    width = out_weight.shape[0]
    chip_width = 2 * width
    pass_flops = 2 * (2 * rows) * (2 * rows) * columns

    def tile(x):
        return ("tile", x)

    def table(name):
        return ("whole", tables[name])

    mr_product = (key_mr.astype(F32) * value_mr.astype(F32)).astype(BF16)
    before = shifted(mr_product, 1)
    cot_full = lax.all_gather(cotangent, "fsdp", axis=1, tiled=True)

    other_weight = core_swap(out_weight)
    weight_pair = jnp.where(
        core == 0,
        jnp.concatenate([out_weight, other_weight], axis=0),
        jnp.concatenate([other_weight, out_weight], axis=0),
    )
    rate = 1.0 / li_time
    coef = li_residue * jnp.sqrt(-jnp.expm1(-2.0 * rate))
    back_factors = lax.optimization_barrier(direct_factors(rate, rows, here // 2, True))
    mr_spec, li_spec = run(
        spectra_body,
        columns,
        [tile(mr_taps), tile(rate), tile(coef), tile(li_skip[None, :]), table("ahead")],
        [(2 * rows, F32), (2 * rows, F32)],
        3 * pass_flops,
    )
    spec, mr_conv, mixed_mr, li_input, ends = run(
        short_body,
        columns,
        [
            tile(before),
            tile(mr_product),
            tile(query_mr),
            tile(key_li),
            tile(mr_spec),
            tile(rate),
            table("ahead"),
            table("back"),
        ],
        [(2 * rows, F32), (rows, F32), (rows, BF16), (rows, BF16), (rate.shape[0], F32)],
        4 * pass_flops,
    )

    states = lax.all_gather(ends, "ctx").reshape(-1, columns)
    gaps = (here - 1 - jnp.arange(ctx_count, dtype=jnp.int32)).astype(F32)
    (li_inner,) = run(
        inner_body,
        columns,
        [tile(li_input), tile(li_spec), table("ahead"), table("back")],
        [(rows, F32)],
        3 * pass_flops,
    )
    li_out, mixed_li = run(
        long_body,
        columns,
        [("scalar", gaps), tile(li_inner), tile(query_li), tile(rate), tile(coef), tile(states)],
        [(rows, F32), (rows, BF16)],
        pass_flops,
    )

    cot_full = after(cot_full, mixed_li)
    cot_parts = [columns_at(cot_full, chip, chip_width)]
    for s in range(1, chips):
        cot_parts.append(chip_swap(columns_at(cot_full, chip ^ s, chip_width), s))

    mixed_parts = [mixed_li] + [chip_swap(mixed_li, s) for s in range(1, chips)]
    out_parts = []
    for s, part in enumerate(mixed_parts):
        found = lax.dot_general(
            part, weight_pair, (((1,), (1,)), ((), ())), preferred_element_type=F32
        ).astype(BF16)
        out_parts.append((chip ^ s, found if s == 0 else chip_swap(found, s)))
    out_full = placed(out_parts)
    output = lax.psum_scatter(out_full, "fsdp", scatter_dimension=1, tiled=True).astype(F32)

    grad_parts = []
    for s, part in enumerate(cot_parts):
        found = jnp.dot(part, weight_pair, preferred_element_type=F32)
        grad_parts.append(found if s == 0 else chip_swap(found.astype(BF16), s))
    grad_mixed, grad_li_out, back_ends = run(
        functools.partial(grad_gate_body, chips - 1),
        columns,
        [tile(grad_parts[0]), tile(query_li), tile(rate)] + [tile(part) for part in grad_parts[1:]],
        [(rows, F32), (rows, F32), (rate.shape[0], F32)],
        pass_flops,
    )
    back_entering = entering_direct(back_ends, back_factors, here, True)
    (grad_inner,) = run(
        grad_inner_body,
        columns,
        [tile(grad_li_out), tile(li_spec), table("ahead"), table("back")],
        [(rows, F32)],
        3 * pass_flops,
    )
    grad_query_li = grad_mixed * li_out
    grad_key_li, grad_query_mr, grad_spec, tap_partial = run(
        grad_long_body,
        columns,
        [
            tile(grad_inner),
            tile(rate),
            tile(coef),
            tile(back_entering),
            tile(mixed_mr),
            tile(key_li),
            tile(query_mr),
            tile(mr_conv),
            tile(spec),
            table("ahead"),
            table("lags"),
        ],
        [(rows, F32), (rows, F32), (2 * rows, F32), (rows, F32)],
        4 * pass_flops,
    )
    own_product, prev_product = run(
        grad_taps_body,
        columns,
        [tile(grad_spec), tile(mr_spec), table("back")],
        [(rows, F32), (rows, BF16)],
        3 * pass_flops,
    )
    arrived = shifted(prev_product, -1)
    grad_key_mr, grad_value_mr = run(
        grad_product_body,
        columns,
        [tile(own_product), tile(arrived), tile(key_mr), tile(value_mr)],
        [(rows, F32), (rows, F32)],
        rows * columns,
    )

    tap_half = tap_partial.shape[0] // 2
    halves = tap_partial.reshape(2, tap_half, columns)
    own_half = lax.dynamic_index_in_dim(halves, core, 0, keepdims=False)
    far_half = lax.dynamic_index_in_dim(halves, 1 - core, 0, keepdims=False)
    chip_half = (own_half + core_swap(far_half)).astype(BF16)
    everywhere = [chip_half] + [chip_swap(chip_half, s) for s in range(1, chips)]
    plane_half = pair_sum([part.astype(F32) for part in everywhere]) * grad_scale
    other_half = core_swap(plane_half)
    grad_taps = jnp.where(
        core == 0,
        jnp.concatenate([plane_half, other_half], axis=0),
        jnp.concatenate([other_half, plane_half], axis=0),
    )

    cot_rows = jnp.concatenate(cot_parts, axis=0)
    mixed_rows = jnp.concatenate(mixed_parts, axis=0)

    def weight_share(which):
        return lax.dot_general(
            columns_at(cot_rows, which, width),
            mixed_rows,
            (((0,), (0,)), ((), ())),
            preferred_element_type=F32,
        )

    far_share = core_swap(weight_share(1 - core).astype(BF16))
    grad_weight = (weight_share(core) + far_share.astype(F32)) * grad_scale
    return (
        output,
        grad_query_mr,
        grad_key_mr,
        grad_value_mr,
        grad_query_li,
        grad_key_li,
        grad_taps,
        grad_weight,
    )


def solution(mesh):
    rows = P("ctx", "fsdp")
    channels = P(None, "fsdp")
    return jax.shard_map(
        shards,
        mesh=mesh,
        in_specs=(rows,) * 5 + (channels,) * 3 + (P("fsdp"),) + (rows,) * 2,
        out_specs=(rows,) * 6 + (channels, rows),
        check_vma=False,
    )
```

```python
import functools
import math

import jax
import jax.numpy as jnp
import ml_dtypes
import numpy as np
from jax import lax
from jax.experimental import pallas as pl
from jax.experimental.pallas import tpu as pltpu
from jax.sharding import PartitionSpec as P

F32 = jnp.float32
BF16 = jnp.bfloat16
TILE = 256
GROUP = 8


def split_parts(matrix):
    high = matrix.astype(ml_dtypes.bfloat16)
    low = (matrix - high.astype(np.float64)).astype(ml_dtypes.bfloat16)
    return high, low


def two_fold(matrix):
    high, low = split_parts(matrix)
    return np.concatenate([high, low], axis=1)


def three_fold(matrix):
    high, low = split_parts(matrix)
    return np.concatenate([high, low, high], axis=1)


@functools.lru_cache(maxsize=None)
def dft_tables(rows):
    size = 2 * rows
    angle = 2.0 * np.pi * (np.arange(rows)[:, None] + 0.5) * np.arange(size)[None, :] / size
    ahead = np.concatenate([np.cos(angle), -np.sin(angle)], axis=0)
    back = ahead.T * (2.0 / size)
    signed = np.concatenate([back[:rows], -back[rows:]], axis=0)
    lags = back[rows - np.arange(rows)]
    return {"ahead": two_fold(ahead), "back": three_fold(signed), "lags": three_fold(lags)}


def half_table(ahead):
    rows = ahead.shape[0] // 2
    high, low = ahead[:, :rows], ahead[:, 2 * rows : 3 * rows]
    return high, low


def apply2(table, x):
    return jnp.dot(table, jnp.concatenate([x, x], axis=0), preferred_element_type=F32)


def apply3(table, x):
    high = x.astype(BF16)
    low = (x - high.astype(F32)).astype(BF16)
    return jnp.dot(table, jnp.concatenate([high, high, low], axis=0), preferred_element_type=F32)


def to_spectrum(ahead, x):
    high, low = half_table(ahead)
    return apply3(jnp.concatenate([high, low, high], axis=1), x)


def to_spectrum_exact(ahead, x):
    return apply2(jnp.concatenate(half_table(ahead), axis=1), x)


def times(x, y):
    half = x.shape[0] // 2
    xr, xi, yr, yi = x[:half], x[half:], y[:half], y[half:]
    return jnp.concatenate([xr * yr - xi * yi, xr * yi + xi * yr], axis=0)


def times_conj(x, y):
    half = x.shape[0] // 2
    xr, xi, yr, yi = x[:half], x[half:], y[:half], y[half:]
    return jnp.concatenate([xr * yr + xi * yi, xi * yr - xr * yi], axis=0)


def group_places(columns):
    return lax.broadcasted_iota(jnp.int32, (GROUP, columns), 0).astype(F32)


def spread_modes(rate, weight, rows, shift, backward):
    columns = rate.shape[1]
    places = group_places(columns)
    if backward:
        places = (GROUP - 1.0) - places
    count = rows // GROUP
    order = range(count - 1, -1, -1) if backward else range(count)
    sums = [None] * count
    for m in range(rate.shape[0]):
        rate_m = rate[m : m + 1]
        current = weight[m : m + 1] * jnp.exp(-rate_m * (places + shift))
        stride = jnp.broadcast_to(jnp.exp(-rate_m * GROUP), current.shape)
        for step, g in enumerate(order):
            sums[g] = current if sums[g] is None else sums[g] + current
            if step < count - 1:
                current = current * stride
    return jnp.concatenate(sums, axis=0)


def fold_modes(signal, rate, backward):
    columns = rate.shape[1]
    places = group_places(columns)
    if not backward:
        places = (GROUP - 1.0) - places
    count = signal.shape[0] // GROUP
    order = range(count - 1, -1, -1) if backward else range(count)
    found = []
    for m in range(rate.shape[0]):
        rate_m = rate[m : m + 1]
        stride = jnp.broadcast_to(jnp.exp(-rate_m * GROUP), (GROUP, columns))
        running = None
        for g in order:
            piece = signal[g * GROUP : (g + 1) * GROUP]
            running = piece if running is None else running * stride + piece
        found.append(jnp.sum(running * jnp.exp(-rate_m * places), axis=0, keepdims=True))
    return jnp.concatenate(found, axis=0)


def spectra_body(taps, rate, coef, skip, ahead, mr_spec, li_spec):
    rows = taps.shape[0]
    table = ahead[...]
    mr_spec[...] = to_spectrum(table, taps[...])
    kernel = spread_modes(rate[...], coef[...], rows, 0.0, False)
    first = lax.broadcasted_iota(jnp.int32, kernel.shape, 0) == 0
    kernel = kernel + jnp.where(first, skip[...], 0.0)
    li_spec[...] = to_spectrum(table, kernel)


def short_body(before, product, query, key, mr_spec, rate, ahead, back, spec, conv, mixed, signal, ends):
    rows = product.shape[0]
    x = jnp.concatenate([before[...], product[...]], axis=0)
    found = apply2(ahead[...], x)
    spec[...] = found
    filtered = -apply3(back[rows:], times(found, mr_spec[...]))
    conv[...] = filtered
    mixed_rows = (query[...].astype(F32) * filtered).astype(BF16)
    mixed[...] = mixed_rows
    rounded = (key[...].astype(F32) * mixed_rows.astype(F32)).astype(BF16)
    signal[...] = rounded
    ends[...] = fold_modes(rounded.astype(F32), rate[...], False)


def inner_body(signal, li_spec, ahead, back, inner):
    rows = signal.shape[0]
    inner[...] = apply3(back[:rows], times(to_spectrum_exact(ahead[...], signal[...]), li_spec[...]))


def gather_states(rate, gaps, states, rows):
    modes = rate.shape[0]
    total = jnp.zeros_like(rate)
    for k in range(states.shape[0] // modes):
        weight = jnp.exp(-rate * (jnp.maximum(gaps[k], 0.0) * float(rows)))
        total = total + jnp.where(gaps[k] >= 0.0, weight * states[k * modes : (k + 1) * modes], 0.0)
    return total


def long_body(gaps, inner, query, rate, coef, states, li_out, mixed):
    rows = inner.shape[0]
    entering = gather_states(rate[...], gaps, states, rows)
    total = inner[...] + spread_modes(rate[...], coef[...] * entering, rows, 1.0, False)
    li_out[...] = total
    mixed[...] = (query[...].astype(F32) * total).astype(BF16)


def grad_gate_body(count, own, query, rate, *rest):
    parts, (grad_mixed, grad_out, ends) = rest[:count], rest[count:]
    total = own[...]
    for part in parts:
        total = total + part[...].astype(F32)
    grad_mixed[...] = total
    gated = total * query[...].astype(F32)
    grad_out[...] = gated
    ends[...] = fold_modes(gated, rate[...], True)


def grad_inner_body(grad_out, li_spec, ahead, back, inner):
    rows = grad_out.shape[0]
    inner[...] = apply3(back[:rows], times_conj(to_spectrum(ahead[...], grad_out[...]), li_spec[...]))


def grad_long_body(
    inner, rate, coef, entering, mixed_mr, key_li, query_mr, conv, spec, ahead, lags,
    grad_key_li, grad_query_mr, grad_spec, taps,
):
    rows = inner.shape[0]
    grad_input = inner[...] + spread_modes(rate[...], coef[...] * entering[...], rows, 1.0, True)
    grad_key_li[...] = grad_input * mixed_mr[...].astype(F32)
    grad_mixed_mr = grad_input * key_li[...].astype(F32)
    grad_query_mr[...] = grad_mixed_mr * conv[...]
    grad_conv = grad_mixed_mr * query_mr[...].astype(F32)
    found = to_spectrum(ahead[...], grad_conv)
    grad_spec[...] = found
    taps[...] = apply3(lags[...], times_conj(spec[...], found))


def grad_taps_body(grad_spec, mr_spec, back, own_product, prev_product):
    rows = own_product.shape[0]
    products = apply3(back[...], times_conj(grad_spec[...], mr_spec[...]))
    own_product[...] = products[:rows]
    prev_product[...] = products[rows:].astype(BF16)


def grad_product_body(own, arrived, key, value, grad_key, grad_value):
    total = own[...] + arrived[...].astype(F32)
    grad_key[...] = total * value[...].astype(F32)
    grad_value[...] = total * key[...].astype(F32)


def run(body, columns, inputs, outputs, flops):
    tile = min(TILE, columns)
    in_specs = []
    moved = 0
    for kind, array in inputs:
        if kind == "tile":
            in_specs.append(pl.BlockSpec((array.shape[0], tile), lambda c: (0, c)))
        elif kind == "whole":
            in_specs.append(pl.BlockSpec(array.shape, lambda c: (0, 0)))
        else:
            in_specs.append(pl.BlockSpec(memory_space=pltpu.SMEM))
        moved += math.prod(array.shape) * array.dtype.itemsize
    for rows, dtype in outputs:
        moved += rows * columns * jnp.dtype(dtype).itemsize
    return pl.pallas_call(
        body,
        grid=(columns // tile,),
        in_specs=in_specs,
        out_specs=[pl.BlockSpec((rows, tile), lambda c: (0, c)) for rows, _ in outputs],
        out_shape=[jax.ShapeDtypeStruct((rows, columns), dtype) for rows, dtype in outputs],
        compiler_params=pltpu.CompilerParams(vmem_limit_bytes=12 * 1024 * 1024),
        cost_estimate=pl.CostEstimate(flops=flops, bytes_accessed=moved if flops else 0, transcendentals=0),
    )(*[array for _, array in inputs])


def chip_swap(x, by):
    size = lax.axis_size("ctx")
    return lax.ppermute(x, "ctx", [(i, i ^ (2 * by)) for i in range(size)])


def core_swap(x):
    size = lax.axis_size("ctx")
    return lax.ppermute(x, "ctx", [(i, i ^ 1) for i in range(size)])


def shifted(x, by):
    size = lax.axis_size("ctx")
    return lax.ppermute(x, "ctx", [(i, i + by) for i in range(size) if 0 <= i + by < size])


def columns_at(x, index, width):
    return lax.dynamic_slice_in_dim(x, index * width, width, 1)


def placed(pieces):
    width = pieces[0][1].shape[1]
    whole = jnp.zeros((pieces[0][1].shape[0], width * len(pieces)), pieces[0][1].dtype)
    for index, piece in pieces:
        whole = lax.dynamic_update_slice_in_dim(whole, piece, index * width, 1)
    return whole


def pair_sum(values):
    while len(values) > 1:
        values = [values[k] + values[k + 1] for k in range(0, len(values), 2)]
    return values[0]


def after(x, *others):
    return lax.optimization_barrier((x,) + others)[0]


def direct_factors(rate, rows, chip, backward):
    factors = [jnp.exp(-rate * float(rows))]
    for s in range(1, lax.axis_size("ctx") // 2):
        gap = (chip ^ s) - chip - 1 if backward else chip - (chip ^ s) - 1
        weight = jnp.exp(-rate * (2 * rows * jnp.maximum(gap, 0)).astype(F32))
        factors.append(jnp.where(gap >= 0, weight, 0.0))
    return factors


def entering_direct(ends, factors, here, backward):
    block = factors[0]
    later_core = ((here & 1) != 0) != backward
    sibling = core_swap(ends)
    total = jnp.where(later_core, block * sibling + ends, block * ends + sibling)
    entering = jnp.zeros_like(ends)
    for s, weight in enumerate(factors[1:], 1):
        entering = entering + weight * chip_swap(total, s)
    return jnp.where(later_core, block * entering + sibling, entering)


def shards(
    query_mr,
    key_mr,
    value_mr,
    query_li,
    key_li,
    mr_taps,
    li_time,
    li_residue,
    li_skip,
    out_weight,
    cotangent,
):
    rows, columns = query_mr.shape
    ctx_count = lax.axis_size("ctx")
    line_count = lax.axis_size("fsdp")
    chips = ctx_count // 2
    here = lax.axis_index("ctx")
    chip, core = here // 2, here % 2
    line = lax.axis_index("fsdp")
    grad_scale = 1.0 / math.sqrt(rows * ctx_count)
    tables = {name: jnp.asarray(table) for name, table in dft_tables(rows).items()}
    width = out_weight.shape[0]
    chip_width = 2 * width
    pass_flops = 2 * (2 * rows) * (2 * rows) * columns

    def tile(x):
        return ("tile", x)

    def table(name):
        return ("whole", tables[name])

    mr_product = (key_mr.astype(F32) * value_mr.astype(F32)).astype(BF16)
    before = shifted(mr_product, 1)
    cot_full = lax.all_gather(cotangent, "fsdp", axis=1, tiled=True)

    other_weight = core_swap(out_weight)
    weight_pair = jnp.where(
        core == 0,
        jnp.concatenate([out_weight, other_weight], axis=0),
        jnp.concatenate([other_weight, out_weight], axis=0),
    )
    rate = 1.0 / li_time
    coef = li_residue * jnp.sqrt(-jnp.expm1(-2.0 * rate))
    back_factors = lax.optimization_barrier(direct_factors(rate, rows, here // 2, True))
    mr_spec, li_spec = run(
        spectra_body,
        columns,
        [tile(mr_taps), tile(rate), tile(coef), tile(li_skip[None, :]), table("ahead")],
        [(2 * rows, F32), (2 * rows, F32)],
        0,
    )
    spec, mr_conv, mixed_mr, li_input, ends = run(
        short_body,
        columns,
        [
            tile(before),
            tile(mr_product),
            tile(query_mr),
            tile(key_li),
            tile(mr_spec),
            tile(rate),
            table("ahead"),
            table("back"),
        ],
        [(2 * rows, F32), (rows, F32), (rows, BF16), (rows, BF16), (rate.shape[0], F32)],
        0,
    )

    states = lax.all_gather(ends, "ctx").reshape(-1, columns)
    gaps = (here - 1 - jnp.arange(ctx_count, dtype=jnp.int32)).astype(F32)
    (li_inner,) = run(
        inner_body,
        columns,
        [tile(li_input), tile(li_spec), table("ahead"), table("back")],
        [(rows, F32)],
        0,
    )
    li_out, mixed_li = run(
        long_body,
        columns,
        [("scalar", gaps), tile(li_inner), tile(query_li), tile(rate), tile(coef), tile(states)],
        [(rows, F32), (rows, BF16)],
        0,
    )

    cot_full, mixed_li = lax.optimization_barrier((cot_full, mixed_li))
    cot_parts = [columns_at(cot_full, chip, chip_width)]
    for s in range(1, chips):
        cot_parts.append(chip_swap(columns_at(cot_full, chip ^ s, chip_width), s))

    mixed_parts = [mixed_li] + [chip_swap(mixed_li, s) for s in range(1, chips)]
    out_parts = []
    for s, part in enumerate(mixed_parts):
        found = lax.dot_general(
            part, weight_pair, (((1,), (1,)), ((), ())), preferred_element_type=F32
        ).astype(BF16)
        out_parts.append((chip ^ s, found if s == 0 else chip_swap(found, s)))
    out_full = placed(out_parts)
    output = lax.psum_scatter(out_full, "fsdp", scatter_dimension=1, tiled=True).astype(F32)

    grad_parts = []
    for s, part in enumerate(cot_parts):
        found = jnp.dot(part, weight_pair, preferred_element_type=F32)
        grad_parts.append(found if s == 0 else chip_swap(found.astype(BF16), s))
    grad_mixed, grad_li_out, back_ends = run(
        functools.partial(grad_gate_body, chips - 1),
        columns,
        [tile(grad_parts[0]), tile(query_li), tile(rate)] + [tile(part) for part in grad_parts[1:]],
        [(rows, F32), (rows, F32), (rate.shape[0], F32)],
        pass_flops,
    )
    back_entering = entering_direct(back_ends, back_factors, here, True)
    (grad_inner,) = run(
        grad_inner_body,
        columns,
        [tile(grad_li_out), tile(li_spec), table("ahead"), table("back")],
        [(rows, F32)],
        3 * pass_flops,
    )
    grad_query_li = grad_mixed * li_out
    grad_key_li, grad_query_mr, grad_spec, tap_partial = run(
        grad_long_body,
        columns,
        [
            tile(grad_inner),
            tile(rate),
            tile(coef),
            tile(back_entering),
            tile(mixed_mr),
            tile(key_li),
            tile(query_mr),
            tile(mr_conv),
            tile(spec),
            table("ahead"),
            table("lags"),
        ],
        [(rows, F32), (rows, F32), (2 * rows, F32), (rows, F32)],
        4 * pass_flops,
    )
    own_product, prev_product = run(
        grad_taps_body,
        columns,
        [tile(grad_spec), tile(mr_spec), table("back")],
        [(rows, F32), (rows, BF16)],
        3 * pass_flops,
    )
    arrived = shifted(prev_product, -1)
    grad_key_mr, grad_value_mr = run(
        grad_product_body,
        columns,
        [tile(own_product), tile(arrived), tile(key_mr), tile(value_mr)],
        [(rows, F32), (rows, F32)],
        rows * columns,
    )

    tap_half = tap_partial.shape[0] // 2
    halves = tap_partial.reshape(2, tap_half, columns)
    own_half = lax.dynamic_index_in_dim(halves, core, 0, keepdims=False)
    far_half = lax.dynamic_index_in_dim(halves, 1 - core, 0, keepdims=False)
    chip_half = (own_half + core_swap(far_half)).astype(BF16)
    everywhere = [chip_half] + [chip_swap(chip_half, s) for s in range(1, chips)]
    plane_half = pair_sum([part.astype(F32) for part in everywhere]) * grad_scale
    other_half = core_swap(plane_half)
    grad_taps = jnp.where(
        core == 0,
        jnp.concatenate([plane_half, other_half], axis=0),
        jnp.concatenate([other_half, plane_half], axis=0),
    )

    cot_rows = jnp.concatenate(cot_parts, axis=0)
    mixed_rows = jnp.concatenate(mixed_parts, axis=0)

    def weight_share(which):
        return lax.dot_general(
            columns_at(cot_rows, which, width),
            mixed_rows,
            (((0,), (0,)), ((), ())),
            preferred_element_type=F32,
        )

    far_share = core_swap(weight_share(1 - core).astype(BF16))
    grad_weight = (weight_share(core) + far_share.astype(F32)) * grad_scale
    return (
        output,
        grad_query_mr,
        grad_key_mr,
        grad_value_mr,
        grad_query_li,
        grad_key_li,
        grad_taps,
        grad_weight,
    )


def solution(mesh):
    rows = P("ctx", "fsdp")
    channels = P(None, "fsdp")
    return jax.shard_map(
        shards,
        mesh=mesh,
        in_specs=(rows,) * 5 + (channels,) * 3 + (P("fsdp"),) + (rows,) * 2,
        out_specs=(rows,) * 6 + (channels, rows),
        check_vma=False,
    )
```

```python
import functools
import math

import jax
import jax.numpy as jnp
import ml_dtypes
import numpy as np
from jax import lax
from jax.experimental import pallas as pl
from jax.experimental.pallas import tpu as pltpu
from jax.sharding import PartitionSpec as P

F32 = jnp.float32
BF16 = jnp.bfloat16
TILE = 256
GROUP = 8


def split_parts(matrix):
    high = matrix.astype(ml_dtypes.bfloat16)
    low = (matrix - high.astype(np.float64)).astype(ml_dtypes.bfloat16)
    return high, low


def two_fold(matrix):
    high, low = split_parts(matrix)
    return np.concatenate([high, low], axis=1)


def three_fold(matrix):
    high, low = split_parts(matrix)
    return np.concatenate([high, low, high], axis=1)


@functools.lru_cache(maxsize=None)
def dft_tables(rows):
    size = 2 * rows
    angle = 2.0 * np.pi * (np.arange(rows)[:, None] + 0.5) * np.arange(size)[None, :] / size
    ahead = np.concatenate([np.cos(angle), -np.sin(angle)], axis=0)
    back = ahead.T * (2.0 / size)
    signed = np.concatenate([back[:rows], -back[rows:]], axis=0)
    lags = back[rows - np.arange(rows)]
    return {"ahead": two_fold(ahead), "back": three_fold(signed), "lags": three_fold(lags)}


def half_table(ahead):
    rows = ahead.shape[0] // 2
    high, low = ahead[:, :rows], ahead[:, 2 * rows : 3 * rows]
    return high, low


def apply2(table, x):
    return jnp.dot(table, jnp.concatenate([x, x], axis=0), preferred_element_type=F32)


def apply3(table, x):
    high = x.astype(BF16)
    low = (x - high.astype(F32)).astype(BF16)
    return jnp.dot(table, jnp.concatenate([high, high, low], axis=0), preferred_element_type=F32)


def to_spectrum(ahead, x):
    high, low = half_table(ahead)
    return apply3(jnp.concatenate([high, low, high], axis=1), x)


def to_spectrum_exact(ahead, x):
    return apply2(jnp.concatenate(half_table(ahead), axis=1), x)


def times(x, y):
    half = x.shape[0] // 2
    xr, xi, yr, yi = x[:half], x[half:], y[:half], y[half:]
    return jnp.concatenate([xr * yr - xi * yi, xr * yi + xi * yr], axis=0)


def times_conj(x, y):
    half = x.shape[0] // 2
    xr, xi, yr, yi = x[:half], x[half:], y[:half], y[half:]
    return jnp.concatenate([xr * yr + xi * yi, xi * yr - xr * yi], axis=0)


def group_places(columns):
    return lax.broadcasted_iota(jnp.int32, (GROUP, columns), 0).astype(F32)


def spread_modes(rate, weight, rows, shift, backward):
    columns = rate.shape[1]
    places = group_places(columns)
    if backward:
        places = (GROUP - 1.0) - places
    count = rows // GROUP
    order = range(count - 1, -1, -1) if backward else range(count)
    sums = [None] * count
    for m in range(rate.shape[0]):
        rate_m = rate[m : m + 1]
        current = weight[m : m + 1] * jnp.exp(-rate_m * (places + shift))
        stride = jnp.broadcast_to(jnp.exp(-rate_m * GROUP), current.shape)
        for step, g in enumerate(order):
            sums[g] = current if sums[g] is None else sums[g] + current
            if step < count - 1:
                current = current * stride
    return jnp.concatenate(sums, axis=0)


def fold_modes(signal, rate, backward):
    columns = rate.shape[1]
    places = group_places(columns)
    if not backward:
        places = (GROUP - 1.0) - places
    count = signal.shape[0] // GROUP
    order = range(count - 1, -1, -1) if backward else range(count)
    found = []
    for m in range(rate.shape[0]):
        rate_m = rate[m : m + 1]
        stride = jnp.broadcast_to(jnp.exp(-rate_m * GROUP), (GROUP, columns))
        running = None
        for g in order:
            piece = signal[g * GROUP : (g + 1) * GROUP]
            running = piece if running is None else running * stride + piece
        found.append(jnp.sum(running * jnp.exp(-rate_m * places), axis=0, keepdims=True))
    return jnp.concatenate(found, axis=0)


def spectra_body(taps, rate, coef, skip, ahead, mr_spec, li_spec):
    rows = taps.shape[0]
    table = ahead[...]
    mr_spec[...] = to_spectrum(table, taps[...])
    kernel = spread_modes(rate[...], coef[...], rows, 0.0, False)
    first = lax.broadcasted_iota(jnp.int32, kernel.shape, 0) == 0
    kernel = kernel + jnp.where(first, skip[...], 0.0)
    li_spec[...] = to_spectrum(table, kernel)


def short_body(before, product, query, key, mr_spec, rate, ahead, back, spec, conv, mixed, signal, ends):
    rows = product.shape[0]
    x = jnp.concatenate([before[...], product[...]], axis=0)
    found = apply2(ahead[...], x)
    spec[...] = found
    filtered = -apply3(back[rows:], times(found, mr_spec[...]))
    conv[...] = filtered
    mixed_rows = (query[...].astype(F32) * filtered).astype(BF16)
    mixed[...] = mixed_rows
    rounded = (key[...].astype(F32) * mixed_rows.astype(F32)).astype(BF16)
    signal[...] = rounded
    ends[...] = fold_modes(rounded.astype(F32), rate[...], False)


def inner_body(signal, li_spec, ahead, back, inner):
    rows = signal.shape[0]
    inner[...] = apply3(back[:rows], times(to_spectrum_exact(ahead[...], signal[...]), li_spec[...]))


def gather_states(rate, gaps, states, rows):
    modes = rate.shape[0]
    total = jnp.zeros_like(rate)
    for k in range(states.shape[0] // modes):
        weight = jnp.exp(-rate * (jnp.maximum(gaps[k], 0.0) * float(rows)))
        total = total + jnp.where(gaps[k] >= 0.0, weight * states[k * modes : (k + 1) * modes], 0.0)
    return total


def long_body(gaps, inner, query, rate, coef, states, li_out, mixed):
    rows = inner.shape[0]
    entering = gather_states(rate[...], gaps, states, rows)
    total = inner[...] + spread_modes(rate[...], coef[...] * entering, rows, 1.0, False)
    li_out[...] = total
    mixed[...] = (query[...].astype(F32) * total).astype(BF16)


def split_body(count, starts, *rest):
    pieces, parts, whole = rest[: -count - 1], rest[-count - 1 : -1], rest[-1]
    for r, piece in enumerate(pieces):
        whole[:, pl.ds(pl.multiple_of(starts[r], 128), piece.shape[1])] = piece[...]
    for h, part in enumerate(parts):
        place = pl.multiple_of(starts[len(pieces) + h], 128)
        part[...] = whole[:, pl.ds(place, part.shape[1])]


def pair_grad_body(count, starts, *rest):
    parts, weights, (own, *others) = rest[:count], rest[count : count + 4], rest[count + 4 :]
    for part, result in zip(parts, (own, *others)):
        total = None
        for m, weight in enumerate(weights):
            block = part[:, pl.ds(pl.multiple_of(starts[m], 128), weight.shape[0])]
            found = jnp.dot(block, weight[...], preferred_element_type=F32)
            total = found if total is None else total + found
        result[...] = total.astype(result.dtype)


def pair_out_body(count, starts, *rest):
    mixed, weights, results = rest[:count], rest[count : count + 4], rest[count + 4 :]
    for rows, result in zip(mixed, results):
        for m, weight in enumerate(weights):
            found = lax.dot_general(rows[...], weight[...], (((1,), (1,)), ((), ())), preferred_element_type=F32)
            result[:, pl.ds(pl.multiple_of(starts[m], 128), weight.shape[0])] = found.astype(BF16)


def stack_body(count, starts, *rest):
    pieces, stack, whole = rest[:-2], rest[-2], rest[-1]
    rows = whole.shape[0]
    for r, piece in enumerate(pieces):
        whole[:, pl.ds(pl.multiple_of(starts[r], 128), piece.shape[1])] = piece[...]
    for h in range(count):
        place = pl.multiple_of(starts[len(pieces) + h], 128)
        stack[h * rows : (h + 1) * rows] = whole[:, pl.ds(place, stack.shape[1])]


def grad_gate_body(count, own, query, rate, li_out, *rest):
    parts, (grad_query, grad_out, ends) = rest[:count], rest[count:]
    total = own[...]
    for part in parts:
        total = total + part[...].astype(F32)
    grad_query[...] = total * li_out[...]
    gated = total * query[...].astype(F32)
    grad_out[...] = gated
    ends[...] = fold_modes(gated, rate[...], True)


def grad_inner_body(grad_out, li_spec, ahead, back, inner):
    rows = grad_out.shape[0]
    inner[...] = apply3(back[:rows], times_conj(to_spectrum(ahead[...], grad_out[...]), li_spec[...]))


def grad_long_body(
    inner, rate, coef, entering, mixed_mr, key_li, query_mr, conv, spec, ahead, lags,
    grad_key_li, grad_query_mr, grad_spec, taps,
):
    rows = inner.shape[0]
    grad_input = inner[...] + spread_modes(rate[...], coef[...] * entering[...], rows, 1.0, True)
    grad_key_li[...] = grad_input * mixed_mr[...].astype(F32)
    grad_mixed_mr = grad_input * key_li[...].astype(F32)
    grad_query_mr[...] = grad_mixed_mr * conv[...]
    grad_conv = grad_mixed_mr * query_mr[...].astype(F32)
    found = to_spectrum(ahead[...], grad_conv)
    grad_spec[...] = found
    taps[...] = apply3(lags[...], times_conj(spec[...], found))


def grad_taps_body(grad_spec, mr_spec, back, own_product, prev_product):
    rows = own_product.shape[0]
    products = apply3(back[...], times_conj(grad_spec[...], mr_spec[...]))
    own_product[...] = products[:rows]
    prev_product[...] = products[rows:].astype(BF16)


def grad_product_body(own, arrived, key, value, grad_key, grad_value):
    total = own[...] + arrived[...].astype(F32)
    grad_key[...] = total * value[...].astype(F32)
    grad_value[...] = total * key[...].astype(F32)


def run(body, columns, inputs, outputs, flops):
    tile = min(TILE, columns)
    in_specs = []
    moved = 0
    for kind, array in inputs:
        if kind == "tile":
            in_specs.append(pl.BlockSpec((array.shape[0], tile), lambda c: (0, c)))
        elif kind == "whole":
            in_specs.append(pl.BlockSpec(array.shape, lambda c: (0, 0)))
        else:
            in_specs.append(pl.BlockSpec(memory_space=pltpu.SMEM))
        moved += math.prod(array.shape) * array.dtype.itemsize
    for rows, dtype in outputs:
        moved += rows * columns * jnp.dtype(dtype).itemsize
    return pl.pallas_call(
        body,
        grid=(columns // tile,),
        in_specs=in_specs,
        out_specs=[pl.BlockSpec((rows, tile), lambda c: (0, c)) for rows, _ in outputs],
        out_shape=[jax.ShapeDtypeStruct((rows, columns), dtype) for rows, dtype in outputs],
        compiler_params=pltpu.CompilerParams(vmem_limit_bytes=12 * 1024 * 1024),
        cost_estimate=pl.CostEstimate(flops=flops, bytes_accessed=moved if flops else 0, transcendentals=0),
    )(*[array for _, array in inputs])


def run_once(body, inputs, outputs, scratch=()):
    return pl.pallas_call(
        body,
        in_specs=[pl.BlockSpec(memory_space=pltpu.SMEM)]
        + [pl.BlockSpec(memory_space=pltpu.VMEM)] * (len(inputs) - 1),
        out_specs=[pl.BlockSpec(memory_space=pltpu.VMEM)] * len(outputs),
        out_shape=[jax.ShapeDtypeStruct(shape, dtype) for shape, dtype in outputs],
        scratch_shapes=scratch,
        compiler_params=pltpu.CompilerParams(vmem_limit_bytes=16 * 1024 * 1024),
        cost_estimate=pl.CostEstimate(flops=0, bytes_accessed=0, transcendentals=0),
    )(*inputs)


def chip_swap(x, by):
    size = lax.axis_size("ctx")
    return lax.ppermute(x, "ctx", [(i, i ^ (2 * by)) for i in range(size)])


def line_swap(x, by):
    size = lax.axis_size("fsdp")
    return lax.ppermute(x, "fsdp", [(i, i ^ by) for i in range(size)])


def core_swap(x):
    size = lax.axis_size("ctx")
    return lax.ppermute(x, "ctx", [(i, i ^ 1) for i in range(size)])


def shifted(x, by):
    size = lax.axis_size("ctx")
    return lax.ppermute(x, "ctx", [(i, i + by) for i in range(size) if 0 <= i + by < size])


def columns_at(x, index, width):
    return lax.dynamic_slice_in_dim(x, index * width, width, 1)


def placed(pieces):
    width = pieces[0][1].shape[1]
    whole = jnp.zeros((pieces[0][1].shape[0], width * len(pieces)), pieces[0][1].dtype)
    for index, piece in pieces:
        whole = lax.dynamic_update_slice_in_dim(whole, piece, index * width, 1)
    return whole


def pair_sum(values):
    while len(values) > 1:
        values = [values[k] + values[k + 1] for k in range(0, len(values), 2)]
    return values[0]


def after(x, *others):
    return lax.optimization_barrier((x,) + others)[0]


def direct_factors(rate, rows, chip, backward):
    factors = [jnp.exp(-rate * float(rows))]
    for s in range(1, lax.axis_size("ctx") // 2):
        gap = (chip ^ s) - chip - 1 if backward else chip - (chip ^ s) - 1
        weight = jnp.exp(-rate * (2 * rows * jnp.maximum(gap, 0)).astype(F32))
        factors.append(jnp.where(gap >= 0, weight, 0.0))
    return factors


def entering_direct(ends, factors, here, backward):
    block = factors[0]
    later_core = ((here & 1) != 0) != backward
    sibling = core_swap(ends)
    total = jnp.where(later_core, block * sibling + ends, block * ends + sibling)
    entering = jnp.zeros_like(ends)
    for s, weight in enumerate(factors[1:], 1):
        entering = entering + weight * chip_swap(total, s)
    return jnp.where(later_core, block * entering + sibling, entering)


def shards(
    query_mr,
    key_mr,
    value_mr,
    query_li,
    key_li,
    mr_taps,
    li_time,
    li_residue,
    li_skip,
    out_weight,
    cotangent,
):
    rows, columns = query_mr.shape
    ctx_count = lax.axis_size("ctx")
    line_count = lax.axis_size("fsdp")
    chips = ctx_count // 2
    here = lax.axis_index("ctx")
    chip, core = here // 2, here % 2
    line = lax.axis_index("fsdp")
    grad_scale = 1.0 / math.sqrt(rows * ctx_count)
    tables = {name: jnp.asarray(table) for name, table in dft_tables(rows).items()}
    width = out_weight.shape[0]
    chip_width = 2 * width
    pass_flops = 2 * (2 * rows) * (2 * rows) * columns

    def tile(x):
        return ("tile", x)

    def table(name):
        return ("whole", tables[name])

    mr_product = (key_mr.astype(F32) * value_mr.astype(F32)).astype(BF16)
    before = shifted(mr_product, 1)
    cot_line = [cotangent] + [line_swap(cotangent, r) for r in range(1, line_count)]
    beside = chip_swap(out_weight, 1)
    pairs = chips // 2
    pair = chip // 2
    pair_width = 4 * width

    rate = 1.0 / li_time
    coef = li_residue * jnp.sqrt(-jnp.expm1(-2.0 * rate))
    back_factors = lax.optimization_barrier(direct_factors(rate, rows, here // 2, True))
    mr_spec, li_spec = run(
        spectra_body,
        columns,
        [tile(mr_taps), tile(rate), tile(coef), tile(li_skip[None, :]), table("ahead")],
        [(2 * rows, F32), (2 * rows, F32)],
        0,
    )
    spec, mr_conv, mixed_mr, li_input, ends = run(
        short_body,
        columns,
        [
            tile(after(before, *cot_line)),
            tile(mr_product),
            tile(query_mr),
            tile(key_li),
            tile(mr_spec),
            tile(rate),
            table("ahead"),
            table("back"),
        ],
        [(2 * rows, F32), (rows, F32), (rows, BF16), (rows, BF16), (rate.shape[0], F32)],
        0,
    )

    states = lax.all_gather(ends, "ctx").reshape(-1, columns)
    gaps = (here - 1 - jnp.arange(ctx_count, dtype=jnp.int32)).astype(F32)
    (li_inner,) = run(
        inner_body,
        columns,
        [tile(li_input), tile(li_spec), table("ahead"), table("back")],
        [(rows, F32)],
        0,
    )
    li_out, mixed_li = run(
        long_body,
        columns,
        [("scalar", gaps), tile(li_inner), tile(query_li), tile(rate), tile(coef), tile(states)],
        [(rows, F32), (rows, BF16)],
        0,
    )

    line_width = cotangent.shape[1]
    whole_width = line_width * line_count
    split_starts = [(line ^ r) * line_width for r in range(line_count)]
    split_starts += [(pair ^ h) * pair_width for h in range(pairs)]
    cot_pairs = run_once(
        functools.partial(split_body, pairs),
        [jnp.stack(split_starts)] + cot_line,
        [((rows, pair_width), BF16)] * pairs,
        [pltpu.VMEM((rows, whole_width), BF16)],
    )
    cot_parts = [cot_pairs[0]] + [chip_swap(cot_pairs[h], 2 * h) for h in range(1, pairs)]
    mixed_parts = [mixed_li] + [chip_swap(mixed_li, 2 * h) for h in range(1, pairs)]
    weights = [out_weight, core_swap(out_weight), beside, core_swap(beside)]
    pair_starts = jnp.stack([((here & 3) ^ m) * width for m in range(4)])

    share_flops = 2 * rows * columns * pair_width * pairs
    grad_own, *grad_sent = run(
        functools.partial(pair_grad_body, pairs),
        columns,
        [("scalar", pair_starts)] + [("whole", after(part, mixed_li)) for part in cot_parts] + [tile(weight) for weight in weights],
        [(rows, F32)] + [(rows, BF16)] * (pairs - 1),
        share_flops,
    )
    grad_parts = [chip_swap(part, 2 * h) for h, part in enumerate(grad_sent, 1)]

    out_own, *out_sent = run_once(
        functools.partial(pair_out_body, pairs),
        [pair_starts, after(mixed_parts[0], grad_own)] + mixed_parts[1:] + weights,
        [((rows, pair_width), BF16)] * pairs,
    )
    out_pairs = [out_own] + [chip_swap(part, 2 * h) for h, part in enumerate(out_sent, 1)]
    out_starts = [(pair ^ h) * pair_width for h in range(pairs)]
    out_starts += [(line ^ r) * line_width for r in range(line_count)]
    (out_line,) = run_once(
        functools.partial(stack_body, line_count),
        [jnp.stack(out_starts)] + out_pairs,
        [((line_count * rows, line_width), BF16)],
        [pltpu.VMEM((rows, whole_width), BF16)],
    )
    by = line_count // 2
    kept, arrived_out = out_line[: by * rows], line_swap(out_line[by * rows :], by)
    while by > 1:
        by //= 2
        total = kept.astype(F32) + arrived_out.astype(F32)
        kept, arrived_out = total[: by * rows], line_swap(total[by * rows :].astype(BF16), by)
    output = kept.astype(F32) + arrived_out.astype(F32)

    grad_query_li, grad_li_out, back_ends = run(
        functools.partial(grad_gate_body, pairs - 1),
        columns,
        [tile(after(grad_own, out_own)), tile(query_li), tile(rate), tile(li_out)] + [tile(part) for part in grad_parts],
        [(rows, F32), (rows, F32), (rate.shape[0], F32)],
        pass_flops,
    )
    back_entering = entering_direct(back_ends, back_factors, here, True)
    (grad_inner,) = run(
        grad_inner_body,
        columns,
        [tile(grad_li_out), tile(li_spec), table("ahead"), table("back")],
        [(rows, F32)],
        3 * pass_flops,
    )
    grad_key_li, grad_query_mr, grad_spec, tap_partial = run(
        grad_long_body,
        columns,
        [
            tile(grad_inner),
            tile(rate),
            tile(coef),
            tile(back_entering),
            tile(mixed_mr),
            tile(key_li),
            tile(query_mr),
            tile(mr_conv),
            tile(spec),
            table("ahead"),
            table("lags"),
        ],
        [(rows, F32), (rows, F32), (2 * rows, F32), (rows, F32)],
        4 * pass_flops,
    )
    own_product, prev_product = run(
        grad_taps_body,
        columns,
        [tile(grad_spec), tile(mr_spec), table("back")],
        [(rows, F32), (rows, BF16)],
        3 * pass_flops,
    )
    arrived = shifted(prev_product, -1)
    grad_key_mr, grad_value_mr = run(
        grad_product_body,
        columns,
        [tile(own_product), tile(arrived), tile(key_mr), tile(value_mr)],
        [(rows, F32), (rows, F32)],
        rows * columns,
    )

    tap_half = tap_partial.shape[0] // 2
    halves = tap_partial.reshape(2, tap_half, columns)
    own_half = lax.dynamic_index_in_dim(halves, core, 0, keepdims=False)
    far_half = lax.dynamic_index_in_dim(halves, 1 - core, 0, keepdims=False)
    chip_half = (own_half + core_swap(far_half)).astype(BF16)
    everywhere = [chip_half] + [chip_swap(chip_half, s) for s in range(1, chips)]
    plane_half = pair_sum([part.astype(F32) for part in everywhere]) * grad_scale
    other_half = core_swap(after(plane_half, arrived_out))
    grad_taps = jnp.where(
        core == 0,
        jnp.concatenate([plane_half, other_half], axis=0),
        jnp.concatenate([other_half, plane_half], axis=0),
    )

    side = chip % 2
    near_cot = jnp.concatenate([columns_at(part, side, chip_width) for part in cot_parts], axis=0)
    far_cot = jnp.concatenate([columns_at(part, 1 - side, chip_width) for part in cot_parts], axis=0)
    far_cot = after(far_cot, back_ends)
    near_mixed = jnp.concatenate(mixed_parts, axis=0)
    if chip_width == columns:
        passed = chip_swap(jnp.concatenate([far_cot, near_mixed], axis=0), 1)
        got_cot, got_mixed = passed[: rows * pairs], passed[rows * pairs :]
    else:
        got_cot, got_mixed = chip_swap(far_cot, 1), chip_swap(near_mixed, 1)
    cot_rows = jnp.concatenate([near_cot, after(got_cot, tap_partial)], axis=0)
    mixed_rows = jnp.concatenate([near_mixed, got_mixed], axis=0)

    def weight_share(which):
        return lax.dot_general(
            columns_at(cot_rows, which, width),
            mixed_rows,
            (((0,), (0,)), ((), ())),
            preferred_element_type=F32,
        )

    far_share = core_swap(weight_share(1 - core).astype(BF16))
    grad_weight = (weight_share(core) + far_share.astype(F32)) * grad_scale
    return (
        output,
        grad_query_mr,
        grad_key_mr,
        grad_value_mr,
        grad_query_li,
        grad_key_li,
        grad_taps,
        grad_weight,
    )


def solution(mesh):
    rows = P("ctx", "fsdp")
    channels = P(None, "fsdp")
    return jax.shard_map(
        shards,
        mesh=mesh,
        in_specs=(rows,) * 5 + (channels,) * 3 + (P("fsdp"),) + (rows,) * 2,
        out_specs=(rows,) * 6 + (channels, rows),
        check_vma=False,
    )
```

```python
import functools
import math

import jax
import jax.numpy as jnp
import ml_dtypes
import numpy as np
from jax import lax
from jax.experimental import pallas as pl
from jax.experimental.pallas import tpu as pltpu
from jax.sharding import PartitionSpec as P

F32 = jnp.float32
BF16 = jnp.bfloat16
TILE = 256
GROUP = 8


def split_parts(matrix):
    high = matrix.astype(ml_dtypes.bfloat16)
    low = (matrix - high.astype(np.float64)).astype(ml_dtypes.bfloat16)
    return high, low


def two_fold(matrix):
    high, low = split_parts(matrix)
    return np.concatenate([high, low], axis=1)


def three_fold(matrix):
    high, low = split_parts(matrix)
    return np.concatenate([high, low, high], axis=1)


@functools.lru_cache(maxsize=None)
def dft_tables(rows):
    size = 2 * rows
    angle = 2.0 * np.pi * (np.arange(rows)[:, None] + 0.5) * np.arange(size)[None, :] / size
    ahead = np.concatenate([np.cos(angle), -np.sin(angle)], axis=0)
    back = ahead.T * (2.0 / size)
    signed = np.concatenate([back[:rows], -back[rows:]], axis=0)
    lags = back[rows - np.arange(rows)]
    return {"ahead": two_fold(ahead), "back": three_fold(signed), "lags": three_fold(lags)}


def half_table(ahead):
    rows = ahead.shape[0] // 2
    high, low = ahead[:, :rows], ahead[:, 2 * rows : 3 * rows]
    return high, low


def apply2(table, x):
    return jnp.dot(table, jnp.concatenate([x, x], axis=0), preferred_element_type=F32)


def apply3(table, x):
    high = x.astype(BF16)
    low = (x - high.astype(F32)).astype(BF16)
    return jnp.dot(table, jnp.concatenate([high, high, low], axis=0), preferred_element_type=F32)


def to_spectrum(ahead, x):
    high, low = half_table(ahead)
    return apply3(jnp.concatenate([high, low, high], axis=1), x)


def to_spectrum_exact(ahead, x):
    return apply2(jnp.concatenate(half_table(ahead), axis=1), x)


def times(x, y):
    half = x.shape[0] // 2
    xr, xi, yr, yi = x[:half], x[half:], y[:half], y[half:]
    return jnp.concatenate([xr * yr - xi * yi, xr * yi + xi * yr], axis=0)


def times_conj(x, y):
    half = x.shape[0] // 2
    xr, xi, yr, yi = x[:half], x[half:], y[:half], y[half:]
    return jnp.concatenate([xr * yr + xi * yi, xi * yr - xr * yi], axis=0)


def group_places(columns):
    return lax.broadcasted_iota(jnp.int32, (GROUP, columns), 0).astype(F32)


def spread_modes(rate, weight, rows, shift, backward):
    columns = rate.shape[1]
    places = group_places(columns)
    if backward:
        places = (GROUP - 1.0) - places
    count = rows // GROUP
    order = range(count - 1, -1, -1) if backward else range(count)
    sums = [None] * count
    for m in range(rate.shape[0]):
        rate_m = rate[m : m + 1]
        current = weight[m : m + 1] * jnp.exp(-rate_m * (places + shift))
        stride = jnp.broadcast_to(jnp.exp(-rate_m * GROUP), current.shape)
        for step, g in enumerate(order):
            sums[g] = current if sums[g] is None else sums[g] + current
            if step < count - 1:
                current = current * stride
    return jnp.concatenate(sums, axis=0)


def fold_modes(signal, rate, backward):
    columns = rate.shape[1]
    places = group_places(columns)
    if not backward:
        places = (GROUP - 1.0) - places
    count = signal.shape[0] // GROUP
    order = range(count - 1, -1, -1) if backward else range(count)
    found = []
    for m in range(rate.shape[0]):
        rate_m = rate[m : m + 1]
        stride = jnp.broadcast_to(jnp.exp(-rate_m * GROUP), (GROUP, columns))
        running = None
        for g in order:
            piece = signal[g * GROUP : (g + 1) * GROUP]
            running = piece if running is None else running * stride + piece
        found.append(jnp.sum(running * jnp.exp(-rate_m * places), axis=0, keepdims=True))
    return jnp.concatenate(found, axis=0)


def spectra_body(taps, rate, coef, skip, ahead, mr_spec, li_spec):
    rows = taps.shape[0]
    table = ahead[...]
    mr_spec[...] = to_spectrum(table, taps[...])
    kernel = spread_modes(rate[...], coef[...], rows, 0.0, False)
    first = lax.broadcasted_iota(jnp.int32, kernel.shape, 0) == 0
    kernel = kernel + jnp.where(first, skip[...], 0.0)
    li_spec[...] = to_spectrum(table, kernel)


def short_body(before, product, query, key, mr_spec, rate, ahead, back, spec, conv, mixed, signal, ends):
    rows = product.shape[0]
    x = jnp.concatenate([before[...], product[...]], axis=0)
    found = apply2(ahead[...], x)
    spec[...] = found
    filtered = -apply3(back[rows:], times(found, mr_spec[...]))
    conv[...] = filtered
    mixed_rows = (query[...].astype(F32) * filtered).astype(BF16)
    mixed[...] = mixed_rows
    rounded = (key[...].astype(F32) * mixed_rows.astype(F32)).astype(BF16)
    signal[...] = rounded
    ends[...] = fold_modes(rounded.astype(F32), rate[...], False)


def inner_body(signal, li_spec, ahead, back, inner):
    rows = signal.shape[0]
    inner[...] = apply3(back[:rows], times(to_spectrum_exact(ahead[...], signal[...]), li_spec[...]))


def gather_states(rate, gaps, states, rows):
    modes = rate.shape[0]
    total = jnp.zeros_like(rate)
    for k in range(states.shape[0] // modes):
        weight = jnp.exp(-rate * (jnp.maximum(gaps[k], 0.0) * float(rows)))
        total = total + jnp.where(gaps[k] >= 0.0, weight * states[k * modes : (k + 1) * modes], 0.0)
    return total


def long_body(gaps, inner, query, rate, coef, states, li_out, mixed):
    rows = inner.shape[0]
    entering = gather_states(rate[...], gaps, states, rows)
    total = inner[...] + spread_modes(rate[...], coef[...] * entering, rows, 1.0, False)
    li_out[...] = total
    mixed[...] = (query[...].astype(F32) * total).astype(BF16)


def split_body(count, starts, *rest):
    pieces, parts, whole = rest[: -count - 1], rest[-count - 1 : -1], rest[-1]
    for r, piece in enumerate(pieces):
        whole[:, pl.ds(pl.multiple_of(starts[r], 128), piece.shape[1])] = piece[...]
    for h, part in enumerate(parts):
        place = pl.multiple_of(starts[len(pieces) + h], 128)
        part[...] = whole[:, pl.ds(place, part.shape[1])]


def pair_grad_body(count, starts, *rest):
    parts, weights, (own, *others) = rest[:count], rest[count : count + 6], rest[count + 6 :]
    for part, result in zip(parts, (own, *others)):
        total = None
        for m, weight in enumerate(weights):
            block = part[:, pl.ds(pl.multiple_of(starts[m], 128), weight.shape[0])]
            found = jnp.dot(block, weight[...], preferred_element_type=F32)
            total = found if total is None else total + found
        result[...] = total.astype(result.dtype)


def pair_out_body(count, starts, *rest):
    mixed, weights, results = rest[:count], rest[count : count + 6], rest[count + 6 :]
    for rows, result in zip(mixed, results):
        for m, weight in enumerate(weights):
            found = lax.dot_general(rows[...], weight[...], (((1,), (1,)), ((), ())), preferred_element_type=F32)
            result[:, pl.ds(pl.multiple_of(starts[m], 128), weight.shape[0])] = found.astype(BF16)


def stack_body(count, starts, *rest):
    pieces, stack, whole = rest[:-2], rest[-2], rest[-1]
    rows = whole.shape[0]
    for r, piece in enumerate(pieces):
        whole[:, pl.ds(pl.multiple_of(starts[r], 128), piece.shape[1])] = piece[...]
    for h in range(count):
        place = pl.multiple_of(starts[len(pieces) + h], 128)
        stack[h * rows : (h + 1) * rows] = whole[:, pl.ds(place, stack.shape[1])]


def grad_gate_body(count, own, query, rate, li_out, *rest):
    parts, (grad_query, grad_out, ends) = rest[:count], rest[count:]
    total = own[...]
    for part in parts:
        total = total + part[...].astype(F32)
    grad_query[...] = total * li_out[...]
    gated = total * query[...].astype(F32)
    grad_out[...] = gated
    ends[...] = fold_modes(gated, rate[...], True)


def grad_inner_body(grad_out, li_spec, ahead, back, inner):
    rows = grad_out.shape[0]
    inner[...] = apply3(back[:rows], times_conj(to_spectrum(ahead[...], grad_out[...]), li_spec[...]))


def grad_long_body(
    inner, rate, coef, entering, mixed_mr, key_li, query_mr, conv, spec, ahead, lags,
    grad_key_li, grad_query_mr, grad_spec, taps,
):
    rows = inner.shape[0]
    grad_input = inner[...] + spread_modes(rate[...], coef[...] * entering[...], rows, 1.0, True)
    grad_key_li[...] = grad_input * mixed_mr[...].astype(F32)
    grad_mixed_mr = grad_input * key_li[...].astype(F32)
    grad_query_mr[...] = grad_mixed_mr * conv[...]
    grad_conv = grad_mixed_mr * query_mr[...].astype(F32)
    found = to_spectrum(ahead[...], grad_conv)
    grad_spec[...] = found
    taps[...] = apply3(lags[...], times_conj(spec[...], found))


def grad_taps_body(grad_spec, mr_spec, back, own_product, prev_product):
    rows = own_product.shape[0]
    products = apply3(back[...], times_conj(grad_spec[...], mr_spec[...]))
    own_product[...] = products[:rows]
    prev_product[...] = products[rows:].astype(BF16)


def grad_product_body(own, arrived, key, value, grad_key, grad_value):
    total = own[...] + arrived[...].astype(F32)
    grad_key[...] = total * value[...].astype(F32)
    grad_value[...] = total * key[...].astype(F32)


def run(body, columns, inputs, outputs, flops):
    tile = min(TILE, columns)
    in_specs = []
    moved = 0
    for kind, array in inputs:
        if kind == "tile":
            in_specs.append(pl.BlockSpec((array.shape[0], tile), lambda c: (0, c)))
        elif kind == "whole":
            in_specs.append(pl.BlockSpec(array.shape, lambda c: (0, 0)))
        else:
            in_specs.append(pl.BlockSpec(memory_space=pltpu.SMEM))
        moved += math.prod(array.shape) * array.dtype.itemsize
    for rows, dtype in outputs:
        moved += rows * columns * jnp.dtype(dtype).itemsize
    return pl.pallas_call(
        body,
        grid=(columns // tile,),
        in_specs=in_specs,
        out_specs=[pl.BlockSpec((rows, tile), lambda c: (0, c)) for rows, _ in outputs],
        out_shape=[jax.ShapeDtypeStruct((rows, columns), dtype) for rows, dtype in outputs],
        compiler_params=pltpu.CompilerParams(vmem_limit_bytes=56 * 1024 * 1024),
        cost_estimate=pl.CostEstimate(flops=flops, bytes_accessed=moved if flops else 0, transcendentals=0),
    )(*[array for _, array in inputs])


def run_once(body, inputs, outputs, scratch=()):
    def block(shape):
        return pl.BlockSpec(shape, lambda c: (0, 0))

    return pl.pallas_call(
        body,
        grid=(1,),
        in_specs=[pl.BlockSpec(memory_space=pltpu.SMEM)] + [block(array.shape) for array in inputs[1:]],
        out_specs=[block(shape) for shape, _ in outputs],
        out_shape=[jax.ShapeDtypeStruct(shape, dtype) for shape, dtype in outputs],
        scratch_shapes=scratch,
        compiler_params=pltpu.CompilerParams(vmem_limit_bytes=56 * 1024 * 1024),
        cost_estimate=pl.CostEstimate(flops=0, bytes_accessed=0, transcendentals=0),
    )(*inputs)


def chip_swap(x, by):
    size = lax.axis_size("ctx")
    return lax.ppermute(x, "ctx", [(i, i ^ (2 * by)) for i in range(size)])


def line_swap(x, by):
    size = lax.axis_size("fsdp")
    return lax.ppermute(x, "fsdp", [(i, i ^ by) for i in range(size)])


def core_swap(x):
    size = lax.axis_size("ctx")
    return lax.ppermute(x, "ctx", [(i, i ^ 1) for i in range(size)])


def shifted(x, by):
    size = lax.axis_size("ctx")
    return lax.ppermute(x, "ctx", [(i, i + by) for i in range(size) if 0 <= i + by < size])


def bit_reversed(count):
    order = [0]
    while len(order) < count:
        order = [2 * k for k in order] + [2 * k + 1 for k in order]
    return order


def columns_at(x, index, width):
    return lax.dynamic_slice_in_dim(x, index * width, width, 1)


def placed(pieces):
    width = pieces[0][1].shape[1]
    whole = jnp.zeros((pieces[0][1].shape[0], width * len(pieces)), pieces[0][1].dtype)
    for index, piece in pieces:
        whole = lax.dynamic_update_slice_in_dim(whole, piece, index * width, 1)
    return whole


def pair_sum(values):
    while len(values) > 1:
        values = [values[k] + values[k + 1] for k in range(0, len(values), 2)]
    return values[0]


def after(x, *others):
    return lax.optimization_barrier((x,) + others)[0]


def direct_factors(rate, rows, chip, backward):
    factors = [jnp.exp(-rate * float(rows))]
    for s in range(1, lax.axis_size("ctx") // 2):
        gap = (chip ^ s) - chip - 1 if backward else chip - (chip ^ s) - 1
        weight = jnp.exp(-rate * (2 * rows * jnp.maximum(gap, 0)).astype(F32))
        factors.append(jnp.where(gap >= 0, weight, 0.0))
    return factors


def entering_direct(ends, factors, here, backward):
    block = factors[0]
    later_core = ((here & 1) != 0) != backward
    sibling = core_swap(ends)
    total = jnp.where(later_core, block * sibling + ends, block * ends + sibling)
    entering = jnp.zeros_like(ends)
    for s, weight in enumerate(factors[1:], 1):
        entering = entering + weight * chip_swap(total, s)
    return jnp.where(later_core, block * entering + sibling, entering)


def shards(
    query_mr,
    key_mr,
    value_mr,
    query_li,
    key_li,
    mr_taps,
    li_time,
    li_residue,
    li_skip,
    out_weight,
    cotangent,
):
    rows, columns = query_mr.shape
    ctx_count = lax.axis_size("ctx")
    line_count = lax.axis_size("fsdp")
    chips = ctx_count // 2
    here = lax.axis_index("ctx")
    chip, core = here // 2, here % 2
    line = lax.axis_index("fsdp")
    grad_scale = 1.0 / math.sqrt(rows * ctx_count)
    tables = {name: jnp.asarray(table) for name, table in dft_tables(rows).items()}
    width = out_weight.shape[0]
    chip_width = 2 * width
    pass_flops = 2 * (2 * rows) * (2 * rows) * columns

    def tile(x):
        return ("tile", x)

    def table(name):
        return ("whole", tables[name])

    mr_product = (key_mr.astype(F32) * value_mr.astype(F32)).astype(BF16)
    before = shifted(mr_product, 1)
    def line_go(numbers, *ready):
        return [line_swap(after(cotangent, *ready), r) for r in numbers]

    middle = 1 + line_count // 2
    half = width // 2
    first_go = line_go(range(1, 2), mr_product)
    first_rows = chip_swap(after(out_weight[:half], before), 1)
    pairs = chips // 2
    pair = chip // 2
    pair_width = 4 * width

    rate = 1.0 / li_time
    coef = li_residue * jnp.sqrt(-jnp.expm1(-2.0 * rate))
    back_factors = lax.optimization_barrier(direct_factors(rate, rows, here // 2, True))
    mr_spec, li_spec = run(
        spectra_body,
        columns,
        [tile(mr_taps), tile(rate), tile(coef), tile(li_skip[None, :]), table("ahead")],
        [(2 * rows, F32), (2 * rows, F32)],
        0,
    )
    second_go = line_go(range(2, middle), mr_spec, *first_go)
    spec, mr_conv, mixed_mr, li_input, ends = run(
        short_body,
        columns,
        [
            tile(after(before, *first_go)),
            tile(mr_product),
            tile(query_mr),
            tile(key_li),
            tile(mr_spec),
            tile(rate),
            table("ahead"),
            table("back"),
        ],
        [(2 * rows, F32), (rows, F32), (rows, BF16), (rows, BF16), (rate.shape[0], F32)],
        0,
    )

    third_go = line_go(range(middle, line_count), ends, *second_go)
    second_rows = chip_swap(after(out_weight[half:], ends, first_rows), 1)
    states = lax.all_gather(after(ends, first_rows, *second_go), "ctx").reshape(-1, columns)
    gaps = (here - 1 - jnp.arange(ctx_count, dtype=jnp.int32)).astype(F32)
    (li_inner,) = run(
        inner_body,
        columns,
        [tile(li_input), tile(li_spec), table("ahead"), table("back")],
        [(rows, F32)],
        0,
    )
    li_out, mixed_li = run(
        long_body,
        columns,
        [("scalar", gaps), tile(after(li_inner, second_rows, *third_go)), tile(query_li), tile(rate), tile(coef), tile(states)],
        [(rows, F32), (rows, BF16)],
        0,
    )

    beside = [first_rows, second_rows]
    cot_line = [after(piece, mixed_li) for piece in [cotangent] + first_go + second_go + third_go]
    line_width = cotangent.shape[1]
    whole_width = line_width * line_count
    split_starts = [(line ^ r) * line_width for r in range(line_count)]
    split_starts += [(pair ^ h) * pair_width for h in range(pairs)]
    cot_pairs = run_once(
        functools.partial(split_body, pairs),
        [jnp.stack(split_starts)] + cot_line,
        [((rows, pair_width), BF16)] * pairs,
        [pltpu.VMEM((rows, whole_width), BF16)],
    )
    cot_parts = [cot_pairs[0]] + [chip_swap(cot_pairs[h], 2 * h) for h in range(1, pairs)]
    mixed_parts = [mixed_li] + [chip_swap(mixed_li, 2 * h) for h in range(1, pairs)]
    weights = [out_weight, core_swap(out_weight)] + beside + [core_swap(piece) for piece in beside]
    places = [(0, 0), (1, 0), (2, 0), (2, half), (3, 0), (3, half)]
    pair_starts = jnp.stack([((here & 3) ^ m) * width + row for m, row in places])

    share_flops = 2 * rows * columns * pair_width * pairs
    grad_own, *grad_sent = run(
        functools.partial(pair_grad_body, pairs),
        columns,
        [("scalar", pair_starts)] + [("whole", after(part, *mixed_parts)) for part in cot_parts] + [tile(weight) for weight in weights],
        [(rows, F32)] + [(rows, BF16)] * (pairs - 1),
        share_flops,
    )
    grad_parts = [chip_swap(part, 2 * h) for h, part in enumerate(grad_sent, 1)]

    out_own, *out_sent = run_once(
        functools.partial(pair_out_body, pairs),
        [pair_starts, after(mixed_parts[0], grad_own)] + mixed_parts[1:] + weights,
        [((rows, pair_width), BF16)] * pairs,
    )
    out_pairs = [out_own] + [chip_swap(part, 2 * h) for h, part in enumerate(out_sent, 1)]
    out_starts = [(pair ^ h) * pair_width for h in range(pairs)]
    out_starts += [(line ^ r) * line_width for r in bit_reversed(line_count)]
    (out_line,) = run_once(
        functools.partial(stack_body, line_count),
        [jnp.stack(out_starts)] + out_pairs,
        [((line_count * rows, line_width), BF16)],
        [pltpu.VMEM((rows, whole_width), BF16)],
    )
    count, by = line_count // 2, 1
    kept, arrived_out = out_line[: count * rows], line_swap(out_line[count * rows :], by)
    first_out = arrived_out
    while count > 1:
        count //= 2
        by *= 2
        total = kept.astype(F32) + arrived_out.astype(F32)
        kept, arrived_out = total[: count * rows], line_swap(total[count * rows :].astype(BF16), by)
    output = kept.astype(F32) + arrived_out.astype(F32)

    side = chip % 2
    near_cot = jnp.concatenate([columns_at(part, side, chip_width) for part in cot_parts], axis=0)
    far_cot = jnp.concatenate([columns_at(part, 1 - side, chip_width) for part in cot_parts], axis=0)
    got_cot = chip_swap(after(far_cot, grad_own), 1)

    grad_query_li, grad_li_out, back_ends = run(
        functools.partial(grad_gate_body, pairs - 1),
        columns,
        [tile(after(grad_own, out_own, got_cot)), tile(query_li), tile(rate), tile(li_out)] + [tile(part) for part in grad_parts],
        [(rows, F32), (rows, F32), (rate.shape[0], F32)],
        pass_flops,
    )
    back_entering = entering_direct(back_ends, back_factors, here, True)
    (grad_inner,) = run(
        grad_inner_body,
        columns,
        [tile(grad_li_out), tile(li_spec), table("ahead"), table("back")],
        [(rows, F32)],
        3 * pass_flops,
    )
    grad_key_li, grad_query_mr, grad_spec, tap_partial = run(
        grad_long_body,
        columns,
        [
            tile(grad_inner),
            tile(rate),
            tile(coef),
            tile(back_entering),
            tile(mixed_mr),
            tile(key_li),
            tile(query_mr),
            tile(mr_conv),
            tile(spec),
            table("ahead"),
            table("lags"),
        ],
        [(rows, F32), (rows, F32), (2 * rows, F32), (rows, F32)],
        4 * pass_flops,
    )
    near_mixed = jnp.concatenate(mixed_parts, axis=0)
    got_mixed = chip_swap(after(near_mixed, back_entering), 1)
    grad_spec = after(grad_spec, got_mixed, first_out)
    own_product, prev_product = run(
        grad_taps_body,
        columns,
        [tile(grad_spec), tile(mr_spec), table("back")],
        [(rows, F32), (rows, BF16)],
        3 * pass_flops,
    )
    arrived = shifted(prev_product, -1)
    grad_key_mr, grad_value_mr = run(
        grad_product_body,
        columns,
        [tile(own_product), tile(arrived), tile(key_mr), tile(value_mr)],
        [(rows, F32), (rows, F32)],
        rows * columns,
    )

    tap_half = tap_partial.shape[0] // 2
    halves = tap_partial.reshape(2, tap_half, columns)
    own_half = lax.dynamic_index_in_dim(halves, core, 0, keepdims=False)
    far_half = lax.dynamic_index_in_dim(halves, 1 - core, 0, keepdims=False)
    chip_half = (own_half + core_swap(far_half)).astype(BF16)
    everywhere = [chip_half] + [chip_swap(chip_half, s) for s in range(1, chips)]
    plane_half = pair_sum([part.astype(F32) for part in everywhere]) * grad_scale
    other_half = core_swap(after(plane_half, arrived_out))
    grad_taps = jnp.where(
        core == 0,
        jnp.concatenate([plane_half, other_half], axis=0),
        jnp.concatenate([other_half, plane_half], axis=0),
    )

    cot_rows = jnp.concatenate([near_cot, got_cot], axis=0)
    mixed_rows = jnp.concatenate([near_mixed, got_mixed], axis=0)

    def weight_share(which):
        return lax.dot_general(
            columns_at(cot_rows, which, width),
            mixed_rows,
            (((0,), (0,)), ((), ())),
            preferred_element_type=F32,
        )

    far_share = core_swap(weight_share(1 - core).astype(BF16))
    grad_weight = (weight_share(core) + far_share.astype(F32)) * grad_scale
    return (
        output,
        grad_query_mr,
        grad_key_mr,
        grad_value_mr,
        grad_query_li,
        grad_key_li,
        grad_taps,
        grad_weight,
    )


def solution(mesh):
    rows = P("ctx", "fsdp")
    channels = P(None, "fsdp")
    return jax.shard_map(
        shards,
        mesh=mesh,
        in_specs=(rows,) * 5 + (channels,) * 3 + (P("fsdp"),) + (rows,) * 2,
        out_specs=(rows,) * 6 + (channels, rows),
        check_vma=False,
    )
```

```python
import functools
import math

import jax
import jax.numpy as jnp
import ml_dtypes
import numpy as np
from jax import lax
from jax.experimental import pallas as pl
from jax.experimental.pallas import tpu as pltpu
from jax.sharding import PartitionSpec as P

F32 = jnp.float32
BF16 = jnp.bfloat16
TILE = 256
GROUP = 8


def split_parts(matrix):
    high = matrix.astype(ml_dtypes.bfloat16)
    low = (matrix - high.astype(np.float64)).astype(ml_dtypes.bfloat16)
    return high, low


def two_fold(matrix):
    high, low = split_parts(matrix)
    return np.concatenate([high, low], axis=1)


def three_fold(matrix):
    high, low = split_parts(matrix)
    return np.concatenate([high, low, high], axis=1)


@functools.lru_cache(maxsize=None)
def dft_tables(rows):
    size = 2 * rows
    angle = 2.0 * np.pi * (np.arange(rows)[:, None] + 0.5) * np.arange(size)[None, :] / size
    ahead = np.concatenate([np.cos(angle), -np.sin(angle)], axis=0)
    back = ahead.T * (2.0 / size)
    signed = np.concatenate([back[:rows], -back[rows:]], axis=0)
    lags = back[rows - np.arange(rows)]
    return {"ahead": two_fold(ahead), "back": three_fold(signed), "lags": three_fold(lags)}


def half_table(ahead):
    rows = ahead.shape[0] // 2
    high, low = ahead[:, :rows], ahead[:, 2 * rows : 3 * rows]
    return high, low


def apply2(table, x):
    return jnp.dot(table, jnp.concatenate([x, x], axis=0), preferred_element_type=F32)


def apply3(table, x):
    high = x.astype(BF16)
    low = (x - high.astype(F32)).astype(BF16)
    return jnp.dot(table, jnp.concatenate([high, high, low], axis=0), preferred_element_type=F32)


def to_spectrum(ahead, x):
    high, low = half_table(ahead)
    return apply3(jnp.concatenate([high, low, high], axis=1), x)


def to_spectrum_exact(ahead, x):
    return apply2(jnp.concatenate(half_table(ahead), axis=1), x)


def times(x, y):
    half = x.shape[0] // 2
    xr, xi, yr, yi = x[:half], x[half:], y[:half], y[half:]
    return jnp.concatenate([xr * yr - xi * yi, xr * yi + xi * yr], axis=0)


def times_conj(x, y):
    half = x.shape[0] // 2
    xr, xi, yr, yi = x[:half], x[half:], y[:half], y[half:]
    return jnp.concatenate([xr * yr + xi * yi, xi * yr - xr * yi], axis=0)


def group_places(columns):
    return lax.broadcasted_iota(jnp.int32, (GROUP, columns), 0).astype(F32)


def spread_modes(rate, weight, rows, shift, backward):
    columns = rate.shape[1]
    places = group_places(columns)
    if backward:
        places = (GROUP - 1.0) - places
    count = rows // GROUP
    order = range(count - 1, -1, -1) if backward else range(count)
    sums = [None] * count
    for m in range(rate.shape[0]):
        rate_m = rate[m : m + 1]
        current = weight[m : m + 1] * jnp.exp(-rate_m * (places + shift))
        stride = jnp.broadcast_to(jnp.exp(-rate_m * GROUP), current.shape)
        for step, g in enumerate(order):
            sums[g] = current if sums[g] is None else sums[g] + current
            if step < count - 1:
                current = current * stride
    return jnp.concatenate(sums, axis=0)


def fold_modes(signal, rate, backward):
    columns = rate.shape[1]
    places = group_places(columns)
    if not backward:
        places = (GROUP - 1.0) - places
    count = signal.shape[0] // GROUP
    order = range(count - 1, -1, -1) if backward else range(count)
    found = []
    for m in range(rate.shape[0]):
        rate_m = rate[m : m + 1]
        stride = jnp.broadcast_to(jnp.exp(-rate_m * GROUP), (GROUP, columns))
        running = None
        for g in order:
            piece = signal[g * GROUP : (g + 1) * GROUP]
            running = piece if running is None else running * stride + piece
        found.append(jnp.sum(running * jnp.exp(-rate_m * places), axis=0, keepdims=True))
    return jnp.concatenate(found, axis=0)


def spectra_body(taps, rate, coef, skip, ahead, mr_spec, li_spec):
    rows = taps.shape[0]
    table = ahead[...]
    mr_spec[...] = to_spectrum(table, taps[...])
    kernel = spread_modes(rate[...], coef[...], rows, 0.0, False)
    first = lax.broadcasted_iota(jnp.int32, kernel.shape, 0) == 0
    kernel = kernel + jnp.where(first, skip[...], 0.0)
    li_spec[...] = to_spectrum(table, kernel)


def short_body(before, product, query, key, mr_spec, rate, ahead, back, spec, conv, mixed, signal, ends):
    rows = product.shape[0]
    x = jnp.concatenate([before[...], product[...]], axis=0)
    found = apply2(ahead[...], x)
    spec[...] = found
    filtered = -apply3(back[rows:], times(found, mr_spec[...]))
    conv[...] = filtered
    mixed_rows = (query[...].astype(F32) * filtered).astype(BF16)
    mixed[...] = mixed_rows
    rounded = (key[...].astype(F32) * mixed_rows.astype(F32)).astype(BF16)
    signal[...] = rounded
    ends[...] = fold_modes(rounded.astype(F32), rate[...], False)


def inner_body(signal, li_spec, ahead, back, inner):
    rows = signal.shape[0]
    inner[...] = apply3(back[:rows], times(to_spectrum_exact(ahead[...], signal[...]), li_spec[...]))


def gather_states(rate, gaps, states, rows):
    modes = rate.shape[0]
    total = jnp.zeros_like(rate)
    for k in range(states.shape[0] // modes):
        weight = jnp.exp(-rate * (jnp.maximum(gaps[k], 0.0) * float(rows)))
        total = total + jnp.where(gaps[k] >= 0.0, weight * states[k * modes : (k + 1) * modes], 0.0)
    return total


def long_body(gaps, inner, query, rate, coef, states, li_out, mixed):
    rows = inner.shape[0]
    entering = gather_states(rate[...], gaps, states, rows)
    total = inner[...] + spread_modes(rate[...], coef[...] * entering, rows, 1.0, False)
    li_out[...] = total
    mixed[...] = (query[...].astype(F32) * total).astype(BF16)


def split_body(count, starts, *rest):
    pieces, parts, whole = rest[: -count - 1], rest[-count - 1 : -1], rest[-1]
    for r, piece in enumerate(pieces):
        whole[:, pl.ds(pl.multiple_of(starts[r], 128), piece.shape[1])] = piece[...]
    for h, part in enumerate(parts):
        place = pl.multiple_of(starts[len(pieces) + h], 128)
        part[...] = whole[:, pl.ds(place, part.shape[1])]


def pair_grad_body(count, starts, *rest):
    parts, weights, (own, *others) = rest[:count], rest[count : count + 6], rest[count + 6 :]
    for part, result in zip(parts, (own, *others)):
        total = None
        for m, weight in enumerate(weights):
            block = part[:, pl.ds(pl.multiple_of(starts[m], 128), weight.shape[0])]
            found = jnp.dot(block, weight[...], preferred_element_type=F32)
            total = found if total is None else total + found
        result[...] = total.astype(result.dtype)


def pair_out_body(count, starts, *rest):
    mixed, weights, results = rest[:count], rest[count : count + 6], rest[count + 6 :]
    for rows, result in zip(mixed, results):
        for m, weight in enumerate(weights):
            found = lax.dot_general(rows[...], weight[...], (((1,), (1,)), ((), ())), preferred_element_type=F32)
            result[:, pl.ds(pl.multiple_of(starts[m], 128), weight.shape[0])] = found.astype(BF16)


def stack_body(count, starts, *rest):
    pieces, stacks, whole = rest[:-3], rest[-3:-1], rest[-1]
    rows = whole.shape[0]
    for r, piece in enumerate(pieces):
        whole[:, pl.ds(pl.multiple_of(starts[r], 128), piece.shape[1])] = piece[...]
    for h in range(count):
        place = pl.multiple_of(starts[len(pieces) + h], 128)
        stack, at = stacks[h // (count // 2)], h % (count // 2)
        stack[at * rows : (at + 1) * rows] = whole[:, pl.ds(place, stack.shape[1])]


def grad_gate_body(count, own, query, rate, li_out, *rest):
    parts, (grad_query, grad_out, ends) = rest[:count], rest[count:]
    total = own[...]
    for part in parts:
        total = total + part[...].astype(F32)
    grad_query[...] = total * li_out[...]
    gated = total * query[...].astype(F32)
    grad_out[...] = gated
    ends[...] = fold_modes(gated, rate[...], True)


def grad_inner_body(grad_out, li_spec, ahead, back, inner):
    rows = grad_out.shape[0]
    inner[...] = apply3(back[:rows], times_conj(to_spectrum(ahead[...], grad_out[...]), li_spec[...]))


def grad_long_body(
    inner, rate, coef, entering, mixed_mr, key_li, query_mr, conv, spec, ahead, lags,
    grad_key_li, grad_query_mr, grad_spec, taps,
):
    rows = inner.shape[0]
    grad_input = inner[...] + spread_modes(rate[...], coef[...] * entering[...], rows, 1.0, True)
    grad_key_li[...] = grad_input * mixed_mr[...].astype(F32)
    grad_mixed_mr = grad_input * key_li[...].astype(F32)
    grad_query_mr[...] = grad_mixed_mr * conv[...]
    grad_conv = grad_mixed_mr * query_mr[...].astype(F32)
    found = to_spectrum(ahead[...], grad_conv)
    grad_spec[...] = found
    taps[...] = apply3(lags[...], times_conj(spec[...], found))


def grad_taps_body(grad_spec, mr_spec, back, own_product, prev_product):
    rows = own_product.shape[0]
    products = apply3(back[...], times_conj(grad_spec[...], mr_spec[...]))
    own_product[...] = products[:rows]
    prev_product[...] = products[rows:].astype(BF16)


def grad_product_body(own, arrived, key, value, grad_key, grad_value):
    total = own[...] + arrived[...].astype(F32)
    grad_key[...] = total * value[...].astype(F32)
    grad_value[...] = total * key[...].astype(F32)


def run(body, columns, inputs, outputs, flops):
    tile = min(TILE, columns)
    in_specs = []
    moved = 0
    for kind, array in inputs:
        if kind == "tile":
            in_specs.append(pl.BlockSpec((array.shape[0], tile), lambda c: (0, c)))
        elif kind == "whole":
            in_specs.append(pl.BlockSpec(array.shape, lambda c: (0, 0)))
        else:
            in_specs.append(pl.BlockSpec(memory_space=pltpu.SMEM))
        moved += math.prod(array.shape) * array.dtype.itemsize
    for rows, dtype in outputs:
        moved += rows * columns * jnp.dtype(dtype).itemsize
    return pl.pallas_call(
        body,
        grid=(columns // tile,),
        in_specs=in_specs,
        out_specs=[pl.BlockSpec((rows, tile), lambda c: (0, c)) for rows, _ in outputs],
        out_shape=[jax.ShapeDtypeStruct((rows, columns), dtype) for rows, dtype in outputs],
        compiler_params=pltpu.CompilerParams(vmem_limit_bytes=12 * 1024 * 1024),
        cost_estimate=pl.CostEstimate(flops=flops, bytes_accessed=moved if flops else 0, transcendentals=0),
    )(*[array for _, array in inputs])


def run_once(body, inputs, outputs, scratch=()):
    def block(shape):
        return pl.BlockSpec(shape, lambda c: (0, 0))

    return pl.pallas_call(
        body,
        grid=(1,),
        in_specs=[pl.BlockSpec(memory_space=pltpu.SMEM)] + [block(array.shape) for array in inputs[1:]],
        out_specs=[block(shape) for shape, _ in outputs],
        out_shape=[jax.ShapeDtypeStruct(shape, dtype) for shape, dtype in outputs],
        scratch_shapes=scratch,
        compiler_params=pltpu.CompilerParams(vmem_limit_bytes=20 * 1024 * 1024),
        cost_estimate=pl.CostEstimate(flops=0, bytes_accessed=0, transcendentals=0),
    )(*inputs)


def chip_swap(x, by):
    size = lax.axis_size("ctx")
    return lax.ppermute(x, "ctx", [(i, i ^ (2 * by)) for i in range(size)])


def line_swap(x, by):
    size = lax.axis_size("fsdp")
    return lax.ppermute(x, "fsdp", [(i, i ^ by) for i in range(size)])


def core_swap(x):
    size = lax.axis_size("ctx")
    return lax.ppermute(x, "ctx", [(i, i ^ 1) for i in range(size)])


def shifted(x, by):
    size = lax.axis_size("ctx")
    return lax.ppermute(x, "ctx", [(i, i + by) for i in range(size) if 0 <= i + by < size])


def bit_reversed(count):
    order = [0]
    while len(order) < count:
        order = [2 * k for k in order] + [2 * k + 1 for k in order]
    return order


def columns_at(x, index, width):
    return lax.dynamic_slice_in_dim(x, index * width, width, 1)


def placed(pieces):
    width = pieces[0][1].shape[1]
    whole = jnp.zeros((pieces[0][1].shape[0], width * len(pieces)), pieces[0][1].dtype)
    for index, piece in pieces:
        whole = lax.dynamic_update_slice_in_dim(whole, piece, index * width, 1)
    return whole


def pair_sum(values):
    while len(values) > 1:
        values = [values[k] + values[k + 1] for k in range(0, len(values), 2)]
    return values[0]


def after(x, *others):
    return lax.optimization_barrier((x,) + others)[0]


def direct_factors(rate, rows, chip, backward):
    factors = [jnp.exp(-rate * float(rows))]
    for s in range(1, lax.axis_size("ctx") // 2):
        gap = (chip ^ s) - chip - 1 if backward else chip - (chip ^ s) - 1
        weight = jnp.exp(-rate * (2 * rows * jnp.maximum(gap, 0)).astype(F32))
        factors.append(jnp.where(gap >= 0, weight, 0.0))
    return factors


def entering_direct(ends, factors, here, backward, ready):
    block = factors[0]
    later_core = ((here & 1) != 0) != backward
    sibling = core_swap(ends)
    total = jnp.where(later_core, block * sibling + ends, block * ends + sibling)
    total = after(total, *ready)
    entering = jnp.zeros_like(ends)
    for s, weight in enumerate(factors[1:], 1):
        entering = entering + weight * chip_swap(total, s)
    return jnp.where(later_core, block * entering + sibling, entering)


def shards(
    query_mr,
    key_mr,
    value_mr,
    query_li,
    key_li,
    mr_taps,
    li_time,
    li_residue,
    li_skip,
    out_weight,
    cotangent,
):
    rows, columns = query_mr.shape
    ctx_count = lax.axis_size("ctx")
    line_count = lax.axis_size("fsdp")
    chips = ctx_count // 2
    here = lax.axis_index("ctx")
    chip, core = here // 2, here % 2
    line = lax.axis_index("fsdp")
    grad_scale = 1.0 / math.sqrt(rows * ctx_count)
    tables = {name: jnp.asarray(table) for name, table in dft_tables(rows).items()}
    width = out_weight.shape[0]
    chip_width = 2 * width
    pass_flops = 2 * (2 * rows) * (2 * rows) * columns

    def tile(x):
        return ("tile", x)

    def table(name):
        return ("whole", tables[name])

    mr_product = (key_mr.astype(F32) * value_mr.astype(F32)).astype(BF16)
    before = shifted(mr_product, 1)
    def line_go(numbers, *ready):
        return [line_swap(after(cotangent, *ready), r) for r in numbers]

    half = width // 2
    first_go = line_go(range(1, 2), mr_product)
    second_go = line_go(range(2, line_count), mr_product)
    pairs = chips // 2
    pair = chip // 2
    pair_width = 4 * width

    rate = 1.0 / after(li_time, mr_product)
    coef = li_residue * jnp.sqrt(-jnp.expm1(-2.0 * rate))
    back_factors = lax.optimization_barrier(direct_factors(rate, rows, here // 2, True))
    mr_spec, li_spec = run(
        spectra_body,
        columns,
        [tile(mr_taps), tile(rate), tile(coef), tile(li_skip[None, :]), table("ahead")],
        [(2 * rows, F32), (2 * rows, F32)],
        0,
    )
    first_rows = chip_swap(after(out_weight[:half], mr_spec), 1)
    spec, mr_conv, mixed_mr, li_input, ends = run(
        short_body,
        columns,
        [
            tile(after(before, *first_go)),
            tile(mr_product),
            tile(query_mr),
            tile(key_li),
            tile(mr_spec),
            tile(rate),
            table("ahead"),
            table("back"),
        ],
        [(2 * rows, F32), (rows, F32), (rows, BF16), (rows, BF16), (rate.shape[0], F32)],
        0,
    )

    cot_line = [cotangent] + first_go + second_go
    line_width = cotangent.shape[1]
    whole_width = line_width * line_count
    split_starts = [(line ^ r) * line_width for r in range(line_count)]
    split_starts += [(pair ^ h) * pair_width for h in range(pairs)]
    cot_pairs = run_once(
        functools.partial(split_body, pairs),
        [jnp.stack(split_starts)] + [after(piece, ends) for piece in cot_line],
        [((rows, pair_width), BF16)] * pairs,
        [pltpu.VMEM((rows, whole_width), BF16)],
    )
    cot_parts = [cot_pairs[0]] + [chip_swap(cot_pairs[h], 2 * h) for h in range(1, pairs)]
    second_rows = chip_swap(after(out_weight[half:], ends, first_rows), 1)
    states = lax.all_gather(after(ends, first_rows, *cot_parts[:1]), "ctx").reshape(-1, columns)
    gaps = (here - 1 - jnp.arange(ctx_count, dtype=jnp.int32)).astype(F32)
    (li_inner,) = run(
        inner_body,
        columns,
        [tile(li_input), tile(li_spec), table("ahead"), table("back")],
        [(rows, F32)],
        0,
    )
    li_out, mixed_li = run(
        long_body,
        columns,
        [("scalar", gaps), tile(after(li_inner, second_rows)), tile(query_li), tile(rate), tile(coef), tile(states)],
        [(rows, F32), (rows, BF16)],
        0,
    )

    beside = [first_rows, second_rows]
    mixed_parts = [mixed_li] + [chip_swap(mixed_li, 2 * h) for h in range(1, pairs)]
    weights = [out_weight, core_swap(out_weight)] + beside + [core_swap(piece) for piece in beside]
    places = [(0, 0), (1, 0), (2, 0), (2, half), (3, 0), (3, half)]
    pair_starts = jnp.stack([((here & 3) ^ m) * width + row for m, row in places])

    share_flops = 2 * rows * columns * pair_width * pairs
    grad_own, *grad_sent = run(
        functools.partial(pair_grad_body, pairs),
        columns,
        [("scalar", pair_starts)] + [("whole", after(part, mixed_li)) for part in cot_parts] + [tile(weight) for weight in weights],
        [(rows, F32)] + [(rows, BF16)] * (pairs - 1),
        share_flops,
    )
    grad_parts = [chip_swap(after(part, *mixed_parts[1:]), 2 * h) for h, part in enumerate(grad_sent, 1)]

    out_own, *out_sent = run_once(
        functools.partial(pair_out_body, pairs),
        [pair_starts, after(mixed_parts[0], grad_own)] + mixed_parts[1:] + weights,
        [((rows, pair_width), BF16)] * pairs,
    )
    out_pairs = [out_own] + [chip_swap(part, 2 * h) for h, part in enumerate(out_sent, 1)]
    out_starts = [(pair ^ h) * pair_width for h in range(pairs)]
    out_starts += [(line ^ r) * line_width for r in bit_reversed(line_count)]
    kept, odd = run_once(
        functools.partial(stack_body, line_count),
        [jnp.stack(out_starts)] + out_pairs,
        [((line_count // 2 * rows, line_width), BF16)] * 2,
        [pltpu.VMEM((rows, whole_width), BF16)],
    )
    count, by = line_count // 2, 1
    first_out = arrived_out = line_swap(odd, by)
    while count > 1:
        count //= 2
        by *= 2
        total = kept.astype(F32) + arrived_out.astype(F32)
        kept, arrived_out = total[: count * rows], line_swap(total[count * rows :].astype(BF16), by)
    output = kept.astype(F32) + arrived_out.astype(F32)

    side = chip % 2
    near_cot = jnp.concatenate([columns_at(part, side, chip_width) for part in cot_parts], axis=0)
    far_cot = jnp.concatenate([columns_at(part, 1 - side, chip_width) for part in cot_parts], axis=0)
    got_cot = chip_swap(far_cot, 1)
    near_mixed = jnp.concatenate([after(part, grad_own) for part in mixed_parts], axis=0)
    got_mixed = chip_swap(after(near_mixed, got_cot, grad_own), 1)

    grad_query_li, grad_li_out, back_ends = run(
        functools.partial(grad_gate_body, pairs - 1),
        columns,
        [tile(after(grad_own, out_own)), tile(query_li), tile(rate), tile(li_out)] + [tile(part) for part in grad_parts],
        [(rows, F32), (rows, F32), (rate.shape[0], F32)],
        pass_flops,
    )
    (grad_inner,) = run(
        grad_inner_body,
        columns,
        [tile(after(grad_li_out, got_cot)), tile(li_spec), table("ahead"), table("back")],
        [(rows, F32)],
        3 * pass_flops,
    )
    back_entering = entering_direct(
        after(back_ends, grad_inner), back_factors, here, True, [got_mixed] + out_pairs[1:]
    )
    cot_rows = jnp.concatenate([near_cot, got_cot], axis=0)
    mixed_rows = jnp.concatenate([near_mixed, got_mixed], axis=0)

    def weight_share(which):
        return lax.dot_general(
            columns_at(cot_rows, which, width),
            mixed_rows,
            (((0,), (0,)), ((), ())),
            preferred_element_type=F32,
        )

    sent_share = weight_share(1 - core).astype(BF16)
    far_share = core_swap(sent_share)
    grad_weight = (weight_share(core) + far_share.astype(F32)) * grad_scale
    grad_key_li, grad_query_mr, grad_spec, tap_partial = run(
        grad_long_body,
        columns,
        [
            tile(after(grad_inner, sent_share)),
            tile(rate),
            tile(coef),
            tile(back_entering),
            tile(mixed_mr),
            tile(key_li),
            tile(query_mr),
            tile(mr_conv),
            tile(spec),
            table("ahead"),
            table("lags"),
        ],
        [(rows, F32), (rows, F32), (2 * rows, F32), (rows, F32)],
        4 * pass_flops,
    )
    grad_spec = after(grad_spec, first_out)
    own_product, prev_product = run(
        grad_taps_body,
        columns,
        [tile(grad_spec), tile(mr_spec), table("back")],
        [(rows, F32), (rows, BF16)],
        3 * pass_flops,
    )
    arrived = shifted(prev_product, -1)
    grad_key_mr, grad_value_mr = run(
        grad_product_body,
        columns,
        [tile(own_product), tile(arrived), tile(key_mr), tile(value_mr)],
        [(rows, F32), (rows, F32)],
        rows * columns,
    )

    tap_half = tap_partial.shape[0] // 2
    halves = tap_partial.reshape(2, tap_half, columns)
    own_half = lax.dynamic_index_in_dim(halves, core, 0, keepdims=False)
    far_half = lax.dynamic_index_in_dim(halves, 1 - core, 0, keepdims=False)
    chip_half = (own_half + core_swap(far_half)).astype(BF16)
    everywhere = [after(chip_half, prev_product, grad_weight)] + [chip_swap(chip_half, s) for s in range(1, chips)]
    plane_half = pair_sum([part.astype(F32) for part in everywhere]) * grad_scale
    other_half = core_swap(after(plane_half, arrived_out))
    grad_taps = jnp.where(
        core == 0,
        jnp.concatenate([plane_half, other_half], axis=0),
        jnp.concatenate([other_half, plane_half], axis=0),
    )

    return (
        output,
        grad_query_mr,
        grad_key_mr,
        grad_value_mr,
        grad_query_li,
        grad_key_li,
        grad_taps,
        grad_weight,
    )


def solution(mesh):
    rows = P("ctx", "fsdp")
    channels = P(None, "fsdp")
    return jax.shard_map(
        shards,
        mesh=mesh,
        in_specs=(rows,) * 5 + (channels,) * 3 + (P("fsdp"),) + (rows,) * 2,
        out_specs=(rows,) * 6 + (channels, rows),
        check_vma=False,
    )
```

```python
import functools
import math

import jax
import jax.numpy as jnp
import ml_dtypes
import numpy as np
from jax import lax
from jax.experimental import pallas as pl
from jax.experimental.pallas import tpu as pltpu
from jax.sharding import PartitionSpec as P

F32 = jnp.float32
BF16 = jnp.bfloat16
TILE = 256
GROUP = 8


def split_parts(matrix):
    high = matrix.astype(ml_dtypes.bfloat16)
    low = (matrix - high.astype(np.float64)).astype(ml_dtypes.bfloat16)
    return high, low


def two_fold(matrix):
    high, low = split_parts(matrix)
    return np.concatenate([high, low], axis=1)


def three_fold(matrix):
    high, low = split_parts(matrix)
    return np.concatenate([high, low, high], axis=1)


@functools.lru_cache(maxsize=None)
def dft_tables(rows):
    size = 2 * rows
    angle = 2.0 * np.pi * (np.arange(rows)[:, None] + 0.5) * np.arange(size)[None, :] / size
    ahead = np.concatenate([np.cos(angle), -np.sin(angle)], axis=0)
    back = ahead.T * (2.0 / size)
    signed = np.concatenate([back[:rows], -back[rows:]], axis=0)
    lags = back[rows - np.arange(rows)]
    return {"ahead": two_fold(ahead), "back": three_fold(signed), "lags": three_fold(lags)}


def half_table(ahead):
    rows = ahead.shape[0] // 2
    high, low = ahead[:, :rows], ahead[:, 2 * rows : 3 * rows]
    return high, low


def apply2(table, x):
    return jnp.dot(table, jnp.concatenate([x, x], axis=0), preferred_element_type=F32)


def apply3(table, x):
    high = x.astype(BF16)
    low = (x - high.astype(F32)).astype(BF16)
    return jnp.dot(table, jnp.concatenate([high, high, low], axis=0), preferred_element_type=F32)


def to_spectrum(ahead, x):
    high, low = half_table(ahead)
    return apply3(jnp.concatenate([high, low, high], axis=1), x)


def to_spectrum_exact(ahead, x):
    return apply2(jnp.concatenate(half_table(ahead), axis=1), x)


def times(x, y):
    half = x.shape[0] // 2
    xr, xi, yr, yi = x[:half], x[half:], y[:half], y[half:]
    return jnp.concatenate([xr * yr - xi * yi, xr * yi + xi * yr], axis=0)


def times_conj(x, y):
    half = x.shape[0] // 2
    xr, xi, yr, yi = x[:half], x[half:], y[:half], y[half:]
    return jnp.concatenate([xr * yr + xi * yi, xi * yr - xr * yi], axis=0)


def group_places(columns):
    return lax.broadcasted_iota(jnp.int32, (GROUP, columns), 0).astype(F32)


def spread_modes(rate, weight, rows, shift, backward):
    columns = rate.shape[1]
    places = group_places(columns)
    if backward:
        places = (GROUP - 1.0) - places
    count = rows // GROUP
    order = range(count - 1, -1, -1) if backward else range(count)
    sums = [None] * count
    for m in range(rate.shape[0]):
        rate_m = rate[m : m + 1]
        current = weight[m : m + 1] * jnp.exp(-rate_m * (places + shift))
        stride = jnp.broadcast_to(jnp.exp(-rate_m * GROUP), current.shape)
        for step, g in enumerate(order):
            sums[g] = current if sums[g] is None else sums[g] + current
            if step < count - 1:
                current = current * stride
    return jnp.concatenate(sums, axis=0)


def fold_modes(signal, rate, backward):
    columns = rate.shape[1]
    places = group_places(columns)
    if not backward:
        places = (GROUP - 1.0) - places
    count = signal.shape[0] // GROUP
    order = range(count - 1, -1, -1) if backward else range(count)
    found = []
    for m in range(rate.shape[0]):
        rate_m = rate[m : m + 1]
        stride = jnp.broadcast_to(jnp.exp(-rate_m * GROUP), (GROUP, columns))
        running = None
        for g in order:
            piece = signal[g * GROUP : (g + 1) * GROUP]
            running = piece if running is None else running * stride + piece
        found.append(jnp.sum(running * jnp.exp(-rate_m * places), axis=0, keepdims=True))
    return jnp.concatenate(found, axis=0)


def spectra_body(taps, rate, coef, skip, ahead, mr_spec, li_spec):
    rows = taps.shape[0]
    table = ahead[...]
    mr_spec[...] = to_spectrum(table, taps[...])
    kernel = spread_modes(rate[...], coef[...], rows, 0.0, False)
    first = lax.broadcasted_iota(jnp.int32, kernel.shape, 0) == 0
    kernel = kernel + jnp.where(first, skip[...], 0.0)
    li_spec[...] = to_spectrum(table, kernel)


def short_body(before, product, query, key, mr_spec, rate, ahead, back, spec, conv, mixed, signal, ends):
    rows = product.shape[0]
    x = jnp.concatenate([before[...], product[...]], axis=0)
    found = apply2(ahead[...], x)
    spec[...] = found
    filtered = -apply3(back[rows:], times(found, mr_spec[...]))
    conv[...] = filtered
    mixed_rows = (query[...].astype(F32) * filtered).astype(BF16)
    mixed[...] = mixed_rows
    rounded = (key[...].astype(F32) * mixed_rows.astype(F32)).astype(BF16)
    signal[...] = rounded
    ends[...] = fold_modes(rounded.astype(F32), rate[...], False)


def inner_body(signal, li_spec, ahead, back, inner):
    rows = signal.shape[0]
    inner[...] = apply3(back[:rows], times(to_spectrum_exact(ahead[...], signal[...]), li_spec[...]))


def gather_states(rate, gaps, states, rows):
    modes = rate.shape[0]
    total = jnp.zeros_like(rate)
    for k in range(states.shape[0] // modes):
        weight = jnp.exp(-rate * (jnp.maximum(gaps[k], 0.0) * float(rows)))
        total = total + jnp.where(gaps[k] >= 0.0, weight * states[k * modes : (k + 1) * modes], 0.0)
    return total


def long_body(gaps, inner, query, rate, coef, states, li_out, mixed):
    rows = inner.shape[0]
    entering = gather_states(rate[...], gaps, states, rows)
    total = inner[...] + spread_modes(rate[...], coef[...] * entering, rows, 1.0, False)
    li_out[...] = total
    mixed[...] = (query[...].astype(F32) * total).astype(BF16)


def split_body(count, starts, *rest):
    pieces, parts, whole = rest[: -count - 1], rest[-count - 1 : -1], rest[-1]
    for r, piece in enumerate(pieces):
        whole[:, pl.ds(pl.multiple_of(starts[r], 128), piece.shape[1])] = piece[...]
    for h, part in enumerate(parts):
        place = pl.multiple_of(starts[len(pieces) + h], 128)
        part[...] = whole[:, pl.ds(place, part.shape[1])]


def pair_grad_body(count, starts, *rest):
    parts, weights, (own, *others) = rest[:count], rest[count : count + 4], rest[count + 4 :]
    for part, result in zip(parts, (own, *others)):
        total = None
        for m, weight in enumerate(weights):
            block = part[:, pl.ds(pl.multiple_of(starts[m], 128), weight.shape[0])]
            found = jnp.dot(block, weight[...], preferred_element_type=F32)
            total = found if total is None else total + found
        result[...] = total.astype(result.dtype)


def pair_out_body(count, starts, *rest):
    mixed, weights, results = rest[:count], rest[count : count + 4], rest[count + 4 :]
    for rows, result in zip(mixed, results):
        for m, weight in enumerate(weights):
            found = lax.dot_general(rows[...], weight[...], (((1,), (1,)), ((), ())), preferred_element_type=F32)
            result[:, pl.ds(pl.multiple_of(starts[m], 128), weight.shape[0])] = found.astype(BF16)


def stack_body(count, starts, *rest):
    pieces, stacks, whole = rest[:-3], rest[-3:-1], rest[-1]
    rows = whole.shape[0]
    for r, piece in enumerate(pieces):
        whole[:, pl.ds(pl.multiple_of(starts[r], 128), piece.shape[1])] = piece[...]
    for h in range(count):
        place = pl.multiple_of(starts[len(pieces) + h], 128)
        stack, at = stacks[h // (count // 2)], h % (count // 2)
        stack[at * rows : (at + 1) * rows] = whole[:, pl.ds(place, stack.shape[1])]


def grad_gate_body(count, own, query, rate, li_out, *rest):
    parts, (grad_query, grad_out, ends) = rest[:count], rest[count:]
    total = own[...]
    for part in parts:
        total = total + part[...].astype(F32)
    grad_query[...] = total * li_out[...]
    gated = total * query[...].astype(F32)
    grad_out[...] = gated
    ends[...] = fold_modes(gated, rate[...], True)


def grad_inner_body(grad_out, li_spec, ahead, back, inner):
    rows = grad_out.shape[0]
    inner[...] = apply3(back[:rows], times_conj(to_spectrum(ahead[...], grad_out[...]), li_spec[...]))


def grad_long_body(
    inner, rate, coef, entering, mixed_mr, key_li, query_mr, conv, spec, ahead, lags,
    grad_key_li, grad_query_mr, grad_spec, taps,
):
    rows = inner.shape[0]
    grad_input = inner[...] + spread_modes(rate[...], coef[...] * entering[...], rows, 1.0, True)
    grad_key_li[...] = grad_input * mixed_mr[...].astype(F32)
    grad_mixed_mr = grad_input * key_li[...].astype(F32)
    grad_query_mr[...] = grad_mixed_mr * conv[...]
    grad_conv = grad_mixed_mr * query_mr[...].astype(F32)
    found = to_spectrum(ahead[...], grad_conv)
    grad_spec[...] = found
    taps[...] = apply3(lags[...], times_conj(spec[...], found))


def grad_taps_body(grad_spec, mr_spec, back, own_product, prev_product):
    rows = own_product.shape[0]
    products = apply3(back[...], times_conj(grad_spec[...], mr_spec[...]))
    own_product[...] = products[:rows]
    prev_product[...] = products[rows:].astype(BF16)


def grad_product_body(own, arrived, key, value, grad_key, grad_value):
    total = own[...] + arrived[...].astype(F32)
    grad_key[...] = total * value[...].astype(F32)
    grad_value[...] = total * key[...].astype(F32)


def run(body, columns, inputs, outputs, flops):
    tile = min(TILE, columns)
    in_specs = []
    moved = 0
    for kind, array in inputs:
        if kind == "tile":
            in_specs.append(pl.BlockSpec((array.shape[0], tile), lambda c: (0, c)))
        elif kind == "whole":
            in_specs.append(pl.BlockSpec(array.shape, lambda c: (0, 0)))
        else:
            in_specs.append(pl.BlockSpec(memory_space=pltpu.SMEM))
        moved += math.prod(array.shape) * array.dtype.itemsize
    for rows, dtype in outputs:
        moved += rows * columns * jnp.dtype(dtype).itemsize
    return pl.pallas_call(
        body,
        grid=(columns // tile,),
        in_specs=in_specs,
        out_specs=[pl.BlockSpec((rows, tile), lambda c: (0, c)) for rows, _ in outputs],
        out_shape=[jax.ShapeDtypeStruct((rows, columns), dtype) for rows, dtype in outputs],
        compiler_params=pltpu.CompilerParams(vmem_limit_bytes=12 * 1024 * 1024),
        cost_estimate=pl.CostEstimate(flops=flops, bytes_accessed=moved if flops else 0, transcendentals=0),
    )(*[array for _, array in inputs])


def run_once(body, inputs, outputs, scratch=()):
    def block(shape):
        return pl.BlockSpec(shape, lambda c: (0, 0))

    return pl.pallas_call(
        body,
        grid=(1,),
        in_specs=[pl.BlockSpec(memory_space=pltpu.SMEM)] + [block(array.shape) for array in inputs[1:]],
        out_specs=[block(shape) for shape, _ in outputs],
        out_shape=[jax.ShapeDtypeStruct(shape, dtype) for shape, dtype in outputs],
        scratch_shapes=scratch,
        compiler_params=pltpu.CompilerParams(vmem_limit_bytes=20 * 1024 * 1024),
        cost_estimate=pl.CostEstimate(flops=0, bytes_accessed=0, transcendentals=0),
    )(*inputs)


def chip_swap(x, by):
    size = lax.axis_size("ctx")
    return lax.ppermute(x, "ctx", [(i, i ^ (2 * by)) for i in range(size)])


def line_swap(x, by):
    size = lax.axis_size("fsdp")
    return lax.ppermute(x, "fsdp", [(i, i ^ by) for i in range(size)])


def core_swap(x):
    size = lax.axis_size("ctx")
    return lax.ppermute(x, "ctx", [(i, i ^ 1) for i in range(size)])


def shifted(x, by):
    size = lax.axis_size("ctx")
    return lax.ppermute(x, "ctx", [(i, i + by) for i in range(size) if 0 <= i + by < size])


def bit_reversed(count):
    order = [0]
    while len(order) < count:
        order = [2 * k for k in order] + [2 * k + 1 for k in order]
    return order


def columns_at(x, index, width):
    return lax.dynamic_slice_in_dim(x, index * width, width, 1)


def placed(pieces):
    width = pieces[0][1].shape[1]
    whole = jnp.zeros((pieces[0][1].shape[0], width * len(pieces)), pieces[0][1].dtype)
    for index, piece in pieces:
        whole = lax.dynamic_update_slice_in_dim(whole, piece, index * width, 1)
    return whole


def pair_sum(values):
    while len(values) > 1:
        values = [values[k] + values[k + 1] for k in range(0, len(values), 2)]
    return values[0]


def after(x, *others):
    return lax.optimization_barrier((x,) + others)[0]


def direct_factors(rate, rows, chip, backward):
    factors = [jnp.exp(-rate * float(rows))]
    for s in range(1, lax.axis_size("ctx") // 2):
        gap = (chip ^ s) - chip - 1 if backward else chip - (chip ^ s) - 1
        weight = jnp.exp(-rate * (2 * rows * jnp.maximum(gap, 0)).astype(F32))
        factors.append(jnp.where(gap >= 0, weight, 0.0))
    return factors


def entering_direct(ends, factors, here, backward, ready):
    block = factors[0]
    later_core = ((here & 1) != 0) != backward
    sibling = core_swap(ends)
    total = jnp.where(later_core, block * sibling + ends, block * ends + sibling)
    total = after(total, *ready)
    entering = jnp.zeros_like(ends)
    for s, weight in enumerate(factors[1:], 1):
        entering = entering + weight * chip_swap(total, s)
    return jnp.where(later_core, block * entering + sibling, entering)


def shards(
    query_mr,
    key_mr,
    value_mr,
    query_li,
    key_li,
    mr_taps,
    li_time,
    li_residue,
    li_skip,
    out_weight,
    cotangent,
):
    rows, columns = query_mr.shape
    ctx_count = lax.axis_size("ctx")
    line_count = lax.axis_size("fsdp")
    chips = ctx_count // 2
    here = lax.axis_index("ctx")
    chip, core = here // 2, here % 2
    line = lax.axis_index("fsdp")
    grad_scale = 1.0 / math.sqrt(rows * ctx_count)
    tables = {name: jnp.asarray(table) for name, table in dft_tables(rows).items()}
    width = out_weight.shape[0]
    chip_width = 2 * width
    pass_flops = 2 * (2 * rows) * (2 * rows) * columns

    def tile(x):
        return ("tile", x)

    def table(name):
        return ("whole", tables[name])

    mr_product = (key_mr.astype(F32) * value_mr.astype(F32)).astype(BF16)
    before = shifted(mr_product, 1)
    cot_line = [cotangent] + [line_swap(after(cotangent, mr_product), r) for r in range(1, line_count)]
    beside = chip_swap(after(out_weight, before), 1)
    pairs = chips // 2
    pair = chip // 2
    pair_width = 4 * width

    rate = 1.0 / after(li_time, mr_product)
    coef = li_residue * jnp.sqrt(-jnp.expm1(-2.0 * rate))
    back_factors = lax.optimization_barrier(direct_factors(rate, rows, here // 2, True))
    mr_spec, li_spec = run(
        spectra_body,
        columns,
        [tile(mr_taps), tile(rate), tile(coef), tile(li_skip[None, :]), table("ahead")],
        [(2 * rows, F32), (2 * rows, F32)],
        0,
    )
    spec, mr_conv, mixed_mr, li_input, ends = run(
        short_body,
        columns,
        [
            tile(before),
            tile(mr_product),
            tile(query_mr),
            tile(key_li),
            tile(mr_spec),
            tile(rate),
            table("ahead"),
            table("back"),
        ],
        [(2 * rows, F32), (rows, F32), (rows, BF16), (rows, BF16), (rate.shape[0], F32)],
        0,
    )

    line_width = cotangent.shape[1]
    whole_width = line_width * line_count
    split_starts = [(line ^ r) * line_width for r in range(line_count)]
    split_starts += [(pair ^ h) * pair_width for h in range(pairs)]
    cot_pairs = run_once(
        functools.partial(split_body, pairs),
        [jnp.stack(split_starts)] + [after(piece, ends) for piece in cot_line],
        [((rows, pair_width), BF16)] * pairs,
        [pltpu.VMEM((rows, whole_width), BF16)],
    )
    cot_parts = [cot_pairs[0]] + [chip_swap(cot_pairs[h], 2 * h) for h in range(1, pairs)]
    states = lax.all_gather(after(ends, beside, *cot_parts[:1]), "ctx").reshape(-1, columns)
    gaps = (here - 1 - jnp.arange(ctx_count, dtype=jnp.int32)).astype(F32)
    (li_inner,) = run(
        inner_body,
        columns,
        [tile(li_input), tile(li_spec), table("ahead"), table("back")],
        [(rows, F32)],
        0,
    )
    li_out, mixed_li = run(
        long_body,
        columns,
        [("scalar", gaps), tile(li_inner), tile(query_li), tile(rate), tile(coef), tile(states)],
        [(rows, F32), (rows, BF16)],
        0,
    )

    mixed_parts = [mixed_li] + [chip_swap(mixed_li, 2 * h) for h in range(1, pairs)]
    weights = [out_weight, core_swap(out_weight), beside, core_swap(beside)]
    pair_starts = jnp.stack([((here & 3) ^ m) * width for m in range(4)])

    share_flops = 2 * rows * columns * pair_width * pairs
    grad_own, *grad_sent = run(
        functools.partial(pair_grad_body, pairs),
        columns,
        [("scalar", pair_starts)] + [("whole", after(part, mixed_li)) for part in cot_parts] + [tile(weight) for weight in weights],
        [(rows, F32)] + [(rows, BF16)] * (pairs - 1),
        share_flops,
    )
    grad_parts = [chip_swap(part, 2 * h) for h, part in enumerate(grad_sent, 1)]

    out_own, *out_sent = run_once(
        functools.partial(pair_out_body, pairs),
        [pair_starts, after(mixed_parts[0], grad_own)] + mixed_parts[1:] + weights,
        [((rows, pair_width), BF16)] * pairs,
    )
    out_pairs = [out_own] + [chip_swap(after(part, *grad_parts), 2 * h) for h, part in enumerate(out_sent, 1)]
    out_starts = [(pair ^ h) * pair_width for h in range(pairs)]
    out_starts += [(line ^ r) * line_width for r in bit_reversed(line_count)]
    kept, odd = run_once(
        functools.partial(stack_body, line_count),
        [jnp.stack(out_starts)] + out_pairs,
        [((line_count // 2 * rows, line_width), BF16)] * 2,
        [pltpu.VMEM((rows, whole_width), BF16)],
    )
    count, by = line_count // 2, 1
    first_out = arrived_out = line_swap(odd, by)
    while count > 1:
        count //= 2
        by *= 2
        total = kept.astype(F32) + arrived_out.astype(F32)
        kept, arrived_out = total[: count * rows], line_swap(total[count * rows :].astype(BF16), by)
    output = kept.astype(F32) + arrived_out.astype(F32)

    side = chip % 2
    near_cot = jnp.concatenate([columns_at(part, side, chip_width) for part in cot_parts], axis=0)
    far_cot = jnp.concatenate([columns_at(part, 1 - side, chip_width) for part in cot_parts], axis=0)
    got_cot = chip_swap(far_cot, 1)
    near_mixed = jnp.concatenate([after(part, grad_own) for part in mixed_parts], axis=0)
    got_mixed = chip_swap(after(near_mixed, got_cot, grad_own), 1)

    grad_query_li, grad_li_out, back_ends = run(
        functools.partial(grad_gate_body, pairs - 1),
        columns,
        [tile(after(grad_own, out_own)), tile(query_li), tile(rate), tile(li_out)] + [tile(part) for part in grad_parts],
        [(rows, F32), (rows, F32), (rate.shape[0], F32)],
        pass_flops,
    )
    (grad_inner,) = run(
        grad_inner_body,
        columns,
        [tile(after(grad_li_out, got_cot)), tile(li_spec), table("ahead"), table("back")],
        [(rows, F32)],
        3 * pass_flops,
    )
    back_entering = entering_direct(
        after(back_ends, grad_inner), back_factors, here, True, [got_mixed] + out_pairs[1:]
    )
    cot_rows = jnp.concatenate([near_cot, got_cot], axis=0)
    mixed_rows = jnp.concatenate([near_mixed, got_mixed], axis=0)

    def weight_share(which):
        return lax.dot_general(
            columns_at(cot_rows, which, width),
            mixed_rows,
            (((0,), (0,)), ((), ())),
            preferred_element_type=F32,
        )

    sent_share = weight_share(1 - core).astype(BF16)
    far_share = core_swap(sent_share)
    grad_weight = (weight_share(core) + far_share.astype(F32)) * grad_scale
    grad_key_li, grad_query_mr, grad_spec, tap_partial = run(
        grad_long_body,
        columns,
        [
            tile(after(grad_inner, sent_share)),
            tile(rate),
            tile(coef),
            tile(back_entering),
            tile(mixed_mr),
            tile(key_li),
            tile(query_mr),
            tile(mr_conv),
            tile(spec),
            table("ahead"),
            table("lags"),
        ],
        [(rows, F32), (rows, F32), (2 * rows, F32), (rows, F32)],
        4 * pass_flops,
    )
    grad_spec = after(grad_spec, first_out)
    own_product, prev_product = run(
        grad_taps_body,
        columns,
        [tile(grad_spec), tile(mr_spec), table("back")],
        [(rows, F32), (rows, BF16)],
        3 * pass_flops,
    )
    arrived = shifted(prev_product, -1)
    grad_key_mr, grad_value_mr = run(
        grad_product_body,
        columns,
        [tile(own_product), tile(arrived), tile(key_mr), tile(value_mr)],
        [(rows, F32), (rows, F32)],
        rows * columns,
    )

    tap_half = tap_partial.shape[0] // 2
    halves = tap_partial.reshape(2, tap_half, columns)
    own_half = lax.dynamic_index_in_dim(halves, core, 0, keepdims=False)
    far_half = lax.dynamic_index_in_dim(halves, 1 - core, 0, keepdims=False)
    chip_half = (own_half + core_swap(far_half)).astype(BF16)
    everywhere = [after(chip_half, prev_product, grad_weight)] + [chip_swap(chip_half, s) for s in range(1, chips)]
    plane_half = pair_sum([part.astype(F32) for part in everywhere]) * grad_scale
    other_half = core_swap(after(plane_half, arrived_out))
    grad_taps = jnp.where(
        core == 0,
        jnp.concatenate([plane_half, other_half], axis=0),
        jnp.concatenate([other_half, plane_half], axis=0),
    )

    return (
        output,
        grad_query_mr,
        grad_key_mr,
        grad_value_mr,
        grad_query_li,
        grad_key_li,
        grad_taps,
        grad_weight,
    )


def solution(mesh):
    rows = P("ctx", "fsdp")
    channels = P(None, "fsdp")
    return jax.shard_map(
        shards,
        mesh=mesh,
        in_specs=(rows,) * 5 + (channels,) * 3 + (P("fsdp"),) + (rows,) * 2,
        out_specs=(rows,) * 6 + (channels, rows),
        check_vma=False,
    )
```

```python
import functools
import math

import jax
import jax.numpy as jnp
import ml_dtypes
import numpy as np
from jax import lax
from jax.experimental import pallas as pl
from jax.experimental.pallas import tpu as pltpu
from jax.sharding import PartitionSpec as P

F32 = jnp.float32
BF16 = jnp.bfloat16
TILE = 256
GROUP = 8


def split_parts(matrix):
    high = matrix.astype(ml_dtypes.bfloat16)
    low = (matrix - high.astype(np.float64)).astype(ml_dtypes.bfloat16)
    return high, low


def two_fold(matrix):
    high, low = split_parts(matrix)
    return np.concatenate([high, low], axis=1)


def three_fold(matrix):
    high, low = split_parts(matrix)
    return np.concatenate([high, low, high], axis=1)


@functools.lru_cache(maxsize=None)
def dft_tables(rows):
    size = 2 * rows
    angle = 2.0 * np.pi * (np.arange(rows)[:, None] + 0.5) * np.arange(size)[None, :] / size
    ahead = np.concatenate([np.cos(angle), -np.sin(angle)], axis=0)
    back = ahead.T * (2.0 / size)
    signed = np.concatenate([back[:rows], -back[rows:]], axis=0)
    lags = back[rows - np.arange(rows)]
    return {"ahead": two_fold(ahead), "back": three_fold(signed), "lags": three_fold(lags)}


def half_table(ahead):
    rows = ahead.shape[0] // 2
    high, low = ahead[:, :rows], ahead[:, 2 * rows : 3 * rows]
    return high, low


def apply2(table, x):
    return jnp.dot(table, jnp.concatenate([x, x], axis=0), preferred_element_type=F32)


def apply3(table, x):
    high = x.astype(BF16)
    low = (x - high.astype(F32)).astype(BF16)
    return jnp.dot(table, jnp.concatenate([high, high, low], axis=0), preferred_element_type=F32)


def to_spectrum(ahead, x):
    high, low = half_table(ahead)
    return apply3(jnp.concatenate([high, low, high], axis=1), x)


def to_spectrum_exact(ahead, x):
    return apply2(jnp.concatenate(half_table(ahead), axis=1), x)


def times(x, y):
    half = x.shape[0] // 2
    xr, xi, yr, yi = x[:half], x[half:], y[:half], y[half:]
    return jnp.concatenate([xr * yr - xi * yi, xr * yi + xi * yr], axis=0)


def times_conj(x, y):
    half = x.shape[0] // 2
    xr, xi, yr, yi = x[:half], x[half:], y[:half], y[half:]
    return jnp.concatenate([xr * yr + xi * yi, xi * yr - xr * yi], axis=0)


def group_places(columns):
    return lax.broadcasted_iota(jnp.int32, (GROUP, columns), 0).astype(F32)


def spread_modes(rate, weight, rows, shift, backward):
    columns = rate.shape[1]
    places = group_places(columns)
    if backward:
        places = (GROUP - 1.0) - places
    count = rows // GROUP
    order = range(count - 1, -1, -1) if backward else range(count)
    sums = [None] * count
    for m in range(rate.shape[0]):
        rate_m = rate[m : m + 1]
        current = weight[m : m + 1] * jnp.exp(-rate_m * (places + shift))
        stride = jnp.broadcast_to(jnp.exp(-rate_m * GROUP), current.shape)
        for step, g in enumerate(order):
            sums[g] = current if sums[g] is None else sums[g] + current
            if step < count - 1:
                current = current * stride
    return jnp.concatenate(sums, axis=0)


def fold_modes(signal, rate, backward):
    columns = rate.shape[1]
    places = group_places(columns)
    if not backward:
        places = (GROUP - 1.0) - places
    count = signal.shape[0] // GROUP
    order = range(count - 1, -1, -1) if backward else range(count)
    found = []
    for m in range(rate.shape[0]):
        rate_m = rate[m : m + 1]
        stride = jnp.broadcast_to(jnp.exp(-rate_m * GROUP), (GROUP, columns))
        running = None
        for g in order:
            piece = signal[g * GROUP : (g + 1) * GROUP]
            running = piece if running is None else running * stride + piece
        found.append(jnp.sum(running * jnp.exp(-rate_m * places), axis=0, keepdims=True))
    return jnp.concatenate(found, axis=0)


def spectra_body(taps, rate, coef, skip, ahead, mr_spec, li_spec):
    rows = taps.shape[0]
    table = ahead[...]
    mr_spec[...] = to_spectrum(table, taps[...])
    kernel = spread_modes(rate[...], coef[...], rows, 0.0, False)
    first = lax.broadcasted_iota(jnp.int32, kernel.shape, 0) == 0
    kernel = kernel + jnp.where(first, skip[...], 0.0)
    li_spec[...] = to_spectrum(table, kernel)


def short_body(before, product, query, key, mr_spec, li_spec, rate, ahead, back, spec, conv, mixed, inner, ends):
    rows = product.shape[0]
    x = jnp.concatenate([before[...], product[...]], axis=0)
    found = apply2(ahead[...], x)
    spec[...] = found
    filtered = -apply3(back[rows:], times(found, mr_spec[...]))
    conv[...] = filtered
    mixed_rows = (query[...].astype(F32) * filtered).astype(BF16)
    mixed[...] = mixed_rows
    rounded = (key[...].astype(F32) * mixed_rows.astype(F32)).astype(BF16)
    ends[...] = fold_modes(rounded.astype(F32), rate[...], False)
    inner[...] = apply3(back[:rows], times(to_spectrum_exact(ahead[...], rounded), li_spec[...]))


def gather_states(rate, gaps, states, rows):
    modes = rate.shape[0]
    total = jnp.zeros_like(rate)
    for k in range(states.shape[0] // modes):
        weight = jnp.exp(-rate * (jnp.maximum(gaps[k], 0.0) * float(rows)))
        total = total + jnp.where(gaps[k] >= 0.0, weight * states[k * modes : (k + 1) * modes], 0.0)
    return total


def long_body(gaps, inner, query, rate, coef, states, li_out, mixed):
    rows = inner.shape[0]
    entering = gather_states(rate[...], gaps, states, rows)
    total = inner[...] + spread_modes(rate[...], coef[...] * entering, rows, 1.0, False)
    li_out[...] = total
    mixed[...] = (query[...].astype(F32) * total).astype(BF16)


def split_body(count, starts, *rest):
    pieces, parts, whole = rest[: -count - 1], rest[-count - 1 : -1], rest[-1]
    for r, piece in enumerate(pieces):
        whole[:, pl.ds(pl.multiple_of(starts[r], 128), piece.shape[1])] = piece[...]
    for h, part in enumerate(parts):
        place = pl.multiple_of(starts[len(pieces) + h], 128)
        part[...] = whole[:, pl.ds(place, part.shape[1])]


def pair_grad_body(count, starts, *rest):
    parts, weights, (own, *others) = rest[:count], rest[count : count + 4], rest[count + 4 :]
    for part, result in zip(parts, (own, *others)):
        total = None
        for m, weight in enumerate(weights):
            block = part[:, pl.ds(pl.multiple_of(starts[m], 128), weight.shape[0])]
            found = jnp.dot(block, weight[...], preferred_element_type=F32)
            total = found if total is None else total + found
        result[...] = total.astype(result.dtype)


def pair_out_body(count, starts, *rest):
    mixed, weights, results = rest[:count], rest[count : count + 4], rest[count + 4 :]
    for rows, result in zip(mixed, results):
        for m, weight in enumerate(weights):
            found = lax.dot_general(rows[...], weight[...], (((1,), (1,)), ((), ())), preferred_element_type=F32)
            result[:, pl.ds(pl.multiple_of(starts[m], 128), weight.shape[0])] = found.astype(BF16)


def stack_body(count, starts, *rest):
    pieces, stacks, whole = rest[:-3], rest[-3:-1], rest[-1]
    rows = whole.shape[0]
    for r, piece in enumerate(pieces):
        whole[:, pl.ds(pl.multiple_of(starts[r], 128), piece.shape[1])] = piece[...]
    for h in range(count):
        place = pl.multiple_of(starts[len(pieces) + h], 128)
        stack, at = stacks[h // (count // 2)], h % (count // 2)
        stack[at * rows : (at + 1) * rows] = whole[:, pl.ds(place, stack.shape[1])]


def grad_gate_body(count, own, query, rate, li_out, li_spec, ahead, back, *rest):
    parts, (grad_query, ends, inner) = rest[:count], rest[count:]
    rows = own.shape[0]
    total = own[...]
    for part in parts:
        total = total + part[...].astype(F32)
    grad_query[...] = total * li_out[...]
    gated = total * query[...].astype(F32)
    ends[...] = fold_modes(gated, rate[...], True)
    inner[...] = apply3(back[:rows], times_conj(to_spectrum(ahead[...], gated), li_spec[...]))


def grad_long_body(
    inner, rate, coef, entering, mixed_mr, key_li, query_mr, conv, spec, ahead, lags,
    grad_key_li, grad_query_mr, grad_spec, taps,
):
    rows = inner.shape[0]
    grad_input = inner[...] + spread_modes(rate[...], coef[...] * entering[...], rows, 1.0, True)
    grad_key_li[...] = grad_input * mixed_mr[...].astype(F32)
    grad_mixed_mr = grad_input * key_li[...].astype(F32)
    grad_query_mr[...] = grad_mixed_mr * conv[...]
    grad_conv = grad_mixed_mr * query_mr[...].astype(F32)
    found = to_spectrum(ahead[...], grad_conv)
    grad_spec[...] = found
    taps[...] = apply3(lags[...], times_conj(spec[...], found))


def grad_taps_body(grad_spec, mr_spec, back, own_product, prev_product):
    rows = own_product.shape[0]
    products = apply3(back[...], times_conj(grad_spec[...], mr_spec[...]))
    own_product[...] = products[:rows]
    prev_product[...] = products[rows:].astype(BF16)


def grad_product_body(own, arrived, key, value, grad_key, grad_value):
    total = own[...] + arrived[...].astype(F32)
    grad_key[...] = total * value[...].astype(F32)
    grad_value[...] = total * key[...].astype(F32)


def run(body, columns, inputs, outputs, flops):
    tile = min(TILE, columns)
    in_specs = []
    moved = 0
    for kind, array in inputs:
        if kind == "tile":
            in_specs.append(pl.BlockSpec((array.shape[0], tile), lambda c: (0, c)))
        elif kind == "whole":
            in_specs.append(pl.BlockSpec(array.shape, lambda c: (0, 0)))
        else:
            in_specs.append(pl.BlockSpec(memory_space=pltpu.SMEM))
        moved += math.prod(array.shape) * array.dtype.itemsize
    for rows, dtype in outputs:
        moved += rows * columns * jnp.dtype(dtype).itemsize
    return pl.pallas_call(
        body,
        grid=(columns // tile,),
        in_specs=in_specs,
        out_specs=[pl.BlockSpec((rows, tile), lambda c: (0, c)) for rows, _ in outputs],
        out_shape=[jax.ShapeDtypeStruct((rows, columns), dtype) for rows, dtype in outputs],
        compiler_params=pltpu.CompilerParams(vmem_limit_bytes=12 * 1024 * 1024),
        cost_estimate=pl.CostEstimate(flops=flops, bytes_accessed=moved if flops else 0, transcendentals=0),
    )(*[array for _, array in inputs])


def run_once(body, inputs, outputs, scratch=()):
    def block(shape):
        return pl.BlockSpec(shape, lambda c: (0, 0))

    return pl.pallas_call(
        body,
        grid=(1,),
        in_specs=[pl.BlockSpec(memory_space=pltpu.SMEM)] + [block(array.shape) for array in inputs[1:]],
        out_specs=[block(shape) for shape, _ in outputs],
        out_shape=[jax.ShapeDtypeStruct(shape, dtype) for shape, dtype in outputs],
        scratch_shapes=scratch,
        compiler_params=pltpu.CompilerParams(vmem_limit_bytes=20 * 1024 * 1024),
        cost_estimate=pl.CostEstimate(flops=0, bytes_accessed=0, transcendentals=0),
    )(*inputs)


def chip_swap(x, by):
    size = lax.axis_size("ctx")
    return lax.ppermute(x, "ctx", [(i, i ^ (2 * by)) for i in range(size)])


def line_swap(x, by):
    size = lax.axis_size("fsdp")
    return lax.ppermute(x, "fsdp", [(i, i ^ by) for i in range(size)])


def core_swap(x):
    size = lax.axis_size("ctx")
    return lax.ppermute(x, "ctx", [(i, i ^ 1) for i in range(size)])


def shifted(x, by):
    size = lax.axis_size("ctx")
    return lax.ppermute(x, "ctx", [(i, i + by) for i in range(size) if 0 <= i + by < size])


def bit_reversed(count):
    order = [0]
    while len(order) < count:
        order = [2 * k for k in order] + [2 * k + 1 for k in order]
    return order


def columns_at(x, index, width):
    return lax.dynamic_slice_in_dim(x, index * width, width, 1)


def placed(pieces):
    width = pieces[0][1].shape[1]
    whole = jnp.zeros((pieces[0][1].shape[0], width * len(pieces)), pieces[0][1].dtype)
    for index, piece in pieces:
        whole = lax.dynamic_update_slice_in_dim(whole, piece, index * width, 1)
    return whole


def pair_sum(values):
    while len(values) > 1:
        values = [values[k] + values[k + 1] for k in range(0, len(values), 2)]
    return values[0]


def after(x, *others):
    return lax.optimization_barrier((x,) + others)[0]


def direct_factors(rate, rows, chip, backward):
    factors = [jnp.exp(-rate * float(rows))]
    for s in range(1, lax.axis_size("ctx") // 2):
        gap = (chip ^ s) - chip - 1 if backward else chip - (chip ^ s) - 1
        weight = jnp.exp(-rate * (2 * rows * jnp.maximum(gap, 0)).astype(F32))
        factors.append(jnp.where(gap >= 0, weight, 0.0))
    return factors


def entering_direct(ends, factors, here, backward, ready):
    block = factors[0]
    later_core = ((here & 1) != 0) != backward
    sibling = core_swap(ends)
    total = jnp.where(later_core, block * sibling + ends, block * ends + sibling)
    total = after(total, *ready)
    entering = jnp.zeros_like(ends)
    for s, weight in enumerate(factors[1:], 1):
        entering = entering + weight * chip_swap(total, s)
    return jnp.where(later_core, block * entering + sibling, entering)


def shards(
    query_mr,
    key_mr,
    value_mr,
    query_li,
    key_li,
    mr_taps,
    li_time,
    li_residue,
    li_skip,
    out_weight,
    cotangent,
):
    rows, columns = query_mr.shape
    ctx_count = lax.axis_size("ctx")
    line_count = lax.axis_size("fsdp")
    chips = ctx_count // 2
    here = lax.axis_index("ctx")
    chip, core = here // 2, here % 2
    line = lax.axis_index("fsdp")
    grad_scale = 1.0 / math.sqrt(rows * ctx_count)
    tables = {name: jnp.asarray(table) for name, table in dft_tables(rows).items()}
    width = out_weight.shape[0]
    chip_width = 2 * width
    pass_flops = 2 * (2 * rows) * (2 * rows) * columns

    def tile(x):
        return ("tile", x)

    def table(name):
        return ("whole", tables[name])

    mr_product = (key_mr.astype(F32) * value_mr.astype(F32)).astype(BF16)
    before = shifted(mr_product, 1)
    cot_line = [cotangent] + [line_swap(after(cotangent, mr_product), r) for r in range(1, line_count)]
    pairs = chips // 2
    pair = chip // 2
    pair_width = 4 * width

    sibling_weight = core_swap(out_weight)
    rate = 1.0 / after(li_time, mr_product)
    beside = chip_swap(after(out_weight, before), 1)
    coef = li_residue * jnp.sqrt(-jnp.expm1(-2.0 * rate))
    back_factors = lax.optimization_barrier(direct_factors(rate, rows, here // 2, True))
    mr_spec, li_spec = run(
        spectra_body,
        columns,
        [tile(mr_taps), tile(rate), tile(coef), tile(li_skip[None, :]), table("ahead")],
        [(2 * rows, F32), (2 * rows, F32)],
        0,
    )
    spec, mr_conv, mixed_mr, li_inner, ends = run(
        short_body,
        columns,
        [
            tile(after(before, sibling_weight)),
            tile(mr_product),
            tile(query_mr),
            tile(key_li),
            tile(mr_spec),
            tile(li_spec),
            tile(rate),
            table("ahead"),
            table("back"),
        ],
        [(2 * rows, F32), (rows, F32), (rows, BF16), (rows, F32), (rate.shape[0], F32)],
        0,
    )

    line_width = cotangent.shape[1]
    whole_width = line_width * line_count
    split_starts = [(line ^ r) * line_width for r in range(line_count)]
    split_starts += [(pair ^ h) * pair_width for h in range(pairs)]
    cot_pairs = run_once(
        functools.partial(split_body, pairs),
        [jnp.stack(split_starts)] + [after(piece, ends) for piece in cot_line],
        [((rows, pair_width), BF16)] * pairs,
        [pltpu.VMEM((rows, whole_width), BF16)],
    )
    cot_parts = [cot_pairs[0]] + [chip_swap(cot_pairs[h], 2 * h) for h in range(1, pairs)]
    states = lax.all_gather(after(ends, beside, *cot_parts[:1]), "ctx").reshape(-1, columns)
    gaps = (here - 1 - jnp.arange(ctx_count, dtype=jnp.int32)).astype(F32)
    li_out, mixed_li = run(
        long_body,
        columns,
        [("scalar", gaps), tile(li_inner), tile(query_li), tile(rate), tile(coef), tile(states)],
        [(rows, F32), (rows, BF16)],
        0,
    )

    mixed_parts = [mixed_li] + [chip_swap(mixed_li, 2 * h) for h in range(1, pairs)]
    weights = [out_weight, sibling_weight, beside, core_swap(after(beside, cot_pairs[0]))]
    pair_starts = jnp.stack([((here & 3) ^ m) * width for m in range(4)])

    share_flops = 2 * rows * columns * pair_width * pairs
    grad_own, *grad_sent = run(
        functools.partial(pair_grad_body, pairs),
        columns,
        [("scalar", pair_starts)] + [("whole", after(part, mixed_li)) for part in cot_parts] + [tile(weight) for weight in weights],
        [(rows, F32)] + [(rows, BF16)] * (pairs - 1),
        share_flops,
    )
    grad_parts = [chip_swap(part, 2 * h) for h, part in enumerate(grad_sent, 1)]

    out_own, *out_sent = run_once(
        functools.partial(pair_out_body, pairs),
        [pair_starts, after(mixed_parts[0], grad_own)] + mixed_parts[1:] + weights,
        [((rows, pair_width), BF16)] * pairs,
    )
    out_pairs = [out_own] + [chip_swap(after(part, *grad_parts), 2 * h) for h, part in enumerate(out_sent, 1)]
    out_starts = [(pair ^ h) * pair_width for h in range(pairs)]
    out_starts += [(line ^ r) * line_width for r in bit_reversed(line_count)]
    kept, odd = run_once(
        functools.partial(stack_body, line_count),
        [jnp.stack(out_starts)] + out_pairs,
        [((line_count // 2 * rows, line_width), BF16)] * 2,
        [pltpu.VMEM((rows, whole_width), BF16)],
    )
    count, by = line_count // 2, 1
    first_out = arrived_out = line_swap(odd, by)
    while count > 1:
        count //= 2
        by *= 2
        total = kept.astype(F32) + arrived_out.astype(F32)
        kept, arrived_out = total[: count * rows], line_swap(total[count * rows :].astype(BF16), by)
    output = kept.astype(F32) + arrived_out.astype(F32)

    side = chip % 2
    used = [after(part, mixed_li) for part in cot_parts]
    near_cot = jnp.concatenate([columns_at(part, side, chip_width) for part in used], axis=0)
    far_cot = jnp.concatenate([columns_at(part, 1 - side, chip_width) for part in used], axis=0)
    got_cot = chip_swap(far_cot, 1)
    near_mixed = jnp.concatenate([after(part, grad_own) for part in mixed_parts], axis=0)
    got_mixed = chip_swap(near_mixed, 1)

    grad_query_li, back_ends, grad_inner = run(
        functools.partial(grad_gate_body, pairs - 1),
        columns,
        [
            tile(after(grad_own, out_own)),
            tile(query_li),
            tile(rate),
            tile(li_out),
            tile(li_spec),
            table("ahead"),
            table("back"),
        ]
        + [tile(part) for part in grad_parts],
        [(rows, F32), (rate.shape[0], F32), (rows, F32)],
        4 * pass_flops,
    )
    back_entering = entering_direct(
        back_ends, back_factors, here, True, [got_cot, got_mixed] + out_pairs[1:]
    )
    cot_rows = jnp.concatenate([near_cot, got_cot], axis=0)
    mixed_rows = jnp.concatenate([near_mixed, got_mixed], axis=0)

    def weight_share(which):
        return lax.dot_general(
            columns_at(cot_rows, which, width),
            mixed_rows,
            (((0,), (0,)), ((), ())),
            preferred_element_type=F32,
        )

    sent_share = weight_share(1 - core).astype(BF16)
    far_share = core_swap(sent_share)
    grad_weight = (weight_share(core) + far_share.astype(F32)) * grad_scale
    grad_key_li, grad_query_mr, grad_spec, tap_partial = run(
        grad_long_body,
        columns,
        [
            tile(after(grad_inner, sent_share)),
            tile(rate),
            tile(coef),
            tile(back_entering),
            tile(mixed_mr),
            tile(key_li),
            tile(query_mr),
            tile(mr_conv),
            tile(spec),
            table("ahead"),
            table("lags"),
        ],
        [(rows, F32), (rows, F32), (2 * rows, F32), (rows, F32)],
        4 * pass_flops,
    )
    grad_spec = after(grad_spec, first_out)
    own_product, prev_product = run(
        grad_taps_body,
        columns,
        [tile(grad_spec), tile(mr_spec), table("back")],
        [(rows, F32), (rows, BF16)],
        3 * pass_flops,
    )
    arrived = shifted(prev_product, -1)
    grad_key_mr, grad_value_mr = run(
        grad_product_body,
        columns,
        [tile(own_product), tile(arrived), tile(key_mr), tile(value_mr)],
        [(rows, F32), (rows, F32)],
        rows * columns,
    )

    tap_half = tap_partial.shape[0] // 2
    halves = tap_partial.reshape(2, tap_half, columns)
    own_half = lax.dynamic_index_in_dim(halves, core, 0, keepdims=False)
    far_half = lax.dynamic_index_in_dim(halves, 1 - core, 0, keepdims=False)
    chip_half = (own_half + core_swap(far_half)).astype(BF16)
    everywhere = [after(chip_half, prev_product, grad_weight)] + [chip_swap(chip_half, s) for s in range(1, chips)]
    plane_half = pair_sum([part.astype(F32) for part in everywhere]) * grad_scale
    other_half = core_swap(after(plane_half, arrived_out))
    grad_taps = jnp.where(
        core == 0,
        jnp.concatenate([plane_half, other_half], axis=0),
        jnp.concatenate([other_half, plane_half], axis=0),
    )

    return (
        output,
        grad_query_mr,
        grad_key_mr,
        grad_value_mr,
        grad_query_li,
        grad_key_li,
        grad_taps,
        grad_weight,
    )


def solution(mesh):
    rows = P("ctx", "fsdp")
    channels = P(None, "fsdp")
    return jax.shard_map(
        shards,
        mesh=mesh,
        in_specs=(rows,) * 5 + (channels,) * 3 + (P("fsdp"),) + (rows,) * 2,
        out_specs=(rows,) * 6 + (channels, rows),
        check_vma=False,
    )
```

```python
import functools
import math

import jax
import jax.numpy as jnp
import ml_dtypes
import numpy as np
from jax import lax
from jax.experimental import pallas as pl
from jax.experimental.pallas import tpu as pltpu
from jax.sharding import PartitionSpec as P

F32 = jnp.float32
BF16 = jnp.bfloat16
BLOCK = 512
TILE = 256
GROUP = 8


def split_parts(matrix):
    high = matrix.astype(ml_dtypes.bfloat16)
    low = (matrix - high.astype(np.float64)).astype(ml_dtypes.bfloat16)
    return high, low


def two_fold(matrix):
    high, low = split_parts(matrix)
    return np.concatenate([high, low], axis=1)


def three_fold(matrix):
    high, low = split_parts(matrix)
    return np.concatenate([high, low, high], axis=1)


@functools.lru_cache(maxsize=None)
def dft_tables(rows):
    size = 2 * rows
    angle = 2.0 * np.pi * (np.arange(rows)[:, None] + 0.5) * np.arange(size)[None, :] / size
    ahead = np.concatenate([np.cos(angle), -np.sin(angle)], axis=0)
    back = ahead.T * (2.0 / size)
    signed = np.concatenate([back[:rows], -back[rows:]], axis=0)
    lags = back[rows - np.arange(rows)]
    return {"ahead": two_fold(ahead), "back": three_fold(signed), "lags": three_fold(lags)}


def half_table(ahead):
    rows = ahead.shape[0] // 2
    high, low = ahead[:, :rows], ahead[:, 2 * rows : 3 * rows]
    return high, low


def apply2(table, x):
    return jnp.dot(table, jnp.concatenate([x, x], axis=0), preferred_element_type=F32)


def apply3(table, x):
    high = x.astype(BF16)
    low = (x - high.astype(F32)).astype(BF16)
    return jnp.dot(table, jnp.concatenate([high, high, low], axis=0), preferred_element_type=F32)


def to_spectrum(ahead, x):
    high, low = half_table(ahead)
    return apply3(jnp.concatenate([high, low, high], axis=1), x)


def to_spectrum_exact(ahead, x):
    return apply2(jnp.concatenate(half_table(ahead), axis=1), x)


def times(x, y):
    half = x.shape[0] // 2
    xr, xi, yr, yi = x[:half], x[half:], y[:half], y[half:]
    return jnp.concatenate([xr * yr - xi * yi, xr * yi + xi * yr], axis=0)


def times_conj(x, y):
    half = x.shape[0] // 2
    xr, xi, yr, yi = x[:half], x[half:], y[:half], y[half:]
    return jnp.concatenate([xr * yr + xi * yi, xi * yr - xr * yi], axis=0)


def group_places(columns):
    return lax.broadcasted_iota(jnp.int32, (GROUP, columns), 0).astype(F32)


def spread_modes(rate, weight, rows, shift, backward):
    columns = rate.shape[1]
    places = group_places(columns)
    if backward:
        places = (GROUP - 1.0) - places
    count = rows // GROUP
    order = range(count - 1, -1, -1) if backward else range(count)
    sums = [None] * count
    for m in range(rate.shape[0]):
        rate_m = rate[m : m + 1]
        current = weight[m : m + 1] * jnp.exp(-rate_m * (places + shift))
        stride = jnp.broadcast_to(jnp.exp(-rate_m * GROUP), current.shape)
        for step, g in enumerate(order):
            sums[g] = current if sums[g] is None else sums[g] + current
            if step < count - 1:
                current = current * stride
    return jnp.concatenate(sums, axis=0)


def fold_modes(signal, rate, backward):
    columns = rate.shape[1]
    places = group_places(columns)
    if not backward:
        places = (GROUP - 1.0) - places
    count = signal.shape[0] // GROUP
    order = range(count - 1, -1, -1) if backward else range(count)
    found = []
    for m in range(rate.shape[0]):
        rate_m = rate[m : m + 1]
        stride = jnp.broadcast_to(jnp.exp(-rate_m * GROUP), (GROUP, columns))
        running = None
        for g in order:
            piece = signal[g * GROUP : (g + 1) * GROUP]
            running = piece if running is None else running * stride + piece
        found.append(jnp.sum(running * jnp.exp(-rate_m * places), axis=0, keepdims=True))
    return jnp.concatenate(found, axis=0)


def spectra_body(taps, rate, coef, skip, ahead, mr_spec, li_spec):
    rows = taps.shape[0]
    table = ahead[...]
    mr_spec[...] = to_spectrum(table, taps[...])
    kernel = spread_modes(rate[...], coef[...], rows, 0.0, False)
    first = lax.broadcasted_iota(jnp.int32, kernel.shape, 0) == 0
    kernel = kernel + jnp.where(first, skip[...], 0.0)
    li_spec[...] = to_spectrum(table, kernel)


def short_body(before, product, query, key, mr_spec, li_spec, rate, ahead, back, spec, conv, mixed, inner, ends):
    rows = product.shape[0]
    x = jnp.concatenate([before[...], product[...]], axis=0)
    found = apply2(ahead[...], x)
    spec[...] = found
    filtered = -apply3(back[rows:], times(found, mr_spec[...]))
    conv[...] = filtered
    mixed_rows = (query[...].astype(F32) * filtered).astype(BF16)
    mixed[...] = mixed_rows
    rounded = (key[...].astype(F32) * mixed_rows.astype(F32)).astype(BF16)
    ends[...] = fold_modes(rounded.astype(F32), rate[...], False)
    inner[...] = apply3(back[:rows], times(to_spectrum_exact(ahead[...], rounded), li_spec[...]))


def gather_states(rate, gaps, states, rows):
    modes = rate.shape[0]
    total = jnp.zeros_like(rate)
    for k in range(states.shape[0] // modes):
        weight = jnp.exp(-rate * (jnp.maximum(gaps[k], 0.0) * float(rows)))
        total = total + jnp.where(gaps[k] >= 0.0, weight * states[k * modes : (k + 1) * modes], 0.0)
    return total


def long_body(gaps, inner, query, rate, coef, states, li_out, mixed):
    rows = inner.shape[0]
    entering = gather_states(rate[...], gaps, states, rows)
    total = inner[...] + spread_modes(rate[...], coef[...] * entering, rows, 1.0, False)
    li_out[...] = total
    mixed[...] = (query[...].astype(F32) * total).astype(BF16)


def split_body(count, starts, *rest):
    pieces, parts, whole = rest[: -count - 1], rest[-count - 1 : -1], rest[-1]
    for r, piece in enumerate(pieces):
        whole[:, pl.ds(pl.multiple_of(starts[r], 128), piece.shape[1])] = piece[...]
    for h, part in enumerate(parts):
        place = pl.multiple_of(starts[len(pieces) + h], 128)
        part[...] = whole[:, pl.ds(place, part.shape[1])]


def pair_grad_body(count, starts, *rest):
    parts, weights, (own, *others) = rest[:count], rest[count : count + 4], rest[count + 4 :]
    for part, result in zip(parts, (own, *others)):
        total = None
        for m, weight in enumerate(weights):
            block = part[:, pl.ds(pl.multiple_of(starts[m], 128), weight.shape[0])]
            found = jnp.dot(block, weight[...], preferred_element_type=F32)
            total = found if total is None else total + found
        result[...] = total.astype(result.dtype)


def pair_out_body(count, starts, *rest):
    mixed, weights, results = rest[:count], rest[count : count + 4], rest[count + 4 :]
    for rows, result in zip(mixed, results):
        for m, weight in enumerate(weights):
            found = lax.dot_general(rows[...], weight[...], (((1,), (1,)), ((), ())), preferred_element_type=F32)
            result[:, pl.ds(pl.multiple_of(starts[m], 128), weight.shape[0])] = found.astype(BF16)


def stack_body(count, starts, *rest):
    pieces, stacks, whole = rest[:-3], rest[-3:-1], rest[-1]
    rows = whole.shape[0]
    for r, piece in enumerate(pieces):
        whole[:, pl.ds(pl.multiple_of(starts[r], 128), piece.shape[1])] = piece[...]
    for h in range(count):
        place = pl.multiple_of(starts[len(pieces) + h], 128)
        stack, at = stacks[h // (count // 2)], h % (count // 2)
        stack[at * rows : (at + 1) * rows] = whole[:, pl.ds(place, stack.shape[1])]


def grad_gate_body(count, own, query, rate, li_out, li_spec, ahead, back, *rest):
    parts, (grad_query, ends, inner) = rest[:count], rest[count:]
    rows = own.shape[0]
    total = own[...]
    for part in parts:
        total = total + part[...].astype(F32)
    grad_query[...] = total * li_out[...]
    gated = total * query[...].astype(F32)
    ends[...] = fold_modes(gated, rate[...], True)
    inner[...] = apply3(back[:rows], times_conj(to_spectrum(ahead[...], gated), li_spec[...]))


def grad_long_body(
    inner, rate, coef, entering, mixed_mr, key_li, query_mr, conv, spec, ahead, lags,
    grad_key_li, grad_query_mr, grad_spec, taps,
):
    rows = inner.shape[0]
    grad_input = inner[...] + spread_modes(rate[...], coef[...] * entering[...], rows, 1.0, True)
    grad_key_li[...] = grad_input * mixed_mr[...].astype(F32)
    grad_mixed_mr = grad_input * key_li[...].astype(F32)
    grad_query_mr[...] = grad_mixed_mr * conv[...]
    grad_conv = grad_mixed_mr * query_mr[...].astype(F32)
    found = to_spectrum(ahead[...], grad_conv)
    grad_spec[...] = found
    taps[...] = apply3(lags[...], times_conj(spec[...], found))


def grad_taps_body(grad_spec, mr_spec, back, own_product, prev_product):
    rows = own_product.shape[0]
    products = apply3(back[...], times_conj(grad_spec[...], mr_spec[...]))
    own_product[...] = products[:rows]
    prev_product[...] = products[rows:].astype(BF16)


def grad_product_body(own, arrived, key, value, grad_key, grad_value):
    total = own[...] + arrived[...].astype(F32)
    grad_key[...] = total * value[...].astype(F32)
    grad_value[...] = total * key[...].astype(F32)


def run(body, columns, inputs, outputs, flops):
    block = min(BLOCK, columns)
    tile = min(TILE, block)
    in_specs = []
    moved = 0
    for kind, array in inputs:
        if kind == "tile":
            in_specs.append(pl.BlockSpec((array.shape[0], block), lambda c: (0, c)))
        elif kind == "whole":
            in_specs.append(pl.BlockSpec(array.shape, lambda c: (0, 0)))
        else:
            in_specs.append(pl.BlockSpec(memory_space=pltpu.SMEM))
        moved += math.prod(array.shape) * array.dtype.itemsize
    for rows, dtype in outputs:
        moved += rows * columns * jnp.dtype(dtype).itemsize
    tiled = [kind == "tile" for kind, _ in inputs] + [True] * len(outputs)

    def body_by_tiles(*refs):
        for first in range(0, block, tile):
            body(*[ref.at[:, pl.ds(first, tile)] if cut else ref for ref, cut in zip(refs, tiled)])

    return pl.pallas_call(
        body_by_tiles,
        grid=(columns // block,),
        in_specs=in_specs,
        out_specs=[pl.BlockSpec((rows, block), lambda c: (0, c)) for rows, _ in outputs],
        out_shape=[jax.ShapeDtypeStruct((rows, columns), dtype) for rows, dtype in outputs],
        compiler_params=pltpu.CompilerParams(vmem_limit_bytes=56 * 1024 * 1024),
        cost_estimate=pl.CostEstimate(flops=flops, bytes_accessed=moved if flops else 0, transcendentals=0),
    )(*[array for _, array in inputs])


def run_once(body, inputs, outputs, scratch=()):
    def block(shape):
        return pl.BlockSpec(shape, lambda c: (0, 0))

    return pl.pallas_call(
        body,
        grid=(1,),
        in_specs=[pl.BlockSpec(memory_space=pltpu.SMEM)] + [block(array.shape) for array in inputs[1:]],
        out_specs=[block(shape) for shape, _ in outputs],
        out_shape=[jax.ShapeDtypeStruct(shape, dtype) for shape, dtype in outputs],
        scratch_shapes=scratch,
        compiler_params=pltpu.CompilerParams(vmem_limit_bytes=56 * 1024 * 1024),
        cost_estimate=pl.CostEstimate(flops=0, bytes_accessed=0, transcendentals=0),
    )(*inputs)


def chip_swap(x, by):
    size = lax.axis_size("ctx")
    return lax.ppermute(x, "ctx", [(i, i ^ (2 * by)) for i in range(size)])


def line_swap(x, by):
    size = lax.axis_size("fsdp")
    return lax.ppermute(x, "fsdp", [(i, i ^ by) for i in range(size)])


def core_swap(x):
    size = lax.axis_size("ctx")
    return lax.ppermute(x, "ctx", [(i, i ^ 1) for i in range(size)])


def shifted(x, by):
    size = lax.axis_size("ctx")
    return lax.ppermute(x, "ctx", [(i, i + by) for i in range(size) if 0 <= i + by < size])


def bit_reversed(count):
    order = [0]
    while len(order) < count:
        order = [2 * k for k in order] + [2 * k + 1 for k in order]
    return order


def columns_at(x, index, width):
    return lax.dynamic_slice_in_dim(x, index * width, width, 1)


def placed(pieces):
    width = pieces[0][1].shape[1]
    whole = jnp.zeros((pieces[0][1].shape[0], width * len(pieces)), pieces[0][1].dtype)
    for index, piece in pieces:
        whole = lax.dynamic_update_slice_in_dim(whole, piece, index * width, 1)
    return whole


def pair_sum(values):
    while len(values) > 1:
        values = [values[k] + values[k + 1] for k in range(0, len(values), 2)]
    return values[0]


def after(x, *others):
    return lax.optimization_barrier((x,) + others)[0]


def direct_factors(rate, rows, chip, backward):
    factors = [jnp.exp(-rate * float(rows))]
    for s in range(1, lax.axis_size("ctx") // 2):
        gap = (chip ^ s) - chip - 1 if backward else chip - (chip ^ s) - 1
        weight = jnp.exp(-rate * (2 * rows * jnp.maximum(gap, 0)).astype(F32))
        factors.append(jnp.where(gap >= 0, weight, 0.0))
    return factors


def entering_direct(ends, factors, here, backward, ready):
    block = factors[0]
    later_core = ((here & 1) != 0) != backward
    sibling = core_swap(ends)
    total = jnp.where(later_core, block * sibling + ends, block * ends + sibling)
    total = after(total, *ready)
    entering = jnp.zeros_like(ends)
    for s, weight in enumerate(factors[1:], 1):
        entering = entering + weight * chip_swap(total, s)
    return jnp.where(later_core, block * entering + sibling, entering)


def shards(
    query_mr,
    key_mr,
    value_mr,
    query_li,
    key_li,
    mr_taps,
    li_time,
    li_residue,
    li_skip,
    out_weight,
    cotangent,
):
    rows, columns = query_mr.shape
    ctx_count = lax.axis_size("ctx")
    line_count = lax.axis_size("fsdp")
    chips = ctx_count // 2
    here = lax.axis_index("ctx")
    chip, core = here // 2, here % 2
    line = lax.axis_index("fsdp")
    grad_scale = 1.0 / math.sqrt(rows * ctx_count)
    tables = {name: jnp.asarray(table) for name, table in dft_tables(rows).items()}
    width = out_weight.shape[0]
    chip_width = 2 * width
    pass_flops = 2 * (2 * rows) * (2 * rows) * columns

    def tile(x):
        return ("tile", x)

    def table(name):
        return ("whole", tables[name])

    mr_product = (key_mr.astype(F32) * value_mr.astype(F32)).astype(BF16)
    before = shifted(mr_product, 1)
    cot_line = [cotangent] + [line_swap(after(cotangent, mr_product), r) for r in range(1, line_count)]
    pairs = chips // 2
    pair = chip // 2
    pair_width = 4 * width

    sibling_weight = core_swap(out_weight)
    rate = 1.0 / after(li_time, mr_product)
    beside = chip_swap(after(out_weight, before), 1)
    coef = li_residue * jnp.sqrt(-jnp.expm1(-2.0 * rate))
    back_factors = lax.optimization_barrier(direct_factors(rate, rows, here // 2, True))
    mr_spec, li_spec = run(
        spectra_body,
        columns,
        [tile(mr_taps), tile(rate), tile(coef), tile(li_skip[None, :]), table("ahead")],
        [(2 * rows, F32), (2 * rows, F32)],
        0,
    )
    spec, mr_conv, mixed_mr, li_inner, ends = run(
        short_body,
        columns,
        [
            tile(after(before, sibling_weight)),
            tile(mr_product),
            tile(query_mr),
            tile(key_li),
            tile(mr_spec),
            tile(li_spec),
            tile(rate),
            table("ahead"),
            table("back"),
        ],
        [(2 * rows, F32), (rows, F32), (rows, BF16), (rows, F32), (rate.shape[0], F32)],
        0,
    )

    line_width = cotangent.shape[1]
    whole_width = line_width * line_count
    split_starts = [(line ^ r) * line_width for r in range(line_count)]
    split_starts += [(pair ^ h) * pair_width for h in range(pairs)]
    cot_pairs = run_once(
        functools.partial(split_body, pairs),
        [jnp.stack(split_starts)] + [after(piece, ends) for piece in cot_line],
        [((rows, pair_width), BF16)] * pairs,
        [pltpu.VMEM((rows, whole_width), BF16)],
    )
    cot_parts = [cot_pairs[0]] + [chip_swap(cot_pairs[h], 2 * h) for h in range(1, pairs)]
    states = lax.all_gather(after(ends, beside, *cot_parts[:1]), "ctx").reshape(-1, columns)
    gaps = (here - 1 - jnp.arange(ctx_count, dtype=jnp.int32)).astype(F32)
    li_out, mixed_li = run(
        long_body,
        columns,
        [("scalar", gaps), tile(li_inner), tile(query_li), tile(rate), tile(coef), tile(states)],
        [(rows, F32), (rows, BF16)],
        0,
    )

    mixed_parts = [mixed_li] + [chip_swap(mixed_li, 2 * h) for h in range(1, pairs)]
    weights = [out_weight, sibling_weight, beside, core_swap(after(beside, cot_pairs[0]))]
    pair_starts = jnp.stack([((here & 3) ^ m) * width for m in range(4)])

    share_flops = 2 * rows * columns * pair_width * pairs
    grad_own, *grad_sent = run(
        functools.partial(pair_grad_body, pairs),
        columns,
        [("scalar", pair_starts)] + [("whole", after(part, mixed_li)) for part in cot_parts] + [tile(weight) for weight in weights],
        [(rows, F32)] + [(rows, BF16)] * (pairs - 1),
        share_flops,
    )
    grad_parts = [chip_swap(part, 2 * h) for h, part in enumerate(grad_sent, 1)]

    out_own, *out_sent = run_once(
        functools.partial(pair_out_body, pairs),
        [pair_starts, after(mixed_parts[0], grad_own)] + mixed_parts[1:] + weights,
        [((rows, pair_width), BF16)] * pairs,
    )
    out_pairs = [out_own] + [chip_swap(after(part, *grad_parts), 2 * h) for h, part in enumerate(out_sent, 1)]
    out_starts = [(pair ^ h) * pair_width for h in range(pairs)]
    out_starts += [(line ^ r) * line_width for r in bit_reversed(line_count)]
    kept, odd = run_once(
        functools.partial(stack_body, line_count),
        [jnp.stack(out_starts)] + out_pairs,
        [((line_count // 2 * rows, line_width), BF16)] * 2,
        [pltpu.VMEM((rows, whole_width), BF16)],
    )
    count, by = line_count // 2, 1
    first_out = arrived_out = line_swap(odd, by)
    while count > 1:
        count //= 2
        by *= 2
        total = kept.astype(F32) + arrived_out.astype(F32)
        kept, arrived_out = total[: count * rows], line_swap(total[count * rows :].astype(BF16), by)
    output = kept.astype(F32) + arrived_out.astype(F32)

    side = chip % 2
    used = [after(part, mixed_li) for part in cot_parts]
    near_cot = jnp.concatenate([columns_at(part, side, chip_width) for part in used], axis=0)
    far_cot = jnp.concatenate([columns_at(part, 1 - side, chip_width) for part in used], axis=0)
    got_cot = chip_swap(far_cot, 1)
    near_mixed = jnp.concatenate([after(part, grad_own) for part in mixed_parts], axis=0)
    got_mixed = chip_swap(near_mixed, 1)

    grad_query_li, back_ends, grad_inner = run(
        functools.partial(grad_gate_body, pairs - 1),
        columns,
        [
            tile(after(grad_own, out_own)),
            tile(query_li),
            tile(rate),
            tile(li_out),
            tile(li_spec),
            table("ahead"),
            table("back"),
        ]
        + [tile(part) for part in grad_parts],
        [(rows, F32), (rate.shape[0], F32), (rows, F32)],
        4 * pass_flops,
    )
    back_entering = entering_direct(
        back_ends, back_factors, here, True, [got_cot, got_mixed] + out_pairs[1:]
    )
    cot_rows = jnp.concatenate([near_cot, after(got_cot, back_ends)], axis=0)
    mixed_rows = jnp.concatenate([near_mixed, after(got_mixed, back_ends)], axis=0)

    def weight_share(which):
        return lax.dot_general(
            columns_at(cot_rows, which, width),
            mixed_rows,
            (((0,), (0,)), ((), ())),
            preferred_element_type=F32,
        )

    sent_share = weight_share(1 - core).astype(BF16)
    far_share = core_swap(sent_share)
    grad_weight = (weight_share(core) + far_share.astype(F32)) * grad_scale
    grad_key_li, grad_query_mr, grad_spec, tap_partial = run(
        grad_long_body,
        columns,
        [
            tile(after(grad_inner, sent_share)),
            tile(rate),
            tile(coef),
            tile(back_entering),
            tile(mixed_mr),
            tile(key_li),
            tile(query_mr),
            tile(mr_conv),
            tile(spec),
            table("ahead"),
            table("lags"),
        ],
        [(rows, F32), (rows, F32), (2 * rows, F32), (rows, F32)],
        4 * pass_flops,
    )
    grad_spec = after(grad_spec, first_out)
    own_product, prev_product = run(
        grad_taps_body,
        columns,
        [tile(grad_spec), tile(mr_spec), table("back")],
        [(rows, F32), (rows, BF16)],
        3 * pass_flops,
    )
    arrived = shifted(prev_product, -1)
    grad_key_mr, grad_value_mr = run(
        grad_product_body,
        columns,
        [tile(own_product), tile(arrived), tile(key_mr), tile(value_mr)],
        [(rows, F32), (rows, F32)],
        rows * columns,
    )

    tap_half = tap_partial.shape[0] // 2
    halves = tap_partial.reshape(2, tap_half, columns)
    own_half = lax.dynamic_index_in_dim(halves, core, 0, keepdims=False)
    far_half = lax.dynamic_index_in_dim(halves, 1 - core, 0, keepdims=False)
    chip_half = (own_half + core_swap(far_half)).astype(BF16)
    everywhere = [after(chip_half, prev_product, grad_weight)] + [chip_swap(chip_half, s) for s in range(1, chips)]
    plane_half = pair_sum([part.astype(F32) for part in everywhere]) * grad_scale
    other_half = core_swap(after(plane_half, arrived_out))
    grad_taps = jnp.where(
        core == 0,
        jnp.concatenate([plane_half, other_half], axis=0),
        jnp.concatenate([other_half, plane_half], axis=0),
    )

    return (
        output,
        grad_query_mr,
        grad_key_mr,
        grad_value_mr,
        grad_query_li,
        grad_key_li,
        grad_taps,
        grad_weight,
    )


def solution(mesh):
    rows = P("ctx", "fsdp")
    channels = P(None, "fsdp")
    return jax.shard_map(
        shards,
        mesh=mesh,
        in_specs=(rows,) * 5 + (channels,) * 3 + (P("fsdp"),) + (rows,) * 2,
        out_specs=(rows,) * 6 + (channels, rows),
        check_vma=False,
    )
```

```python
import functools
import math

import jax
import jax.numpy as jnp
import ml_dtypes
import numpy as np
from jax import lax
from jax.experimental import pallas as pl
from jax.experimental.pallas import tpu as pltpu
from jax.sharding import PartitionSpec as P

F32 = jnp.float32
BF16 = jnp.bfloat16
BLOCK = 512
TILE = 256
GROUP = 8


def split_parts(matrix):
    high = matrix.astype(ml_dtypes.bfloat16)
    low = (matrix - high.astype(np.float64)).astype(ml_dtypes.bfloat16)
    return high, low


def two_fold(matrix):
    high, low = split_parts(matrix)
    return np.concatenate([high, low], axis=1)


def three_fold(matrix):
    high, low = split_parts(matrix)
    return np.concatenate([high, low, high], axis=1)


@functools.lru_cache(maxsize=None)
def dft_tables(rows):
    size = 2 * rows
    angle = 2.0 * np.pi * (np.arange(rows)[:, None] + 0.5) * np.arange(size)[None, :] / size
    ahead = np.concatenate([np.cos(angle), -np.sin(angle)], axis=0)
    back = ahead.T * (2.0 / size)
    signed = np.concatenate([back[:rows], -back[rows:]], axis=0)
    lags = back[rows - np.arange(rows)]
    return {"ahead": two_fold(ahead), "back": three_fold(signed), "lags": three_fold(lags)}


def half_table(ahead):
    rows = ahead.shape[0] // 2
    high, low = ahead[:, :rows], ahead[:, 2 * rows : 3 * rows]
    return high, low


def apply2(table, x):
    return jnp.dot(table, jnp.concatenate([x, x], axis=0), preferred_element_type=F32)


def apply3(table, x):
    high = x.astype(BF16)
    low = (x - high.astype(F32)).astype(BF16)
    return jnp.dot(table, jnp.concatenate([high, high, low], axis=0), preferred_element_type=F32)


def to_spectrum(ahead, x):
    high, low = half_table(ahead)
    return apply3(jnp.concatenate([high, low, high], axis=1), x)


def to_spectrum_exact(ahead, x):
    return apply2(jnp.concatenate(half_table(ahead), axis=1), x)


def times(x, y):
    half = x.shape[0] // 2
    xr, xi, yr, yi = x[:half], x[half:], y[:half], y[half:]
    return jnp.concatenate([xr * yr - xi * yi, xr * yi + xi * yr], axis=0)


def times_conj(x, y):
    half = x.shape[0] // 2
    xr, xi, yr, yi = x[:half], x[half:], y[:half], y[half:]
    return jnp.concatenate([xr * yr + xi * yi, xi * yr - xr * yi], axis=0)


def group_places(columns):
    return lax.broadcasted_iota(jnp.int32, (GROUP, columns), 0).astype(F32)


def spread_modes(rate, weight, rows, shift, backward):
    columns = rate.shape[1]
    places = group_places(columns)
    if backward:
        places = (GROUP - 1.0) - places
    count = rows // GROUP
    order = range(count - 1, -1, -1) if backward else range(count)
    sums = [None] * count
    for m in range(rate.shape[0]):
        rate_m = rate[m : m + 1]
        current = weight[m : m + 1] * jnp.exp(-rate_m * (places + shift))
        stride = jnp.broadcast_to(jnp.exp(-rate_m * GROUP), current.shape)
        for step, g in enumerate(order):
            sums[g] = current if sums[g] is None else sums[g] + current
            if step < count - 1:
                current = current * stride
    return jnp.concatenate(sums, axis=0)


def fold_modes(signal, rate, backward):
    columns = rate.shape[1]
    places = group_places(columns)
    if not backward:
        places = (GROUP - 1.0) - places
    count = signal.shape[0] // GROUP
    order = range(count - 1, -1, -1) if backward else range(count)
    found = []
    for m in range(rate.shape[0]):
        rate_m = rate[m : m + 1]
        stride = jnp.broadcast_to(jnp.exp(-rate_m * GROUP), (GROUP, columns))
        running = None
        for g in order:
            piece = signal[g * GROUP : (g + 1) * GROUP]
            running = piece if running is None else running * stride + piece
        found.append(jnp.sum(running * jnp.exp(-rate_m * places), axis=0, keepdims=True))
    return jnp.concatenate(found, axis=0)


def spectra_body(taps, rate, coef, skip, ahead, mr_spec, li_spec):
    rows = taps.shape[0]
    table = ahead[...]
    mr_spec[...] = to_spectrum(table, taps[...])
    kernel = spread_modes(rate[...], coef[...], rows, 0.0, False)
    first = lax.broadcasted_iota(jnp.int32, kernel.shape, 0) == 0
    kernel = kernel + jnp.where(first, skip[...], 0.0)
    li_spec[...] = to_spectrum(table, kernel)


def short_body(before, product, query, key, mr_spec, li_spec, rate, ahead, back, spec, conv, mixed, inner, ends):
    rows = product.shape[0]
    x = jnp.concatenate([before[...], product[...]], axis=0)
    found = apply2(ahead[...], x)
    spec[...] = found
    filtered = -apply3(back[rows:], times(found, mr_spec[...]))
    conv[...] = filtered
    mixed_rows = (query[...].astype(F32) * filtered).astype(BF16)
    mixed[...] = mixed_rows
    rounded = (key[...].astype(F32) * mixed_rows.astype(F32)).astype(BF16)
    ends[...] = fold_modes(rounded.astype(F32), rate[...], False)
    inner[...] = apply3(back[:rows], times(to_spectrum_exact(ahead[...], rounded), li_spec[...]))


def gather_states(rate, gaps, states, rows):
    modes = rate.shape[0]
    total = jnp.zeros_like(rate)
    for k in range(states.shape[0] // modes):
        weight = jnp.exp(-rate * (jnp.maximum(gaps[k], 0.0) * float(rows)))
        total = total + jnp.where(gaps[k] >= 0.0, weight * states[k * modes : (k + 1) * modes], 0.0)
    return total


def long_body(gaps, inner, query, rate, coef, states, li_out, mixed):
    rows = inner.shape[0]
    entering = gather_states(rate[...], gaps, states, rows)
    total = inner[...] + spread_modes(rate[...], coef[...] * entering, rows, 1.0, False)
    li_out[...] = total
    mixed[...] = (query[...].astype(F32) * total).astype(BF16)


def split_body(count, starts, *rest):
    pieces, parts, whole = rest[: -count - 1], rest[-count - 1 : -1], rest[-1]
    for r, piece in enumerate(pieces):
        whole[:, pl.ds(pl.multiple_of(starts[r], 128), piece.shape[1])] = piece[...]
    for h, part in enumerate(parts):
        place = pl.multiple_of(starts[len(pieces) + h], 128)
        part[...] = whole[:, pl.ds(place, part.shape[1])]


def pair_grad_body(count, starts, *rest):
    parts, weights, (own, *others) = rest[:count], rest[count : count + 4], rest[count + 4 :]
    for part, result in zip(parts, (own, *others)):
        total = None
        for m, weight in enumerate(weights):
            block = part[:, pl.ds(pl.multiple_of(starts[m], 128), weight.shape[0])]
            found = jnp.dot(block, weight[...], preferred_element_type=F32)
            total = found if total is None else total + found
        result[...] = total.astype(result.dtype)


def pair_out_body(count, starts, *rest):
    mixed, weights, results = rest[:count], rest[count : count + 4], rest[count + 4 :]
    for rows, result in zip(mixed, results):
        for m, weight in enumerate(weights):
            found = lax.dot_general(rows[...], weight[...], (((1,), (1,)), ((), ())), preferred_element_type=F32)
            result[:, pl.ds(pl.multiple_of(starts[m], 128), weight.shape[0])] = found.astype(BF16)


def stack_body(count, starts, *rest):
    pieces, stacks, whole = rest[:-3], rest[-3:-1], rest[-1]
    rows = whole.shape[0]
    for r, piece in enumerate(pieces):
        whole[:, pl.ds(pl.multiple_of(starts[r], 128), piece.shape[1])] = piece[...]
    for h in range(count):
        place = pl.multiple_of(starts[len(pieces) + h], 128)
        stack, at = stacks[h // (count // 2)], h % (count // 2)
        stack[at * rows : (at + 1) * rows] = whole[:, pl.ds(place, stack.shape[1])]


def grad_gate_body(count, own, query, rate, li_out, li_spec, ahead, back, *rest):
    parts, (grad_query, ends, inner) = rest[:count], rest[count:]
    rows = own.shape[0]
    total = own[...]
    for part in parts:
        total = total + part[...].astype(F32)
    grad_query[...] = total * li_out[...]
    gated = total * query[...].astype(F32)
    ends[...] = fold_modes(gated, rate[...], True)
    inner[...] = apply3(back[:rows], times_conj(to_spectrum(ahead[...], gated), li_spec[...]))


def grad_long_body(
    inner, rate, coef, entering, mixed_mr, key_li, query_mr, conv, spec, ahead, lags,
    grad_key_li, grad_query_mr, grad_spec, taps,
):
    rows = inner.shape[0]
    grad_input = inner[...] + spread_modes(rate[...], coef[...] * entering[...], rows, 1.0, True)
    grad_key_li[...] = grad_input * mixed_mr[...].astype(F32)
    grad_mixed_mr = grad_input * key_li[...].astype(F32)
    grad_query_mr[...] = grad_mixed_mr * conv[...]
    grad_conv = grad_mixed_mr * query_mr[...].astype(F32)
    found = to_spectrum(ahead[...], grad_conv)
    grad_spec[...] = found
    taps[...] = apply3(lags[...], times_conj(spec[...], found))


def grad_taps_body(grad_spec, mr_spec, back, own_product, prev_product):
    rows = own_product.shape[0]
    products = apply3(back[...], times_conj(grad_spec[...], mr_spec[...]))
    own_product[...] = products[:rows]
    prev_product[...] = products[rows:].astype(BF16)


def grad_product_body(own, arrived, key, value, grad_key, grad_value):
    total = own[...] + arrived[...].astype(F32)
    grad_key[...] = total * value[...].astype(F32)
    grad_value[...] = total * key[...].astype(F32)


def run(body, columns, inputs, outputs, flops):
    block = min(BLOCK, columns)
    tile = min(TILE, block)
    in_specs = []
    moved = 0
    for kind, array in inputs:
        if kind == "tile":
            in_specs.append(pl.BlockSpec((array.shape[0], block), lambda c: (0, c)))
        elif kind == "whole":
            in_specs.append(pl.BlockSpec(array.shape, lambda c: (0, 0)))
        else:
            in_specs.append(pl.BlockSpec(memory_space=pltpu.SMEM))
        moved += math.prod(array.shape) * array.dtype.itemsize
    for rows, dtype in outputs:
        moved += rows * columns * jnp.dtype(dtype).itemsize
    tiled = [kind == "tile" for kind, _ in inputs] + [True] * len(outputs)

    def body_by_tiles(*refs):
        for first in range(0, block, tile):
            body(*[ref.at[:, pl.ds(first, tile)] if cut else ref for ref, cut in zip(refs, tiled)])

    return pl.pallas_call(
        body_by_tiles,
        grid=(columns // block,),
        in_specs=in_specs,
        out_specs=[pl.BlockSpec((rows, block), lambda c: (0, c)) for rows, _ in outputs],
        out_shape=[jax.ShapeDtypeStruct((rows, columns), dtype) for rows, dtype in outputs],
        compiler_params=pltpu.CompilerParams(vmem_limit_bytes=56 * 1024 * 1024),
        cost_estimate=pl.CostEstimate(flops=flops, bytes_accessed=moved if flops else 0, transcendentals=0),
    )(*[array for _, array in inputs])


def run_once(body, inputs, outputs, scratch=()):
    def block(shape):
        return pl.BlockSpec(shape, lambda c: (0, 0))

    return pl.pallas_call(
        body,
        grid=(1,),
        in_specs=[pl.BlockSpec(memory_space=pltpu.SMEM)] + [block(array.shape) for array in inputs[1:]],
        out_specs=[block(shape) for shape, _ in outputs],
        out_shape=[jax.ShapeDtypeStruct(shape, dtype) for shape, dtype in outputs],
        scratch_shapes=scratch,
        compiler_params=pltpu.CompilerParams(vmem_limit_bytes=56 * 1024 * 1024),
        cost_estimate=pl.CostEstimate(flops=0, bytes_accessed=0, transcendentals=0),
    )(*inputs)


def chip_swap(x, by):
    size = lax.axis_size("ctx")
    return lax.ppermute(x, "ctx", [(i, i ^ (2 * by)) for i in range(size)])


def line_swap(x, by):
    size = lax.axis_size("fsdp")
    return lax.ppermute(x, "fsdp", [(i, i ^ by) for i in range(size)])


def core_swap(x):
    size = lax.axis_size("ctx")
    return lax.ppermute(x, "ctx", [(i, i ^ 1) for i in range(size)])


def shifted(x, by):
    size = lax.axis_size("ctx")
    return lax.ppermute(x, "ctx", [(i, i + by) for i in range(size) if 0 <= i + by < size])


def bit_reversed(count):
    order = [0]
    while len(order) < count:
        order = [2 * k for k in order] + [2 * k + 1 for k in order]
    return order


def columns_at(x, index, width):
    return lax.dynamic_slice_in_dim(x, index * width, width, 1)


def placed(pieces):
    width = pieces[0][1].shape[1]
    whole = jnp.zeros((pieces[0][1].shape[0], width * len(pieces)), pieces[0][1].dtype)
    for index, piece in pieces:
        whole = lax.dynamic_update_slice_in_dim(whole, piece, index * width, 1)
    return whole


def pair_sum(values):
    while len(values) > 1:
        values = [values[k] + values[k + 1] for k in range(0, len(values), 2)]
    return values[0]


def after(x, *others):
    return lax.optimization_barrier((x,) + others)[0]


def direct_factors(rate, rows, chip, backward):
    factors = [jnp.exp(-rate * float(rows))]
    for s in range(1, lax.axis_size("ctx") // 2):
        gap = (chip ^ s) - chip - 1 if backward else chip - (chip ^ s) - 1
        weight = jnp.exp(-rate * (2 * rows * jnp.maximum(gap, 0)).astype(F32))
        factors.append(jnp.where(gap >= 0, weight, 0.0))
    return factors


def entering_direct(ends, factors, here, backward, ready):
    block = factors[0]
    later_core = ((here & 1) != 0) != backward
    sibling = core_swap(ends)
    total = jnp.where(later_core, block * sibling + ends, block * ends + sibling)
    total = after(total, *ready)
    entering = jnp.zeros_like(ends)
    for s, weight in enumerate(factors[1:], 1):
        entering = entering + weight * chip_swap(total, s)
    return jnp.where(later_core, block * entering + sibling, entering)


def shards(
    query_mr,
    key_mr,
    value_mr,
    query_li,
    key_li,
    mr_taps,
    li_time,
    li_residue,
    li_skip,
    out_weight,
    cotangent,
):
    rows, columns = query_mr.shape
    ctx_count = lax.axis_size("ctx")
    line_count = lax.axis_size("fsdp")
    chips = ctx_count // 2
    here = lax.axis_index("ctx")
    chip, core = here // 2, here % 2
    line = lax.axis_index("fsdp")
    grad_scale = 1.0 / math.sqrt(rows * ctx_count)
    tables = {name: jnp.asarray(table) for name, table in dft_tables(rows).items()}
    width = out_weight.shape[0]
    chip_width = 2 * width
    pass_flops = 2 * (2 * rows) * (2 * rows) * columns

    def tile(x):
        return ("tile", x)

    def table(name):
        return ("whole", tables[name])

    mr_product = (key_mr.astype(F32) * value_mr.astype(F32)).astype(BF16)
    before = shifted(mr_product, 1)
    cot_line = [cotangent] + [line_swap(after(cotangent, mr_product), r) for r in range(1, line_count)]
    pairs = chips // 2
    pair = chip // 2
    pair_width = 4 * width

    rate = 1.0 / after(li_time, mr_product)
    beside = chip_swap(after(out_weight, before), 1)
    coef = li_residue * jnp.sqrt(-jnp.expm1(-2.0 * rate))
    back_factors = lax.optimization_barrier(direct_factors(rate, rows, here // 2, True))
    mr_spec, li_spec = run(
        spectra_body,
        columns,
        [tile(mr_taps), tile(rate), tile(coef), tile(li_skip[None, :]), table("ahead")],
        [(2 * rows, F32), (2 * rows, F32)],
        0,
    )
    spec, mr_conv, mixed_mr, li_inner, ends = run(
        short_body,
        columns,
        [
            tile(before),
            tile(mr_product),
            tile(query_mr),
            tile(key_li),
            tile(mr_spec),
            tile(li_spec),
            tile(rate),
            table("ahead"),
            table("back"),
        ],
        [(2 * rows, F32), (rows, F32), (rows, BF16), (rows, F32), (rate.shape[0], F32)],
        0,
    )

    states = lax.all_gather(after(ends, beside, *cot_line), "ctx").reshape(-1, columns)
    line_width = cotangent.shape[1]
    whole_width = line_width * line_count
    split_starts = [(line ^ r) * line_width for r in range(line_count)]
    split_starts += [(pair ^ h) * pair_width for h in range(pairs)]
    cot_pairs = run_once(
        functools.partial(split_body, pairs),
        [jnp.stack(split_starts)] + [after(piece, states) for piece in cot_line],
        [((rows, pair_width), BF16)] * pairs,
        [pltpu.VMEM((rows, whole_width), BF16)],
    )
    cot_parts = [cot_pairs[0]] + [chip_swap(cot_pairs[h], 2 * h) for h in range(1, pairs)]
    gaps = (here - 1 - jnp.arange(ctx_count, dtype=jnp.int32)).astype(F32)
    li_out, mixed_li = run(
        long_body,
        columns,
        [("scalar", gaps), tile(li_inner), tile(query_li), tile(rate), tile(coef), tile(states)],
        [(rows, F32), (rows, BF16)],
        0,
    )

    mixed_parts = [mixed_li] + [chip_swap(mixed_li, 2 * h) for h in range(1, pairs)]
    weights = [out_weight, core_swap(after(out_weight, mixed_li)), beside, core_swap(after(beside, mixed_li))]
    pair_starts = jnp.stack([((here & 3) ^ m) * width for m in range(4)])

    share_flops = 2 * rows * columns * pair_width * pairs
    grad_own, *grad_sent = run(
        functools.partial(pair_grad_body, pairs),
        columns,
        [("scalar", pair_starts)] + [("whole", after(part, mixed_li)) for part in cot_parts] + [tile(weight) for weight in weights],
        [(rows, F32)] + [(rows, BF16)] * (pairs - 1),
        share_flops,
    )
    grad_parts = [chip_swap(part, 2 * h) for h, part in enumerate(grad_sent, 1)]

    out_own, *out_sent = run_once(
        functools.partial(pair_out_body, pairs),
        [pair_starts, after(mixed_parts[0], grad_own)] + mixed_parts[1:] + weights,
        [((rows, pair_width), BF16)] * pairs,
    )
    out_pairs = [out_own] + [chip_swap(after(part, *grad_parts), 2 * h) for h, part in enumerate(out_sent, 1)]
    out_starts = [(pair ^ h) * pair_width for h in range(pairs)]
    out_starts += [(line ^ r) * line_width for r in bit_reversed(line_count)]
    kept, odd = run_once(
        functools.partial(stack_body, line_count),
        [jnp.stack(out_starts)] + out_pairs,
        [((line_count // 2 * rows, line_width), BF16)] * 2,
        [pltpu.VMEM((rows, whole_width), BF16)],
    )
    count, by = line_count // 2, 1
    first_out = arrived_out = line_swap(odd, by)
    while count > 1:
        count //= 2
        by *= 2
        total = kept.astype(F32) + arrived_out.astype(F32)
        kept, arrived_out = total[: count * rows], line_swap(total[count * rows :].astype(BF16), by)
    output = kept.astype(F32) + arrived_out.astype(F32)

    side = chip % 2
    used = [after(part, grad_own) for part in cot_parts]
    near_cot = jnp.concatenate([columns_at(part, side, chip_width) for part in used], axis=0)
    far_cot = jnp.concatenate([columns_at(part, 1 - side, chip_width) for part in used], axis=0)
    got_cot = chip_swap(far_cot, 1)
    near_mixed = jnp.concatenate([after(part, grad_own) for part in mixed_parts], axis=0)
    got_mixed = chip_swap(near_mixed, 1)

    grad_query_li, back_ends, grad_inner = run(
        functools.partial(grad_gate_body, pairs - 1),
        columns,
        [
            tile(after(grad_own, out_own)),
            tile(query_li),
            tile(rate),
            tile(li_out),
            tile(li_spec),
            table("ahead"),
            table("back"),
        ]
        + [tile(part) for part in grad_parts],
        [(rows, F32), (rate.shape[0], F32), (rows, F32)],
        4 * pass_flops,
    )
    back_entering = entering_direct(
        back_ends, back_factors, here, True, [got_cot, got_mixed] + out_pairs[1:]
    )
    cot_rows = jnp.concatenate([near_cot, after(got_cot, back_ends)], axis=0)
    mixed_rows = jnp.concatenate([near_mixed, after(got_mixed, back_ends)], axis=0)

    def weight_share(which):
        return lax.dot_general(
            columns_at(cot_rows, which, width),
            mixed_rows,
            (((0,), (0,)), ((), ())),
            preferred_element_type=F32,
        )

    sent_share = weight_share(1 - core).astype(BF16)
    far_share = core_swap(sent_share)
    grad_weight = (weight_share(core) + far_share.astype(F32)) * grad_scale
    grad_key_li, grad_query_mr, grad_spec, tap_partial = run(
        grad_long_body,
        columns,
        [
            tile(after(grad_inner, sent_share)),
            tile(rate),
            tile(coef),
            tile(back_entering),
            tile(mixed_mr),
            tile(key_li),
            tile(query_mr),
            tile(mr_conv),
            tile(spec),
            table("ahead"),
            table("lags"),
        ],
        [(rows, F32), (rows, F32), (2 * rows, F32), (rows, F32)],
        4 * pass_flops,
    )
    grad_spec = after(grad_spec, first_out)
    own_product, prev_product = run(
        grad_taps_body,
        columns,
        [tile(grad_spec), tile(mr_spec), table("back")],
        [(rows, F32), (rows, BF16)],
        3 * pass_flops,
    )
    arrived = shifted(prev_product, -1)
    grad_key_mr, grad_value_mr = run(
        grad_product_body,
        columns,
        [tile(own_product), tile(arrived), tile(key_mr), tile(value_mr)],
        [(rows, F32), (rows, F32)],
        rows * columns,
    )

    tap_half = tap_partial.shape[0] // 2
    halves = tap_partial.reshape(2, tap_half, columns)
    own_half = lax.dynamic_index_in_dim(halves, core, 0, keepdims=False)
    far_half = lax.dynamic_index_in_dim(halves, 1 - core, 0, keepdims=False)
    chip_half = (own_half + core_swap(far_half)).astype(BF16)
    everywhere = [after(chip_half, prev_product, grad_weight)] + [chip_swap(chip_half, s) for s in range(1, chips)]
    plane_half = pair_sum([part.astype(F32) for part in everywhere]) * grad_scale
    other_half = core_swap(after(plane_half, arrived_out))
    grad_taps = jnp.where(
        core == 0,
        jnp.concatenate([plane_half, other_half], axis=0),
        jnp.concatenate([other_half, plane_half], axis=0),
    )

    return (
        output,
        grad_query_mr,
        grad_key_mr,
        grad_value_mr,
        grad_query_li,
        grad_key_li,
        grad_taps,
        grad_weight,
    )


def solution(mesh):
    rows = P("ctx", "fsdp")
    channels = P(None, "fsdp")
    return jax.shard_map(
        shards,
        mesh=mesh,
        in_specs=(rows,) * 5 + (channels,) * 3 + (P("fsdp"),) + (rows,) * 2,
        out_specs=(rows,) * 6 + (channels, rows),
        check_vma=False,
    )
```

```python
import functools
import math

import jax
import jax.numpy as jnp
import ml_dtypes
import numpy as np
from jax import lax
from jax.experimental import pallas as pl
from jax.experimental.pallas import tpu as pltpu
from jax.sharding import PartitionSpec as P

F32 = jnp.float32
BF16 = jnp.bfloat16
BLOCK = 512
TILE = 256
GROUP = 8


def split_parts(matrix):
    high = matrix.astype(ml_dtypes.bfloat16)
    low = (matrix - high.astype(np.float64)).astype(ml_dtypes.bfloat16)
    return high, low


def two_fold(matrix):
    high, low = split_parts(matrix)
    return np.concatenate([high, low], axis=1)


def three_fold(matrix):
    high, low = split_parts(matrix)
    return np.concatenate([high, low, high], axis=1)


@functools.lru_cache(maxsize=None)
def dft_tables(rows):
    size = 2 * rows
    angle = 2.0 * np.pi * (np.arange(rows)[:, None] + 0.5) * np.arange(size)[None, :] / size
    ahead = np.concatenate([np.cos(angle), -np.sin(angle)], axis=0)
    back = ahead.T * (2.0 / size)
    signed = np.concatenate([back[:rows], -back[rows:]], axis=0)
    lags = back[rows - np.arange(rows)]
    return {"ahead": two_fold(ahead), "back": three_fold(signed), "lags": three_fold(lags)}


def half_table(ahead):
    rows = ahead.shape[0] // 2
    high, low = ahead[:, :rows], ahead[:, 2 * rows : 3 * rows]
    return high, low


def apply2(table, x):
    return jnp.dot(table, jnp.concatenate([x, x], axis=0), preferred_element_type=F32)


def apply3(table, x):
    high = x.astype(BF16)
    low = (x - high.astype(F32)).astype(BF16)
    return jnp.dot(table, jnp.concatenate([high, high, low], axis=0), preferred_element_type=F32)


def to_spectrum(ahead, x):
    high, low = half_table(ahead)
    return apply3(jnp.concatenate([high, low, high], axis=1), x)


def to_spectrum_exact(ahead, x):
    return apply2(jnp.concatenate(half_table(ahead), axis=1), x)


def times(x, y):
    half = x.shape[0] // 2
    xr, xi, yr, yi = x[:half], x[half:], y[:half], y[half:]
    return jnp.concatenate([xr * yr - xi * yi, xr * yi + xi * yr], axis=0)


def times_conj(x, y):
    half = x.shape[0] // 2
    xr, xi, yr, yi = x[:half], x[half:], y[:half], y[half:]
    return jnp.concatenate([xr * yr + xi * yi, xi * yr - xr * yi], axis=0)


def group_places(columns):
    return lax.broadcasted_iota(jnp.int32, (GROUP, columns), 0).astype(F32)


def spread_modes(rate, weight, rows, shift, backward):
    columns = rate.shape[1]
    places = group_places(columns)
    if backward:
        places = (GROUP - 1.0) - places
    count = rows // GROUP
    order = range(count - 1, -1, -1) if backward else range(count)
    sums = [None] * count
    for m in range(rate.shape[0]):
        rate_m = rate[m : m + 1]
        current = weight[m : m + 1] * jnp.exp(-rate_m * (places + shift))
        stride = jnp.broadcast_to(jnp.exp(-rate_m * GROUP), current.shape)
        for step, g in enumerate(order):
            sums[g] = current if sums[g] is None else sums[g] + current
            if step < count - 1:
                current = current * stride
    return jnp.concatenate(sums, axis=0)


def fold_modes(signal, rate, backward):
    columns = rate.shape[1]
    places = group_places(columns)
    if not backward:
        places = (GROUP - 1.0) - places
    count = signal.shape[0] // GROUP
    order = range(count - 1, -1, -1) if backward else range(count)
    found = []
    for m in range(rate.shape[0]):
        rate_m = rate[m : m + 1]
        stride = jnp.broadcast_to(jnp.exp(-rate_m * GROUP), (GROUP, columns))
        running = None
        for g in order:
            piece = signal[g * GROUP : (g + 1) * GROUP]
            running = piece if running is None else running * stride + piece
        found.append(jnp.sum(running * jnp.exp(-rate_m * places), axis=0, keepdims=True))
    return jnp.concatenate(found, axis=0)


def spectra_body(taps, rate, coef, skip, ahead, mr_spec, li_spec):
    rows = taps.shape[0]
    table = ahead[...]
    mr_spec[...] = to_spectrum(table, taps[...])
    kernel = spread_modes(rate[...], coef[...], rows, 0.0, False)
    first = lax.broadcasted_iota(jnp.int32, kernel.shape, 0) == 0
    kernel = kernel + jnp.where(first, skip[...], 0.0)
    li_spec[...] = to_spectrum(table, kernel)


def short_body(before, product, query, key, mr_spec, li_spec, rate, ahead, back, spec, conv, mixed, inner, ends):
    rows = product.shape[0]
    x = jnp.concatenate([before[...], product[...]], axis=0)
    found = apply2(ahead[...], x)
    spec[...] = found
    filtered = -apply3(back[rows:], times(found, mr_spec[...]))
    conv[...] = filtered
    mixed_rows = (query[...].astype(F32) * filtered).astype(BF16)
    mixed[...] = mixed_rows
    rounded = (key[...].astype(F32) * mixed_rows.astype(F32)).astype(BF16)
    ends[...] = fold_modes(rounded.astype(F32), rate[...], False)
    inner[...] = apply3(back[:rows], times(to_spectrum_exact(ahead[...], rounded), li_spec[...]))


def gather_states(rate, gaps, states, rows):
    modes = rate.shape[0]
    total = jnp.zeros_like(rate)
    for k in range(states.shape[0] // modes):
        weight = jnp.exp(-rate * (jnp.maximum(gaps[k], 0.0) * float(rows)))
        total = total + jnp.where(gaps[k] >= 0.0, weight * states[k * modes : (k + 1) * modes], 0.0)
    return total


def long_body(gaps, inner, query, rate, coef, states, li_out, mixed):
    rows = inner.shape[0]
    entering = gather_states(rate[...], gaps, states, rows)
    total = inner[...] + spread_modes(rate[...], coef[...] * entering, rows, 1.0, False)
    li_out[...] = total
    mixed[...] = (query[...].astype(F32) * total).astype(BF16)


def split_body(count, base, starts, *rest):
    pieces, parts, whole = rest[: -count - 1], rest[-count - 1 : -1], rest[-1]
    for r, piece in enumerate(pieces):
        whole[:, pl.ds(pl.multiple_of(starts[base + r], 128), piece.shape[1])] = piece[...]
    for h, part in enumerate(parts):
        place = pl.multiple_of(starts[base + len(pieces) + h], 128)
        part[...] = whole[:, pl.ds(place, part.shape[1])]


def pair_grad_body(count, base, starts, *rest):
    parts, weights, results = rest[:count], rest[count : count + 4], rest[count + 4 :]
    rows = parts[0].shape[0]
    total = None
    for m, weight in enumerate(weights):
        place = pl.ds(pl.multiple_of(starts[base + m], 128), weight.shape[0])
        block = jnp.concatenate([part[:, place] for part in parts], axis=0)
        found = jnp.dot(block, weight[...], preferred_element_type=F32)
        total = found if total is None else total + found
    for h, result in enumerate(results):
        result[...] = total[h * rows : (h + 1) * rows].astype(result.dtype)


def pair_out_body(count, base, starts, *rest):
    mixed, weights, results = rest[:count], rest[count : count + 4], rest[count + 4 :]
    rows = mixed[0].shape[0]
    block = jnp.concatenate([part[...] for part in mixed], axis=0)
    for m, weight in enumerate(weights):
        place = pl.ds(pl.multiple_of(starts[base + m], 128), weight.shape[0])
        found = lax.dot_general(block, weight[...], (((1,), (1,)), ((), ())), preferred_element_type=F32)
        for h, result in enumerate(results):
            result[:, place] = found[h * rows : (h + 1) * rows].astype(BF16)


def stack_body(count, base, starts, *rest):
    pieces, stacks, whole = rest[:-3], rest[-3:-1], rest[-1]
    rows = whole.shape[0]
    for r, piece in enumerate(pieces):
        whole[:, pl.ds(pl.multiple_of(starts[base + r], 128), piece.shape[1])] = piece[...]
    for h in range(count):
        place = pl.multiple_of(starts[base + len(pieces) + h], 128)
        stack, at = stacks[h // (count // 2)], h % (count // 2)
        stack[at * rows : (at + 1) * rows] = whole[:, pl.ds(place, stack.shape[1])]


def grad_gate_body(count, own, query, rate, li_out, li_spec, ahead, back, *rest):
    parts, (grad_query, ends, inner) = rest[:count], rest[count:]
    rows = own.shape[0]
    total = own[...]
    for part in parts:
        total = total + part[...].astype(F32)
    grad_query[...] = total * li_out[...]
    gated = total * query[...].astype(F32)
    ends[...] = fold_modes(gated, rate[...], True)
    inner[...] = apply3(back[:rows], times_conj(to_spectrum(ahead[...], gated), li_spec[...]))


def grad_long_body(
    inner, rate, coef, entering, mixed_mr, key_li, query_mr, conv, spec, ahead, lags,
    grad_key_li, grad_query_mr, grad_spec, taps,
):
    rows = inner.shape[0]
    grad_input = inner[...] + spread_modes(rate[...], coef[...] * entering[...], rows, 1.0, True)
    grad_key_li[...] = grad_input * mixed_mr[...].astype(F32)
    grad_mixed_mr = grad_input * key_li[...].astype(F32)
    grad_query_mr[...] = grad_mixed_mr * conv[...]
    grad_conv = grad_mixed_mr * query_mr[...].astype(F32)
    found = to_spectrum(ahead[...], grad_conv)
    grad_spec[...] = found
    taps[...] = apply3(lags[...], times_conj(spec[...], found))


def grad_taps_body(grad_spec, mr_spec, back, own_product, prev_product):
    rows = own_product.shape[0]
    products = apply3(back[...], times_conj(grad_spec[...], mr_spec[...]))
    own_product[...] = products[:rows]
    prev_product[...] = products[rows:].astype(BF16)


def grad_product_body(own, arrived, key, value, grad_key, grad_value):
    total = own[...] + arrived[...].astype(F32)
    grad_key[...] = total * value[...].astype(F32)
    grad_value[...] = total * key[...].astype(F32)


def run(body, columns, inputs, outputs, flops):
    block = min(BLOCK, columns)
    tile = min(TILE, block)
    in_specs = []
    moved = 0
    for kind, array in inputs:
        if kind == "tile":
            in_specs.append(pl.BlockSpec((array.shape[0], block), lambda c: (0, c)))
        elif kind == "whole":
            in_specs.append(pl.BlockSpec(array.shape, lambda c: (0, 0)))
        else:
            in_specs.append(pl.BlockSpec(memory_space=pltpu.SMEM))
        moved += math.prod(array.shape) * array.dtype.itemsize
    for rows, dtype in outputs:
        moved += rows * columns * jnp.dtype(dtype).itemsize
    tiled = [kind == "tile" for kind, _ in inputs] + [True] * len(outputs)

    def body_by_tiles(*refs):
        for first in range(0, block, tile):
            body(*[ref.at[:, pl.ds(first, tile)] if cut else ref for ref, cut in zip(refs, tiled)])

    return pl.pallas_call(
        body_by_tiles,
        grid=(columns // block,),
        in_specs=in_specs,
        out_specs=[pl.BlockSpec((rows, block), lambda c: (0, c)) for rows, _ in outputs],
        out_shape=[jax.ShapeDtypeStruct((rows, columns), dtype) for rows, dtype in outputs],
        compiler_params=pltpu.CompilerParams(vmem_limit_bytes=56 * 1024 * 1024),
        cost_estimate=pl.CostEstimate(flops=flops, bytes_accessed=moved if flops else 0, transcendentals=0),
    )(*[array for _, array in inputs])


def run_once(body, inputs, outputs, scratch=()):
    def block(shape):
        return pl.BlockSpec(shape, lambda c: (0, 0))

    return pl.pallas_call(
        body,
        grid=(1,),
        in_specs=[pl.BlockSpec(memory_space=pltpu.SMEM)] + [block(array.shape) for array in inputs[1:]],
        out_specs=[block(shape) for shape, _ in outputs],
        out_shape=[jax.ShapeDtypeStruct(shape, dtype) for shape, dtype in outputs],
        scratch_shapes=scratch,
        compiler_params=pltpu.CompilerParams(vmem_limit_bytes=56 * 1024 * 1024),
        cost_estimate=pl.CostEstimate(flops=0, bytes_accessed=0, transcendentals=0),
    )(*inputs)


def chip_swap(x, by):
    size = lax.axis_size("ctx")
    return lax.ppermute(x, "ctx", [(i, i ^ (2 * by)) for i in range(size)])


def line_swap(x, by):
    size = lax.axis_size("fsdp")
    return lax.ppermute(x, "fsdp", [(i, i ^ by) for i in range(size)])


def core_swap(x):
    size = lax.axis_size("ctx")
    return lax.ppermute(x, "ctx", [(i, i ^ 1) for i in range(size)])


def shifted(x, by):
    size = lax.axis_size("ctx")
    return lax.ppermute(x, "ctx", [(i, i + by) for i in range(size) if 0 <= i + by < size])


def bit_reversed(count):
    order = [0]
    while len(order) < count:
        order = [2 * k for k in order] + [2 * k + 1 for k in order]
    return order


def columns_at(x, index, width):
    return lax.dynamic_slice_in_dim(x, index * width, width, 1)


def placed(pieces):
    width = pieces[0][1].shape[1]
    whole = jnp.zeros((pieces[0][1].shape[0], width * len(pieces)), pieces[0][1].dtype)
    for index, piece in pieces:
        whole = lax.dynamic_update_slice_in_dim(whole, piece, index * width, 1)
    return whole


def pair_sum(values):
    while len(values) > 1:
        values = [values[k] + values[k + 1] for k in range(0, len(values), 2)]
    return values[0]


def after(x, *others):
    return lax.optimization_barrier((x,) + others)[0]


def direct_factors(rate, rows, chip, backward):
    factors = [jnp.exp(-rate * float(rows))]
    for s in range(1, lax.axis_size("ctx") // 2):
        gap = (chip ^ s) - chip - 1 if backward else chip - (chip ^ s) - 1
        weight = jnp.exp(-rate * (2 * rows * jnp.maximum(gap, 0)).astype(F32))
        factors.append(jnp.where(gap >= 0, weight, 0.0))
    return factors


def entering_direct(ends, factors, here, backward, ready):
    block = factors[0]
    later_core = ((here & 1) != 0) != backward
    sibling = core_swap(ends)
    total = jnp.where(later_core, block * sibling + ends, block * ends + sibling)
    total = after(total, *ready)
    entering = jnp.zeros_like(ends)
    for s, weight in enumerate(factors[1:], 1):
        entering = entering + weight * chip_swap(total, s)
    return jnp.where(later_core, block * entering + sibling, entering)


def shards(
    query_mr,
    key_mr,
    value_mr,
    query_li,
    key_li,
    mr_taps,
    li_time,
    li_residue,
    li_skip,
    out_weight,
    cotangent,
):
    rows, columns = query_mr.shape
    ctx_count = lax.axis_size("ctx")
    line_count = lax.axis_size("fsdp")
    chips = ctx_count // 2
    here = lax.axis_index("ctx")
    chip, core = here // 2, here % 2
    line = lax.axis_index("fsdp")
    grad_scale = 1.0 / math.sqrt(rows * ctx_count)
    tables = {name: jnp.asarray(table) for name, table in dft_tables(rows).items()}
    width = out_weight.shape[0]
    chip_width = 2 * width
    pass_flops = 2 * (2 * rows) * (2 * rows) * columns

    def tile(x):
        return ("tile", x)

    def table(name):
        return ("whole", tables[name])

    mr_product = (key_mr.astype(F32) * value_mr.astype(F32)).astype(BF16)
    before = shifted(mr_product, 1)
    cot_line = [cotangent] + [line_swap(after(cotangent, mr_product), r) for r in range(1, line_count)]
    pairs = chips // 2
    pair = chip // 2
    pair_width = 4 * width

    sibling_weight = core_swap(out_weight)
    line_width = cotangent.shape[1]
    places = [(line ^ r) * line_width for r in range(line_count)] + [(pair ^ h) * pair_width for h in range(pairs)]
    pair_base = len(places)
    places += [((here & 3) ^ m) * width for m in range(4)]
    out_base = len(places)
    places += [(pair ^ h) * pair_width for h in range(pairs)]
    places += [(line ^ r) * line_width for r in bit_reversed(line_count)]
    starts = jnp.stack(places)

    rate = 1.0 / after(li_time, mr_product)
    beside = chip_swap(after(out_weight, before), 1)
    coef = li_residue * jnp.sqrt(-jnp.expm1(-2.0 * rate))
    back_factors = lax.optimization_barrier(direct_factors(rate, rows, here // 2, True))
    mr_spec, li_spec = run(
        spectra_body,
        columns,
        [tile(mr_taps), tile(rate), tile(coef), tile(li_skip[None, :]), table("ahead")],
        [(2 * rows, F32), (2 * rows, F32)],
        0,
    )
    spec, mr_conv, mixed_mr, li_inner, ends = run(
        short_body,
        columns,
        [
            tile(after(before, sibling_weight)),
            tile(mr_product),
            tile(query_mr),
            tile(key_li),
            tile(mr_spec),
            tile(li_spec),
            tile(rate),
            table("ahead"),
            table("back"),
        ],
        [(2 * rows, F32), (rows, F32), (rows, BF16), (rows, F32), (rate.shape[0], F32)],
        0,
    )

    whole_width = line_width * line_count
    cot_pairs = run_once(
        functools.partial(split_body, pairs, 0),
        [starts] + [after(piece, ends) for piece in cot_line],
        [((rows, pair_width), BF16)] * pairs,
        [pltpu.VMEM((rows, whole_width), BF16)],
    )
    cot_parts = [cot_pairs[0]] + [chip_swap(cot_pairs[h], 2 * h) for h in range(1, pairs)]
    states = lax.all_gather(after(ends, beside, *cot_parts[:1]), "ctx").reshape(-1, columns)
    gaps = (here - 1 - jnp.arange(ctx_count, dtype=jnp.int32)).astype(F32)
    li_out, mixed_li = run(
        long_body,
        columns,
        [("scalar", gaps), tile(li_inner), tile(query_li), tile(rate), tile(coef), tile(states)],
        [(rows, F32), (rows, BF16)],
        0,
    )

    mixed_parts = [mixed_li] + [chip_swap(mixed_li, 2 * h) for h in range(1, pairs)]
    weights = [out_weight, sibling_weight, beside, core_swap(after(beside, cot_pairs[0]))]

    share_flops = 2 * rows * columns * pair_width * pairs
    grad_own, *grad_sent = run(
        functools.partial(pair_grad_body, pairs, pair_base),
        columns,
        [("scalar", starts)] + [("whole", after(part, mixed_li)) for part in cot_parts] + [tile(weight) for weight in weights],
        [(rows, F32)] + [(rows, BF16)] * (pairs - 1),
        share_flops,
    )
    grad_parts = [chip_swap(part, 2 * h) for h, part in enumerate(grad_sent, 1)]

    out_own, *out_sent = run_once(
        functools.partial(pair_out_body, pairs, pair_base),
        [starts, after(mixed_parts[0], grad_own)] + mixed_parts[1:] + weights,
        [((rows, pair_width), BF16)] * pairs,
    )
    out_pairs = [out_own] + [chip_swap(after(part, *grad_parts), 2 * h) for h, part in enumerate(out_sent, 1)]
    kept, odd = run_once(
        functools.partial(stack_body, line_count, out_base),
        [starts] + out_pairs,
        [((line_count // 2 * rows, line_width), BF16)] * 2,
        [pltpu.VMEM((rows, whole_width), BF16)],
    )
    count, by = line_count // 2, 1
    first_out = arrived_out = line_swap(odd, by)
    while count > 1:
        count //= 2
        by *= 2
        total = kept.astype(F32) + arrived_out.astype(F32)
        kept, arrived_out = total[: count * rows], line_swap(total[count * rows :].astype(BF16), by)
    output = kept.astype(F32) + arrived_out.astype(F32)

    side = chip % 2
    used = [after(part, mixed_li) for part in cot_parts]
    near_cot = jnp.concatenate([columns_at(part, side, chip_width) for part in used], axis=0)
    far_cot = jnp.concatenate([columns_at(part, 1 - side, chip_width) for part in used], axis=0)
    got_cot = chip_swap(far_cot, 1)
    near_mixed = jnp.concatenate([after(part, grad_own) for part in mixed_parts], axis=0)
    got_mixed = chip_swap(near_mixed, 1)

    grad_query_li, back_ends, grad_inner = run(
        functools.partial(grad_gate_body, pairs - 1),
        columns,
        [
            tile(after(grad_own, out_own)),
            tile(query_li),
            tile(rate),
            tile(li_out),
            tile(li_spec),
            table("ahead"),
            table("back"),
        ]
        + [tile(part) for part in grad_parts],
        [(rows, F32), (rate.shape[0], F32), (rows, F32)],
        4 * pass_flops,
    )
    back_entering = entering_direct(
        back_ends, back_factors, here, True, [got_cot, got_mixed] + out_pairs[1:]
    )
    cot_rows = jnp.concatenate([near_cot, after(got_cot, back_ends)], axis=0)
    mixed_rows = jnp.concatenate([near_mixed, after(got_mixed, back_ends)], axis=0)

    def weight_share(which):
        return lax.dot_general(
            columns_at(cot_rows, which, width),
            mixed_rows,
            (((0,), (0,)), ((), ())),
            preferred_element_type=F32,
        )

    sent_share = weight_share(1 - core).astype(BF16)
    far_share = core_swap(sent_share)
    grad_weight = (weight_share(core) + far_share.astype(F32)) * grad_scale
    grad_key_li, grad_query_mr, grad_spec, tap_partial = run(
        grad_long_body,
        columns,
        [
            tile(after(grad_inner, sent_share)),
            tile(rate),
            tile(coef),
            tile(back_entering),
            tile(mixed_mr),
            tile(key_li),
            tile(query_mr),
            tile(mr_conv),
            tile(spec),
            table("ahead"),
            table("lags"),
        ],
        [(rows, F32), (rows, F32), (2 * rows, F32), (rows, F32)],
        4 * pass_flops,
    )
    grad_spec = after(grad_spec, first_out)
    own_product, prev_product = run(
        grad_taps_body,
        columns,
        [tile(grad_spec), tile(mr_spec), table("back")],
        [(rows, F32), (rows, BF16)],
        3 * pass_flops,
    )
    arrived = shifted(prev_product, -1)
    grad_key_mr, grad_value_mr = run(
        grad_product_body,
        columns,
        [tile(own_product), tile(arrived), tile(key_mr), tile(value_mr)],
        [(rows, F32), (rows, F32)],
        rows * columns,
    )

    tap_half = tap_partial.shape[0] // 2
    halves = tap_partial.reshape(2, tap_half, columns)
    own_half = lax.dynamic_index_in_dim(halves, core, 0, keepdims=False)
    far_half = lax.dynamic_index_in_dim(halves, 1 - core, 0, keepdims=False)
    chip_half = (own_half + core_swap(far_half)).astype(BF16)
    everywhere = [after(chip_half, prev_product, grad_weight)] + [chip_swap(chip_half, s) for s in range(1, chips)]
    plane_half = pair_sum([part.astype(F32) for part in everywhere]) * grad_scale
    other_half = core_swap(after(plane_half, arrived_out))
    grad_taps = jnp.where(
        core == 0,
        jnp.concatenate([plane_half, other_half], axis=0),
        jnp.concatenate([other_half, plane_half], axis=0),
    )

    return (
        output,
        grad_query_mr,
        grad_key_mr,
        grad_value_mr,
        grad_query_li,
        grad_key_li,
        grad_taps,
        grad_weight,
    )


def solution(mesh):
    rows = P("ctx", "fsdp")
    channels = P(None, "fsdp")
    return jax.shard_map(
        shards,
        mesh=mesh,
        in_specs=(rows,) * 5 + (channels,) * 3 + (P("fsdp"),) + (rows,) * 2,
        out_specs=(rows,) * 6 + (channels, rows),
        check_vma=False,
    )
```

```python
import functools
import math

import jax
import jax.numpy as jnp
import ml_dtypes
import numpy as np
from jax import lax
from jax.experimental import pallas as pl
from jax.experimental.pallas import tpu as pltpu
from jax.sharding import PartitionSpec as P

F32 = jnp.float32
BF16 = jnp.bfloat16
BLOCK = 512
TILE = 256
GROUP = 8


def split_parts(matrix):
    high = matrix.astype(ml_dtypes.bfloat16)
    low = (matrix - high.astype(np.float64)).astype(ml_dtypes.bfloat16)
    return high, low


def two_fold(matrix):
    high, low = split_parts(matrix)
    return np.concatenate([high, low], axis=1)


def three_fold(matrix):
    high, low = split_parts(matrix)
    return np.concatenate([high, low, high], axis=1)


@functools.lru_cache(maxsize=None)
def dft_tables(rows):
    size = 2 * rows
    angle = 2.0 * np.pi * (np.arange(rows)[:, None] + 0.5) * np.arange(size)[None, :] / size
    ahead = np.concatenate([np.cos(angle), -np.sin(angle)], axis=0)
    back = ahead.T * (2.0 / size)
    signed = np.concatenate([back[:rows], -back[rows:]], axis=0)
    lags = back[rows - np.arange(rows)]
    return {"ahead": two_fold(ahead), "back": three_fold(signed), "lags": three_fold(lags)}


def half_table(ahead):
    rows = ahead.shape[0] // 2
    high, low = ahead[:, :rows], ahead[:, 2 * rows : 3 * rows]
    return high, low


def apply2(table, x):
    return jnp.dot(table, jnp.concatenate([x, x], axis=0), preferred_element_type=F32)


def apply3(table, x):
    high = x.astype(BF16)
    low = (x - high.astype(F32)).astype(BF16)
    return jnp.dot(table, jnp.concatenate([high, high, low], axis=0), preferred_element_type=F32)


def to_spectrum(ahead, x):
    high, low = half_table(ahead)
    return apply3(jnp.concatenate([high, low, high], axis=1), x)


def to_spectrum_exact(ahead, x):
    return apply2(jnp.concatenate(half_table(ahead), axis=1), x)


def times(x, y):
    half = x.shape[0] // 2
    xr, xi, yr, yi = x[:half], x[half:], y[:half], y[half:]
    return jnp.concatenate([xr * yr - xi * yi, xr * yi + xi * yr], axis=0)


def times_conj(x, y):
    half = x.shape[0] // 2
    xr, xi, yr, yi = x[:half], x[half:], y[:half], y[half:]
    return jnp.concatenate([xr * yr + xi * yi, xi * yr - xr * yi], axis=0)


def group_places(columns):
    return lax.broadcasted_iota(jnp.int32, (GROUP, columns), 0).astype(F32)


def spread_modes(rate, weight, rows, shift, backward):
    columns = rate.shape[1]
    places = group_places(columns)
    if backward:
        places = (GROUP - 1.0) - places
    count = rows // GROUP
    order = range(count - 1, -1, -1) if backward else range(count)
    sums = [None] * count
    for m in range(rate.shape[0]):
        rate_m = rate[m : m + 1]
        current = weight[m : m + 1] * jnp.exp(-rate_m * (places + shift))
        stride = jnp.broadcast_to(jnp.exp(-rate_m * GROUP), current.shape)
        for step, g in enumerate(order):
            sums[g] = current if sums[g] is None else sums[g] + current
            if step < count - 1:
                current = current * stride
    return jnp.concatenate(sums, axis=0)


def fold_modes(signal, rate, backward):
    columns = rate.shape[1]
    places = group_places(columns)
    if not backward:
        places = (GROUP - 1.0) - places
    count = signal.shape[0] // GROUP
    order = range(count - 1, -1, -1) if backward else range(count)
    found = []
    for m in range(rate.shape[0]):
        rate_m = rate[m : m + 1]
        stride = jnp.broadcast_to(jnp.exp(-rate_m * GROUP), (GROUP, columns))
        running = None
        for g in order:
            piece = signal[g * GROUP : (g + 1) * GROUP]
            running = piece if running is None else running * stride + piece
        found.append(jnp.sum(running * jnp.exp(-rate_m * places), axis=0, keepdims=True))
    return jnp.concatenate(found, axis=0)


def spectra_body(taps, rate, coef, skip, ahead, mr_spec, li_spec):
    rows = taps.shape[0]
    table = ahead[...]
    mr_spec[...] = to_spectrum(table, taps[...])
    kernel = spread_modes(rate[...], coef[...], rows, 0.0, False)
    first = lax.broadcasted_iota(jnp.int32, kernel.shape, 0) == 0
    kernel = kernel + jnp.where(first, skip[...], 0.0)
    li_spec[...] = to_spectrum(table, kernel)


def short_body(before, product, query, key, mr_spec, li_spec, rate, ahead, back, spec, conv, mixed, inner, ends):
    rows = product.shape[0]
    x = jnp.concatenate([before[...], product[...]], axis=0)
    found = apply2(ahead[...], x)
    spec[...] = found
    filtered = -apply3(back[rows:], times(found, mr_spec[...]))
    conv[...] = filtered
    mixed_rows = (query[...].astype(F32) * filtered).astype(BF16)
    mixed[...] = mixed_rows
    rounded = (key[...].astype(F32) * mixed_rows.astype(F32)).astype(BF16)
    ends[...] = fold_modes(rounded.astype(F32), rate[...], False)
    inner[...] = apply3(back[:rows], times(to_spectrum_exact(ahead[...], rounded), li_spec[...]))


def gather_states(rate, gaps, states, rows):
    modes = rate.shape[0]
    total = jnp.zeros_like(rate)
    for k in range(states.shape[0] // modes):
        weight = jnp.exp(-rate * (jnp.maximum(gaps[k], 0.0) * float(rows)))
        total = total + jnp.where(gaps[k] >= 0.0, weight * states[k * modes : (k + 1) * modes], 0.0)
    return total


def long_body(gaps, inner, query, rate, coef, states, li_out, mixed):
    rows = inner.shape[0]
    entering = gather_states(rate[...], gaps, states, rows)
    total = inner[...] + spread_modes(rate[...], coef[...] * entering, rows, 1.0, False)
    li_out[...] = total
    mixed[...] = (query[...].astype(F32) * total).astype(BF16)


def split_body(count, base, starts, *rest):
    pieces, parts, whole = rest[: -count - 1], rest[-count - 1 : -1], rest[-1]
    for r, piece in enumerate(pieces):
        whole[:, pl.ds(pl.multiple_of(starts[base + r], 128), piece.shape[1])] = piece[...]
    for h, part in enumerate(parts):
        place = pl.multiple_of(starts[base + len(pieces) + h], 128)
        part[...] = whole[:, pl.ds(place, part.shape[1])]


def pair_grad_body(count, base, starts, *rest):
    parts, weights, results = rest[:count], rest[count : count + 4], rest[count + 4 :]
    rows = parts[0].shape[0]
    total = None
    for m, weight in enumerate(weights):
        place = pl.ds(pl.multiple_of(starts[base + m], 128), weight.shape[0])
        block = jnp.concatenate([part[:, place] for part in parts], axis=0)
        found = jnp.dot(block, weight[...], preferred_element_type=F32)
        total = found if total is None else total + found
    for h, result in enumerate(results):
        result[...] = total[h * rows : (h + 1) * rows].astype(result.dtype)


def pair_out_body(count, base, starts, *rest):
    mixed, weights, results = rest[:count], rest[count : count + 4], rest[count + 4 :]
    rows = mixed[0].shape[0]
    block = jnp.concatenate([part[...] for part in mixed], axis=0)
    for m, weight in enumerate(weights):
        place = pl.ds(pl.multiple_of(starts[base + m], 128), weight.shape[0])
        found = lax.dot_general(block, weight[...], (((1,), (1,)), ((), ())), preferred_element_type=F32)
        for h, result in enumerate(results):
            result[:, place] = found[h * rows : (h + 1) * rows].astype(BF16)


def stack_body(count, base, starts, *rest):
    pieces, stacks, whole = rest[:-3], rest[-3:-1], rest[-1]
    rows = whole.shape[0]
    for r, piece in enumerate(pieces):
        whole[:, pl.ds(pl.multiple_of(starts[base + r], 128), piece.shape[1])] = piece[...]
    for h in range(count):
        place = pl.multiple_of(starts[base + len(pieces) + h], 128)
        stack, at = stacks[h // (count // 2)], h % (count // 2)
        stack[at * rows : (at + 1) * rows] = whole[:, pl.ds(place, stack.shape[1])]


def grad_gate_body(count, own, query, rate, li_out, li_spec, ahead, back, *rest):
    parts, (grad_query, ends, inner) = rest[:count], rest[count:]
    rows = own.shape[0]
    total = own[...]
    for part in parts:
        total = total + part[...].astype(F32)
    grad_query[...] = total * li_out[...]
    gated = total * query[...].astype(F32)
    ends[...] = fold_modes(gated, rate[...], True)
    inner[...] = apply3(back[:rows], times_conj(to_spectrum(ahead[...], gated), li_spec[...]))


def grad_long_body(
    inner, rate, coef, entering, mixed_mr, key_li, query_mr, conv, spec, ahead, lags,
    grad_key_li, grad_query_mr, grad_spec, taps,
):
    rows = inner.shape[0]
    grad_input = inner[...] + spread_modes(rate[...], coef[...] * entering[...], rows, 1.0, True)
    grad_key_li[...] = grad_input * mixed_mr[...].astype(F32)
    grad_mixed_mr = grad_input * key_li[...].astype(F32)
    grad_query_mr[...] = grad_mixed_mr * conv[...]
    grad_conv = grad_mixed_mr * query_mr[...].astype(F32)
    found = to_spectrum(ahead[...], grad_conv)
    grad_spec[...] = found
    taps[...] = apply3(lags[...], times_conj(spec[...], found))


def grad_taps_body(grad_spec, mr_spec, back, own_product, prev_product):
    rows = own_product.shape[0]
    products = apply3(back[...], times_conj(grad_spec[...], mr_spec[...]))
    own_product[...] = products[:rows]
    prev_product[...] = products[rows:].astype(BF16)


def grad_product_body(own, arrived, key, value, grad_key, grad_value):
    total = own[...] + arrived[...].astype(F32)
    grad_key[...] = total * value[...].astype(F32)
    grad_value[...] = total * key[...].astype(F32)


def run(body, columns, inputs, outputs, flops):
    block = min(BLOCK, columns)
    tile = min(TILE, block)
    in_specs = []
    moved = 0
    for kind, array in inputs:
        if kind == "tile":
            in_specs.append(pl.BlockSpec((array.shape[0], block), lambda c: (0, c)))
        elif kind == "whole":
            in_specs.append(pl.BlockSpec(array.shape, lambda c: (0, 0)))
        else:
            in_specs.append(pl.BlockSpec(memory_space=pltpu.SMEM))
        moved += math.prod(array.shape) * array.dtype.itemsize
    for rows, dtype in outputs:
        moved += rows * columns * jnp.dtype(dtype).itemsize
    tiled = [kind == "tile" for kind, _ in inputs] + [True] * len(outputs)

    def body_by_tiles(*refs):
        for first in range(0, block, tile):
            body(*[ref.at[:, pl.ds(first, tile)] if cut else ref for ref, cut in zip(refs, tiled)])

    return pl.pallas_call(
        body_by_tiles,
        grid=(columns // block,),
        in_specs=in_specs,
        out_specs=[pl.BlockSpec((rows, block), lambda c: (0, c)) for rows, _ in outputs],
        out_shape=[jax.ShapeDtypeStruct((rows, columns), dtype) for rows, dtype in outputs],
        compiler_params=pltpu.CompilerParams(vmem_limit_bytes=56 * 1024 * 1024),
        cost_estimate=pl.CostEstimate(flops=flops, bytes_accessed=moved if flops else 0, transcendentals=0),
    )(*[array for _, array in inputs])


def run_once(body, inputs, outputs, scratch=()):
    def block(shape):
        return pl.BlockSpec(shape, lambda c: (0, 0))

    return pl.pallas_call(
        body,
        grid=(1,),
        in_specs=[pl.BlockSpec(memory_space=pltpu.SMEM)] + [block(array.shape) for array in inputs[1:]],
        out_specs=[block(shape) for shape, _ in outputs],
        out_shape=[jax.ShapeDtypeStruct(shape, dtype) for shape, dtype in outputs],
        scratch_shapes=scratch,
        compiler_params=pltpu.CompilerParams(vmem_limit_bytes=56 * 1024 * 1024),
        cost_estimate=pl.CostEstimate(flops=0, bytes_accessed=0, transcendentals=0),
    )(*inputs)


def chip_swap(x, by):
    size = lax.axis_size("ctx")
    return lax.ppermute(x, "ctx", [(i, i ^ (2 * by)) for i in range(size)])


def line_swap(x, by):
    size = lax.axis_size("fsdp")
    return lax.ppermute(x, "fsdp", [(i, i ^ by) for i in range(size)])


def core_swap(x):
    size = lax.axis_size("ctx")
    return lax.ppermute(x, "ctx", [(i, i ^ 1) for i in range(size)])


def shifted(x, by):
    size = lax.axis_size("ctx")
    return lax.ppermute(x, "ctx", [(i, i + by) for i in range(size) if 0 <= i + by < size])


def bit_reversed(count):
    order = [0]
    while len(order) < count:
        order = [2 * k for k in order] + [2 * k + 1 for k in order]
    return order


def columns_at(x, index, width):
    return lax.dynamic_slice_in_dim(x, index * width, width, 1)


def placed(pieces):
    width = pieces[0][1].shape[1]
    whole = jnp.zeros((pieces[0][1].shape[0], width * len(pieces)), pieces[0][1].dtype)
    for index, piece in pieces:
        whole = lax.dynamic_update_slice_in_dim(whole, piece, index * width, 1)
    return whole


def pair_sum(values):
    while len(values) > 1:
        values = [values[k] + values[k + 1] for k in range(0, len(values), 2)]
    return values[0]


def after(x, *others):
    return lax.optimization_barrier((x,) + others)[0]


def direct_factors(rate, rows, chip, backward):
    factors = [jnp.exp(-rate * float(rows))]
    for s in range(1, lax.axis_size("ctx") // 2):
        gap = (chip ^ s) - chip - 1 if backward else chip - (chip ^ s) - 1
        weight = jnp.exp(-rate * (2 * rows * jnp.maximum(gap, 0)).astype(F32))
        factors.append(jnp.where(gap >= 0, weight, 0.0))
    return factors


def entering_direct(ends, factors, here, backward, ready):
    block = factors[0]
    later_core = ((here & 1) != 0) != backward
    sibling = core_swap(ends)
    total = jnp.where(later_core, block * sibling + ends, block * ends + sibling)
    total = after(total, *ready)
    entering = jnp.zeros_like(ends)
    for s, weight in enumerate(factors[1:], 1):
        entering = entering + weight * chip_swap(total, s)
    return jnp.where(later_core, block * entering + sibling, entering)


def shards(
    query_mr,
    key_mr,
    value_mr,
    query_li,
    key_li,
    mr_taps,
    li_time,
    li_residue,
    li_skip,
    out_weight,
    cotangent,
):
    rows, columns = query_mr.shape
    ctx_count = lax.axis_size("ctx")
    line_count = lax.axis_size("fsdp")
    chips = ctx_count // 2
    here = lax.axis_index("ctx")
    chip, core = here // 2, here % 2
    line = lax.axis_index("fsdp")
    grad_scale = 1.0 / math.sqrt(rows * ctx_count)
    tables = {name: jnp.asarray(table) for name, table in dft_tables(rows).items()}
    width = out_weight.shape[0]
    chip_width = 2 * width
    pass_flops = 2 * (2 * rows) * (2 * rows) * columns

    def tile(x):
        return ("tile", x)

    def table(name):
        return ("whole", tables[name])

    mr_product = (key_mr.astype(F32) * value_mr.astype(F32)).astype(BF16)
    before = shifted(mr_product, 1)
    cot_line = [cotangent] + [line_swap(after(cotangent, mr_product), r) for r in range(1, line_count)]
    pairs = chips // 2
    pair = chip // 2
    pair_width = 4 * width

    sibling_weight = core_swap(out_weight)
    line_width = cotangent.shape[1]
    places = [(line ^ r) * line_width for r in range(line_count)] + [(pair ^ h) * pair_width for h in range(pairs)]
    pair_base = len(places)
    places += [((here & 3) ^ m) * width for m in range(4)]
    out_base = len(places)
    places += [(pair ^ h) * pair_width for h in range(pairs)]
    places += [(line ^ r) * line_width for r in bit_reversed(line_count)]
    starts = jnp.stack(places)

    rate = 1.0 / after(li_time, mr_product)
    beside = chip_swap(after(out_weight, before), 1)
    coef = li_residue * jnp.sqrt(-jnp.expm1(-2.0 * rate))
    back_factors = lax.optimization_barrier(direct_factors(rate, rows, here // 2, True))
    mr_spec, li_spec = run(
        spectra_body,
        columns,
        [tile(mr_taps), tile(rate), tile(coef), tile(li_skip[None, :]), table("ahead")],
        [(2 * rows, F32), (2 * rows, F32)],
        0,
    )
    spec, mr_conv, mixed_mr, li_inner, ends = run(
        short_body,
        columns,
        [
            tile(after(before, sibling_weight)),
            tile(mr_product),
            tile(query_mr),
            tile(key_li),
            tile(mr_spec),
            tile(li_spec),
            tile(rate),
            table("ahead"),
            table("back"),
        ],
        [(2 * rows, F32), (rows, F32), (rows, BF16), (rows, F32), (rate.shape[0], F32)],
        0,
    )

    whole_width = line_width * line_count
    cot_pairs = run_once(
        functools.partial(split_body, pairs, 0),
        [starts] + [after(piece, ends) for piece in cot_line],
        [((rows, pair_width), BF16)] * pairs,
        [pltpu.VMEM((rows, whole_width), BF16)],
    )
    cot_parts = [cot_pairs[0]] + [chip_swap(cot_pairs[h], 2 * h) for h in range(1, pairs)]
    states = lax.all_gather(after(ends, beside, *cot_parts[:1]), "ctx").reshape(-1, columns)
    gaps = (here - 1 - jnp.arange(ctx_count, dtype=jnp.int32)).astype(F32)
    li_out, mixed_li = run(
        long_body,
        columns,
        [("scalar", gaps), tile(li_inner), tile(query_li), tile(rate), tile(coef), tile(states)],
        [(rows, F32), (rows, BF16)],
        0,
    )

    mixed_parts = [mixed_li] + [chip_swap(mixed_li, 2 * h) for h in range(1, pairs)]
    weights = [out_weight, sibling_weight, beside, core_swap(after(beside, cot_pairs[0]))]

    share_flops = 2 * rows * columns * pair_width * pairs
    grad_own, *grad_sent = run(
        functools.partial(pair_grad_body, pairs, pair_base),
        columns,
        [("scalar", starts)] + [("whole", after(part, mixed_li)) for part in cot_parts] + [tile(weight) for weight in weights],
        [(rows, F32)] + [(rows, BF16)] * (pairs - 1),
        share_flops,
    )
    grad_parts = [chip_swap(part, 2 * h) for h, part in enumerate(grad_sent, 1)]

    out_own, *out_sent = run_once(
        functools.partial(pair_out_body, pairs, pair_base),
        [starts, after(mixed_parts[0], grad_own)] + mixed_parts[1:] + weights,
        [((rows, pair_width), BF16)] * pairs,
    )
    out_pairs = [out_own] + [chip_swap(after(part, *grad_parts), 2 * h) for h, part in enumerate(out_sent, 1)]
    kept, odd = run_once(
        functools.partial(stack_body, line_count, out_base),
        [starts] + out_pairs,
        [((line_count // 2 * rows, line_width), BF16)] * 2,
        [pltpu.VMEM((rows, whole_width), BF16)],
    )
    count, by = line_count // 2, 1
    first_out = arrived_out = line_swap(odd, by)
    while count > 1:
        count //= 2
        by *= 2
        total = kept.astype(F32) + arrived_out.astype(F32)
        kept, arrived_out = total[: count * rows], line_swap(total[count * rows :].astype(BF16), by)
    output = kept.astype(F32) + arrived_out.astype(F32)

    side = chip % 2
    used = [after(part, mixed_li) for part in cot_parts]
    near_cot = jnp.concatenate([columns_at(part, side, chip_width) for part in used], axis=0)
    far_cot = jnp.concatenate([columns_at(part, 1 - side, chip_width) for part in used], axis=0)
    got_cot = chip_swap(far_cot, 1)
    near_mixed = jnp.concatenate([after(part, grad_own) for part in mixed_parts], axis=0)
    got_mixed = chip_swap(near_mixed, 1)

    grad_query_li, back_ends, grad_inner = run(
        functools.partial(grad_gate_body, pairs - 1),
        columns,
        [
            tile(after(grad_own, out_own)),
            tile(query_li),
            tile(rate),
            tile(li_out),
            tile(li_spec),
            table("ahead"),
            table("back"),
        ]
        + [tile(part) for part in grad_parts],
        [(rows, F32), (rate.shape[0], F32), (rows, F32)],
        4 * pass_flops,
    )
    back_entering = entering_direct(
        back_ends, back_factors, here, True, [got_cot, got_mixed] + out_pairs[1:]
    )
    cot_rows = jnp.concatenate([near_cot, after(got_cot, back_ends)], axis=0)
    mixed_rows = jnp.concatenate([near_mixed, after(got_mixed, back_ends)], axis=0)

    def weight_share(which):
        return lax.dot_general(
            columns_at(cot_rows, which, width),
            mixed_rows,
            (((0,), (0,)), ((), ())),
            preferred_element_type=F32,
        )

    sent_share = weight_share(1 - core).astype(BF16)
    far_share = core_swap(sent_share)
    grad_weight = (weight_share(core) + far_share.astype(F32)) * grad_scale
    grad_key_li, grad_query_mr, grad_spec, tap_partial = run(
        grad_long_body,
        columns,
        [
            tile(after(grad_inner, sent_share)),
            tile(rate),
            tile(coef),
            tile(back_entering),
            tile(mixed_mr),
            tile(key_li),
            tile(query_mr),
            tile(mr_conv),
            tile(spec),
            table("ahead"),
            table("lags"),
        ],
        [(rows, F32), (rows, F32), (2 * rows, F32), (rows, F32)],
        4 * pass_flops,
    )
    grad_spec = after(grad_spec, first_out)
    own_product, prev_product = run(
        grad_taps_body,
        columns,
        [tile(grad_spec), tile(mr_spec), table("back")],
        [(rows, F32), (rows, BF16)],
        3 * pass_flops,
    )
    arrived = shifted(prev_product, -1)
    grad_key_mr, grad_value_mr = run(
        grad_product_body,
        columns,
        [tile(own_product), tile(arrived), tile(key_mr), tile(value_mr)],
        [(rows, F32), (rows, F32)],
        rows * columns,
    )

    tap_half = tap_partial.shape[0] // 2
    halves = tap_partial.reshape(2, tap_half, columns)
    own_half = lax.dynamic_index_in_dim(halves, core, 0, keepdims=False)
    far_half = lax.dynamic_index_in_dim(halves, 1 - core, 0, keepdims=False)
    chip_half = (own_half + core_swap(far_half)).astype(BF16)
    everywhere = [after(chip_half, prev_product, grad_weight)] + [chip_swap(chip_half, s) for s in range(1, chips)]
    plane_half = pair_sum([part.astype(F32) for part in everywhere]) * grad_scale
    other_half = core_swap(after(plane_half, arrived_out, grad_key_mr))
    grad_taps = jnp.where(
        core == 0,
        jnp.concatenate([plane_half, other_half], axis=0),
        jnp.concatenate([other_half, plane_half], axis=0),
    )

    return (
        output,
        grad_query_mr,
        grad_key_mr,
        grad_value_mr,
        grad_query_li,
        grad_key_li,
        grad_taps,
        grad_weight,
    )


def solution(mesh):
    rows = P("ctx", "fsdp")
    channels = P(None, "fsdp")
    return jax.shard_map(
        shards,
        mesh=mesh,
        in_specs=(rows,) * 5 + (channels,) * 3 + (P("fsdp"),) + (rows,) * 2,
        out_specs=(rows,) * 6 + (channels, rows),
        check_vma=False,
    )
```

```python
import functools
import math

import jax
import jax.numpy as jnp
import ml_dtypes
import numpy as np
from jax import lax
from jax.experimental import pallas as pl
from jax.experimental.pallas import tpu as pltpu
from jax.sharding import PartitionSpec as P

F32 = jnp.float32
BF16 = jnp.bfloat16
BLOCK = 512
TILE = 256
GROUP = 8


def split_parts(matrix):
    high = matrix.astype(ml_dtypes.bfloat16)
    low = (matrix - high.astype(np.float64)).astype(ml_dtypes.bfloat16)
    return high, low


def two_fold(matrix):
    high, low = split_parts(matrix)
    return np.concatenate([high, low], axis=1)


def three_fold(matrix):
    high, low = split_parts(matrix)
    return np.concatenate([high, low, high], axis=1)


@functools.lru_cache(maxsize=None)
def dft_tables(rows):
    size = 2 * rows
    angle = 2.0 * np.pi * (np.arange(rows)[:, None] + 0.5) * np.arange(size)[None, :] / size
    ahead = np.concatenate([np.cos(angle), -np.sin(angle)], axis=0)
    back = ahead.T * (2.0 / size)
    signed = np.concatenate([back[:rows], -back[rows:]], axis=0)
    lags = back[rows - np.arange(rows)]
    return {"ahead": two_fold(ahead), "back": three_fold(signed), "lags": three_fold(lags)}


def half_table(ahead):
    rows = ahead.shape[0] // 2
    high, low = ahead[:, :rows], ahead[:, 2 * rows : 3 * rows]
    return high, low


def apply2(table, x):
    return jnp.dot(table, jnp.concatenate([x, x], axis=0), preferred_element_type=F32)


def apply3(table, x):
    high = x.astype(BF16)
    low = (x - high.astype(F32)).astype(BF16)
    return jnp.dot(table, jnp.concatenate([high, high, low], axis=0), preferred_element_type=F32)


def to_spectrum(ahead, x):
    high, low = half_table(ahead)
    return apply3(jnp.concatenate([high, low, high], axis=1), x)


def to_spectrum_exact(ahead, x):
    return apply2(jnp.concatenate(half_table(ahead), axis=1), x)


def times(x, y):
    half = x.shape[0] // 2
    xr, xi, yr, yi = x[:half], x[half:], y[:half], y[half:]
    return jnp.concatenate([xr * yr - xi * yi, xr * yi + xi * yr], axis=0)


def times_conj(x, y):
    half = x.shape[0] // 2
    xr, xi, yr, yi = x[:half], x[half:], y[:half], y[half:]
    return jnp.concatenate([xr * yr + xi * yi, xi * yr - xr * yi], axis=0)


def group_places(columns):
    return lax.broadcasted_iota(jnp.int32, (GROUP, columns), 0).astype(F32)


def spread_modes(rate, weight, rows, shift, backward):
    columns = rate.shape[1]
    places = group_places(columns)
    if backward:
        places = (GROUP - 1.0) - places
    count = rows // GROUP
    order = range(count - 1, -1, -1) if backward else range(count)
    sums = [None] * count
    for m in range(rate.shape[0]):
        rate_m = rate[m : m + 1]
        current = weight[m : m + 1] * jnp.exp(-rate_m * (places + shift))
        stride = jnp.broadcast_to(jnp.exp(-rate_m * GROUP), current.shape)
        for step, g in enumerate(order):
            sums[g] = current if sums[g] is None else sums[g] + current
            if step < count - 1:
                current = current * stride
    return jnp.concatenate(sums, axis=0)


def fold_modes(signal, rate, backward):
    columns = rate.shape[1]
    places = group_places(columns)
    if not backward:
        places = (GROUP - 1.0) - places
    count = signal.shape[0] // GROUP
    order = range(count - 1, -1, -1) if backward else range(count)
    found = []
    for m in range(rate.shape[0]):
        rate_m = rate[m : m + 1]
        stride = jnp.broadcast_to(jnp.exp(-rate_m * GROUP), (GROUP, columns))
        running = None
        for g in order:
            piece = signal[g * GROUP : (g + 1) * GROUP]
            running = piece if running is None else running * stride + piece
        found.append(jnp.sum(running * jnp.exp(-rate_m * places), axis=0, keepdims=True))
    return jnp.concatenate(found, axis=0)


def spectra_body(taps, rate, coef, skip, ahead, mr_spec, li_spec):
    rows = taps.shape[0]
    table = ahead[...]
    mr_spec[...] = to_spectrum(table, taps[...])
    kernel = spread_modes(rate[...], coef[...], rows, 0.0, False)
    first = lax.broadcasted_iota(jnp.int32, kernel.shape, 0) == 0
    kernel = kernel + jnp.where(first, skip[...], 0.0)
    li_spec[...] = to_spectrum(table, kernel)


def short_body(before, product, query, key, mr_spec, li_spec, rate, ahead, back, spec, conv, mixed, inner, ends):
    rows = product.shape[0]
    x = jnp.concatenate([before[...], product[...]], axis=0)
    found = apply2(ahead[...], x)
    spec[...] = found
    filtered = -apply3(back[rows:], times(found, mr_spec[...]))
    conv[...] = filtered
    mixed_rows = (query[...].astype(F32) * filtered).astype(BF16)
    mixed[...] = mixed_rows
    rounded = (key[...].astype(F32) * mixed_rows.astype(F32)).astype(BF16)
    ends[...] = fold_modes(rounded.astype(F32), rate[...], False)
    inner[...] = apply3(back[:rows], times(to_spectrum_exact(ahead[...], rounded), li_spec[...]))


def gather_states(rate, gaps, states, rows):
    modes = rate.shape[0]
    total = jnp.zeros_like(rate)
    for k in range(states.shape[0] // modes):
        weight = jnp.exp(-rate * (jnp.maximum(gaps[k], 0.0) * float(rows)))
        total = total + jnp.where(gaps[k] >= 0.0, weight * states[k * modes : (k + 1) * modes], 0.0)
    return total


def long_body(gaps, inner, query, rate, coef, states, li_out, mixed):
    rows = inner.shape[0]
    entering = gather_states(rate[...], gaps, states, rows)
    total = inner[...] + spread_modes(rate[...], coef[...] * entering, rows, 1.0, False)
    li_out[...] = total
    mixed[...] = (query[...].astype(F32) * total).astype(BF16)


def split_body(count, base, starts, *rest):
    pieces, parts, whole = rest[: -count - 1], rest[-count - 1 : -1], rest[-1]
    for r, piece in enumerate(pieces):
        whole[:, pl.ds(pl.multiple_of(starts[base + r], 128), piece.shape[1])] = piece[...]
    for h, part in enumerate(parts):
        place = pl.multiple_of(starts[base + len(pieces) + h], 128)
        part[...] = whole[:, pl.ds(place, part.shape[1])]


def pair_grad_body(count, base, starts, *rest):
    parts, weights, results = rest[:count], rest[count : count + 4], rest[count + 4 :]
    rows = parts[0].shape[0]
    total = None
    for m, weight in enumerate(weights):
        place = pl.ds(pl.multiple_of(starts[base + m], 128), weight.shape[0])
        block = jnp.concatenate([part[:, place] for part in parts], axis=0)
        found = jnp.dot(block, weight[...], preferred_element_type=F32)
        total = found if total is None else total + found
    for h, result in enumerate(results):
        result[...] = total[h * rows : (h + 1) * rows].astype(result.dtype)


def pair_out_body(count, base, starts, *rest):
    mixed, weights, results = rest[:count], rest[count : count + 4], rest[count + 4 :]
    rows = mixed[0].shape[0]
    block = jnp.concatenate([part[...] for part in mixed], axis=0)
    for m, weight in enumerate(weights):
        place = pl.ds(pl.multiple_of(starts[base + m], 128), weight.shape[0])
        found = lax.dot_general(block, weight[...], (((1,), (1,)), ((), ())), preferred_element_type=F32)
        for h, result in enumerate(results):
            result[:, place] = found[h * rows : (h + 1) * rows].astype(BF16)


def stack_body(count, base, starts, *rest):
    pieces, stacks, whole = rest[:-3], rest[-3:-1], rest[-1]
    rows = whole.shape[0]
    for r, piece in enumerate(pieces):
        whole[:, pl.ds(pl.multiple_of(starts[base + r], 128), piece.shape[1])] = piece[...]
    for h in range(count):
        place = pl.multiple_of(starts[base + len(pieces) + h], 128)
        stack, at = stacks[h // (count // 2)], h % (count // 2)
        stack[at * rows : (at + 1) * rows] = whole[:, pl.ds(place, stack.shape[1])]


def grad_gate_body(count, own, query, rate, li_out, li_spec, ahead, back, *rest):
    parts, (grad_query, ends, inner) = rest[:count], rest[count:]
    rows = own.shape[0]
    total = own[...]
    for part in parts:
        total = total + part[...].astype(F32)
    grad_query[...] = total * li_out[...]
    gated = total * query[...].astype(F32)
    ends[...] = fold_modes(gated, rate[...], True)
    inner[...] = apply3(back[:rows], times_conj(to_spectrum(ahead[...], gated), li_spec[...]))


def grad_long_body(
    inner, rate, coef, entering, mixed_mr, key_li, query_mr, conv, spec, ahead, lags,
    grad_key_li, grad_query_mr, grad_spec, taps,
):
    rows = inner.shape[0]
    grad_input = inner[...] + spread_modes(rate[...], coef[...] * entering[...], rows, 1.0, True)
    grad_key_li[...] = grad_input * mixed_mr[...].astype(F32)
    grad_mixed_mr = grad_input * key_li[...].astype(F32)
    grad_query_mr[...] = grad_mixed_mr * conv[...]
    grad_conv = grad_mixed_mr * query_mr[...].astype(F32)
    found = to_spectrum(ahead[...], grad_conv)
    grad_spec[...] = found
    taps[...] = apply3(lags[...], times_conj(spec[...], found))


def grad_taps_body(grad_spec, mr_spec, back, own_product, prev_product):
    rows = own_product.shape[0]
    products = apply3(back[...], times_conj(grad_spec[...], mr_spec[...]))
    own_product[...] = products[:rows]
    prev_product[...] = products[rows:].astype(BF16)


def grad_product_body(own, arrived, key, value, grad_key, grad_value):
    total = own[...] + arrived[...].astype(F32)
    grad_key[...] = total * value[...].astype(F32)
    grad_value[...] = total * key[...].astype(F32)


def run(body, columns, inputs, outputs, flops):
    block = min(BLOCK, columns)
    tile = min(TILE, block)
    in_specs = []
    moved = 0
    for kind, array in inputs:
        if kind == "tile":
            in_specs.append(pl.BlockSpec((array.shape[0], block), lambda c: (0, c)))
        elif kind == "whole":
            in_specs.append(pl.BlockSpec(array.shape, lambda c: (0, 0)))
        else:
            in_specs.append(pl.BlockSpec(memory_space=pltpu.SMEM))
        moved += math.prod(array.shape) * array.dtype.itemsize
    for rows, dtype in outputs:
        moved += rows * columns * jnp.dtype(dtype).itemsize
    tiled = [kind == "tile" for kind, _ in inputs] + [True] * len(outputs)

    def body_by_tiles(*refs):
        for first in range(0, block, tile):
            body(*[ref.at[:, pl.ds(first, tile)] if cut else ref for ref, cut in zip(refs, tiled)])

    return pl.pallas_call(
        body_by_tiles,
        grid=(columns // block,),
        in_specs=in_specs,
        out_specs=[pl.BlockSpec((rows, block), lambda c: (0, c)) for rows, _ in outputs],
        out_shape=[jax.ShapeDtypeStruct((rows, columns), dtype) for rows, dtype in outputs],
        compiler_params=pltpu.CompilerParams(vmem_limit_bytes=56 * 1024 * 1024),
        cost_estimate=pl.CostEstimate(flops=flops, bytes_accessed=moved if flops else 0, transcendentals=0),
    )(*[array for _, array in inputs])


def run_once(body, inputs, outputs, scratch=()):
    def block(shape):
        return pl.BlockSpec(shape, lambda c: (0, 0))

    return pl.pallas_call(
        body,
        grid=(1,),
        in_specs=[pl.BlockSpec(memory_space=pltpu.SMEM)] + [block(array.shape) for array in inputs[1:]],
        out_specs=[block(shape) for shape, _ in outputs],
        out_shape=[jax.ShapeDtypeStruct(shape, dtype) for shape, dtype in outputs],
        scratch_shapes=scratch,
        compiler_params=pltpu.CompilerParams(vmem_limit_bytes=56 * 1024 * 1024),
        cost_estimate=pl.CostEstimate(flops=0, bytes_accessed=0, transcendentals=0),
    )(*inputs)


def chip_swap(x, by):
    size = lax.axis_size("ctx")
    return lax.ppermute(x, "ctx", [(i, i ^ (2 * by)) for i in range(size)])


def line_swap(x, by):
    size = lax.axis_size("fsdp")
    return lax.ppermute(x, "fsdp", [(i, i ^ by) for i in range(size)])


def core_swap(x):
    size = lax.axis_size("ctx")
    return lax.ppermute(x, "ctx", [(i, i ^ 1) for i in range(size)])


def shifted(x, by):
    size = lax.axis_size("ctx")
    return lax.ppermute(x, "ctx", [(i, i + by) for i in range(size) if 0 <= i + by < size])


def bit_reversed(count):
    order = [0]
    while len(order) < count:
        order = [2 * k for k in order] + [2 * k + 1 for k in order]
    return order


def columns_at(x, index, width):
    return lax.dynamic_slice_in_dim(x, index * width, width, 1)


def placed(pieces):
    width = pieces[0][1].shape[1]
    whole = jnp.zeros((pieces[0][1].shape[0], width * len(pieces)), pieces[0][1].dtype)
    for index, piece in pieces:
        whole = lax.dynamic_update_slice_in_dim(whole, piece, index * width, 1)
    return whole


def pair_sum(values):
    while len(values) > 1:
        values = [values[k] + values[k + 1] for k in range(0, len(values), 2)]
    return values[0]


def after(x, *others):
    return lax.optimization_barrier((x,) + others)[0]


def direct_factors(rate, rows, chip, backward):
    factors = [jnp.exp(-rate * float(rows))]
    for s in range(1, lax.axis_size("ctx") // 2):
        gap = (chip ^ s) - chip - 1 if backward else chip - (chip ^ s) - 1
        weight = jnp.exp(-rate * (2 * rows * jnp.maximum(gap, 0)).astype(F32))
        factors.append(jnp.where(gap >= 0, weight, 0.0))
    return factors


def entering_direct(ends, factors, here, backward, ready):
    block = factors[0]
    later_core = ((here & 1) != 0) != backward
    sibling = core_swap(ends)
    total = jnp.where(later_core, block * sibling + ends, block * ends + sibling)
    total = after(total, *ready)
    entering = jnp.zeros_like(ends)
    for s, weight in enumerate(factors[1:], 1):
        entering = entering + weight * chip_swap(total, s)
    return jnp.where(later_core, block * entering + sibling, entering)


def shards(
    query_mr,
    key_mr,
    value_mr,
    query_li,
    key_li,
    mr_taps,
    li_time,
    li_residue,
    li_skip,
    out_weight,
    cotangent,
):
    rows, columns = query_mr.shape
    ctx_count = lax.axis_size("ctx")
    line_count = lax.axis_size("fsdp")
    chips = ctx_count // 2
    here = lax.axis_index("ctx")
    chip, core = here // 2, here % 2
    line = lax.axis_index("fsdp")
    grad_scale = 1.0 / math.sqrt(rows * ctx_count)
    tables = {name: jnp.asarray(table) for name, table in dft_tables(rows).items()}
    width = out_weight.shape[0]
    chip_width = 2 * width
    pass_flops = 2 * (2 * rows) * (2 * rows) * columns

    def tile(x):
        return ("tile", x)

    def table(name):
        return ("whole", tables[name])

    mr_product = (key_mr.astype(F32) * value_mr.astype(F32)).astype(BF16)
    before = shifted(mr_product, 1)
    cot_line = [cotangent] + [line_swap(after(cotangent, mr_product), r) for r in range(1, line_count)]
    pairs = chips // 2
    pair = chip // 2
    pair_width = 4 * width

    sibling_weight = core_swap(out_weight)
    line_width = cotangent.shape[1]
    places = [(line ^ r) * line_width for r in range(line_count)] + [(pair ^ h) * pair_width for h in range(pairs)]
    pair_base = len(places)
    places += [((here & 3) ^ m) * width for m in range(4)]
    out_base = len(places)
    places += [(pair ^ h) * pair_width for h in range(pairs)]
    places += [(line ^ r) * line_width for r in bit_reversed(line_count)]
    starts = jnp.stack(places)

    rate = 1.0 / after(li_time, mr_product)
    beside = chip_swap(after(out_weight, before), 1)
    coef = li_residue * jnp.sqrt(-jnp.expm1(-2.0 * rate))
    back_factors = lax.optimization_barrier(direct_factors(rate, rows, here // 2, True))
    mr_spec, li_spec = run(
        spectra_body,
        columns,
        [tile(mr_taps), tile(rate), tile(coef), tile(li_skip[None, :]), table("ahead")],
        [(2 * rows, F32), (2 * rows, F32)],
        0,
    )
    spec, mr_conv, mixed_mr, li_inner, ends = run(
        short_body,
        columns,
        [
            tile(after(before, sibling_weight)),
            tile(mr_product),
            tile(query_mr),
            tile(key_li),
            tile(mr_spec),
            tile(li_spec),
            tile(rate),
            table("ahead"),
            table("back"),
        ],
        [(2 * rows, F32), (rows, F32), (rows, BF16), (rows, F32), (rate.shape[0], F32)],
        0,
    )

    whole_width = line_width * line_count
    cot_pairs = run_once(
        functools.partial(split_body, pairs, 0),
        [starts] + [after(piece, ends) for piece in cot_line],
        [((rows, pair_width), BF16)] * pairs,
        [pltpu.VMEM((rows, whole_width), BF16)],
    )
    cot_parts = [cot_pairs[0]] + [chip_swap(cot_pairs[h], 2 * h) for h in range(1, pairs)]
    states = lax.all_gather(after(ends, beside, *cot_parts[:1]), "ctx").reshape(-1, columns)
    gaps = (here - 1 - jnp.arange(ctx_count, dtype=jnp.int32)).astype(F32)
    li_out, mixed_li = run(
        long_body,
        columns,
        [("scalar", gaps), tile(li_inner), tile(query_li), tile(rate), tile(coef), tile(states)],
        [(rows, F32), (rows, BF16)],
        0,
    )

    mixed_parts = [mixed_li] + [chip_swap(mixed_li, 2 * h) for h in range(1, pairs)]
    weights = [out_weight, sibling_weight, beside, core_swap(after(beside, cot_pairs[0]))]

    share_flops = 2 * rows * columns * pair_width * pairs
    grad_own, *grad_sent = run(
        functools.partial(pair_grad_body, pairs, pair_base),
        columns,
        [("scalar", starts)] + [("whole", after(part, mixed_li)) for part in cot_parts] + [tile(weight) for weight in weights],
        [(rows, F32)] + [(rows, BF16)] * (pairs - 1),
        share_flops,
    )
    grad_parts = [chip_swap(part, 2 * h) for h, part in enumerate(grad_sent, 1)]

    out_own, *out_sent = run_once(
        functools.partial(pair_out_body, pairs, pair_base),
        [starts, after(mixed_parts[0], grad_own)] + mixed_parts[1:] + weights,
        [((rows, pair_width), BF16)] * pairs,
    )
    out_pairs = [out_own] + [chip_swap(after(part, *grad_parts), 2 * h) for h, part in enumerate(out_sent, 1)]
    kept, odd = run_once(
        functools.partial(stack_body, line_count, out_base),
        [starts] + out_pairs,
        [((line_count // 2 * rows, line_width), BF16)] * 2,
        [pltpu.VMEM((rows, whole_width), BF16)],
    )
    count, by = line_count // 2, 1
    first_out = arrived_out = line_swap(odd, by)
    while count > 1:
        count //= 2
        by *= 2
        total = kept.astype(F32) + arrived_out.astype(F32)
        kept, arrived_out = total[: count * rows], line_swap(total[count * rows :].astype(BF16), by)
    output = kept.astype(F32) + arrived_out.astype(F32)

    side = chip % 2
    used = [after(part, mixed_li) for part in cot_parts]
    near_cot = jnp.concatenate([columns_at(part, side, chip_width) for part in used], axis=0)
    far_cot = jnp.concatenate([columns_at(part, 1 - side, chip_width) for part in used], axis=0)
    got_cot = chip_swap(far_cot, 1)
    near_mixed = jnp.concatenate([after(part, grad_own) for part in mixed_parts], axis=0)
    got_mixed = chip_swap(near_mixed, 1)

    grad_query_li, back_ends, grad_inner = run(
        functools.partial(grad_gate_body, pairs - 1),
        columns,
        [
            tile(after(grad_own, out_own)),
            tile(query_li),
            tile(rate),
            tile(li_out),
            tile(li_spec),
            table("ahead"),
            table("back"),
        ]
        + [tile(part) for part in grad_parts],
        [(rows, F32), (rate.shape[0], F32), (rows, F32)],
        4 * pass_flops,
    )
    back_entering = entering_direct(
        back_ends, back_factors, here, True, [got_cot, got_mixed] + out_pairs[1:]
    )
    grad_key_li, grad_query_mr, grad_spec, tap_partial = run(
        grad_long_body,
        columns,
        [
            tile(after(grad_inner, odd)),
            tile(rate),
            tile(coef),
            tile(back_entering),
            tile(mixed_mr),
            tile(key_li),
            tile(query_mr),
            tile(mr_conv),
            tile(spec),
            table("ahead"),
            table("lags"),
        ],
        [(rows, F32), (rows, F32), (2 * rows, F32), (rows, F32)],
        4 * pass_flops,
    )
    cot_rows = jnp.concatenate([near_cot, after(got_cot, back_ends)], axis=0)
    mixed_rows = jnp.concatenate([near_mixed, after(got_mixed, tap_partial)], axis=0)

    def weight_share(which):
        return lax.dot_general(
            columns_at(cot_rows, which, width),
            mixed_rows,
            (((0,), (0,)), ((), ())),
            preferred_element_type=F32,
        )

    sent_share = weight_share(1 - core).astype(BF16)
    far_share = core_swap(sent_share)
    grad_weight = (weight_share(core) + far_share.astype(F32)) * grad_scale
    grad_spec = after(grad_spec, first_out)
    own_product, prev_product = run(
        grad_taps_body,
        columns,
        [tile(grad_spec), tile(mr_spec), table("back")],
        [(rows, F32), (rows, BF16)],
        3 * pass_flops,
    )
    arrived = shifted(prev_product, -1)
    grad_key_mr, grad_value_mr = run(
        grad_product_body,
        columns,
        [tile(own_product), tile(arrived), tile(key_mr), tile(value_mr)],
        [(rows, F32), (rows, F32)],
        rows * columns,
    )

    tap_half = tap_partial.shape[0] // 2
    halves = tap_partial.reshape(2, tap_half, columns)
    own_half = lax.dynamic_index_in_dim(halves, core, 0, keepdims=False)
    far_half = lax.dynamic_index_in_dim(halves, 1 - core, 0, keepdims=False)
    chip_half = (own_half + core_swap(after(far_half, first_out))).astype(BF16)
    everywhere = [after(chip_half, prev_product, grad_weight)] + [chip_swap(chip_half, s) for s in range(1, chips)]
    plane_half = pair_sum([part.astype(F32) for part in everywhere]) * grad_scale
    other_half = core_swap(after(plane_half, arrived_out))
    grad_taps = jnp.where(
        core == 0,
        jnp.concatenate([plane_half, other_half], axis=0),
        jnp.concatenate([other_half, plane_half], axis=0),
    )

    return (
        output,
        grad_query_mr,
        grad_key_mr,
        grad_value_mr,
        grad_query_li,
        grad_key_li,
        grad_taps,
        grad_weight,
    )


def solution(mesh):
    rows = P("ctx", "fsdp")
    channels = P(None, "fsdp")
    return jax.shard_map(
        shards,
        mesh=mesh,
        in_specs=(rows,) * 5 + (channels,) * 3 + (P("fsdp"),) + (rows,) * 2,
        out_specs=(rows,) * 6 + (channels, rows),
        check_vma=False,
    )
```

```python
import functools
import math

import jax
import jax.numpy as jnp
import ml_dtypes
import numpy as np
from jax import lax
from jax.experimental import pallas as pl
from jax.experimental.pallas import tpu as pltpu
from jax.sharding import PartitionSpec as P

F32 = jnp.float32
BF16 = jnp.bfloat16
BLOCK = 1024
TILE = 256
GROUP = 8


def split_parts(matrix):
    high = matrix.astype(ml_dtypes.bfloat16)
    low = (matrix - high.astype(np.float64)).astype(ml_dtypes.bfloat16)
    return high, low


def two_fold(matrix):
    high, low = split_parts(matrix)
    return np.concatenate([high, low], axis=1)


def three_fold(matrix):
    high, low = split_parts(matrix)
    return np.concatenate([high, low, high], axis=1)


@functools.lru_cache(maxsize=None)
def dft_tables(rows):
    size = 2 * rows
    angle = 2.0 * np.pi * (np.arange(rows)[:, None] + 0.5) * np.arange(size)[None, :] / size
    ahead = np.concatenate([np.cos(angle), -np.sin(angle)], axis=0)
    back = ahead.T * (2.0 / size)
    signed = np.concatenate([back[:rows], -back[rows:]], axis=0)
    lags = back[rows - np.arange(rows)]
    return {"ahead": two_fold(ahead), "back": three_fold(signed), "lags": three_fold(lags)}


def half_table(ahead):
    rows = ahead.shape[0] // 2
    high, low = ahead[:, :rows], ahead[:, 2 * rows : 3 * rows]
    return high, low


def apply2(table, x):
    return jnp.dot(table, jnp.concatenate([x, x], axis=0), preferred_element_type=F32)


def apply3(table, x):
    high = x.astype(BF16)
    low = (x - high.astype(F32)).astype(BF16)
    return jnp.dot(table, jnp.concatenate([high, high, low], axis=0), preferred_element_type=F32)


def to_spectrum(ahead, x):
    high, low = half_table(ahead)
    return apply3(jnp.concatenate([high, low, high], axis=1), x)


def to_spectrum_exact(ahead, x):
    return apply2(jnp.concatenate(half_table(ahead), axis=1), x)


def times(x, y):
    half = x.shape[0] // 2
    xr, xi, yr, yi = x[:half], x[half:], y[:half], y[half:]
    return jnp.concatenate([xr * yr - xi * yi, xr * yi + xi * yr], axis=0)


def times_conj(x, y):
    half = x.shape[0] // 2
    xr, xi, yr, yi = x[:half], x[half:], y[:half], y[half:]
    return jnp.concatenate([xr * yr + xi * yi, xi * yr - xr * yi], axis=0)


def group_places(columns):
    return lax.broadcasted_iota(jnp.int32, (GROUP, columns), 0).astype(F32)


def spread_modes(rate, weight, rows, shift, backward):
    columns = rate.shape[1]
    places = group_places(columns)
    if backward:
        places = (GROUP - 1.0) - places
    count = rows // GROUP
    order = range(count - 1, -1, -1) if backward else range(count)
    sums = [None] * count
    for m in range(rate.shape[0]):
        rate_m = rate[m : m + 1]
        current = weight[m : m + 1] * jnp.exp(-rate_m * (places + shift))
        stride = jnp.broadcast_to(jnp.exp(-rate_m * GROUP), current.shape)
        for step, g in enumerate(order):
            sums[g] = current if sums[g] is None else sums[g] + current
            if step < count - 1:
                current = current * stride
    return jnp.concatenate(sums, axis=0)


def fold_modes(signal, rate, backward):
    columns = rate.shape[1]
    places = group_places(columns)
    if not backward:
        places = (GROUP - 1.0) - places
    count = signal.shape[0] // GROUP
    order = range(count - 1, -1, -1) if backward else range(count)
    found = []
    for m in range(rate.shape[0]):
        rate_m = rate[m : m + 1]
        stride = jnp.broadcast_to(jnp.exp(-rate_m * GROUP), (GROUP, columns))
        running = None
        for g in order:
            piece = signal[g * GROUP : (g + 1) * GROUP]
            running = piece if running is None else running * stride + piece
        found.append(jnp.sum(running * jnp.exp(-rate_m * places), axis=0, keepdims=True))
    return jnp.concatenate(found, axis=0)


def spectra_body(taps, rate, coef, skip, ahead, mr_spec, li_spec):
    rows = taps.shape[0]
    table = ahead[...]
    mr_spec[...] = to_spectrum(table, taps[...])
    kernel = spread_modes(rate[...], coef[...], rows, 0.0, False)
    first = lax.broadcasted_iota(jnp.int32, kernel.shape, 0) == 0
    kernel = kernel + jnp.where(first, skip[...], 0.0)
    li_spec[...] = to_spectrum(table, kernel)


def short_body(before, product, query, key, mr_spec, li_spec, rate, ahead, back, spec, conv, mixed, inner, ends):
    rows = product.shape[0]
    x = jnp.concatenate([before[...], product[...]], axis=0)
    found = apply2(ahead[...], x)
    spec[...] = found
    filtered = -apply3(back[rows:], times(found, mr_spec[...]))
    conv[...] = filtered
    mixed_rows = (query[...].astype(F32) * filtered).astype(BF16)
    mixed[...] = mixed_rows
    rounded = (key[...].astype(F32) * mixed_rows.astype(F32)).astype(BF16)
    ends[...] = fold_modes(rounded.astype(F32), rate[...], False)
    inner[...] = apply3(back[:rows], times(to_spectrum_exact(ahead[...], rounded), li_spec[...]))


def gather_states(rate, gaps, states, rows):
    modes = rate.shape[0]
    total = jnp.zeros_like(rate)
    for k in range(states.shape[0] // modes):
        weight = jnp.exp(-rate * (jnp.maximum(gaps[k], 0.0) * float(rows)))
        total = total + jnp.where(gaps[k] >= 0.0, weight * states[k * modes : (k + 1) * modes], 0.0)
    return total


def long_body(gaps, inner, query, rate, coef, states, li_out, mixed):
    rows = inner.shape[0]
    entering = gather_states(rate[...], gaps, states, rows)
    total = inner[...] + spread_modes(rate[...], coef[...] * entering, rows, 1.0, False)
    li_out[...] = total
    mixed[...] = (query[...].astype(F32) * total).astype(BF16)


def split_body(count, base, starts, *rest):
    pieces, parts, whole = rest[: -count - 1], rest[-count - 1 : -1], rest[-1]
    for r, piece in enumerate(pieces):
        whole[:, pl.ds(pl.multiple_of(starts[base + r], 128), piece.shape[1])] = piece[...]
    for h, part in enumerate(parts):
        place = pl.multiple_of(starts[base + len(pieces) + h], 128)
        part[...] = whole[:, pl.ds(place, part.shape[1])]


def pair_grad_body(count, base, starts, *rest):
    parts, weights, results = rest[:count], rest[count : count + 4], rest[count + 4 :]
    rows = parts[0].shape[0]
    total = None
    for m, weight in enumerate(weights):
        place = pl.ds(pl.multiple_of(starts[base + m], 128), weight.shape[0])
        block = jnp.concatenate([part[:, place] for part in parts], axis=0)
        found = jnp.dot(block, weight[...], preferred_element_type=F32)
        total = found if total is None else total + found
    for h, result in enumerate(results):
        result[...] = total[h * rows : (h + 1) * rows].astype(result.dtype)


def pair_out_body(count, base, starts, *rest):
    mixed, weights, results = rest[:count], rest[count : count + 4], rest[count + 4 :]
    rows = mixed[0].shape[0]
    block = jnp.concatenate([part[...] for part in mixed], axis=0)
    for m, weight in enumerate(weights):
        place = pl.ds(pl.multiple_of(starts[base + m], 128), weight.shape[0])
        found = lax.dot_general(block, weight[...], (((1,), (1,)), ((), ())), preferred_element_type=F32)
        for h, result in enumerate(results):
            result[:, place] = found[h * rows : (h + 1) * rows].astype(BF16)


def stack_body(count, base, starts, *rest):
    pieces, stacks, whole = rest[:-3], rest[-3:-1], rest[-1]
    rows = whole.shape[0]
    for r, piece in enumerate(pieces):
        whole[:, pl.ds(pl.multiple_of(starts[base + r], 128), piece.shape[1])] = piece[...]
    for h in range(count):
        place = pl.multiple_of(starts[base + len(pieces) + h], 128)
        stack, at = stacks[h // (count // 2)], h % (count // 2)
        stack[at * rows : (at + 1) * rows] = whole[:, pl.ds(place, stack.shape[1])]


def grad_gate_body(count, own, query, rate, li_out, li_spec, ahead, back, *rest):
    parts, (grad_query, ends, inner) = rest[:count], rest[count:]
    rows = own.shape[0]
    total = own[...]
    for part in parts:
        total = total + part[...].astype(F32)
    grad_query[...] = total * li_out[...]
    gated = total * query[...].astype(F32)
    ends[...] = fold_modes(gated, rate[...], True)
    inner[...] = apply3(back[:rows], times_conj(to_spectrum(ahead[...], gated), li_spec[...]))


def grad_long_body(
    inner, rate, coef, entering, mixed_mr, key_li, query_mr, conv, spec, ahead, lags,
    grad_key_li, grad_query_mr, grad_spec, taps,
):
    rows = inner.shape[0]
    grad_input = inner[...] + spread_modes(rate[...], coef[...] * entering[...], rows, 1.0, True)
    grad_key_li[...] = grad_input * mixed_mr[...].astype(F32)
    grad_mixed_mr = grad_input * key_li[...].astype(F32)
    grad_query_mr[...] = grad_mixed_mr * conv[...]
    grad_conv = grad_mixed_mr * query_mr[...].astype(F32)
    found = to_spectrum(ahead[...], grad_conv)
    grad_spec[...] = found
    taps[...] = apply3(lags[...], times_conj(spec[...], found))


def grad_taps_body(grad_spec, mr_spec, back, own_product, prev_product):
    rows = own_product.shape[0]
    products = apply3(back[...], times_conj(grad_spec[...], mr_spec[...]))
    own_product[...] = products[:rows]
    prev_product[...] = products[rows:].astype(BF16)


def grad_product_body(own, arrived, key, value, grad_key, grad_value):
    total = own[...] + arrived[...].astype(F32)
    grad_key[...] = total * value[...].astype(F32)
    grad_value[...] = total * key[...].astype(F32)


def run(body, columns, inputs, outputs, flops):
    block = min(BLOCK, columns)
    tile = min(TILE, block)
    in_specs = []
    moved = 0
    for kind, array in inputs:
        if kind == "tile":
            in_specs.append(pl.BlockSpec((array.shape[0], block), lambda c: (0, c)))
        elif kind == "whole":
            in_specs.append(pl.BlockSpec(array.shape, lambda c: (0, 0)))
        else:
            in_specs.append(pl.BlockSpec(memory_space=pltpu.SMEM))
        moved += math.prod(array.shape) * array.dtype.itemsize
    for rows, dtype in outputs:
        moved += rows * columns * jnp.dtype(dtype).itemsize
    tiled = [kind == "tile" for kind, _ in inputs] + [True] * len(outputs)

    def body_by_tiles(*refs):
        for first in range(0, block, tile):
            body(*[ref.at[:, pl.ds(first, tile)] if cut else ref for ref, cut in zip(refs, tiled)])

    return pl.pallas_call(
        body_by_tiles,
        grid=(columns // block,),
        in_specs=in_specs,
        out_specs=[pl.BlockSpec((rows, block), lambda c: (0, c)) for rows, _ in outputs],
        out_shape=[jax.ShapeDtypeStruct((rows, columns), dtype) for rows, dtype in outputs],
        compiler_params=pltpu.CompilerParams(vmem_limit_bytes=56 * 1024 * 1024),
        cost_estimate=pl.CostEstimate(flops=flops, bytes_accessed=moved if flops else 0, transcendentals=0),
    )(*[array for _, array in inputs])


def run_once(body, inputs, outputs, scratch=()):
    def block(shape):
        return pl.BlockSpec(shape, lambda c: (0, 0))

    return pl.pallas_call(
        body,
        grid=(1,),
        in_specs=[pl.BlockSpec(memory_space=pltpu.SMEM)] + [block(array.shape) for array in inputs[1:]],
        out_specs=[block(shape) for shape, _ in outputs],
        out_shape=[jax.ShapeDtypeStruct(shape, dtype) for shape, dtype in outputs],
        scratch_shapes=scratch,
        compiler_params=pltpu.CompilerParams(vmem_limit_bytes=56 * 1024 * 1024),
        cost_estimate=pl.CostEstimate(flops=0, bytes_accessed=0, transcendentals=0),
    )(*inputs)


def chip_swap(x, by):
    size = lax.axis_size("ctx")
    return lax.ppermute(x, "ctx", [(i, i ^ (2 * by)) for i in range(size)])


def line_swap(x, by):
    size = lax.axis_size("fsdp")
    return lax.ppermute(x, "fsdp", [(i, i ^ by) for i in range(size)])


def core_swap(x):
    size = lax.axis_size("ctx")
    return lax.ppermute(x, "ctx", [(i, i ^ 1) for i in range(size)])


def shifted(x, by):
    size = lax.axis_size("ctx")
    return lax.ppermute(x, "ctx", [(i, i + by) for i in range(size) if 0 <= i + by < size])


def bit_reversed(count):
    order = [0]
    while len(order) < count:
        order = [2 * k for k in order] + [2 * k + 1 for k in order]
    return order


def columns_at(x, index, width):
    return lax.dynamic_slice_in_dim(x, index * width, width, 1)


def placed(pieces):
    width = pieces[0][1].shape[1]
    whole = jnp.zeros((pieces[0][1].shape[0], width * len(pieces)), pieces[0][1].dtype)
    for index, piece in pieces:
        whole = lax.dynamic_update_slice_in_dim(whole, piece, index * width, 1)
    return whole


def pair_sum(values):
    while len(values) > 1:
        values = [values[k] + values[k + 1] for k in range(0, len(values), 2)]
    return values[0]


def after(x, *others):
    return lax.optimization_barrier((x,) + others)[0]


def direct_factors(rate, rows, chip, backward):
    factors = [jnp.exp(-rate * float(rows))]
    for s in range(1, lax.axis_size("ctx") // 2):
        gap = (chip ^ s) - chip - 1 if backward else chip - (chip ^ s) - 1
        weight = jnp.exp(-rate * (2 * rows * jnp.maximum(gap, 0)).astype(F32))
        factors.append(jnp.where(gap >= 0, weight, 0.0))
    return factors


def entering_direct(ends, factors, here, backward, ready):
    block = factors[0]
    later_core = ((here & 1) != 0) != backward
    sibling = core_swap(ends)
    total = jnp.where(later_core, block * sibling + ends, block * ends + sibling)
    total = after(total, *ready)
    entering = jnp.zeros_like(ends)
    for s, weight in enumerate(factors[1:], 1):
        entering = entering + weight * chip_swap(total, s)
    return jnp.where(later_core, block * entering + sibling, entering)


def shards(
    query_mr,
    key_mr,
    value_mr,
    query_li,
    key_li,
    mr_taps,
    li_time,
    li_residue,
    li_skip,
    out_weight,
    cotangent,
):
    rows, columns = query_mr.shape
    ctx_count = lax.axis_size("ctx")
    line_count = lax.axis_size("fsdp")
    chips = ctx_count // 2
    here = lax.axis_index("ctx")
    chip, core = here // 2, here % 2
    line = lax.axis_index("fsdp")
    grad_scale = 1.0 / math.sqrt(rows * ctx_count)
    tables = {name: jnp.asarray(table) for name, table in dft_tables(rows).items()}
    width = out_weight.shape[0]
    chip_width = 2 * width
    pass_flops = 2 * (2 * rows) * (2 * rows) * columns

    def tile(x):
        return ("tile", x)

    def table(name):
        return ("whole", tables[name])

    mr_product = (key_mr.astype(F32) * value_mr.astype(F32)).astype(BF16)
    before = shifted(mr_product, 1)
    cot_line = [cotangent] + [line_swap(after(cotangent, mr_product), r) for r in range(1, line_count)]
    pairs = chips // 2
    pair = chip // 2
    pair_width = 4 * width

    sibling_weight = core_swap(out_weight)
    line_width = cotangent.shape[1]
    places = [(line ^ r) * line_width for r in range(line_count)] + [(pair ^ h) * pair_width for h in range(pairs)]
    pair_base = len(places)
    places += [((here & 3) ^ m) * width for m in range(4)]
    out_base = len(places)
    places += [(pair ^ h) * pair_width for h in range(pairs)]
    places += [(line ^ r) * line_width for r in bit_reversed(line_count)]
    starts = jnp.stack(places)

    rate = 1.0 / after(li_time, mr_product)
    beside = chip_swap(after(out_weight, before), 1)
    coef = li_residue * jnp.sqrt(-jnp.expm1(-2.0 * rate))
    back_factors = lax.optimization_barrier(direct_factors(rate, rows, here // 2, True))
    mr_spec, li_spec = run(
        spectra_body,
        columns,
        [tile(mr_taps), tile(rate), tile(coef), tile(li_skip[None, :]), table("ahead")],
        [(2 * rows, F32), (2 * rows, F32)],
        0,
    )
    spec, mr_conv, mixed_mr, li_inner, ends = run(
        short_body,
        columns,
        [
            tile(after(before, sibling_weight)),
            tile(mr_product),
            tile(query_mr),
            tile(key_li),
            tile(mr_spec),
            tile(li_spec),
            tile(rate),
            table("ahead"),
            table("back"),
        ],
        [(2 * rows, F32), (rows, F32), (rows, BF16), (rows, F32), (rate.shape[0], F32)],
        0,
    )

    whole_width = line_width * line_count
    cot_pairs = run_once(
        functools.partial(split_body, pairs, 0),
        [starts] + [after(piece, ends) for piece in cot_line],
        [((rows, pair_width), BF16)] * pairs,
        [pltpu.VMEM((rows, whole_width), BF16)],
    )
    cot_parts = [cot_pairs[0]] + [chip_swap(cot_pairs[h], 2 * h) for h in range(1, pairs)]
    states = lax.all_gather(after(ends, beside, *cot_parts[:1]), "ctx").reshape(-1, columns)
    gaps = (here - 1 - jnp.arange(ctx_count, dtype=jnp.int32)).astype(F32)
    li_out, mixed_li = run(
        long_body,
        columns,
        [("scalar", gaps), tile(li_inner), tile(query_li), tile(rate), tile(coef), tile(states)],
        [(rows, F32), (rows, BF16)],
        0,
    )

    mixed_parts = [mixed_li] + [chip_swap(mixed_li, 2 * h) for h in range(1, pairs)]
    weights = [out_weight, sibling_weight, beside, core_swap(after(beside, cot_pairs[0]))]

    share_flops = 2 * rows * columns * pair_width * pairs
    grad_own, *grad_sent = run(
        functools.partial(pair_grad_body, pairs, pair_base),
        columns,
        [("scalar", starts)] + [("whole", after(part, mixed_li)) for part in cot_parts] + [tile(weight) for weight in weights],
        [(rows, F32)] + [(rows, BF16)] * (pairs - 1),
        share_flops,
    )
    grad_parts = [chip_swap(part, 2 * h) for h, part in enumerate(grad_sent, 1)]

    out_own, *out_sent = run_once(
        functools.partial(pair_out_body, pairs, pair_base),
        [starts, after(mixed_parts[0], grad_own)] + mixed_parts[1:] + weights,
        [((rows, pair_width), BF16)] * pairs,
    )
    out_pairs = [out_own] + [chip_swap(after(part, *grad_parts), 2 * h) for h, part in enumerate(out_sent, 1)]
    kept, odd = run_once(
        functools.partial(stack_body, line_count, out_base),
        [starts] + out_pairs,
        [((line_count // 2 * rows, line_width), BF16)] * 2,
        [pltpu.VMEM((rows, whole_width), BF16)],
    )
    count, by = line_count // 2, 1
    first_out = arrived_out = line_swap(odd, by)
    while count > 1:
        count //= 2
        by *= 2
        total = kept.astype(F32) + arrived_out.astype(F32)
        kept, arrived_out = total[: count * rows], line_swap(total[count * rows :].astype(BF16), by)
    output = kept.astype(F32) + arrived_out.astype(F32)

    side = chip % 2
    used = [after(part, mixed_li) for part in cot_parts]
    near_cot = jnp.concatenate([columns_at(part, side, chip_width) for part in used], axis=0)
    far_cot = jnp.concatenate([columns_at(part, 1 - side, chip_width) for part in used], axis=0)
    got_cot = chip_swap(far_cot, 1)
    near_mixed = jnp.concatenate([after(part, grad_own) for part in mixed_parts], axis=0)
    got_mixed = chip_swap(near_mixed, 1)

    grad_query_li, back_ends, grad_inner = run(
        functools.partial(grad_gate_body, pairs - 1),
        columns,
        [
            tile(after(grad_own, out_own)),
            tile(query_li),
            tile(rate),
            tile(li_out),
            tile(li_spec),
            table("ahead"),
            table("back"),
        ]
        + [tile(part) for part in grad_parts],
        [(rows, F32), (rate.shape[0], F32), (rows, F32)],
        4 * pass_flops,
    )
    back_entering = entering_direct(
        back_ends, back_factors, here, True, [got_cot, got_mixed] + out_pairs[1:]
    )
    cot_rows = jnp.concatenate([near_cot, after(got_cot, back_ends)], axis=0)
    mixed_rows = jnp.concatenate([near_mixed, after(got_mixed, back_ends)], axis=0)

    def weight_share(which):
        return lax.dot_general(
            columns_at(cot_rows, which, width),
            mixed_rows,
            (((0,), (0,)), ((), ())),
            preferred_element_type=F32,
        )

    sent_share = weight_share(1 - core).astype(BF16)
    far_share = core_swap(sent_share)
    grad_weight = (weight_share(core) + far_share.astype(F32)) * grad_scale
    grad_key_li, grad_query_mr, grad_spec, tap_partial = run(
        grad_long_body,
        columns,
        [
            tile(after(grad_inner, sent_share)),
            tile(rate),
            tile(coef),
            tile(back_entering),
            tile(mixed_mr),
            tile(key_li),
            tile(query_mr),
            tile(mr_conv),
            tile(spec),
            table("ahead"),
            table("lags"),
        ],
        [(rows, F32), (rows, F32), (2 * rows, F32), (rows, F32)],
        4 * pass_flops,
    )
    grad_spec = after(grad_spec, first_out)
    own_product, prev_product = run(
        grad_taps_body,
        columns,
        [tile(grad_spec), tile(mr_spec), table("back")],
        [(rows, F32), (rows, BF16)],
        3 * pass_flops,
    )
    arrived = shifted(prev_product, -1)
    grad_key_mr, grad_value_mr = run(
        grad_product_body,
        columns,
        [tile(own_product), tile(arrived), tile(key_mr), tile(value_mr)],
        [(rows, F32), (rows, F32)],
        rows * columns,
    )

    tap_half = tap_partial.shape[0] // 2
    halves = tap_partial.reshape(2, tap_half, columns)
    own_half = lax.dynamic_index_in_dim(halves, core, 0, keepdims=False)
    far_half = lax.dynamic_index_in_dim(halves, 1 - core, 0, keepdims=False)
    chip_half = (own_half + core_swap(far_half)).astype(BF16)
    everywhere = [after(chip_half, prev_product, grad_weight)] + [chip_swap(chip_half, s) for s in range(1, chips)]
    plane_half = pair_sum([part.astype(F32) for part in everywhere]) * grad_scale
    other_half = core_swap(after(plane_half, arrived_out))
    grad_taps = jnp.where(
        core == 0,
        jnp.concatenate([plane_half, other_half], axis=0),
        jnp.concatenate([other_half, plane_half], axis=0),
    )

    return (
        output,
        grad_query_mr,
        grad_key_mr,
        grad_value_mr,
        grad_query_li,
        grad_key_li,
        grad_taps,
        grad_weight,
    )


def solution(mesh):
    rows = P("ctx", "fsdp")
    channels = P(None, "fsdp")
    return jax.shard_map(
        shards,
        mesh=mesh,
        in_specs=(rows,) * 5 + (channels,) * 3 + (P("fsdp"),) + (rows,) * 2,
        out_specs=(rows,) * 6 + (channels, rows),
        check_vma=False,
    )
```
